32 devices in a mesh: section: 4 (over y, x), batch: 8 (over z, core).
Axes of the slice: x: 2, y: 2, z: 4, core: 2. Of those that a mesh axis runs over, the one named last changes fastest.
Arguments:
- images: bfloat16 [4, 2048, 512], P(None, 'batch'), may hold values from -6 to 6
- crop_big: int32 [4, 8], P(None, 'batch'), may hold values from 0 to 2
- w_point: float32 [4, 512, 512], P('section', 'batch')
- w_spatial: float32 [4, 9, 512, 512], P('section', None, 'batch')
- norm_params: float32 [4, 4, 512], P('section'), as said below
- mom_point: float32 [4, 512, 512], P('section', 'batch'), may hold values from -0.078125 to 0.078125
- mom_spatial: float32 [4, 9, 512, 512], P('section', None, 'batch'), may hold values from -0.02734375 to 0.02734375
- mom_norm: float32 [4, 4, 512], P('section'), may hold values from -0.4375 to 0.4375
- out_grad: bfloat16 [4, 2048, 512], P(None, 'batch'), may hold values from -6 to 6
Outputs:
- features: float32 [4, 2048, 512], P('section', 'batch')
- in_grad: float32 [4, 2048, 512], P('section', 'batch')
- new_point: float32 [4, 512, 512], P('section', 'batch')
- new_spatial: float32 [4, 9, 512, 512], P('section', None, 'batch')
- new_norm: float32 [4, 4, 512], P('section')
- new_mom_point: float32 [4, 512, 512], P('section', 'batch')
- new_mom_spatial: float32 [4, 9, 512, 512], P('section', None, 'batch')
- new_mom_norm: float32 [4, 4, 512], P('section')
The draws below stay inside these ranges and needn't reach their ends.
Inputs may be any that keep to these rules, and one draw needn't show every extreme that they name: `crop_big`: each value is the number of big crops at the head of one device's 256 rows of one micro-batch; small crops fill the rows after them as described. `norm_params`: rows 0 and 2 are gains, rows 1 and 3 shifts.
All inputs are finite; a program needn't handle non-finite values.
Results may differ from the reference program's by a relative error of at most 0.02.
Values may be sent and summed in bfloat16 or wider, within the bound.
A program may use at most 256 MiB of HBM per device.

```python
from functools import partial
import jax
import jax.numpy as jnp
from jax import lax

D = 512
PIX = 256
BIG_SIDE = 7
SMALL_SIDE = 3
WARMUP = 20
STEP = 9
BLOCKS = 4
MICRO = 4
ROWS = 2048
BIG_MOST = 2
N_BATCH = 8


def rising_weight(key, shape, row_dim, fan_in, rise):
    values = jnp.clip(jax.random.normal(key, shape, jnp.float32), -6.0, 6.0)
    channel = jnp.arange(shape[row_dim], dtype=jnp.float32) / (shape[row_dim] - 1)
    scales = rise ** channel
    view = [1] * len(shape)
    view[row_dim] = shape[row_dim]
    return values * scales.reshape(view) * fan_in ** (-0.5)


def draw_w_point(key, part):
    key = jax.random.fold_in(key, 5)
    return rising_weight(key, (BLOCKS, D, D), 1, D, 6.0)


def draw_w_spatial(key, part):
    key = jax.random.fold_in(key, 7)
    return rising_weight(key, (BLOCKS, 9, D, D), 2, 9 * D, 6.0)


def draw_norm_params(key, part):
    key = jax.random.fold_in(key, 11)
    gain_key, shift_key = jax.random.split(key)
    gains = jax.random.uniform(gain_key, (BLOCKS, 2, D), jnp.float32, 0.5, 1.5)
    shifts = 0.3 * jax.random.normal(shift_key, (BLOCKS, 2, D), jnp.float32)
    return jnp.stack([gains[:, 0], shifts[:, 0], gains[:, 1], shifts[:, 1]], 1)


def touch_ends(drawn, stream_key, smallest, high):
    extent = drawn.shape
    index_at = [jax.random.randint(jax.random.fold_in(stream_key, axis), (), 0, extent[axis]) for axis in range(len(extent))]
    drawn = drawn.at[tuple(index_at)].set(smallest)
    longest = extent.index(max(extent))
    index_at[longest] = (index_at[longest] + 1) % extent[longest]
    return drawn.at[tuple(index_at)].set(high)


def shard_levels(key, extent, pieces, low, top_value):
    level = 1.0
    for dim, parts in pieces:
        heights = jax.random.uniform(jax.random.fold_in(jax.random.fold_in(key, 6), dim), (parts,), jnp.float32, low / len(pieces), top_value / len(pieces))
        level = level * jnp.repeat(jnp.exp(heights), extent[dim] // parts).reshape((-1,) + (1,) * (len(extent) - 1 - dim))
    return level


def normal_values(key, shape, spread, bound, pieces=(), kind=jnp.bfloat16):
    values = spread * jax.random.normal(key, shape, jnp.float32)
    if pieces:
        values = values * shard_levels(key, shape, pieces, -0.22, 0.18)
    return jnp.clip(values, -bound, bound).astype(kind)


def setup_inputs(seed: int = 0) -> dict:
    key_list = jax.random.split(jax.random.key(seed), 10)
    return {
        "images": normal_values(key_list[0], (MICRO, ROWS, D), 1.0, 6.0, ((1, 8),)),
        "crop_big": touch_ends(jax.random.randint(key_list[1], (MICRO, N_BATCH), 0, BIG_MOST + 1), jax.random.fold_in(key_list[1], 1), 0, BIG_MOST).astype(jnp.int32),
        "w_point": draw_w_point(jax.random.fold_in(key_list[9], 71), 0),
        "w_spatial": draw_w_spatial(jax.random.fold_in(key_list[9], 71), 0),
        "norm_params": draw_norm_params(jax.random.fold_in(key_list[9], 71), 0),
        "mom_point": normal_values(key_list[5], (BLOCKS, D, D), 0.005, 0.078125, ((0, 4), (1, 8)), jnp.float32),
        "mom_spatial": normal_values(key_list[6], (BLOCKS, 9, D, D), 0.0018, 0.02734375, ((0, 4), (2, 8)), jnp.float32),
        "mom_norm": normal_values(key_list[7], (BLOCKS, 4, D), 0.03, 0.4375, ((0, 4),), jnp.float32),
        "out_grad": normal_values(key_list[8], (MICRO, ROWS, D), 1.0, 6.0, ((1, 8),)),
    }


EPS = 1e-05
EPS_NORM = 1e-06
BASE_RATE = 6.0
MOMENTUM = 0.9
TRUST_COEF = 0.1

@jax.custom_vjp
def low(v):
    return lax.optimization_barrier(v.astype(jnp.bfloat16)).astype(jnp.float32)

@jax.custom_vjp
def low_back(v):
    return v

def low_keep(v):
    return (low(v), None)

def low_pass(kept, grad):
    return (grad,)

def back_keep(v):
    return (v, None)

def back_low(kept, grad):
    return (low(grad),)
low.defvjp(low_keep, low_pass)
low_back.defvjp(back_keep, back_low)

def crop_table(big_count, total_rows):
    places = jnp.arange(total_rows, dtype=jnp.int32)
    big_area = BIG_SIDE * BIG_SIDE
    small_area = SMALL_SIDE * SMALL_SIDE
    big_rows = big_count * big_area
    small_rows = (total_rows - big_rows) // small_area * small_area
    in_big = places < big_rows
    offsets = places - big_rows
    sides = jnp.where(in_big, BIG_SIDE, SMALL_SIDE)
    within = jnp.where(in_big, places % big_area, offsets % small_area)
    starts = places - within
    valid_rows = places < big_rows + small_rows
    row_pos = within // sides
    col_pos = within % sides
    indices = []
    masks = []
    for row_step in (-1, 0, 1):
        for col_step in (-1, 0, 1):
            new_row = row_pos + row_step
            new_col = col_pos + col_step
            inside = valid_rows & (new_row >= 0) & (new_row < sides) & (new_col >= 0) & (new_col < sides)
            indices.append(jnp.where(inside, starts + new_row * sides + new_col, places))
            masks.append(inside)
    return (jnp.stack(indices, 1).astype(jnp.int32), jnp.stack(masks, 1).astype(jnp.float32), valid_rows.astype(jnp.float32))

def mish(values):
    return values * jnp.tanh(jax.nn.softplus(values))

def normalize(proj, valid_rows, row_count, gain, shift):
    weighted = valid_rows[:, None] * proj
    center = lax.optimization_barrier(jnp.sum(weighted, 0)) / row_count
    second = lax.optimization_barrier(jnp.sum(weighted * proj, 0)) / row_count
    inv_std = lax.rsqrt(second - center * center + EPS)
    return gain * ((proj - center) * inv_std) + shift

def residual_block(hidden, point_low, spatial_low, affine, tap_index, tap_mask, valid_rows, row_count):
    inputs = low(hidden)
    proj_one = low_back(jnp.dot(inputs, point_low, precision=lax.Precision.HIGHEST, preferred_element_type=jnp.float32))
    mixed_one = low(mish(normalize(proj_one, valid_rows, row_count, affine[0], affine[1])))
    summed = jnp.zeros_like(hidden)
    for tap_number in range(9):
        gathered = tap_mask[:, tap_number:tap_number + 1] * mixed_one[tap_index[:, tap_number]]
        summed = summed + jnp.dot(gathered, spatial_low[tap_number], precision=lax.Precision.HIGHEST, preferred_element_type=jnp.float32)
    proj_two = low_back(summed)
    mixed_two = mish(normalize(proj_two, valid_rows, row_count, affine[2], affine[3]))
    return hidden + valid_rows[:, None] * mixed_two

def lars_step(param, grad, momentum, axes, rate):
    param_norm = jnp.sqrt(lax.optimization_barrier(jnp.sum(param * param, axes, keepdims=True)))
    grad_norm = jnp.sqrt(lax.optimization_barrier(jnp.sum(grad * grad, axes, keepdims=True)))
    trust = TRUST_COEF * param_norm / (grad_norm + EPS_NORM)
    new_mom = MOMENTUM * momentum + rate * trust * grad
    return (param - new_mom, new_mom)

def reference(images, crop_big, w_point, w_spatial, norm_params, mom_point, mom_spatial, mom_norm, out_grad):
    table_fn = partial(crop_table, total_rows=PIX)
    tap_index, tap_mask, valid_rows = jax.vmap(jax.vmap(table_fn))(crop_big)
    shifts = (jnp.arange(N_BATCH, dtype=jnp.int32) * PIX)[None, :, None, None]
    tap_index = (tap_index + shifts).astype(jnp.int32).reshape(MICRO, ROWS, 9)
    tap_mask = tap_mask.reshape(MICRO, ROWS, 9)
    valid_rows = valid_rows.reshape(MICRO, ROWS)
    block_fn = jax.checkpoint(residual_block)

    def forward(pictures, points, spatials, affines):
        points_low = low(points)
        spatials_low = low(spatials)
        results = []
        for micro_index in range(MICRO):
            hidden = pictures[micro_index]
            row_count = jnp.sum(valid_rows[micro_index])
            for block_index in range(BLOCKS):
                hidden = block_fn(hidden, points_low[block_index], spatials_low[block_index], affines[block_index], tap_index[micro_index], tap_mask[micro_index], valid_rows[micro_index], row_count)
            results.append(hidden)
        return jnp.stack(results)
    features, pullback = jax.vjp(forward, images.astype(jnp.float32), w_point, w_spatial, norm_params)
    in_grad, grad_point, grad_spatial, grad_norm = pullback(out_grad.astype(jnp.float32))
    rate = BASE_RATE * (STEP + 1) / WARMUP
    new_point, new_mom_point = lars_step(w_point, grad_point, mom_point, (1, 2), rate)
    new_spatial, new_mom_spatial = lars_step(w_spatial, grad_spatial, mom_spatial, (1, 2, 3), rate)
    new_norm, new_mom_norm = lars_step(norm_params, grad_norm, mom_norm, (2,), rate)
    return (features, in_grad, new_point, new_spatial, new_norm, new_mom_point, new_mom_spatial, new_mom_norm)
```

```python
import jax
import jax.numpy as jnp
from jax import lax
from jax.experimental import pallas as pl
from jax.experimental.pallas import tpu as pltpu
from jax.sharding import PartitionSpec as P

BIG_SIDE = 7
SMALL_SIDE = 3
WARMUP = 20
STEP = 9


EPS = 1e-05
EPS_NORM = 1e-06
BASE_RATE = 6.0
MOMENTUM = 0.9
TRUST_COEF = 0.1


def from_behind(block, axis, distance):
    devices = range(lax.axis_size(axis))
    route = [(i - distance, i) for i in devices if i - distance in devices]
    return lax.ppermute(block, axis, route)


def crop_table(big_count, total_rows):
    places = jnp.arange(total_rows, dtype=jnp.int32)
    big_area = BIG_SIDE * BIG_SIDE
    small_area = SMALL_SIDE * SMALL_SIDE
    big_rows = big_count * big_area
    small_rows = (total_rows - big_rows) // small_area * small_area
    in_big = places < big_rows
    offsets = places - big_rows
    sides = jnp.where(in_big, BIG_SIDE, SMALL_SIDE)
    within = jnp.where(in_big, places % big_area, offsets % small_area)
    starts = places - within
    valid_rows = places < big_rows + small_rows
    row_pos = within // sides
    col_pos = within % sides
    indices = []
    masks = []
    for row_step in (-1, 0, 1):
        for col_step in (-1, 0, 1):
            new_row = row_pos + row_step
            new_col = col_pos + col_step
            inside = (
                valid_rows & (new_row >= 0) & (new_row < sides) & (new_col >= 0) & (new_col < sides)
            )
            indices.append(jnp.where(inside, starts + new_row * sides + new_col, places))
            masks.append(inside)
    return (
        jnp.stack(indices, 1),
        jnp.stack(masks, 1).astype(jnp.float32),
        valid_rows.astype(jnp.float32),
    )


def mish(values):
    return values * jnp.tanh(jax.nn.softplus(values))


def mish_parts(values):
    tangent = jnp.tanh(jax.nn.softplus(values))
    slope = tangent + values * jax.nn.sigmoid(values) * (1.0 - tangent * tangent)
    return (values * tangent, slope)


def mish_slope(values):
    tangent = jnp.tanh(jax.nn.softplus(values))
    return tangent + values * jax.nn.sigmoid(values) * (1.0 - tangent * tangent)


def batch_moments(proj, valid_rows):
    weighted = valid_rows[:, None] * proj
    summed, squared, row_count = lax.psum(
        (jnp.sum(weighted, 0), jnp.sum(weighted * proj, 0), jnp.sum(valid_rows)), "batch"
    )
    center = summed / row_count
    inv_std = lax.rsqrt(squared / row_count - center * center + EPS)
    return (center, inv_std, row_count)


def spatial_apply(source, tap_index, tap_mask, weights):
    stacked = source[tap_index] * tap_mask[:, :, None].astype(source.dtype)
    result = lax.dot_general(
        stacked, weights, (((1, 2), (0, 1)), ((), ())), preferred_element_type=jnp.float32
    )
    return (result, stacked)


def forward_block(hidden, point_low, spatial_low, affine, tap_index, tap_mask, valid_rows):
    proj_one = jnp.dot(hidden.astype(jnp.bfloat16), point_low, preferred_element_type=jnp.float32)
    center_one, inv_one, row_count = batch_moments(proj_one, valid_rows)
    mixed_one = mish(affine[0] * ((proj_one - center_one) * inv_one) + affine[1])
    proj_two, stacked = spatial_apply(
        mixed_one.astype(jnp.bfloat16), tap_index, tap_mask, spatial_low
    )
    center_two, inv_two, count_two = batch_moments(proj_two, valid_rows)
    mixed_two = mish(affine[2] * ((proj_two - center_two) * inv_two) + affine[3])
    moments = jnp.stack([center_one, inv_one, center_two, inv_two])
    return (hidden + valid_rows[:, None] * mixed_two, moments, row_count)


def norm_back(d_value, normed, inv_std, gain, valid_rows, row_count):
    first_sum, second_sum = lax.psum((jnp.sum(d_value, 0), jnp.sum(d_value * normed, 0)), "batch")
    d_proj = (
        gain
        * inv_std
        * (d_value - valid_rows[:, None] * (first_sum + normed * second_sum) / row_count)
    )
    return (d_proj.astype(jnp.bfloat16), first_sum, second_sum)


def backward_block(
    hidden,
    upstream,
    point_low,
    spatial_low,
    affine,
    moments,
    row_count,
    tap_index,
    tap_mask,
    valid_rows,
):
    inputs = hidden.astype(jnp.bfloat16)
    proj_one = jnp.dot(inputs, point_low, preferred_element_type=jnp.float32)
    normed_one = (proj_one - moments[0]) * moments[1]
    mixed_one, slope_one = mish_parts(affine[0] * normed_one + affine[1])
    proj_two, stacked = spatial_apply(
        mixed_one.astype(jnp.bfloat16), tap_index, tap_mask, spatial_low
    )
    normed_two = (proj_two - moments[2]) * moments[3]
    slope_two = mish_slope(affine[2] * normed_two + affine[3])
    d_two, first_two, second_two = norm_back(
        valid_rows[:, None] * upstream * slope_two,
        normed_two,
        moments[3],
        affine[2],
        valid_rows,
        row_count,
    )
    grad_spatial = lax.dot_general(
        stacked, d_two, (((0,), (0,)), ((), ())), preferred_element_type=jnp.float32
    )
    flipped = d_two[tap_index[:, ::-1]] * tap_mask[:, ::-1, None].astype(jnp.bfloat16)
    d_mixed = lax.dot_general(
        flipped, spatial_low, (((1, 2), (0, 2)), ((), ())), preferred_element_type=jnp.float32
    )
    d_one, first_one, second_one = norm_back(
        d_mixed * slope_one, normed_one, moments[1], affine[0], valid_rows, row_count
    )
    grad_point = lax.dot_general(
        inputs, d_one, (((0,), (0,)), ((), ())), preferred_element_type=jnp.float32
    )
    d_hidden = upstream + lax.dot_general(
        d_one, point_low, (((1,), (1,)), ((), ())), preferred_element_type=jnp.float32
    )
    grad_affine = jnp.stack([second_one, first_one, second_two, first_two])
    return (d_hidden, grad_point, grad_spatial, grad_affine)


def store_slot(buffer, value, slot_index, active):
    previous = lax.dynamic_index_in_dim(buffer, slot_index, 0, keepdims=False)
    return lax.dynamic_update_index_in_dim(
        buffer, jnp.where(active, value, previous), slot_index, 0
    )


def lars_update(param, grad, momentum, param_sq, grad_sq, rate):
    trust = TRUST_COEF * jnp.sqrt(param_sq) / (jnp.sqrt(grad_sq) + EPS_NORM)
    new_mom = MOMENTUM * momentum + rate * trust * grad
    return (param - new_mom, new_mom)


def on_device(
    images, crop_big, w_point, w_spatial, norm_params, mom_point, mom_spatial, mom_norm, out_grad
):
    section_count = lax.axis_size("section")
    section_rank = lax.axis_index("section")
    micro_count = images.shape[0]
    total_rows = images.shape[1]
    width = images.shape[2]
    point = w_point[0]
    spatial = w_spatial[0]
    affine = norm_params[0]
    crop_counts = crop_big[:, 0]
    turns = micro_count + section_count - 1
    point_low, spatial_low = (
        lax.all_gather(point.astype(jnp.bfloat16), "batch", axis=0, tiled=True),
        lax.all_gather(spatial.astype(jnp.bfloat16), "batch", axis=1, tiled=True),
    )
    kept_inputs = jnp.zeros((micro_count, total_rows, width), jnp.float32)
    kept_moments = jnp.zeros((micro_count, 4, width), jnp.float32)
    kept_counts = jnp.zeros((micro_count,), jnp.float32)
    results = jnp.zeros((micro_count, total_rows, width), jnp.float32)
    incoming = jnp.zeros((total_rows, width), jnp.float32)
    for phase_turn in range(turns):
        slot_raw = phase_turn - section_rank
        active = (slot_raw >= 0) & (slot_raw < micro_count)
        slot_index = jnp.clip(slot_raw, 0, micro_count - 1)
        fresh_rows = lax.dynamic_index_in_dim(images, slot_index, 0, keepdims=False).astype(
            jnp.float32
        )
        hidden = jnp.where(section_rank == 0, fresh_rows, incoming)
        tap_index, tap_mask, valid_rows = crop_table(crop_counts[slot_index], total_rows)
        output, moments, row_count = forward_block(
            hidden, point_low, spatial_low, affine, tap_index, tap_mask, valid_rows
        )
        kept_inputs = store_slot(kept_inputs, hidden, slot_index, active)
        kept_moments = store_slot(kept_moments, moments, slot_index, active)
        kept_counts = store_slot(kept_counts, row_count, slot_index, active)
        results = store_slot(
            results, output, slot_index, active & (section_rank == section_count - 1)
        )
        if phase_turn + 1 < turns:
            incoming = from_behind(output.astype(jnp.bfloat16), "section", 1).astype(output.dtype)
    point_low, spatial_low = (
        lax.all_gather(point.astype(jnp.bfloat16), "batch", axis=0, tiled=True),
        lax.all_gather(spatial.astype(jnp.bfloat16), "batch", axis=1, tiled=True),
    )
    grad_point = jnp.zeros((width, width), jnp.float32)
    grad_spatial = jnp.zeros((9, width, width), jnp.float32)
    grad_affine = jnp.zeros((4, width), jnp.float32)
    collected = jnp.zeros((micro_count, total_rows, width), jnp.float32)
    returning = jnp.zeros((total_rows, width), jnp.float32)
    for phase_turn in range(turns):
        slot_raw = micro_count - 1 - phase_turn + (section_count - 1 - section_rank)
        active = (slot_raw >= 0) & (slot_raw < micro_count)
        slot_index = jnp.clip(slot_raw, 0, micro_count - 1)
        seeded = lax.dynamic_index_in_dim(out_grad, slot_index, 0, keepdims=False).astype(
            jnp.float32
        )
        upstream = jnp.where(section_rank == section_count - 1, seeded, returning)
        upstream = jnp.where(active, upstream, 0.0)
        tap_index, tap_mask, valid_rows = crop_table(crop_counts[slot_index], total_rows)
        hidden = lax.dynamic_index_in_dim(kept_inputs, slot_index, 0, keepdims=False)
        moments = lax.dynamic_index_in_dim(kept_moments, slot_index, 0, keepdims=False)
        row_count = lax.dynamic_index_in_dim(kept_counts, slot_index, 0, keepdims=False)
        d_hidden, part_point, part_spatial, part_affine = backward_block(
            hidden,
            upstream,
            point_low,
            spatial_low,
            affine,
            moments,
            row_count,
            tap_index,
            tap_mask,
            valid_rows,
        )
        grad_point = grad_point + part_point
        grad_spatial = grad_spatial + part_spatial
        grad_affine = grad_affine + part_affine
        collected = store_slot(collected, d_hidden, slot_index, active & (section_rank == 0))
        if phase_turn + 1 < turns:
            returning = from_behind(d_hidden.astype(jnp.bfloat16), "section", -1).astype(
                d_hidden.dtype
            )
    point_grad, spatial_grad = (
        lax.psum_scatter(grad_point, "batch", scatter_dimension=0, tiled=True),
        lax.psum_scatter(grad_spatial, "batch", scatter_dimension=1, tiled=True),
    )
    point_sq, spatial_sq, gpoint_sq, gspatial_sq = lax.psum(
        (
            jnp.sum(point * point),
            jnp.sum(spatial * spatial),
            jnp.sum(point_grad * point_grad),
            jnp.sum(spatial_grad * spatial_grad),
        ),
        "batch",
    )
    rate = BASE_RATE * (STEP + 1) / WARMUP
    new_point, new_mom_point = lars_update(
        point, point_grad, mom_point[0], point_sq, gpoint_sq, rate
    )
    new_spatial, new_mom_spatial = lars_update(
        spatial, spatial_grad, mom_spatial[0], spatial_sq, gspatial_sq, rate
    )
    affine_sq = jnp.sum(affine * affine, 1, keepdims=True)
    gaffine_sq = jnp.sum(grad_affine * grad_affine, 1, keepdims=True)
    new_affine, new_mom_affine = lars_update(
        affine, grad_affine, mom_norm[0], affine_sq, gaffine_sq, rate
    )
    sent_out = jnp.where(section_rank == section_count - 1, results, 0.0)
    sent_back = jnp.where(section_rank == 0, collected, 0.0)
    got_out, got_back = (
        lax.all_to_all(
            sent_out.astype(jnp.bfloat16), "section", split_axis=0, concat_axis=0, tiled=True
        ).astype(sent_out.dtype),
        lax.all_to_all(
            sent_back.astype(jnp.bfloat16), "section", split_axis=0, concat_axis=0, tiled=True
        ).astype(sent_back.dtype),
    )
    features = got_out[section_count - 1 : section_count]
    in_grad = got_back[0:1]
    return (
        features,
        in_grad,
        new_point[None],
        new_spatial[None],
        new_affine[None],
        new_mom_point[None],
        new_mom_spatial[None],
        new_mom_affine[None],
    )


def swap_copy(source, target, sent, landed, section, batch):
    return pltpu.make_async_remote_copy(
        src_ref=source,
        dst_ref=target,
        send_sem=sent,
        recv_sem=landed,
        device_id=(section, batch),
        device_id_type=pl.DeviceIdType.MESH,
    )


def drain(like, sem):
    pltpu.make_async_copy(like, like, sem).wait()


def mish_terms(v):
    e = jnp.exp(jnp.minimum(v, 20.0))
    w = e * (e + 2.0)
    r = 1.0 / (w + 2.0)
    t = w * r
    return v * t, t + v * (4.0 * e * (1.0 + e)) * (r * r)


def pack(first, second):
    parts = [v[:, i * 128 : (i + 1) * 128] for v in (first, second) for i in range(4)]
    return jnp.concatenate(parts, axis=0)


def unpack(tile):
    rows = [tile[i : i + 1] for i in range(8)]
    return jnp.concatenate(rows[:4], axis=1), jnp.concatenate(rows[4:], axis=1)


def crop_codes(places, big, total_rows):
    big_area = float(BIG_SIDE * BIG_SIDE)
    small_area = float(SMALL_SIDE * SMALL_SIDE)
    big_rows = big * big_area
    small_rows = jnp.floor((total_rows - big_rows + 0.5) / small_area) * small_area
    in_big = places < big_rows
    offset = jnp.where(in_big, places, places - big_rows)
    area = jnp.where(in_big, big_area, small_area)
    side = jnp.where(in_big, float(BIG_SIDE), float(SMALL_SIDE))
    crop = jnp.floor((offset + 0.5) / area)
    within = offset - crop * area
    row = jnp.floor((within + 0.5) / side)
    col = within - row * side
    crop = jnp.where(in_big, crop, crop + big)
    return crop * 1024.0 + (row + 1.0) * 32.0 + (col + 1.0), places < big_rows + small_rows


NT = (((1,), (1,)), ((), ()))
TAPS = 10
HALF = 5


def train_kernel(
    images, crop, w_point, w_spatial, norm_in, mom_point, mom_spatial, mom_norm, out_grad,
    features, in_grad, new_point, new_spatial, new_norm, new_mom_point, new_mom_spatial,
    new_mom_norm,
    W, wown, pbuf, mbuf, h, g, zbuf, sv, gi, abuf, gbuf, Gm, caq, stage, Hb, GcT, dzq, gout, yrecv,
    zs1, zrecv, fin, gfin, aff, gaff, gsend, st_in, st_own, st_all, cnt, cntx, cown,
    sL, sS_s, sS_r, sZ_s, sZ_r, sH_s, sH_r, sA_s, sA_r, sB_s, sB_r, sD_s, sD_r,
    sE_in_s, sE_in_r, sE_s, sE_r, sC_s, sC_r, sF_s, sF_r, sQ_s, sQ_r, sX_s, sX_r,
    sY_s, sY_r, sK_s, sK_r, sR_s, sR_r, sG_s, sG_r, sO_s, sO_r, sW,
):
    s = lax.axis_index("section")
    bat = lax.axis_index("batch")
    z = bat // 2
    c = lax.rem(bat, 2)
    x = lax.rem(s, 2)
    y = s // 2
    u = 2 * x + c
    R, D = h.shape

    loads = [
        pltpu.make_async_copy(w_point.at[0], pbuf.at[9], sL.at[0]),
        pltpu.make_async_copy(w_spatial.at[0], pbuf.at[pl.ds(0, 9)], sL.at[1]),
        pltpu.make_async_copy(images.at[s], abuf, sL.at[2]),
        pltpu.make_async_copy(out_grad.at[s], gbuf, sL.at[3]),
        pltpu.make_async_copy(mom_point.at[0], mbuf.at[9], sL.at[4]),
        pltpu.make_async_copy(mom_spatial.at[0], mbuf.at[pl.ds(0, 9)], sL.at[5]),
    ]
    for load in loads:
        load.start()

    barrier = pltpu.get_barrier_semaphore()
    greet = [(s, bat ^ j) for j in range(1, 8)]
    greet += [(s ^ d, bat ^ j) for d in range(1, 4) for j in range(2)]
    for sec, other in greet:
        pl.semaphore_signal(
            barrier, inc=1, device_id=(sec, other), device_id_type=pl.DeviceIdType.MESH
        )
    pl.semaphore_wait(barrier, len(greet))

    loads[0].wait()
    loads[1].wait()
    for k in range(TAPS):
        wown[k] = pbuf[k].astype(jnp.bfloat16).reshape(4, 16, D)

    def scatter(d):
        q = s ^ d
        return swap_copy(
            wown.at[:, q], W.at[s, :, bat, q], sS_s.at[d], sS_r.at[s, c], q, 2 * z
        )

    for d in range(1, 4):
        scatter(d).start()

    @pl.when(c == 1)
    def _():
        scatter(0).start()

    @pl.when(c == 0)
    def _():
        pltpu.make_async_copy(wown.at[:, s], W.at[s, :, bat, s], sS_r.at[s, c]).start()

    cown[...] = jnp.full((8, 128), crop[s, 0].astype(jnp.float32))
    aff[s] = jnp.concatenate([norm_in[0], jnp.zeros((4, D), jnp.float32)], axis=0)
    cnt[bat] = cown[...]
    cntx[u] = cown[...]
    for j in range(1, 8):
        swap_copy(cown, cnt.at[bat], sC_s.at[j], sC_r.at[bat], s, bat ^ j).start()
    for j in range(2):
        swap_copy(cown, cntx.at[u], sC_s.at[8 + j], sC_r.at[8 + u], s ^ 1, bat ^ j).start()
    for d in range(1, 4):
        swap_copy(aff.at[s], aff.at[s], sF_s.at[d], sF_r.at[s], s ^ d, bat).start()

    half = pl.ds(HALF * c, HALF)
    first = jnp.where(c == 0, s ^ 1, s ^ 2)
    second = jnp.where(c == 0, s ^ 2, s ^ 1)
    both = s ^ 3

    def pair(b, taps, zz, q):
        return W.at[b, taps, pl.ds(2 * zz, 2), q]

    def to_sibling(b, zz):
        ref = pair(b, slice(None), zz, s)
        return swap_copy(ref, ref, sH_s.at[b, zz], sH_r.at[b, zz], s, bat ^ 1)

    def along_first(b, zz):
        ref = pair(b, half, zz, s)
        return swap_copy(ref, ref, sA_s.at[b, zz], sA_r.at[b, zz], first, bat)

    def along_second(b, which, zz):
        ref = pair(b, half, zz, s if which == 0 else first)
        return swap_copy(ref, ref, sB_s.at[b, which, zz], sB_r.at[b, which, zz], second, bat)

    def quarter_to_sibling(b, which):
        ref = W.at[b, half, :, (first, second, both)[which]]
        return swap_copy(ref, ref, sD_s.at[b, which], sD_r.at[b, which], s, bat ^ 1)

    def own_ready(b, zz):
        @pl.when(c == 0)
        def _():
            to_sibling(b, zz).start()

        @pl.when(c == 1)
        def _():
            to_sibling(b, zz).wait_recv()

        along_first(b, zz).start()
        along_second(b, 0, zz).start()

    def spread_z(b, j):
        ref = pair(b, slice(None), z, s)
        return swap_copy(ref, ref, sZ_s.at[b, j], sZ_r.at[b, z], s, bat ^ (2 * j))

    def from_z(b, zz):
        ref = pair(b, slice(None), zz, s)
        return swap_copy(ref, ref, sZ_s.at[b, 0], sZ_r.at[b, zz], s, bat)

    @pl.loop(0, 4)
    def _(b):
        @pl.when(c == 0)
        def _():
            for cc in range(2):
                drain(W.at[b, :, 2 * z + cc, s], sS_r.at[b, cc])
            for j in range(1, 4):
                spread_z(b, j).start()

        own_ready(b, z)

    def gather_z(b):
        for j in range(1, 4):
            zz = z ^ j

            @pl.when(c == 0)
            def _():
                from_z(b, zz).wait_recv()

            own_ready(b, zz)

    def gather_first(b):
        for j in range(4):
            zz = z ^ j
            ref = pair(b, half, zz, first)
            swap_copy(ref, ref, sA_s.at[b, zz], sA_r.at[b, zz], first, bat).wait_recv()
            along_second(b, 1, zz).start()
        quarter_to_sibling(b, 0).start()

    def gather_second(b):
        for which in range(2):
            q = (second, both)[which]
            for j in range(4):
                zz = z ^ j
                ref = pair(b, half, zz, q)
                swap_copy(
                    ref, ref, sB_s.at[b, which, zz], sB_r.at[b, which, zz], second, bat
                ).wait_recv()
            quarter_to_sibling(b, 1 + which).start()
        other = pl.ds(HALF * (1 - c), HALF)
        for which in range(3):
            drain(W.at[b, other, :, (second, first, both)[which]], sD_r.at[b, which])

    for j in range(1, 8):
        drain(cnt.at[bat ^ j], sC_r.at[bat ^ j])
    for j in range(2):
        v = 2 * (1 - x) + j
        drain(cntx.at[v], sC_r.at[8 + v])
    cntx[2 * x + (1 - c)] = cnt[bat ^ 1]
    total = jnp.zeros((1, 1), jnp.float32)
    for j in range(8):
        big = cnt[j][0:1, 0:1]
        big_rows = big * float(BIG_SIDE * BIG_SIDE)
        area = float(SMALL_SIDE * SMALL_SIDE)
        total = total + big_rows + jnp.floor((R - big_rows + 0.5) / area) * area
    row_count = total
    down = lax.broadcasted_iota(jnp.int32, (R, 1), 0).astype(jnp.float32)
    across = lax.broadcasted_iota(jnp.int32, (1, R), 1).astype(jnp.float32)

    @pl.loop(0, 4)
    def _(v):
        big = cntx[v][0:1, 0:1]
        code_down, ok_down = crop_codes(down, big, R)
        code_across, ok_across = crop_codes(across, big, R)
        code_down = jnp.where(ok_down, code_down, -5000.0)
        code_across = jnp.where(ok_across, code_across, -1.0)
        for k in range(9):
            step = float(32 * (k // 3 - 1) + (k % 3 - 1))
            hit = (code_down + step) == code_across
            Gm[v, pl.ds(k * R, R)] = jnp.where(hit, 1.0, 0.0).astype(jnp.bfloat16)

    _, own_valid = crop_codes(down, cown[0:1, 0:1], R)
    valid = own_valid.astype(jnp.float32)
    for d in range(1, 4):
        drain(aff.at[s ^ d], sF_r.at[s ^ d])
    loads[2].wait()
    h[...] = abuf[...].astype(jnp.float32)

    def sums_start(e, first_sum, second_sum):
        st_own[e] = pack(first_sum, second_sum)

        @pl.when(c == 0)
        def _():
            swap_copy(st_own.at[e], st_in.at[e], sE_in_s.at[e], sE_in_r.at[e], s, bat ^ 1).start()

        @pl.when(c == 1)
        def _():
            swap_copy(
                st_own.at[e], st_in.at[e], sE_in_s.at[e], sE_in_r.at[e], s, bat ^ 1
            ).wait_recv()
            st_all[e, z] = st_own[e] + st_in[e]
            for j in (7, 6, 5, 4, 3, 2, 1):
                swap_copy(
                    st_all.at[e, z], st_all.at[e, z], sE_s.at[e, j], sE_r.at[e, z], s, bat ^ j
                ).start()

    def sums_finish(e):
        for j in range(1, 4):
            zz = z ^ j
            drain(st_all.at[e, zz], sE_r.at[e, zz])

        @pl.when(c == 0)
        def _():
            drain(st_all.at[e, z], sE_r.at[e, z])

        return unpack(st_all[e, 0] + st_all[e, 1] + st_all[e, 2] + st_all[e, 3])

    def sums_close(e):
        @pl.when(c == 0)
        def _():
            drain(st_own.at[e], sE_in_s.at[e])

        @pl.when(c == 1)
        def _():
            for j in range(1, 8):
                drain(st_own.at[e], sE_s.at[e, j])

    def moments(sums):
        center = sums[0] / row_count
        spread = lax.rsqrt(sums[1] / row_count - center * center + EPS)
        return center, spread

    def share(b, kind, rows):
        turned = rows.T
        for cc in range(2):
            for xx in range(2):
                for yy in range(2):
                    for zz in range(4):
                        at = (2 * zz + cc) * 64 + (2 * yy + xx) * 16
                        stage[b, kind, 2 * xx + cc, 4 * yy + zz] = turned[at : at + 16].astype(
                            jnp.bfloat16
                        )
        for j in range(1, 4):
            v = u ^ j
            swap_copy(
                stage.at[b, kind, v], caq.at[b, kind, u], sQ_s.at[b, kind, j],
                sQ_r.at[b, kind, u], s ^ (j // 2), bat ^ (j % 2),
            ).start()
        caq[b, kind, u] = stage[b, kind, u]

    def forward(b):
        gather_second(b)
        hidden = h[...]
        zbuf[...] = jnp.dot(
            hidden.astype(jnp.bfloat16), W[b, 9].reshape(D, D), preferred_element_type=jnp.float32
        )
        z1 = zbuf[...]
        kept = valid * z1
        sums_start(
            2 * b, jnp.sum(kept, 0, keepdims=True), jnp.sum(kept * z1, 0, keepdims=True)
        )
        share(b, 1, hidden)
        norms = aff[b]
        center, spread = moments(sums_finish(2 * b))
        gi[b, 0:1] = norms[0:1] * spread
        for i in range(0, R, 64):
            xhat = (zbuf[i : i + 64] - center) * spread
            value, slope = mish_terms(norms[0:1] * xhat + norms[1:2])
            sv[b, 0, i : i + 64] = xhat.astype(sv.dtype)
            sv[b, 1, i : i + 64] = slope.astype(sv.dtype)
            abuf[i : i + 64] = value.astype(jnp.bfloat16)
        mixed = abuf[...]
        for k in range(9):
            Hb[:, k * D : (k + 1) * D] = jnp.dot(
                Gm[u, pl.ds(k * R, R)], mixed, preferred_element_type=jnp.float32
            ).astype(jnp.bfloat16)
        zbuf[...] = jnp.dot(
            Hb[...], W[b, 0:9].reshape(9 * D, D), preferred_element_type=jnp.float32
        )
        z2 = zbuf[...]
        kept = valid * z2
        sums_start(
            2 * b + 1, jnp.sum(kept, 0, keepdims=True), jnp.sum(kept * z2, 0, keepdims=True)
        )
        share(b, 0, mixed.astype(jnp.float32))
        center, spread = moments(sums_finish(2 * b + 1))
        gi[b, 1:2] = norms[2:3] * spread
        for i in range(0, R, 64):
            xhat = (zbuf[i : i + 64] - center) * spread
            value, slope = mish_terms(norms[2:3] * xhat + norms[3:4])
            sv[b, 2, i : i + 64] = xhat.astype(sv.dtype)
            sv[b, 3, i : i + 64] = slope.astype(sv.dtype)
            h[i : i + 64] = h[i : i + 64] + valid[i : i + 64] * value

    gather_z(0)
    gather_first(0)
    gather_z(1)
    gather_first(1)

    @pl.loop(0, 4)
    def _(b):
        forward(b)

        @pl.when(b < 2)
        def _():
            gather_z(b + 2)
            gather_first(b + 2)

    out_features = pltpu.make_async_copy(h, features.at[0], sO_s.at[0])
    out_features.start()
    loads[3].wait()
    g[...] = gbuf[...].astype(jnp.float32)

    def dz_copy(b, par, kind, j):
        return swap_copy(
            dzq.at[par, kind, u], dzq.at[par, kind, u], sX_s.at[b, kind, j],
            sX_r.at[b, kind, u], s ^ (j // 2), bat ^ (j % 2),
        )

    def send_dz(b, par, kind):
        for j in range(1, 4):
            dz_copy(b, par, kind, j).start()

    def wait_dz(b, par, kind):
        for j in range(1, 4):
            v = u ^ j
            drain(dzq.at[par, kind, v], sX_r.at[b, kind, v])

    CHUNKS = ((0, 5), (5, 4), (9, 1))

    def y_copy(b, par, i):
        at, size = CHUNKS[i]
        return swap_copy(
            gout.at[par, 1 - y, pl.ds(at, size)], yrecv.at[b, pl.ds(at, size)],
            sY_s.at[b, i], sY_r.at[b, i], s ^ 2, bat,
        )

    def grad_tap(par, k, left, right):
        part = jnp.dot(left, right, preferred_element_type=jnp.float32).astype(jnp.bfloat16)
        for yy in range(2):
            gout[par, yy, k] = part[64 * yy : 64 * yy + 64].reshape(4, 16, D)

    def grad_spatial(b, par):
        for v in range(4):
            left = caq[b, 0, v].reshape(128, R)
            for k in range(9):
                GcT[k, :, v * R : (v + 1) * R] = lax.dot_general(
                    left, Gm[v, pl.ds(k * R, R)], NT, preferred_element_type=jnp.float32
                ).astype(jnp.bfloat16)
        wait_dz(b, par, 1)
        right = dzq[par, 1].reshape(4 * R, D)
        for k in range(9):
            grad_tap(par, k, GcT[k], right)
            if k == 4:
                y_copy(b, par, 0).start()
        y_copy(b, par, 1).start()

    def grad_point(b, par):
        wait_dz(b, par, 0)
        left = jnp.concatenate([caq[b, 1, v].reshape(128, R) for v in range(4)], axis=1)
        grad_tap(par, 9, left, dzq[par, 0].reshape(4 * R, D))
        y_copy(b, par, 2).start()

    def add_y(b, par, i):
        at, size = CHUNKS[i]
        y_copy(b, par, i).wait_recv()
        for k in range(at, at + size):
            yrecv[b, k] = (
                yrecv[b, k].astype(jnp.float32) + gout[par, y, k].astype(jnp.float32)
            ).astype(jnp.bfloat16)

    def core_copy(b, i):
        at, size = CHUNKS[i]
        return swap_copy(
            yrecv.at[b, pl.ds(at, size)], zs1.at[b, pl.ds(at, size)],
            sK_s.at[b, i], sK_r.at[b, i], s, bat ^ 1,
        )

    def z_copy(b, i, cc, j):
        at, size = CHUNKS[i]
        source = (yrecv, zs1)[cc].at[b, pl.ds(at, size), z ^ j]
        return swap_copy(
            source, zrecv.at[b, z, pl.ds(at, size)], sR_s.at[b, i, cc, j], sR_r.at[b, i, z],
            s, 2 * (z ^ j) + cc,
        )

    def reduce_plane(b, par, i):
        add_y(b, par, i)

        @pl.when(c == 1)
        def _():
            core_copy(b, i).start()

    def reduce_z(b, i):
        @pl.when(c == 0)
        def _():
            core_copy(b, i).wait_recv()
            for cc in range(2):
                for j in range(1, 4):
                    z_copy(b, i, cc, j).start()

    def finish_z(b):
        for i, (at, size) in enumerate(CHUNKS):
            for j in range(1, 4):
                drain(zrecv.at[b, z ^ j, pl.ds(at, size)], sR_r.at[b, i, z ^ j])
        for k in range(TAPS):
            done = yrecv[b, k, z].astype(jnp.float32)
            for j in range(1, 4):
                done = done + zrecv[b, z ^ j, k].astype(jnp.float32)
            fin[b, k] = done.astype(jnp.bfloat16)

        @pl.when(b == s)
        def _():
            gfin[:, s] = fin[b]

        @pl.when(b != s)
        def _():
            swap_copy(fin.at[b], gfin.at[:, s], sG_s.at[b], sG_r.at[s], b, bat).start()

    def backward(bi):
        b = 3 - bi
        par = lax.rem(bi, 2)
        e = 8 + 2 * bi
        first_sum = jnp.zeros((1, D), jnp.float32)
        second_sum = jnp.zeros((1, D), jnp.float32)
        for i in range(0, R, 64):
            du = valid[i : i + 64] * g[i : i + 64] * sv[b, 3, i : i + 64].astype(jnp.float32)
            zbuf[i : i + 64] = du
            first_sum += jnp.sum(du, 0, keepdims=True)
            second_sum += jnp.sum(du * sv[b, 2, i : i + 64].astype(jnp.float32), 0, keepdims=True)
        sums_start(e, first_sum, second_sum)

        @pl.when(bi > 0)
        def _():
            grad_point(b + 1, 1 - par)

        @pl.when(bi > 1)
        def _():
            for i in range(3):
                reduce_plane(b + 2, par, i)
            for i in range(3):
                y_copy(b + 2, par, i).wait_send()
            for kind in range(2):
                for j in range(1, 4):
                    dz_copy(b + 2, par, kind, j).wait_send()

        total_first, total_second = sums_finish(e)
        for i in range(0, R, 64):
            xhat = sv[b, 2, i : i + 64].astype(jnp.float32)
            inner = zbuf[i : i + 64] - valid[i : i + 64] * (
                (total_first + xhat * total_second) / row_count
            )
            dzq[par, 1, u, i : i + 64] = (gi[b, 1:2] * inner).astype(jnp.bfloat16)
        send_dz(b, par, 1)
        gsend[b, 2:3] = total_second
        gsend[b, 3:4] = total_first
        d_two = dzq[par, 1, u]
        for k in range(9):
            Hb[:, k * D : (k + 1) * D] = jnp.dot(
                Gm[u, pl.ds((8 - k) * R, R)], d_two, preferred_element_type=jnp.float32
            ).astype(jnp.bfloat16)
        mixed = None
        for k in range(9):
            part = lax.dot_general(
                Hb[:, k * D : (k + 1) * D], W[b, k].reshape(D, D), NT,
                preferred_element_type=jnp.float32,
            )
            mixed = part if mixed is None else mixed + part
        zbuf[...] = mixed
        first_sum = jnp.zeros((1, D), jnp.float32)
        second_sum = jnp.zeros((1, D), jnp.float32)
        for i in range(0, R, 64):
            du = zbuf[i : i + 64] * sv[b, 1, i : i + 64].astype(jnp.float32)
            zbuf[i : i + 64] = du
            first_sum += jnp.sum(du, 0, keepdims=True)
            second_sum += jnp.sum(du * sv[b, 0, i : i + 64].astype(jnp.float32), 0, keepdims=True)
        sums_start(e + 1, first_sum, second_sum)
        for j in range(1, 4):
            v = u ^ j
            for kind in range(2):
                drain(caq.at[b, kind, v], sQ_r.at[b, kind, v])
        grad_spatial(b, par)

        @pl.when(bi > 1)
        def _():
            for i in range(3):
                reduce_z(b + 2, i)

        total_first, total_second = sums_finish(e + 1)
        for i in range(0, R, 64):
            xhat = sv[b, 0, i : i + 64].astype(jnp.float32)
            inner = zbuf[i : i + 64] - valid[i : i + 64] * (
                (total_first + xhat * total_second) / row_count
            )
            dzq[par, 0, u, i : i + 64] = (gi[b, 0:1] * inner).astype(jnp.bfloat16)
        send_dz(b, par, 0)
        gsend[b, 0:1] = total_second
        gsend[b, 1:2] = total_first
        g[...] = g[...] + lax.dot_general(
            dzq[par, 0, u], W[b, 9].reshape(D, D), NT, preferred_element_type=jnp.float32
        )

        @pl.when(b == s)
        def _():
            gaff[s] = gsend[b]

        @pl.when(b != s)
        def _():
            swap_copy(gsend.at[b], gaff.at[s], sO_s.at[4 + b], sO_r.at[s], b, bat).start()

    @pl.loop(0, 4)
    def _(bi):
        backward(bi)

    out_grad_in = pltpu.make_async_copy(g, in_grad.at[0], sO_s.at[1])
    out_grad_in.start()

    finish_z(3)
    for i in range(3):
        reduce_plane(1, 0, i)
    for i in range(3):
        reduce_z(1, i)
    grad_point(0, 1)
    finish_z(2)
    for i in range(3):
        reduce_plane(0, 1, i)
        reduce_z(0, i)
    finish_z(1)
    finish_z(0)
    loads[4].wait()
    loads[5].wait()
    for d in range(1, 4):
        drain(gfin.at[:, s ^ d], sG_r.at[s ^ d])
        drain(gaff.at[s ^ d], sO_r.at[s ^ d])

    def square(ref, taps):
        part = jnp.zeros((1, D), jnp.float32)
        for k in taps:
            v = ref[k].astype(jnp.float32).reshape(64, D)
            part += jnp.sum(v * v, 0, keepdims=True)
        return part

    def lane_sum(v):
        return jnp.sum(v, axis=1, keepdims=True)

    squares = [square(r, t) for r in (pbuf, gfin) for t in (range(9, 10), range(9))]
    lanes = lax.broadcasted_iota(jnp.int32, (1, D), 1)
    tile = jnp.zeros((1, D), jnp.float32)
    for i, part in enumerate(squares):
        tile = jnp.where(lanes == i, lane_sum(part), tile)
    sums_start(16, tile, tile)
    totals, _ = sums_finish(16)
    rate = BASE_RATE * (STEP + 1) / WARMUP
    point_sq, spatial_sq, gpoint_sq, gspatial_sq = [totals[:, i : i + 1] for i in range(4)]
    step_point = rate * TRUST_COEF * jnp.sqrt(point_sq) / (jnp.sqrt(gpoint_sq) + EPS_NORM)
    step_spatial = rate * TRUST_COEF * jnp.sqrt(spatial_sq) / (jnp.sqrt(gspatial_sq) + EPS_NORM)
    for k in range(TAPS):
        grad = gfin[k].astype(jnp.float32).reshape(64, D)
        moved = MOMENTUM * mbuf[k] + (step_point if k == 9 else step_spatial) * grad
        mbuf[k] = moved
        pbuf[k] = pbuf[k] - moved
    outs = [
        pltpu.make_async_copy(pbuf.at[9], new_point.at[0], sW.at[0]),
        pltpu.make_async_copy(pbuf.at[pl.ds(0, 9)], new_spatial.at[0], sW.at[1]),
        pltpu.make_async_copy(mbuf.at[9], new_mom_point.at[0], sW.at[2]),
        pltpu.make_async_copy(mbuf.at[pl.ds(0, 9)], new_mom_spatial.at[0], sW.at[3]),
    ]
    for out in outs:
        out.start()
    affine_grad = (gaff[0] + gaff[1] + gaff[2] + gaff[3])[0:4]
    affine = norm_in[0]
    affine_sq = lane_sum(affine * affine)
    gaffine_sq = lane_sum(affine_grad * affine_grad)
    trust = TRUST_COEF * jnp.sqrt(affine_sq) / (jnp.sqrt(gaffine_sq) + EPS_NORM)
    moved = MOMENTUM * mom_norm[0] + rate * trust * affine_grad
    new_mom_norm[0] = moved
    new_norm[0] = affine - moved

    for d in range(1, 4):
        scatter(d).wait_send()
        swap_copy(aff.at[s], aff.at[s], sF_s.at[d], sF_r.at[s], s ^ d, bat).wait_send()

    @pl.when(c == 1)
    def _():
        scatter(0).wait_send()

    for j in range(1, 10):
        if j != 0:
            drain(cown, sC_s.at[j])

    @pl.loop(0, 4)
    def _(b):
        for zz in range(4):
            drain(pair(b, half, zz, s), sA_s.at[b, zz])
            for which in range(2):
                drain(pair(b, half, zz, s), sB_s.at[b, which, zz])
        for which in range(3):
            drain(W.at[b, half, :, s], sD_s.at[b, which])
        for kind in range(2):
            for j in range(1, 4):
                drain(stage.at[b, kind, u], sQ_s.at[b, kind, j])

        @pl.when(c == 0)
        def _():
            for j in range(1, 4):
                drain(pair(b, slice(None), z, s), sZ_s.at[b, j])
            for zz in range(4):
                drain(pair(b, slice(None), zz, s), sH_s.at[b, zz])
            for i, (at, size) in enumerate(CHUNKS):
                for cc in range(2):
                    for j in range(1, 4):
                        drain(zrecv.at[b, z, pl.ds(at, size)], sR_s.at[b, i, cc, j])

        @pl.when(c == 1)
        def _():
            for i, (at, size) in enumerate(CHUNKS):
                drain(zs1.at[b, pl.ds(at, size)], sK_s.at[b, i])

        @pl.when(b != s)
        def _():
            drain(fin.at[b], sG_s.at[b])
            drain(gsend.at[b], sO_s.at[4 + b])

        @pl.when(b < 2)
        def _():
            par = lax.rem(3 - b, 2)
            for i in range(3):
                y_copy(b, par, i).wait_send()
            for kind in range(2):
                for j in range(1, 4):
                    dz_copy(b, par, kind, j).wait_send()

    @pl.loop(0, 17)
    def _(e):
        sums_close(e)

    out_features.wait()
    out_grad_in.wait()
    for out in outs:
        out.wait()


def train_step(images, crop, w_point, w_spatial, norm_params, mom_point, mom_spatial, mom_norm, out_grad):
    R, D = images.shape[1:]
    f32, bf16 = jnp.float32, jnp.bfloat16
    dma = pltpu.SemaphoreType.DMA
    anywhere = pl.BlockSpec(memory_space=pl.ANY)
    vmem = pl.BlockSpec(memory_space=pltpu.VMEM)
    smem = pl.BlockSpec(memory_space=pltpu.SMEM)
    V = pltpu.VMEM
    scratch = dict(
        W=V((4, TAPS, 8, 4, 16, D), bf16), wown=V((TAPS, 4, 16, D), bf16),
        pbuf=V((TAPS, 64, D), f32), mbuf=V((TAPS, 64, D), f32),
        h=V((R, D), f32), g=V((R, D), f32), zbuf=V((R, D), f32),
        sv=V((4, 4, R, D), bf16), gi=V((4, 8, D), f32),
        abuf=V((R, D), bf16), gbuf=V((R, D), bf16),
        Gm=V((4, 9 * R, R), bf16), caq=V((4, 2, 4, 8, 16, R), bf16),
        stage=V((4, 2, 4, 8, 16, R), bf16), Hb=V((R, 9 * D), bf16),
        GcT=V((9, 128, 4 * R), bf16), dzq=V((2, 2, 4, R, D), bf16),
        gout=V((2, 2, TAPS, 4, 16, D), bf16), yrecv=V((4, TAPS, 4, 16, D), bf16),
        zs1=V((4, TAPS, 4, 16, D), bf16), zrecv=V((4, 4, TAPS, 16, D), bf16),
        fin=V((4, TAPS, 16, D), bf16), gfin=V((TAPS, 4, 16, D), bf16),
        aff=V((4, 8, D), f32), gaff=V((4, 8, D), f32), gsend=V((4, 8, D), f32),
        st_in=V((17, 8, 128), f32), st_own=V((17, 8, 128), f32), st_all=V((17, 4, 8, 128), f32),
        cnt=V((8, 8, 128), f32), cntx=V((4, 8, 128), f32), cown=V((8, 128), f32),
        sL=dma((6,)), sS_s=dma((4,)), sS_r=dma((4, 2)), sZ_s=dma((4, 4)), sZ_r=dma((4, 4)),
        sH_s=dma((4, 4)), sH_r=dma((4, 4)), sA_s=dma((4, 4)), sA_r=dma((4, 4)),
        sB_s=dma((4, 2, 4)), sB_r=dma((4, 2, 4)), sD_s=dma((4, 3)), sD_r=dma((4, 3)),
        sE_in_s=dma((17,)), sE_in_r=dma((17,)), sE_s=dma((17, 8)), sE_r=dma((17, 4)),
        sC_s=dma((12,)), sC_r=dma((12,)), sF_s=dma((4,)), sF_r=dma((4,)),
        sQ_s=dma((4, 2, 4)), sQ_r=dma((4, 2, 4)), sX_s=dma((4, 2, 4)), sX_r=dma((4, 2, 4)),
        sY_s=dma((4, 3)), sY_r=dma((4, 3)), sK_s=dma((4, 3)), sK_r=dma((4, 3)),
        sR_s=dma((4, 3, 2, 4)), sR_r=dma((4, 3, 4)), sG_s=dma((4,)), sG_r=dma((4,)),
        sO_s=dma((8,)), sO_r=dma((4,)), sW=dma((4,)),
    )
    shape = jax.ShapeDtypeStruct
    return pl.pallas_call(
        train_kernel,
        out_shape=(
            shape((1, R, D), f32), shape((1, R, D), f32),
            shape(w_point.shape, f32), shape(w_spatial.shape, f32), shape(norm_params.shape, f32),
            shape(w_point.shape, f32), shape(w_spatial.shape, f32), shape(norm_params.shape, f32),
        ),
        in_specs=[anywhere, smem, anywhere, anywhere, vmem, anywhere, anywhere, vmem, anywhere],
        out_specs=(anywhere, anywhere, anywhere, anywhere, vmem, anywhere, anywhere, vmem),
        scratch_shapes=list(scratch.values()),
        compiler_params=pltpu.CompilerParams(
            collective_id=0, has_side_effects=True, vmem_limit_bytes=64 * 1024 * 1024
        ),
    )(images, crop, w_point, w_spatial, norm_params, mom_point, mom_spatial, mom_norm, out_grad)


def solution(mesh):
    tuned = mesh.shape["section"] == 4 and mesh.shape["batch"] == 8
    return jax.shard_map(
        train_step if tuned else on_device,
        mesh=mesh,
        in_specs=(
            P(None, "batch", None),
            P(None, "batch"),
            P("section", "batch", None),
            P("section", None, "batch", None),
            P("section", None, None),
            P("section", "batch", None),
            P("section", None, "batch", None),
            P("section", None, None),
            P(None, "batch", None),
        ),
        out_specs=(
            P("section", "batch", None),
            P("section", "batch", None),
            P("section", "batch", None),
            P("section", None, "batch", None),
            P("section", None, None),
            P("section", "batch", None),
            P("section", None, "batch", None),
            P("section", None, None),
        ),
        check_vma=False,
    )
```

```python
import jax
import jax.numpy as jnp
from jax import lax
from jax.experimental import pallas as pl
from jax.experimental.pallas import tpu as pltpu
from jax.sharding import PartitionSpec as P

BIG_SIDE = 7
SMALL_SIDE = 3
WARMUP = 20
STEP = 9


EPS = 1e-05
EPS_NORM = 1e-06
BASE_RATE = 6.0
MOMENTUM = 0.9
TRUST_COEF = 0.1


def from_behind(block, axis, distance):
    devices = range(lax.axis_size(axis))
    route = [(i - distance, i) for i in devices if i - distance in devices]
    return lax.ppermute(block, axis, route)


def crop_table(big_count, total_rows):
    places = jnp.arange(total_rows, dtype=jnp.int32)
    big_area = BIG_SIDE * BIG_SIDE
    small_area = SMALL_SIDE * SMALL_SIDE
    big_rows = big_count * big_area
    small_rows = (total_rows - big_rows) // small_area * small_area
    in_big = places < big_rows
    offsets = places - big_rows
    sides = jnp.where(in_big, BIG_SIDE, SMALL_SIDE)
    within = jnp.where(in_big, places % big_area, offsets % small_area)
    starts = places - within
    valid_rows = places < big_rows + small_rows
    row_pos = within // sides
    col_pos = within % sides
    indices = []
    masks = []
    for row_step in (-1, 0, 1):
        for col_step in (-1, 0, 1):
            new_row = row_pos + row_step
            new_col = col_pos + col_step
            inside = (
                valid_rows & (new_row >= 0) & (new_row < sides) & (new_col >= 0) & (new_col < sides)
            )
            indices.append(jnp.where(inside, starts + new_row * sides + new_col, places))
            masks.append(inside)
    return (
        jnp.stack(indices, 1),
        jnp.stack(masks, 1).astype(jnp.float32),
        valid_rows.astype(jnp.float32),
    )


def mish(values):
    return values * jnp.tanh(jax.nn.softplus(values))


def mish_parts(values):
    tangent = jnp.tanh(jax.nn.softplus(values))
    slope = tangent + values * jax.nn.sigmoid(values) * (1.0 - tangent * tangent)
    return (values * tangent, slope)


def mish_slope(values):
    tangent = jnp.tanh(jax.nn.softplus(values))
    return tangent + values * jax.nn.sigmoid(values) * (1.0 - tangent * tangent)


def batch_moments(proj, valid_rows):
    weighted = valid_rows[:, None] * proj
    summed, squared, row_count = lax.psum(
        (jnp.sum(weighted, 0), jnp.sum(weighted * proj, 0), jnp.sum(valid_rows)), "batch"
    )
    center = summed / row_count
    inv_std = lax.rsqrt(squared / row_count - center * center + EPS)
    return (center, inv_std, row_count)


def spatial_apply(source, tap_index, tap_mask, weights):
    stacked = source[tap_index] * tap_mask[:, :, None].astype(source.dtype)
    result = lax.dot_general(
        stacked, weights, (((1, 2), (0, 1)), ((), ())), preferred_element_type=jnp.float32
    )
    return (result, stacked)


def forward_block(hidden, point_low, spatial_low, affine, tap_index, tap_mask, valid_rows):
    proj_one = jnp.dot(hidden.astype(jnp.bfloat16), point_low, preferred_element_type=jnp.float32)
    center_one, inv_one, row_count = batch_moments(proj_one, valid_rows)
    mixed_one = mish(affine[0] * ((proj_one - center_one) * inv_one) + affine[1])
    proj_two, stacked = spatial_apply(
        mixed_one.astype(jnp.bfloat16), tap_index, tap_mask, spatial_low
    )
    center_two, inv_two, count_two = batch_moments(proj_two, valid_rows)
    mixed_two = mish(affine[2] * ((proj_two - center_two) * inv_two) + affine[3])
    moments = jnp.stack([center_one, inv_one, center_two, inv_two])
    return (hidden + valid_rows[:, None] * mixed_two, moments, row_count)


def norm_back(d_value, normed, inv_std, gain, valid_rows, row_count):
    first_sum, second_sum = lax.psum((jnp.sum(d_value, 0), jnp.sum(d_value * normed, 0)), "batch")
    d_proj = (
        gain
        * inv_std
        * (d_value - valid_rows[:, None] * (first_sum + normed * second_sum) / row_count)
    )
    return (d_proj.astype(jnp.bfloat16), first_sum, second_sum)


def backward_block(
    hidden,
    upstream,
    point_low,
    spatial_low,
    affine,
    moments,
    row_count,
    tap_index,
    tap_mask,
    valid_rows,
):
    inputs = hidden.astype(jnp.bfloat16)
    proj_one = jnp.dot(inputs, point_low, preferred_element_type=jnp.float32)
    normed_one = (proj_one - moments[0]) * moments[1]
    mixed_one, slope_one = mish_parts(affine[0] * normed_one + affine[1])
    proj_two, stacked = spatial_apply(
        mixed_one.astype(jnp.bfloat16), tap_index, tap_mask, spatial_low
    )
    normed_two = (proj_two - moments[2]) * moments[3]
    slope_two = mish_slope(affine[2] * normed_two + affine[3])
    d_two, first_two, second_two = norm_back(
        valid_rows[:, None] * upstream * slope_two,
        normed_two,
        moments[3],
        affine[2],
        valid_rows,
        row_count,
    )
    grad_spatial = lax.dot_general(
        stacked, d_two, (((0,), (0,)), ((), ())), preferred_element_type=jnp.float32
    )
    flipped = d_two[tap_index[:, ::-1]] * tap_mask[:, ::-1, None].astype(jnp.bfloat16)
    d_mixed = lax.dot_general(
        flipped, spatial_low, (((1, 2), (0, 2)), ((), ())), preferred_element_type=jnp.float32
    )
    d_one, first_one, second_one = norm_back(
        d_mixed * slope_one, normed_one, moments[1], affine[0], valid_rows, row_count
    )
    grad_point = lax.dot_general(
        inputs, d_one, (((0,), (0,)), ((), ())), preferred_element_type=jnp.float32
    )
    d_hidden = upstream + lax.dot_general(
        d_one, point_low, (((1,), (1,)), ((), ())), preferred_element_type=jnp.float32
    )
    grad_affine = jnp.stack([second_one, first_one, second_two, first_two])
    return (d_hidden, grad_point, grad_spatial, grad_affine)


def store_slot(buffer, value, slot_index, active):
    previous = lax.dynamic_index_in_dim(buffer, slot_index, 0, keepdims=False)
    return lax.dynamic_update_index_in_dim(
        buffer, jnp.where(active, value, previous), slot_index, 0
    )


def lars_update(param, grad, momentum, param_sq, grad_sq, rate):
    trust = TRUST_COEF * jnp.sqrt(param_sq) / (jnp.sqrt(grad_sq) + EPS_NORM)
    new_mom = MOMENTUM * momentum + rate * trust * grad
    return (param - new_mom, new_mom)


def on_device(
    images, crop_big, w_point, w_spatial, norm_params, mom_point, mom_spatial, mom_norm, out_grad
):
    section_count = lax.axis_size("section")
    section_rank = lax.axis_index("section")
    micro_count = images.shape[0]
    total_rows = images.shape[1]
    width = images.shape[2]
    point = w_point[0]
    spatial = w_spatial[0]
    affine = norm_params[0]
    crop_counts = crop_big[:, 0]
    turns = micro_count + section_count - 1
    point_low, spatial_low = (
        lax.all_gather(point.astype(jnp.bfloat16), "batch", axis=0, tiled=True),
        lax.all_gather(spatial.astype(jnp.bfloat16), "batch", axis=1, tiled=True),
    )
    kept_inputs = jnp.zeros((micro_count, total_rows, width), jnp.float32)
    kept_moments = jnp.zeros((micro_count, 4, width), jnp.float32)
    kept_counts = jnp.zeros((micro_count,), jnp.float32)
    results = jnp.zeros((micro_count, total_rows, width), jnp.float32)
    incoming = jnp.zeros((total_rows, width), jnp.float32)
    for phase_turn in range(turns):
        slot_raw = phase_turn - section_rank
        active = (slot_raw >= 0) & (slot_raw < micro_count)
        slot_index = jnp.clip(slot_raw, 0, micro_count - 1)
        fresh_rows = lax.dynamic_index_in_dim(images, slot_index, 0, keepdims=False).astype(
            jnp.float32
        )
        hidden = jnp.where(section_rank == 0, fresh_rows, incoming)
        tap_index, tap_mask, valid_rows = crop_table(crop_counts[slot_index], total_rows)
        output, moments, row_count = forward_block(
            hidden, point_low, spatial_low, affine, tap_index, tap_mask, valid_rows
        )
        kept_inputs = store_slot(kept_inputs, hidden, slot_index, active)
        kept_moments = store_slot(kept_moments, moments, slot_index, active)
        kept_counts = store_slot(kept_counts, row_count, slot_index, active)
        results = store_slot(
            results, output, slot_index, active & (section_rank == section_count - 1)
        )
        if phase_turn + 1 < turns:
            incoming = from_behind(output.astype(jnp.bfloat16), "section", 1).astype(output.dtype)
    point_low, spatial_low = (
        lax.all_gather(point.astype(jnp.bfloat16), "batch", axis=0, tiled=True),
        lax.all_gather(spatial.astype(jnp.bfloat16), "batch", axis=1, tiled=True),
    )
    grad_point = jnp.zeros((width, width), jnp.float32)
    grad_spatial = jnp.zeros((9, width, width), jnp.float32)
    grad_affine = jnp.zeros((4, width), jnp.float32)
    collected = jnp.zeros((micro_count, total_rows, width), jnp.float32)
    returning = jnp.zeros((total_rows, width), jnp.float32)
    for phase_turn in range(turns):
        slot_raw = micro_count - 1 - phase_turn + (section_count - 1 - section_rank)
        active = (slot_raw >= 0) & (slot_raw < micro_count)
        slot_index = jnp.clip(slot_raw, 0, micro_count - 1)
        seeded = lax.dynamic_index_in_dim(out_grad, slot_index, 0, keepdims=False).astype(
            jnp.float32
        )
        upstream = jnp.where(section_rank == section_count - 1, seeded, returning)
        upstream = jnp.where(active, upstream, 0.0)
        tap_index, tap_mask, valid_rows = crop_table(crop_counts[slot_index], total_rows)
        hidden = lax.dynamic_index_in_dim(kept_inputs, slot_index, 0, keepdims=False)
        moments = lax.dynamic_index_in_dim(kept_moments, slot_index, 0, keepdims=False)
        row_count = lax.dynamic_index_in_dim(kept_counts, slot_index, 0, keepdims=False)
        d_hidden, part_point, part_spatial, part_affine = backward_block(
            hidden,
            upstream,
            point_low,
            spatial_low,
            affine,
            moments,
            row_count,
            tap_index,
            tap_mask,
            valid_rows,
        )
        grad_point = grad_point + part_point
        grad_spatial = grad_spatial + part_spatial
        grad_affine = grad_affine + part_affine
        collected = store_slot(collected, d_hidden, slot_index, active & (section_rank == 0))
        if phase_turn + 1 < turns:
            returning = from_behind(d_hidden.astype(jnp.bfloat16), "section", -1).astype(
                d_hidden.dtype
            )
    point_grad, spatial_grad = (
        lax.psum_scatter(grad_point, "batch", scatter_dimension=0, tiled=True),
        lax.psum_scatter(grad_spatial, "batch", scatter_dimension=1, tiled=True),
    )
    point_sq, spatial_sq, gpoint_sq, gspatial_sq = lax.psum(
        (
            jnp.sum(point * point),
            jnp.sum(spatial * spatial),
            jnp.sum(point_grad * point_grad),
            jnp.sum(spatial_grad * spatial_grad),
        ),
        "batch",
    )
    rate = BASE_RATE * (STEP + 1) / WARMUP
    new_point, new_mom_point = lars_update(
        point, point_grad, mom_point[0], point_sq, gpoint_sq, rate
    )
    new_spatial, new_mom_spatial = lars_update(
        spatial, spatial_grad, mom_spatial[0], spatial_sq, gspatial_sq, rate
    )
    affine_sq = jnp.sum(affine * affine, 1, keepdims=True)
    gaffine_sq = jnp.sum(grad_affine * grad_affine, 1, keepdims=True)
    new_affine, new_mom_affine = lars_update(
        affine, grad_affine, mom_norm[0], affine_sq, gaffine_sq, rate
    )
    sent_out = jnp.where(section_rank == section_count - 1, results, 0.0)
    sent_back = jnp.where(section_rank == 0, collected, 0.0)
    got_out, got_back = (
        lax.all_to_all(
            sent_out.astype(jnp.bfloat16), "section", split_axis=0, concat_axis=0, tiled=True
        ).astype(sent_out.dtype),
        lax.all_to_all(
            sent_back.astype(jnp.bfloat16), "section", split_axis=0, concat_axis=0, tiled=True
        ).astype(sent_back.dtype),
    )
    features = got_out[section_count - 1 : section_count]
    in_grad = got_back[0:1]
    return (
        features,
        in_grad,
        new_point[None],
        new_spatial[None],
        new_affine[None],
        new_mom_point[None],
        new_mom_spatial[None],
        new_mom_affine[None],
    )


def swap_copy(source, target, sent, landed, section, batch):
    return pltpu.make_async_remote_copy(
        src_ref=source,
        dst_ref=target,
        send_sem=sent,
        recv_sem=landed,
        device_id=(section, batch),
        device_id_type=pl.DeviceIdType.MESH,
    )


def drain(like, sem):
    pltpu.make_async_copy(like, like, sem).wait()


def mish_terms(v):
    e = jnp.exp(jnp.minimum(v, 20.0))
    w = e * (e + 2.0)
    r = 1.0 / (w + 2.0)
    t = w * r
    return v * t, t + v * (4.0 * e * (1.0 + e)) * (r * r)


def pack(first, second):
    parts = [v[:, i * 128 : (i + 1) * 128] for v in (first, second) for i in range(4)]
    return jnp.concatenate(parts, axis=0)


def unpack(tile):
    rows = [tile[i : i + 1] for i in range(8)]
    return jnp.concatenate(rows[:4], axis=1), jnp.concatenate(rows[4:], axis=1)


def crop_codes(places, big, total_rows):
    big_area = float(BIG_SIDE * BIG_SIDE)
    small_area = float(SMALL_SIDE * SMALL_SIDE)
    big_rows = big * big_area
    small_rows = jnp.floor((total_rows - big_rows + 0.5) / small_area) * small_area
    in_big = places < big_rows
    offset = jnp.where(in_big, places, places - big_rows)
    area = jnp.where(in_big, big_area, small_area)
    side = jnp.where(in_big, float(BIG_SIDE), float(SMALL_SIDE))
    crop = jnp.floor((offset + 0.5) / area)
    within = offset - crop * area
    row = jnp.floor((within + 0.5) / side)
    col = within - row * side
    crop = jnp.where(in_big, crop, crop + big)
    return crop * 1024.0 + (row + 1.0) * 32.0 + (col + 1.0), places < big_rows + small_rows


NT = (((1,), (1,)), ((), ()))
TAPS = 10
HALF = 5


def train_kernel(
    images, crop, w_point, w_spatial, norm_in, out_grad,
    features, in_grad, grads, totals_out, affine_out,
    W, wown, F, sv, gi, abuf, gbuf, Gm, caq, stage, Hb, dzq, gout, yrecv,
    zs1, zrecv, gfin, aff, gaff, gsend, st_in, st_own, st_all, cnt, cntx, cown,
    sL, sS_s, sS_r, sZ_s, sZ_r, sH_s, sH_r, sA_s, sA_r, sB_s, sB_r, sD_s, sD_r,
    sE_in_s, sE_in_r, sE_s, sE_r, sC_s, sC_r, sF_s, sF_r, sQ_s, sQ_r, sX_s, sX_r,
    sY_s, sY_r, sK_s, sK_r, sN_s, sN_r, sT_s, sT_r, sG_s, sG_r, sO_s, sO_r,
):
    s = lax.axis_index("section")
    bat = lax.axis_index("batch")
    z = bat // 2
    c = lax.rem(bat, 2)
    x = lax.rem(s, 2)
    y = s // 2
    u = 2 * x + c
    R, D = abuf.shape
    h = F.at[pl.ds(0, R)]
    g = F.at[pl.ds(R, R)]
    zbuf = F.at[pl.ds(2 * R, R)]

    loads = [
        pltpu.make_async_copy(w_point.at[0], F.at[pl.ds(9 * 64, 64)], sL.at[9]),
        *[
            pltpu.make_async_copy(w_spatial.at[0, k], F.at[pl.ds(k * 64, 64)], sL.at[k])
            for k in range(9)
        ],
        pltpu.make_async_copy(images.at[s], abuf, sL.at[10]),
        pltpu.make_async_copy(out_grad.at[s], gbuf, sL.at[11]),
    ]
    for load in loads:
        load.start()

    barrier = pltpu.get_barrier_semaphore()
    greet = [(s, bat ^ j) for j in range(1, 8)]
    greet += [(s ^ d, bat ^ j) for d in range(1, 4) for j in range(2)]
    for sec, other in greet:
        pl.semaphore_signal(
            barrier, inc=1, device_id=(sec, other), device_id_type=pl.DeviceIdType.MESH
        )

    def square(rows):
        return jnp.sum(rows * rows, 0, keepdims=True)

    spatial_squares = jnp.zeros((1, D), jnp.float32)
    for load in loads[:10]:
        load.wait()
    for k in range(TAPS):
        rows = F[k * 64 : k * 64 + 64]
        wown[k] = rows.astype(jnp.bfloat16).reshape(4, 16, D)
        if k < 9:
            spatial_squares += square(rows)
        else:
            point_squares = square(rows)
    with jax.named_scope("greet"):
        pl.semaphore_wait(barrier, len(greet))

    def scatter(d):
        q = s ^ d
        return swap_copy(
            wown.at[:, q], W.at[s, :, bat, q], sS_s, sS_r.at[s, c], q, 2 * z
        )

    for d in range(1, 4):
        scatter(d).start()

    @pl.when(c == 1)
    def _():
        scatter(0).start()

    @pl.when(c == 0)
    def _():
        pltpu.make_async_copy(wown.at[:, s], W.at[s, :, bat, s], sS_r.at[s, c]).start()

    cown[...] = jnp.full((8, 128), crop[0, s].astype(jnp.float32))
    aff[s] = jnp.concatenate([norm_in[0], jnp.zeros((4, D), jnp.float32)], axis=0)
    cnt[bat] = cown[...]
    cntx[c] = cown[...]
    for j in range(1, 8):
        swap_copy(cown, cnt.at[bat], sC_s, sC_r.at[0], s, bat ^ j).start()
    for j in range(2):
        swap_copy(cown, cntx.at[2 + c], sC_s, sC_r.at[1], s ^ 1, bat ^ j).start()
    for d in range(1, 4):
        swap_copy(aff.at[s], aff.at[s], sF_s, sF_r, s ^ d, bat).start()

    half = pl.ds(HALF * c, HALF)
    first = jnp.where(c == 0, s ^ 1, s ^ 2)
    second = jnp.where(c == 0, s ^ 2, s ^ 1)
    both = s ^ 3

    def pair(b, taps, zz, q):
        return W.at[b, taps, pl.ds(2 * zz, 2), q]

    def to_sibling(b, zz):
        ref = pair(b, slice(None), zz, s)
        return swap_copy(ref, ref, sH_s.at[b], sH_r.at[b, zz], s, bat ^ 1)

    def along_first(b, zz):
        ref = pair(b, half, zz, s)
        return swap_copy(ref, ref, sA_s.at[b], sA_r.at[b, zz], first, bat)

    def along_second(b, which, zz):
        ref = pair(b, half, zz, s if which == 0 else first)
        return swap_copy(ref, ref, sB_s.at[b, which], sB_r.at[b, which], second, bat)

    def quarter_to_sibling(b, which):
        ref = W.at[b, half, :, (first, second, both)[which]]
        return swap_copy(ref, ref, sD_s.at[b, which], sD_r.at[b, which], s, bat ^ 1)

    def own_ready(b, zz):
        @pl.when(c == 0)
        def _():
            to_sibling(b, zz).start()

        @pl.when(c == 1)
        def _():
            to_sibling(b, zz).wait_recv()

        along_first(b, zz).start()
        along_second(b, 0, zz).start()

    def spread_z(b, j):
        ref = pair(b, slice(None), z, s)
        return swap_copy(ref, ref, sZ_s.at[b], sZ_r.at[b, z], s, bat ^ (2 * j))

    def from_z(b, zz):
        ref = pair(b, slice(None), zz, s)
        return swap_copy(ref, ref, sZ_s.at[b], sZ_r.at[b, zz], s, bat)

    @pl.loop(0, 4)
    @jax.named_scope("own_quarter")
    def _(b):
        @pl.when(c == 0)
        def _():
            for cc in range(2):
                drain(W.at[b, :, 2 * z + cc, s], sS_r.at[b, cc])
            for j in range(1, 4):
                spread_z(b, j).start()

        @pl.when(b < 2)
        def _():
            own_ready(b, z)

    @jax.named_scope("gather_z")
    def gather_z(b):
        for j in range(1, 4):
            zz = z ^ j

            @pl.when(c == 0)
            def _():
                from_z(b, zz).wait_recv()

            own_ready(b, zz)

    @jax.named_scope("gather_first")
    def gather_first(b):
        for j in range(4):
            zz = z ^ j
            ref = pair(b, half, zz, first)
            swap_copy(ref, ref, sA_s.at[b], sA_r.at[b, zz], first, bat).wait_recv()
            along_second(b, 1, zz).start()
        quarter_to_sibling(b, 0).start()

    @jax.named_scope("gather_second")
    def gather_second(b):
        for which in range(2):
            drain(W.at[b, half, :, (second, both)[which]], sB_r.at[b, which])
            quarter_to_sibling(b, 1 + which).start()

    @jax.named_scope("gather_last")
    def gather_last(b):
        other = pl.ds(HALF * (1 - c), HALF)
        for which in range(3):
            drain(W.at[b, other, :, (second, first, both)[which]], sD_r.at[b, which])

    drain(cnt.at[pl.ds(0, 7)], sC_r.at[0])
    drain(cntx.at[pl.ds(2, 2)], sC_r.at[1])
    cntx[1 - c] = cnt[bat ^ 1]
    total = jnp.zeros((1, 1), jnp.float32)
    for j in range(8):
        big = cnt[j][0:1, 0:1]
        big_rows = big * float(BIG_SIDE * BIG_SIDE)
        area = float(SMALL_SIDE * SMALL_SIDE)
        total = total + big_rows + jnp.floor((R - big_rows + 0.5) / area) * area
    row_count = total
    down = lax.broadcasted_iota(jnp.int32, (R, 1), 0).astype(jnp.float32)
    across = lax.broadcasted_iota(jnp.int32, (1, R), 1).astype(jnp.float32)

    @pl.loop(0, 4)
    @jax.named_scope("tables")
    def _(v):
        big = cntx[v][0:1, 0:1]
        code_down, ok_down = crop_codes(down, big, R)
        code_across, ok_across = crop_codes(across, big, R)
        code_down = jnp.where(ok_down, code_down, -5000.0)
        code_across = jnp.where(ok_across, code_across, -1.0)
        for k in range(9):
            step = float(32 * (k // 3 - 1) + (k % 3 - 1))
            hit = (code_down + step) == code_across
            Gm[v, pl.ds(k * R, R)] = jnp.where(hit, 1.0, 0.0).astype(jnp.bfloat16)

    _, own_valid = crop_codes(down, cown[0:1, 0:1], R)
    valid = own_valid.astype(jnp.float32)
    drain(aff.at[pl.ds(0, 3)], sF_r)
    loads[10].wait()
    h[...] = abuf[...].astype(jnp.float32)

    @jax.named_scope("sums_start")
    def sums_start(e, first_sum, second_sum):
        st_own[e] = pack(first_sum, second_sum)

        @pl.when(c == 0)
        def _():
            swap_copy(st_own.at[e], st_in.at[e], sE_in_s.at[e], sE_in_r.at[e], s, bat ^ 1).start()

        @pl.when(c == 1)
        def _():
            swap_copy(
                st_own.at[e], st_in.at[e], sE_in_s.at[e], sE_in_r.at[e], s, bat ^ 1
            ).wait_recv()
            st_all[e, z] = st_own[e] + st_in[e]
            for j in (7, 6, 5, 4, 3, 2, 1):
                swap_copy(
                    st_all.at[e, z], st_all.at[e, z], sE_s.at[e], sE_r.at[e], s, bat ^ j
                ).start()

    @jax.named_scope("sums_finish")
    def sums_finish(e):
        @pl.when(c == 0)
        def _():
            drain(st_all.at[e], sE_r.at[e])

        @pl.when(c == 1)
        def _():
            drain(st_all.at[e, pl.ds(0, 3)], sE_r.at[e])

        return unpack(st_all[e, 0] + st_all[e, 1] + st_all[e, 2] + st_all[e, 3])

    def sums_close(e):
        @pl.when(c == 0)
        def _():
            drain(st_own.at[e], sE_in_s.at[e])

        @pl.when(c == 1)
        def _():
            drain(cnt.at[pl.ds(0, 7)], sE_s.at[e])

    def moments(sums):
        center = sums[0] / row_count
        spread = lax.rsqrt(sums[1] / row_count - center * center + EPS)
        return center, spread

    @jax.named_scope("share")
    def share(b, kind, rows):
        turned = rows.T
        for cc in range(2):
            for xx in range(2):
                for yy in range(2):
                    for zz in range(4):
                        at = (2 * zz + cc) * 64 + (2 * yy + xx) * 16
                        stage[b, kind, 2 * xx + cc, 4 * yy + zz] = turned[at : at + 16].astype(
                            jnp.bfloat16
                        )
        caq[b, kind, u] = stage[b, kind, u]

        @pl.when(b == 3)
        def _():
            send_share(b, kind)

    def send_share(b, kind):
        for j in range(1, 4):
            swap_copy(
                stage.at[b, kind, u ^ j], caq.at[b, kind, u], sQ_s.at[b, kind],
                sQ_r.at[b, kind], s ^ (j // 2), bat ^ (j % 2),
            ).start()

    @jax.named_scope("wait_share")
    def wait_share(b, kind):
        drain(caq.at[b, kind, pl.ds(0, 3)], sQ_r.at[b, kind])

    @jax.named_scope("forward")
    def forward(b):
        gather_last(b)

        @pl.when(b == 3)
        def _():
            for early in (2, 1):
                for kind in range(2):
                    send_share(early, kind)

        hidden = h[...]
        zbuf[...] = jnp.dot(
            hidden.astype(jnp.bfloat16), W[b, 9].reshape(D, D), preferred_element_type=jnp.float32
        )
        z1 = zbuf[...]
        kept = valid * z1
        sums_start(
            2 * b, jnp.sum(kept, 0, keepdims=True), jnp.sum(kept * z1, 0, keepdims=True)
        )
        share(b, 1, hidden)

        @pl.when(b < 2)
        def _():
            gather_z(b + 2)

        norms = aff[b]
        center, spread = moments(sums_finish(2 * b))
        gi[b, 0:1] = norms[0:1] * spread
        for i in range(0, R, 64):
            xhat = (zbuf[i : i + 64] - center) * spread
            value, slope = mish_terms(norms[0:1] * xhat + norms[1:2])
            sv[b, 0, i : i + 64] = xhat.astype(sv.dtype)
            sv[b, 1, i : i + 64] = slope.astype(sv.dtype)
            abuf[i : i + 64] = value.astype(jnp.bfloat16)
        mixed = abuf[...]
        for k in range(9):
            Hb[:, k * D : (k + 1) * D] = jnp.dot(
                Gm[c, pl.ds(k * R, R)], mixed, preferred_element_type=jnp.float32
            ).astype(jnp.bfloat16)
        zbuf[...] = jnp.dot(
            Hb[...], W[b, 0:9].reshape(9 * D, D), preferred_element_type=jnp.float32
        )
        z2 = zbuf[...]
        kept = valid * z2
        sums_start(
            2 * b + 1, jnp.sum(kept, 0, keepdims=True), jnp.sum(kept * z2, 0, keepdims=True)
        )
        share(b, 0, mixed.astype(jnp.float32))

        @pl.when(b < 2)
        def _():
            gather_first(b + 2)

        @pl.when(b < 3)
        def _():
            gather_second(b + 1)

        center, spread = moments(sums_finish(2 * b + 1))
        gi[b, 1:2] = norms[2:3] * spread
        for i in range(0, R, 64):
            xhat = (zbuf[i : i + 64] - center) * spread
            value, slope = mish_terms(norms[2:3] * xhat + norms[3:4])
            sv[b, 2, i : i + 64] = xhat.astype(sv.dtype)
            sv[b, 3, i : i + 64] = slope.astype(sv.dtype)
            h[i : i + 64] = h[i : i + 64] + valid[i : i + 64] * value

    gather_z(0)
    own_ready(2, z)
    gather_first(0)
    own_ready(3, z)
    gather_z(1)
    gather_first(1)
    gather_second(0)

    @pl.loop(0, 4)
    def _(b):
        forward(b)

    out_features = pltpu.make_async_copy(h, features.at[0], sO_s.at[0])
    out_features.start()
    loads[11].wait()
    g[...] = gbuf[...].astype(jnp.float32)

    @jax.named_scope("close_gather")
    def close_gather():
        drain(aff.at[pl.ds(0, 3)], sF_s)
        drain(st_own.at[pl.ds(0, 9)], sC_s)

        @pl.when(c == 0)
        def _():
            drain(wown.at[:, pl.ds(0, 3)], sS_s)

        @pl.when(c == 1)
        def _():
            drain(wown, sS_s)

        @pl.loop(0, 4)
        def _(b):
            drain(W.at[b, half, :, s], sA_s.at[b])
            for which in range(2):
                drain(W.at[b, half, :, s], sB_s.at[b, which])
            for which in range(3):
                drain(W.at[b, half, :, s], sD_s.at[b, which])

            @pl.when(c == 0)
            def _():
                drain(W.at[b, :, pl.ds(0, 6), s], sZ_s.at[b])
                drain(W.at[b, :, :, s], sH_s.at[b])

    @jax.named_scope("close_rest")
    def close_rest():
        @pl.loop(0, 4)
        def _(b):
            for kind in range(2):
                drain(stage.at[b, kind, pl.ds(0, 3)], sQ_s.at[b, kind])
                drain(dzq.at[b, kind, pl.ds(0, 3)], sX_s.at[b, kind])

            @pl.when(b != s)
            def _():
                drain(gsend.at[b], sO_s.at[4 + b])

            for i in range(3):
                y_copy(b, i).wait_send()

            @pl.when(c == 1)
            def _():
                for i, (at, size) in enumerate(CHUNKS):
                    drain(zs1.at[b, pl.ds(at, size)], sK_s.at[b, i])

            @pl.when(c == 0)
            def _():
                for i, (at, size) in enumerate(CHUNKS):
                    drain(zrecv.at[b, :, pl.ds(0, 2), pl.ds(at, size)], sN_s.at[b, i])
                    drain(zrecv.at[b, :, 2, pl.ds(at, size)], sT_s.at[b, i])

        @pl.loop(0, 16)
        def _(e):
            sums_close(e)

    CHUNKS = ((0, 5), (5, 4), (9, 1))

    def dz_copy(b, kind, j):
        v = u ^ 2 if j == 3 else u
        ref = dzq.at[b, kind, v]
        return swap_copy(
            ref, ref, sX_s.at[b, kind], sX_r.at[b, kind, v],
            s ^ 1 if j == 2 else s, bat if j == 2 else bat ^ 1,
        )

    def send_dz(b, kind):
        dz_copy(b, kind, 2).start()
        dz_copy(b, kind, 1).start()

    @jax.named_scope("forward_dz")
    def forward_dz(b, kind):
        v = u ^ 2
        drain(dzq.at[b, kind, v], sX_r.at[b, kind, v])
        dz_copy(b, kind, 3).start()

    @jax.named_scope("wait_dz")
    def wait_dz(b, kind):
        for v in (u ^ 1, u ^ 3):
            drain(dzq.at[b, kind, v], sX_r.at[b, kind, v])

    def y_copy(b, i):
        at, size = CHUNKS[i]
        return swap_copy(
            gout.at[b, 1 - y, pl.ds(at, size)], yrecv.at[b, pl.ds(at, size)],
            sY_s.at[b, i], sY_r.at[b, i], s ^ 2, bat,
        )

    def grad_tap(b, k, left, right):
        part = jnp.dot(left, right, preferred_element_type=jnp.float32).astype(jnp.bfloat16)
        for yy in range(2):
            gout[b, yy, k] = part[64 * yy : 64 * yy + 64].reshape(4, 16, D)

    @jax.named_scope("grad_spatial")
    def grad_spatial(b):
        wait_share(b, 0)
        wait_dz(b, 1)
        tables = [jnp.where(x == v // 2, 0, 2) + v % 2 for v in range(4)]
        right = dzq[b, 1].reshape(4 * R, D)
        for k in range(9):
            left = [
                lax.dot_general(
                    caq[b, 0, v].reshape(128, R), Gm[tables[v], pl.ds(k * R, R)], NT,
                    preferred_element_type=jnp.float32,
                ).astype(jnp.bfloat16)
                for v in range(4)
            ]
            grad_tap(b, k, jnp.concatenate(left, axis=1), right)
            if k == 4:
                y_copy(b, 0).start()
        y_copy(b, 1).start()

    @jax.named_scope("grad_point")
    def grad_point(b):
        wait_share(b, 1)
        wait_dz(b, 0)
        left = jnp.concatenate([caq[b, 1, v].reshape(128, R) for v in range(4)], axis=1)
        grad_tap(b, 9, left, dzq[b, 0].reshape(4 * R, D))
        y_copy(b, 2).start()

    def core_copy(b, i):
        at, size = CHUNKS[i]
        return swap_copy(
            yrecv.at[b, pl.ds(at, size)], zs1.at[b, pl.ds(at, size)],
            sK_s.at[b, i], sK_r.at[b, i], s, bat ^ 1,
        )

    @jax.named_scope("reduce_plane")
    def reduce_plane(b, i):
        at, size = CHUNKS[i]
        y_copy(b, i).wait_recv()
        for k in range(at, at + size):
            yrecv[b, k] = (
                yrecv[b, k].astype(jnp.float32) + gout[b, y, k].astype(jnp.float32)
            ).astype(jnp.bfloat16)

        @pl.when(c == 1)
        def _():
            core_copy(b, i).start()

    def z_near(b, i, cc, slot):
        at, size = CHUNKS[i]
        return swap_copy(
            (yrecv, zs1)[cc].at[b, pl.ds(at, size), z ^ (3 if slot else 1)],
            zrecv.at[b, cc, slot, pl.ds(at, size)], sN_s.at[b, i], sN_r.at[b, i], s, bat ^ 2,
        )

    def z_far(b, i, cc):
        at, size = CHUNKS[i]
        return swap_copy(
            zrecv.at[b, cc, 1, pl.ds(at, size)], zrecv.at[b, cc, 2, pl.ds(at, size)],
            sT_s.at[b, i], sT_r.at[b, i], s, bat ^ 4,
        )

    @jax.named_scope("reduce_near")
    def reduce_near(b, i):
        @pl.when(c == 0)
        def _():
            core_copy(b, i).wait_recv()
            for cc in range(2):
                for slot in (1, 0):
                    z_near(b, i, cc, slot).start()

    @jax.named_scope("reduce_far")
    def reduce_far(b, i):
        at, size = CHUNKS[i]

        @pl.when(c == 0)
        def _():
            drain(zrecv.at[b, :, pl.ds(0, 2), pl.ds(at, size)], sN_r.at[b, i])
            for cc in range(2):
                mine = (yrecv, zs1)[cc]
                for k in range(at, at + size):
                    zrecv[b, cc, 1, k] = (
                        zrecv[b, cc, 1, k].astype(jnp.float32) + mine[b, k, z ^ 2].astype(jnp.float32)
                    ).astype(jnp.bfloat16)
                z_far(b, i, cc).start()

    @jax.named_scope("finish")
    def finish(b, i):
        at, size = CHUNKS[i]

        @pl.when(c == 0)
        def _():
            drain(zrecv.at[b, :, 2, pl.ds(at, size)], sT_r.at[b, i])
            for cc in range(2):
                mine = (yrecv, zs1)[cc]
                for k in range(at, at + size):
                    zrecv[b, cc, 0, k] = (
                        zrecv[b, cc, 0, k].astype(jnp.float32)
                        + zrecv[b, cc, 2, k].astype(jnp.float32)
                        + mine[b, k, z].astype(jnp.float32)
                    ).astype(jnp.bfloat16)

                def deliver(section, core):
                    swap_copy(
                        zrecv.at[b, cc, 0, pl.ds(at, size)], gfin.at[pl.ds(at, size), s],
                        sG_s.at[b, cc], sG_r.at[s], section, 2 * z + core,
                    ).start()

                @pl.when(b != s)
                def _():
                    deliver(b, cc)

                @pl.when(b == s)
                def _():
                    if cc == 0:
                        for k in range(at, at + size):
                            gfin[k, s] = zrecv[b, 0, 0, k]
                    else:
                        deliver(s, 1)

    @jax.named_scope("backward")
    def backward(bi):
        b = 3 - bi
        e = 8 + 2 * bi
        first_sum = jnp.zeros((1, D), jnp.float32)
        second_sum = jnp.zeros((1, D), jnp.float32)
        for i in range(0, R, 64):
            du = valid[i : i + 64] * g[i : i + 64] * sv[b, 3, i : i + 64].astype(jnp.float32)
            zbuf[i : i + 64] = du
            first_sum += jnp.sum(du, 0, keepdims=True)
            second_sum += jnp.sum(du * sv[b, 2, i : i + 64].astype(jnp.float32), 0, keepdims=True)
        sums_start(e, first_sum, second_sum)

        @pl.when(bi == 0)
        def _():
            close_gather()

        @pl.when(bi > 0)
        def _():
            forward_dz(b + 1, 1)

        @pl.when(bi > 1)
        def _():
            grad_point(b + 2)

        @pl.when(bi > 2)
        def _():
            reduce_near(3, 0)
            reduce_plane(3, 1)
            reduce_plane(3, 2)

        total_first, total_second = sums_finish(e)
        for i in range(0, R, 64):
            xhat = sv[b, 2, i : i + 64].astype(jnp.float32)
            inner = zbuf[i : i + 64] - valid[i : i + 64] * (
                (total_first + xhat * total_second) / row_count
            )
            dzq[b, 1, u, i : i + 64] = (gi[b, 1:2] * inner).astype(jnp.bfloat16)
        send_dz(b, 1)

        @pl.when(bi == 3)
        def _():
            send_share(0, 1)

        gsend[b, 2:3] = total_second
        gsend[b, 3:4] = total_first
        d_two = dzq[b, 1, u]
        for k in range(9):
            Hb[:, k * D : (k + 1) * D] = jnp.dot(
                Gm[c, pl.ds((8 - k) * R, R)], d_two, preferred_element_type=jnp.float32
            ).astype(jnp.bfloat16)
        mixed = None
        for k in range(9):
            part = lax.dot_general(
                Hb[:, k * D : (k + 1) * D], W[b, k].reshape(D, D), NT,
                preferred_element_type=jnp.float32,
            )
            mixed = part if mixed is None else mixed + part
        zbuf[...] = mixed
        first_sum = jnp.zeros((1, D), jnp.float32)
        second_sum = jnp.zeros((1, D), jnp.float32)
        for i in range(0, R, 64):
            du = zbuf[i : i + 64] * sv[b, 1, i : i + 64].astype(jnp.float32)
            zbuf[i : i + 64] = du
            first_sum += jnp.sum(du, 0, keepdims=True)
            second_sum += jnp.sum(du * sv[b, 0, i : i + 64].astype(jnp.float32), 0, keepdims=True)
        sums_start(e + 1, first_sum, second_sum)

        @pl.when(bi > 0)
        def _():
            grad_spatial(b + 1)
            forward_dz(b + 1, 0)

        @pl.when(bi == 2)
        def _():
            reduce_plane(3, 0)

        @pl.when(bi > 2)
        def _():
            reduce_near(3, 1)
            reduce_near(3, 2)
            reduce_plane(2, 0)
            reduce_far(3, 0)

        total_first, total_second = sums_finish(e + 1)
        for i in range(0, R, 64):
            xhat = sv[b, 0, i : i + 64].astype(jnp.float32)
            inner = zbuf[i : i + 64] - valid[i : i + 64] * (
                (total_first + xhat * total_second) / row_count
            )
            dzq[b, 0, u, i : i + 64] = (gi[b, 0:1] * inner).astype(jnp.bfloat16)
        send_dz(b, 0)

        @pl.when(bi == 2)
        def _():
            send_share(0, 0)

        gsend[b, 0:1] = total_second
        gsend[b, 1:2] = total_first
        g[...] = g[...] + lax.dot_general(
            dzq[b, 0, u], W[b, 9].reshape(D, D), NT, preferred_element_type=jnp.float32
        )

        @pl.when(b == s)
        def _():
            gaff[s] = gsend[b]

        @pl.when(b != s)
        def _():
            swap_copy(gsend.at[b], gaff.at[s], sO_s.at[4 + b], sO_r, b, bat).start()

    @pl.loop(0, 4)
    def _(bi):
        backward(bi)

    out_grad_in = pltpu.make_async_copy(g, in_grad.at[0], sO_s.at[1])
    out_grad_in.start()

    reduce_near(2, 0)
    grad_point(1)
    reduce_far(3, 1)
    reduce_far(3, 2)
    reduce_plane(2, 1)
    forward_dz(0, 1)
    grad_spatial(0)
    reduce_near(2, 1)
    reduce_plane(2, 2)
    reduce_far(2, 0)
    finish(3, 0)
    finish(3, 1)
    reduce_near(2, 2)
    forward_dz(0, 0)
    reduce_plane(1, 0)
    grad_point(0)
    reduce_near(1, 0)
    reduce_far(2, 1)
    finish(3, 2)
    finish(2, 0)
    reduce_far(2, 2)
    reduce_plane(1, 1)
    reduce_plane(1, 2)
    reduce_near(1, 1)
    reduce_near(1, 2)
    reduce_far(1, 0)
    finish(2, 1)
    finish(2, 2)
    reduce_plane(0, 0)
    reduce_near(0, 0)
    reduce_far(1, 1)
    reduce_far(1, 2)
    finish(1, 0)
    finish(1, 1)
    reduce_plane(0, 1)
    reduce_plane(0, 2)
    reduce_near(0, 1)
    reduce_near(0, 2)
    reduce_far(0, 0)
    finish(1, 2)
    finish(0, 0)
    reduce_far(0, 1)
    reduce_far(0, 2)
    finish(0, 1)
    close_rest()
    finish(0, 2)
    for d in range(1, 4):
        drain(gfin.at[:, s ^ d], sG_r.at[s ^ d])

    @pl.when(c == 1)
    def _():
        drain(gfin.at[:, s], sG_r.at[s])

    grads_out = pltpu.make_async_copy(gfin, grads, sO_s.at[2])
    grads_out.start()

    def lane_sum(v):
        return jnp.sum(v, axis=1, keepdims=True)

    gspatial_squares = jnp.zeros((1, D), jnp.float32)
    for k in range(9):
        gspatial_squares += square(gfin[k].astype(jnp.float32).reshape(64, D))
    gpoint_squares = square(gfin[9].astype(jnp.float32).reshape(64, D))
    lanes = lax.broadcasted_iota(jnp.int32, (1, D), 1)
    tile = jnp.zeros((1, D), jnp.float32)
    for i, part in enumerate((point_squares, spatial_squares, gpoint_squares, gspatial_squares)):
        tile = jnp.where(lanes == i, lane_sum(part), tile)
    sums_start(16, tile, tile)
    drain(gaff.at[pl.ds(0, 3)], sO_r)
    affine_out[...] = gaff[0] + gaff[1] + gaff[2] + gaff[3]
    totals, _ = sums_finish(16)
    totals_out[...] = jnp.concatenate([totals] * 8, axis=0)

    with jax.named_scope("close_last"):
        sums_close(16)

        @pl.when(c == 0)
        def _():
            @pl.loop(0, 4)
            def _(b):
                drain(zrecv.at[b, 1, 0], sG_s.at[b, 1])

                @pl.when(b != s)
                def _():
                    drain(zrecv.at[b, 0, 0], sG_s.at[b, 0])

    with jax.named_scope("close_outputs"):
        grads_out.wait()
        out_features.wait()
        out_grad_in.wait()


def lars_kernel(
    feat, ing, grads_in, totals_in, affine_in, w_point, w_spatial, norm_in, mom_point, mom_spatial, mom_norm,
    features, in_grad, new_point, new_spatial, new_norm, new_mom_point, new_mom_spatial, new_mom_norm,
    P, M, G, feat_rows, grad_rows, totals, affine_grad, affine, affine_mom, sem, out_sem,
):
    loads = [
        (totals_in, totals), (affine_in, affine_grad), (norm_in.at[0], affine), (mom_norm.at[0], affine_mom),
        (grads_in, G), (w_spatial.at[0], P.at[pl.ds(0, 9)]), (mom_spatial.at[0], M.at[pl.ds(0, 9)]),
        (w_point.at[0], P.at[9]), (mom_point.at[0], M.at[9]),
    ]
    loads = [pltpu.make_async_copy(a, b, sem.at[i]) for i, (a, b) in enumerate(loads)]
    for load in loads:
        load.start()
    passed = [
        pltpu.make_async_copy(feat, feat_rows, sem.at[9]),
        pltpu.make_async_copy(ing, grad_rows, sem.at[10]),
    ]
    for copy in passed:
        copy.start()
    for load in loads:
        load.wait()
    D = affine.shape[1]
    rate = BASE_RATE * (STEP + 1) / WARMUP
    point_sq, spatial_sq, gpoint_sq, gspatial_sq = [totals[0:1, i : i + 1] for i in range(4)]
    step_point = rate * TRUST_COEF * jnp.sqrt(point_sq) / (jnp.sqrt(gpoint_sq) + EPS_NORM)
    step_spatial = rate * TRUST_COEF * jnp.sqrt(spatial_sq) / (jnp.sqrt(gspatial_sq) + EPS_NORM)
    outs = []

    def store(source, target):
        outs.append(pltpu.make_async_copy(source, target, out_sem.at[len(outs)]))
        outs[-1].start()

    for k in range(10):
        grad = G[k].astype(jnp.float32).reshape(64, D)
        moved = MOMENTUM * M[k] + (step_point if k == 9 else step_spatial) * grad
        M[k] = moved
        P[k] = P[k] - moved
        if k in (2, 5, 8):
            taps = pl.ds(k - 2, 3)
            store(M.at[taps], new_mom_spatial.at[0, taps])
            store(P.at[taps], new_spatial.at[0, taps])
    for copy, rows, target in zip(passed, (feat_rows, grad_rows), (features, in_grad)):
        copy.wait()
        store(rows, target)
    store(M.at[9], new_mom_point.at[0])
    store(P.at[9], new_point.at[0])
    grad = affine_grad[0:4]
    old = affine[...]
    affine_sq = jnp.sum(old * old, axis=1, keepdims=True)
    gaffine_sq = jnp.sum(grad * grad, axis=1, keepdims=True)
    trust = TRUST_COEF * jnp.sqrt(affine_sq) / (jnp.sqrt(gaffine_sq) + EPS_NORM)
    moved = MOMENTUM * affine_mom[...] + rate * trust * grad
    affine_mom[...] = moved
    affine[...] = old - moved
    store(affine_mom, new_mom_norm.at[0])
    store(affine, new_norm.at[0])
    for copy in outs:
        copy.wait()


def train_step(images, crop, w_point, w_spatial, norm_params, mom_point, mom_spatial, mom_norm, out_grad):
    R, D = images.shape[1:]
    f32, bf16 = jnp.float32, jnp.bfloat16
    dma = pltpu.SemaphoreType.DMA
    anywhere = pl.BlockSpec(memory_space=pl.ANY)
    vmem = pl.BlockSpec(memory_space=pltpu.VMEM)
    hbm = pl.BlockSpec(memory_space=pltpu.HBM)
    smem = pl.BlockSpec(memory_space=pltpu.SMEM)
    V = pltpu.VMEM
    scratch = dict(
        W=V((4, TAPS, 8, 4, 16, D), bf16), wown=V((TAPS, 4, 16, D), bf16),
        F=V((3 * R, D), f32),
        sv=V((4, 4, R, D), bf16), gi=V((4, 8, D), f32),
        abuf=V((R, D), bf16), gbuf=V((R, D), bf16),
        Gm=V((4, 9 * R, R), bf16), caq=V((4, 2, 4, 8, 16, R), bf16),
        stage=V((4, 2, 4, 8, 16, R), bf16), Hb=V((R, 9 * D), bf16),
        dzq=V((4, 2, 4, R, D), bf16),
        gout=V((4, 2, TAPS, 4, 16, D), bf16), yrecv=V((4, TAPS, 4, 16, D), bf16),
        zs1=V((4, TAPS, 4, 16, D), bf16), zrecv=V((4, 2, 3, TAPS, 16, D), bf16),
        gfin=V((TAPS, 4, 16, D), bf16),
        aff=V((4, 8, D), f32), gaff=V((4, 8, D), f32), gsend=V((4, 8, D), f32),
        st_in=V((17, 8, 128), f32), st_own=V((17, 8, 128), f32), st_all=V((17, 4, 8, 128), f32),
        cnt=V((8, 8, 128), f32), cntx=V((4, 8, 128), f32), cown=V((8, 128), f32),
        sL=dma((12,)), sS_s=dma, sS_r=dma((4, 2)), sZ_s=dma((4,)), sZ_r=dma((4, 4)),
        sH_s=dma((4,)), sH_r=dma((4, 4)), sA_s=dma((4,)), sA_r=dma((4, 4)),
        sB_s=dma((4, 2)), sB_r=dma((4, 2)), sD_s=dma((4, 3)), sD_r=dma((4, 3)),
        sE_in_s=dma((17,)), sE_in_r=dma((17,)), sE_s=dma((17,)), sE_r=dma((17,)),
        sC_s=dma, sC_r=dma((2,)), sF_s=dma, sF_r=dma,
        sQ_s=dma((4, 2)), sQ_r=dma((4, 2)), sX_s=dma((4, 2)), sX_r=dma((4, 2, 4)),
        sY_s=dma((4, 3)), sY_r=dma((4, 3)), sK_s=dma((4, 3)), sK_r=dma((4, 3)),
        sN_s=dma((4, 3)), sN_r=dma((4, 3)), sT_s=dma((4, 3)), sT_r=dma((4, 3)), sG_s=dma((4, 2)), sG_r=dma((4,)),
        sO_s=dma((8,)), sO_r=dma,
    )
    shape = jax.ShapeDtypeStruct
    feat, ing, grads, totals, affine_grad = pl.pallas_call(
        train_kernel,
        out_shape=(
            shape((1, R, D), f32), shape((1, R, D), f32), shape((TAPS, 4, 16, D), bf16),
            shape((8, D), f32), shape((8, D), f32),
        ),
        in_specs=[anywhere, smem, anywhere, anywhere, vmem, anywhere],
        out_specs=(anywhere, anywhere, anywhere, vmem, vmem),
        scratch_shapes=list(scratch.values()),
        compiler_params=pltpu.CompilerParams(
            collective_id=0, has_side_effects=True, vmem_limit_bytes=64 * 1024 * 1024
        ),
    )(images, crop.T, w_point, w_spatial, norm_params, out_grad)
    return pl.pallas_call(
        lars_kernel,
        out_shape=(
            shape((1, R, D), f32), shape((1, R, D), f32),
            shape(w_point.shape, f32), shape(w_spatial.shape, f32), shape(norm_params.shape, f32),
            shape(w_point.shape, f32), shape(w_spatial.shape, f32), shape(norm_params.shape, f32),
        ),
        in_specs=[hbm] * 11,
        out_specs=(hbm,) * 8,
        scratch_shapes=[
            V((TAPS, 64, D), f32), V((TAPS, 64, D), f32), V((TAPS, 4, 16, D), bf16), V((1, R, D), f32),
            V((1, R, D), f32), V((8, D), f32), V((8, D), f32), V((4, D), f32), V((4, D), f32), dma((11,)), dma((12,)),
        ],
        compiler_params=pltpu.CompilerParams(vmem_limit_bytes=64 * 1024 * 1024),
    )(feat, ing, grads, totals, affine_grad, w_point, w_spatial, norm_params, mom_point, mom_spatial, mom_norm)


def solution(mesh):
    tuned = mesh.shape["section"] == 4 and mesh.shape["batch"] == 8
    return jax.shard_map(
        train_step if tuned else on_device,
        mesh=mesh,
        in_specs=(
            P(None, "batch", None),
            P(None, "batch"),
            P("section", "batch", None),
            P("section", None, "batch", None),
            P("section", None, None),
            P("section", "batch", None),
            P("section", None, "batch", None),
            P("section", None, None),
            P(None, "batch", None),
        ),
        out_specs=(
            P("section", "batch", None),
            P("section", "batch", None),
            P("section", "batch", None),
            P("section", None, "batch", None),
            P("section", None, None),
            P("section", "batch", None),
            P("section", None, "batch", None),
            P("section", None, None),
        ),
        check_vma=False,
    )
```

```python
import functools

import jax
import jax.numpy as jnp
from jax import lax
from jax.experimental import pallas as pl
from jax.experimental.pallas import tpu as pltpu
from jax.sharding import PartitionSpec as P

BIG_SIDE = 7
SMALL_SIDE = 3
WARMUP = 20
STEP = 9


EPS = 1e-05
EPS_NORM = 1e-06
BASE_RATE = 6.0
MOMENTUM = 0.9
TRUST_COEF = 0.1


def from_behind(block, axis, distance):
    devices = range(lax.axis_size(axis))
    route = [(i - distance, i) for i in devices if i - distance in devices]
    return lax.ppermute(block, axis, route)


def crop_table(big_count, total_rows):
    places = jnp.arange(total_rows, dtype=jnp.int32)
    big_area = BIG_SIDE * BIG_SIDE
    small_area = SMALL_SIDE * SMALL_SIDE
    big_rows = big_count * big_area
    small_rows = (total_rows - big_rows) // small_area * small_area
    in_big = places < big_rows
    offsets = places - big_rows
    sides = jnp.where(in_big, BIG_SIDE, SMALL_SIDE)
    within = jnp.where(in_big, places % big_area, offsets % small_area)
    starts = places - within
    valid_rows = places < big_rows + small_rows
    row_pos = within // sides
    col_pos = within % sides
    indices = []
    masks = []
    for row_step in (-1, 0, 1):
        for col_step in (-1, 0, 1):
            new_row = row_pos + row_step
            new_col = col_pos + col_step
            inside = (
                valid_rows & (new_row >= 0) & (new_row < sides) & (new_col >= 0) & (new_col < sides)
            )
            indices.append(jnp.where(inside, starts + new_row * sides + new_col, places))
            masks.append(inside)
    return (
        jnp.stack(indices, 1),
        jnp.stack(masks, 1).astype(jnp.float32),
        valid_rows.astype(jnp.float32),
    )


def mish(values):
    return values * jnp.tanh(jax.nn.softplus(values))


def mish_parts(values):
    tangent = jnp.tanh(jax.nn.softplus(values))
    slope = tangent + values * jax.nn.sigmoid(values) * (1.0 - tangent * tangent)
    return (values * tangent, slope)


def mish_slope(values):
    tangent = jnp.tanh(jax.nn.softplus(values))
    return tangent + values * jax.nn.sigmoid(values) * (1.0 - tangent * tangent)


def batch_moments(proj, valid_rows):
    weighted = valid_rows[:, None] * proj
    summed, squared, row_count = lax.psum(
        (jnp.sum(weighted, 0), jnp.sum(weighted * proj, 0), jnp.sum(valid_rows)), "batch"
    )
    center = summed / row_count
    inv_std = lax.rsqrt(squared / row_count - center * center + EPS)
    return (center, inv_std, row_count)


def spatial_apply(source, tap_index, tap_mask, weights):
    stacked = source[tap_index] * tap_mask[:, :, None].astype(source.dtype)
    result = lax.dot_general(
        stacked, weights, (((1, 2), (0, 1)), ((), ())), preferred_element_type=jnp.float32
    )
    return (result, stacked)


def forward_block(hidden, point_low, spatial_low, affine, tap_index, tap_mask, valid_rows):
    proj_one = jnp.dot(hidden.astype(jnp.bfloat16), point_low, preferred_element_type=jnp.float32)
    center_one, inv_one, row_count = batch_moments(proj_one, valid_rows)
    mixed_one = mish(affine[0] * ((proj_one - center_one) * inv_one) + affine[1])
    proj_two, stacked = spatial_apply(
        mixed_one.astype(jnp.bfloat16), tap_index, tap_mask, spatial_low
    )
    center_two, inv_two, count_two = batch_moments(proj_two, valid_rows)
    mixed_two = mish(affine[2] * ((proj_two - center_two) * inv_two) + affine[3])
    moments = jnp.stack([center_one, inv_one, center_two, inv_two])
    return (hidden + valid_rows[:, None] * mixed_two, moments, row_count)


def norm_back(d_value, normed, inv_std, gain, valid_rows, row_count):
    first_sum, second_sum = lax.psum((jnp.sum(d_value, 0), jnp.sum(d_value * normed, 0)), "batch")
    d_proj = (
        gain
        * inv_std
        * (d_value - valid_rows[:, None] * (first_sum + normed * second_sum) / row_count)
    )
    return (d_proj.astype(jnp.bfloat16), first_sum, second_sum)


def backward_block(
    hidden,
    upstream,
    point_low,
    spatial_low,
    affine,
    moments,
    row_count,
    tap_index,
    tap_mask,
    valid_rows,
):
    inputs = hidden.astype(jnp.bfloat16)
    proj_one = jnp.dot(inputs, point_low, preferred_element_type=jnp.float32)
    normed_one = (proj_one - moments[0]) * moments[1]
    mixed_one, slope_one = mish_parts(affine[0] * normed_one + affine[1])
    proj_two, stacked = spatial_apply(
        mixed_one.astype(jnp.bfloat16), tap_index, tap_mask, spatial_low
    )
    normed_two = (proj_two - moments[2]) * moments[3]
    slope_two = mish_slope(affine[2] * normed_two + affine[3])
    d_two, first_two, second_two = norm_back(
        valid_rows[:, None] * upstream * slope_two,
        normed_two,
        moments[3],
        affine[2],
        valid_rows,
        row_count,
    )
    grad_spatial = lax.dot_general(
        stacked, d_two, (((0,), (0,)), ((), ())), preferred_element_type=jnp.float32
    )
    flipped = d_two[tap_index[:, ::-1]] * tap_mask[:, ::-1, None].astype(jnp.bfloat16)
    d_mixed = lax.dot_general(
        flipped, spatial_low, (((1, 2), (0, 2)), ((), ())), preferred_element_type=jnp.float32
    )
    d_one, first_one, second_one = norm_back(
        d_mixed * slope_one, normed_one, moments[1], affine[0], valid_rows, row_count
    )
    grad_point = lax.dot_general(
        inputs, d_one, (((0,), (0,)), ((), ())), preferred_element_type=jnp.float32
    )
    d_hidden = upstream + lax.dot_general(
        d_one, point_low, (((1,), (1,)), ((), ())), preferred_element_type=jnp.float32
    )
    grad_affine = jnp.stack([second_one, first_one, second_two, first_two])
    return (d_hidden, grad_point, grad_spatial, grad_affine)


def store_slot(buffer, value, slot_index, active):
    previous = lax.dynamic_index_in_dim(buffer, slot_index, 0, keepdims=False)
    return lax.dynamic_update_index_in_dim(
        buffer, jnp.where(active, value, previous), slot_index, 0
    )


def lars_update(param, grad, momentum, param_sq, grad_sq, rate):
    trust = TRUST_COEF * jnp.sqrt(param_sq) / (jnp.sqrt(grad_sq) + EPS_NORM)
    new_mom = MOMENTUM * momentum + rate * trust * grad
    return (param - new_mom, new_mom)


def on_device(
    images, crop_big, w_point, w_spatial, norm_params, mom_point, mom_spatial, mom_norm, out_grad
):
    section_count = lax.axis_size("section")
    section_rank = lax.axis_index("section")
    micro_count = images.shape[0]
    total_rows = images.shape[1]
    width = images.shape[2]
    point = w_point[0]
    spatial = w_spatial[0]
    affine = norm_params[0]
    crop_counts = crop_big[:, 0]
    turns = micro_count + section_count - 1
    point_low, spatial_low = (
        lax.all_gather(point.astype(jnp.bfloat16), "batch", axis=0, tiled=True),
        lax.all_gather(spatial.astype(jnp.bfloat16), "batch", axis=1, tiled=True),
    )
    kept_inputs = jnp.zeros((micro_count, total_rows, width), jnp.float32)
    kept_moments = jnp.zeros((micro_count, 4, width), jnp.float32)
    kept_counts = jnp.zeros((micro_count,), jnp.float32)
    results = jnp.zeros((micro_count, total_rows, width), jnp.float32)
    incoming = jnp.zeros((total_rows, width), jnp.float32)
    for phase_turn in range(turns):
        slot_raw = phase_turn - section_rank
        active = (slot_raw >= 0) & (slot_raw < micro_count)
        slot_index = jnp.clip(slot_raw, 0, micro_count - 1)
        fresh_rows = lax.dynamic_index_in_dim(images, slot_index, 0, keepdims=False).astype(
            jnp.float32
        )
        hidden = jnp.where(section_rank == 0, fresh_rows, incoming)
        tap_index, tap_mask, valid_rows = crop_table(crop_counts[slot_index], total_rows)
        output, moments, row_count = forward_block(
            hidden, point_low, spatial_low, affine, tap_index, tap_mask, valid_rows
        )
        kept_inputs = store_slot(kept_inputs, hidden, slot_index, active)
        kept_moments = store_slot(kept_moments, moments, slot_index, active)
        kept_counts = store_slot(kept_counts, row_count, slot_index, active)
        results = store_slot(
            results, output, slot_index, active & (section_rank == section_count - 1)
        )
        if phase_turn + 1 < turns:
            incoming = from_behind(output.astype(jnp.bfloat16), "section", 1).astype(output.dtype)
    point_low, spatial_low = (
        lax.all_gather(point.astype(jnp.bfloat16), "batch", axis=0, tiled=True),
        lax.all_gather(spatial.astype(jnp.bfloat16), "batch", axis=1, tiled=True),
    )
    grad_point = jnp.zeros((width, width), jnp.float32)
    grad_spatial = jnp.zeros((9, width, width), jnp.float32)
    grad_affine = jnp.zeros((4, width), jnp.float32)
    collected = jnp.zeros((micro_count, total_rows, width), jnp.float32)
    returning = jnp.zeros((total_rows, width), jnp.float32)
    for phase_turn in range(turns):
        slot_raw = micro_count - 1 - phase_turn + (section_count - 1 - section_rank)
        active = (slot_raw >= 0) & (slot_raw < micro_count)
        slot_index = jnp.clip(slot_raw, 0, micro_count - 1)
        seeded = lax.dynamic_index_in_dim(out_grad, slot_index, 0, keepdims=False).astype(
            jnp.float32
        )
        upstream = jnp.where(section_rank == section_count - 1, seeded, returning)
        upstream = jnp.where(active, upstream, 0.0)
        tap_index, tap_mask, valid_rows = crop_table(crop_counts[slot_index], total_rows)
        hidden = lax.dynamic_index_in_dim(kept_inputs, slot_index, 0, keepdims=False)
        moments = lax.dynamic_index_in_dim(kept_moments, slot_index, 0, keepdims=False)
        row_count = lax.dynamic_index_in_dim(kept_counts, slot_index, 0, keepdims=False)
        d_hidden, part_point, part_spatial, part_affine = backward_block(
            hidden,
            upstream,
            point_low,
            spatial_low,
            affine,
            moments,
            row_count,
            tap_index,
            tap_mask,
            valid_rows,
        )
        grad_point = grad_point + part_point
        grad_spatial = grad_spatial + part_spatial
        grad_affine = grad_affine + part_affine
        collected = store_slot(collected, d_hidden, slot_index, active & (section_rank == 0))
        if phase_turn + 1 < turns:
            returning = from_behind(d_hidden.astype(jnp.bfloat16), "section", -1).astype(
                d_hidden.dtype
            )
    point_grad, spatial_grad = (
        lax.psum_scatter(grad_point, "batch", scatter_dimension=0, tiled=True),
        lax.psum_scatter(grad_spatial, "batch", scatter_dimension=1, tiled=True),
    )
    point_sq, spatial_sq, gpoint_sq, gspatial_sq = lax.psum(
        (
            jnp.sum(point * point),
            jnp.sum(spatial * spatial),
            jnp.sum(point_grad * point_grad),
            jnp.sum(spatial_grad * spatial_grad),
        ),
        "batch",
    )
    rate = BASE_RATE * (STEP + 1) / WARMUP
    new_point, new_mom_point = lars_update(
        point, point_grad, mom_point[0], point_sq, gpoint_sq, rate
    )
    new_spatial, new_mom_spatial = lars_update(
        spatial, spatial_grad, mom_spatial[0], spatial_sq, gspatial_sq, rate
    )
    affine_sq = jnp.sum(affine * affine, 1, keepdims=True)
    gaffine_sq = jnp.sum(grad_affine * grad_affine, 1, keepdims=True)
    new_affine, new_mom_affine = lars_update(
        affine, grad_affine, mom_norm[0], affine_sq, gaffine_sq, rate
    )
    sent_out = jnp.where(section_rank == section_count - 1, results, 0.0)
    sent_back = jnp.where(section_rank == 0, collected, 0.0)
    got_out, got_back = (
        lax.all_to_all(
            sent_out.astype(jnp.bfloat16), "section", split_axis=0, concat_axis=0, tiled=True
        ).astype(sent_out.dtype),
        lax.all_to_all(
            sent_back.astype(jnp.bfloat16), "section", split_axis=0, concat_axis=0, tiled=True
        ).astype(sent_back.dtype),
    )
    features = got_out[section_count - 1 : section_count]
    in_grad = got_back[0:1]
    return (
        features,
        in_grad,
        new_point[None],
        new_spatial[None],
        new_affine[None],
        new_mom_point[None],
        new_mom_spatial[None],
        new_mom_affine[None],
    )


def swap_copy(source, target, sent, landed, section, batch):
    return pltpu.make_async_remote_copy(
        src_ref=source,
        dst_ref=target,
        send_sem=sent,
        recv_sem=landed,
        device_id=(section, batch),
        device_id_type=pl.DeviceIdType.MESH,
    )


def drain(like, sem):
    pltpu.make_async_copy(like, like, sem).wait()


def mish_terms(v):
    e = jnp.exp(jnp.minimum(v, 20.0))
    w = e * (e + 2.0)
    r = 1.0 / (w + 2.0)
    t = w * r
    return v * t, t + v * (4.0 * e * (1.0 + e)) * (r * r)


def pack(first, second):
    parts = [v[:, i * 128 : (i + 1) * 128] for v in (first, second) for i in range(4)]
    return jnp.concatenate(parts, axis=0)


def unpack(tile):
    rows = [tile[i : i + 1] for i in range(8)]
    return jnp.concatenate(rows[:4], axis=1), jnp.concatenate(rows[4:], axis=1)


def crop_codes(places, big, total_rows):
    big_area = float(BIG_SIDE * BIG_SIDE)
    small_area = float(SMALL_SIDE * SMALL_SIDE)
    big_rows = big * big_area
    small_rows = jnp.floor((total_rows - big_rows + 0.5) / small_area) * small_area
    in_big = places < big_rows
    offset = jnp.where(in_big, places, places - big_rows)
    area = jnp.where(in_big, big_area, small_area)
    side = jnp.where(in_big, float(BIG_SIDE), float(SMALL_SIDE))
    crop = jnp.floor((offset + 0.5) / area)
    within = offset - crop * area
    row = jnp.floor((within + 0.5) / side)
    col = within - row * side
    crop = jnp.where(in_big, crop, crop + big)
    return crop * 1024.0 + (row + 1.0) * 32.0 + (col + 1.0), places < big_rows + small_rows


NT = (((1,), (1,)), ((), ()))
TAPS = 10
HALF = 5


def train_kernel(
    images, crop, w_point, w_spatial, norm_in, out_grad,
    features, in_grad, grads, totals_out, affine_out,
    W, wown, F, sv, gi, abuf, Gm, caq, stage, stage_a, Hb, dzq, dz1q, pgrad, precv, gout, yrecv,
    zs1, zrecv, gfin, aff, gaff, gsend, st_in, st_own, st_all, cnt, cntx, cown,
    sL, sS_s, sS_r, sZ_s, sZ_r, sH_s, sH_r, sA_s, sA_r, sB_s, sB_r, sD_s, sD_r,
    sE_in_s, sE_in_r, sE_s, sE_r, sC_s, sC_r, sF_s, sF_r, sQ_s, sQ_r, sX_s, sX_r, sM_s, sM_r, sP_s, sP_r,
    sY_s, sY_r, sK_s, sK_r, sN_s, sN_r, sT_s, sT_r, sG_s, sG_r, sO_s, sO_r,
):
    s = lax.axis_index("section")
    bat = lax.axis_index("batch")
    z = bat // 2
    c = lax.rem(bat, 2)
    x = lax.rem(s, 2)
    y = s // 2
    R, D = abuf.shape
    h = F.at[pl.ds(0, R)]
    g = F.at[pl.ds(R, R)]
    zbuf = F.at[pl.ds(2 * R, R)]

    loads = [
        pltpu.make_async_copy(w_point.at[0], F.at[pl.ds(9 * 64, 64)], sL.at[9]),
        *[
            pltpu.make_async_copy(w_spatial.at[0, k], F.at[pl.ds(k * 64, 64)], sL.at[k])
            for k in range(9)
        ],
        pltpu.make_async_copy(images.at[s], abuf, sL.at[10]),
    ]
    for load in loads:
        load.start()

    barrier = pltpu.get_barrier_semaphore()
    greet = [(s, bat ^ j) for j in range(1, 8)]
    greet += [(s ^ d, bat ^ j) for d in range(1, 4) for j in range(2)]
    for sec, other in greet:
        pl.semaphore_signal(
            barrier, inc=1, device_id=(sec, other), device_id_type=pl.DeviceIdType.MESH
        )

    def square(rows):
        return jnp.sum(rows * rows, 0, keepdims=True)

    spatial_squares = jnp.zeros((1, D), jnp.float32)
    for load in loads[:10]:
        load.wait()
    for k in range(TAPS):
        rows = F[k * 64 : k * 64 + 64]
        wown[k] = rows.astype(jnp.bfloat16).reshape(4, 16, D)
        if k < 9:
            spatial_squares += square(rows)
        else:
            point_squares = square(rows)
    with jax.named_scope("greet"):
        pl.semaphore_wait(barrier, len(greet))

    def scatter(d):
        q = s ^ d
        return swap_copy(
            wown.at[:, q], W.at[s, :, bat, q], sS_s, sS_r.at[s, c], q, 2 * z
        )

    for d in range(1, 4):
        scatter(d).start()

    @pl.when(c == 1)
    def _():
        scatter(0).start()

    @pl.when(c == 0)
    def _():
        pltpu.make_async_copy(wown.at[:, s], W.at[s, :, bat, s], sS_r.at[s, c]).start()

    cown[...] = jnp.full((8, 128), crop[0, s].astype(jnp.float32))
    aff[s] = jnp.concatenate([norm_in[0], jnp.zeros((4, D), jnp.float32)], axis=0)
    cnt[bat] = cown[...]
    cntx[c] = cown[...]
    for j in range(1, 8):
        swap_copy(cown, cnt.at[bat], sC_s, sC_r.at[0], s, bat ^ j).start()
    for j in range(2):
        for near in (1, 2):
            swap_copy(cown, cntx.at[2 * near + c], sC_s, sC_r.at[1], s ^ near, bat ^ j).start()
    for d in range(1, 4):
        swap_copy(aff.at[s], aff.at[s], sF_s, sF_r, s ^ d, bat).start()

    half = pl.ds(HALF * c, HALF)
    first = jnp.where(c == 0, s ^ 1, s ^ 2)
    second = jnp.where(c == 0, s ^ 2, s ^ 1)
    both = s ^ 3

    def pair(b, taps, zz, q):
        return W.at[b, taps, pl.ds(2 * zz, 2), q]

    def to_sibling(b, zz):
        ref = pair(b, slice(None), zz, s)
        return swap_copy(ref, ref, sH_s.at[b], sH_r.at[b, zz], s, bat ^ 1)

    def along_first(b, zz):
        ref = pair(b, half, zz, s)
        return swap_copy(ref, ref, sA_s.at[b], sA_r.at[b, zz], first, bat)

    def along_second(b, which, zz):
        ref = pair(b, half, zz, s if which == 0 else first)
        return swap_copy(ref, ref, sB_s.at[b, which], sB_r.at[b, which], second, bat)

    def quarter_to_sibling(b, which):
        ref = W.at[b, half, :, (first, second, both)[which]]
        return swap_copy(ref, ref, sD_s.at[b, which], sD_r.at[b, which], s, bat ^ 1)

    def own_ready(b, zz):
        @pl.when(c == 0)
        def _():
            to_sibling(b, zz).start()

        @pl.when(c == 1)
        def _():
            to_sibling(b, zz).wait_recv()

        along_first(b, zz).start()
        along_second(b, 0, zz).start()

    def spread_z(b, j):
        ref = pair(b, slice(None), z, s)
        return swap_copy(ref, ref, sZ_s.at[b], sZ_r.at[b, z], s, bat ^ (2 * j))

    def from_z(b, zz):
        ref = pair(b, slice(None), zz, s)
        return swap_copy(ref, ref, sZ_s.at[b], sZ_r.at[b, zz], s, bat)

    @pl.loop(0, 4)
    @jax.named_scope("own_quarter")
    def _(b):
        @pl.when(c == 0)
        def _():
            for cc in range(2):
                drain(W.at[b, :, 2 * z + cc, s], sS_r.at[b, cc])
            for j in range(1, 4):
                spread_z(b, j).start()

        @pl.when(b < 3)
        def _():
            own_ready(b, z)

    @jax.named_scope("gather_z")
    def gather_z(b):
        for j in range(1, 4):
            zz = z ^ j

            @pl.when(c == 0)
            def _():
                from_z(b, zz).wait_recv()

            own_ready(b, zz)

    @jax.named_scope("gather_first")
    def gather_first(b):
        for j in range(4):
            zz = z ^ j
            ref = pair(b, half, zz, first)
            swap_copy(ref, ref, sA_s.at[b], sA_r.at[b, zz], first, bat).wait_recv()
            along_second(b, 1, zz).start()
        quarter_to_sibling(b, 0).start()

    @jax.named_scope("gather_second")
    def gather_second(b):
        for which in range(2):
            drain(W.at[b, half, :, (second, both)[which]], sB_r.at[b, which])
            quarter_to_sibling(b, 1 + which).start()

    @jax.named_scope("gather_last")
    def gather_last(b):
        other = pl.ds(HALF * (1 - c), HALF)
        for which in range(3):
            drain(W.at[b, other, :, (second, first, both)[which]], sD_r.at[b, which])

    drain(cnt.at[pl.ds(0, 7)], sC_r.at[0])
    drain(cntx.at[pl.ds(2, 4)], sC_r.at[1])
    cntx[1 - c] = cnt[bat ^ 1]
    total = jnp.zeros((1, 1), jnp.float32)
    for j in range(8):
        big = cnt[j][0:1, 0:1]
        big_rows = big * float(BIG_SIDE * BIG_SIDE)
        area = float(SMALL_SIDE * SMALL_SIDE)
        total = total + big_rows + jnp.floor((R - big_rows + 0.5) / area) * area
    row_count = total
    down = lax.broadcasted_iota(jnp.int32, (R, 1), 0).astype(jnp.float32)
    across = lax.broadcasted_iota(jnp.int32, (1, R), 1).astype(jnp.float32)

    @pl.loop(0, 6)
    @jax.named_scope("tables")
    def _(v):
        big = cntx[v][0:1, 0:1]
        code_down, ok_down = crop_codes(down, big, R)
        code_across, ok_across = crop_codes(across, big, R)
        code_down = jnp.where(ok_down, code_down, -5000.0)
        code_across = jnp.where(ok_across, code_across, -1.0)
        for k in range(9):
            step = float(32 * (k // 3 - 1) + (k % 3 - 1))
            hit = (code_down + step) == code_across
            Gm[v, pl.ds(k * R, R)] = jnp.where(hit, 1.0, 0.0).astype(jnp.bfloat16)

    _, own_valid = crop_codes(down, cown[0:1, 0:1], R)
    valid = own_valid.astype(jnp.float32)
    drain(aff.at[pl.ds(0, 3)], sF_r)
    loads[10].wait()
    h[...] = abuf[...].astype(jnp.float32)

    @jax.named_scope("sums_start")
    def sums_start(e, first_sum, second_sum):
        st_own[e] = pack(first_sum, second_sum)

        @pl.when(c == 0)
        def _():
            swap_copy(st_own.at[e], st_in.at[e], sE_in_s.at[e], sE_in_r.at[e], s, bat ^ 1).start()

        @pl.when(c == 1)
        def _():
            swap_copy(
                st_own.at[e], st_in.at[e], sE_in_s.at[e], sE_in_r.at[e], s, bat ^ 1
            ).wait_recv()
            st_all[e, z] = st_own[e] + st_in[e]
            for j in (7, 6, 5, 4, 3, 2, 1):
                swap_copy(
                    st_all.at[e, z], st_all.at[e, z], sE_s.at[e], sE_r.at[e], s, bat ^ j
                ).start()

    @jax.named_scope("sums_finish")
    def sums_finish(e):
        @pl.when(c == 0)
        def _():
            drain(st_all.at[e], sE_r.at[e])

        @pl.when(c == 1)
        def _():
            drain(st_all.at[e, pl.ds(0, 3)], sE_r.at[e])

        return unpack(st_all[e, 0] + st_all[e, 1] + st_all[e, 2] + st_all[e, 3])

    def sums_close(e):
        @pl.when(c == 0)
        def _():
            drain(st_own.at[e], sE_in_s.at[e])

        @pl.when(c == 1)
        def _():
            drain(cnt.at[pl.ds(0, 7)], sE_s.at[e])

    def moments(sums):
        center = sums[0] / row_count
        spread = lax.rsqrt(sums[1] / row_count - center * center + EPS)
        return center, spread

    def pairing(b):
        odd = lax.rem(b, 2) == 1
        return jnp.where(odd, x, y), jnp.where(odd, y, x), jnp.where(odd, 1, 2)

    @jax.named_scope("share")
    def share(b, kind, rows):
        turned = rows.T
        rows_to = stage_a if kind == 1 else stage.at[b]
        if kind == 1:
            @pl.when(b > 0)
            def _():
                drain(stage_a.at[pl.ds(0, 2)], sQ_s.at[b - 1, 1])

        odd = lax.rem(b, 2) == 1
        for cc in range(2):
            for xx in range(2):
                for yy in range(2):
                    one, two = jnp.where(odd, xx, yy), jnp.where(odd, yy, xx)
                    for zz in range(4):
                        at = (2 * zz + cc) * 64 + (2 * yy + xx) * 16
                        rows_to[2 * one + cc, 4 * two + zz] = turned[at : at + 16].astype(
                            jnp.bfloat16
                        )
        if kind == 1:
            for half_of_pair in range(2):
                v = 2 * half_of_pair
                caq[b, 1, v + c] = stage_a[v + c]
                swap_copy(
                    stage_a.at[v + 1 - c], caq.at[b, 1, v + c], sQ_s.at[b, 1], sQ_r.at[b, 1], s, bat ^ 1
                ).start()
        else:
            u = 2 * pairing(b)[0] + c
            caq[b, 0, u] = stage[b, u]

            @pl.when(b == 3)
            def _():
                send_share(b)

    def send_share(b):
        mine, _, near = pairing(b)
        u = 2 * mine + c
        for j in range(1, 4):
            swap_copy(
                stage.at[b, u ^ j], caq.at[b, 0, u], sQ_s.at[b, 0], sQ_r.at[b, 0],
                s ^ near if j > 1 else s, bat ^ (j % 2),
            ).start()

    def wait_share(b, kind):
        drain(caq.at[b, kind, pl.ds(0, 2 if kind == 1 else 3)], sQ_r.at[b, kind])

    @jax.named_scope("forward")
    def forward(b):
        gather_last(b)

        @pl.when(b == 3)
        def _():
            for early in (2, 1, 0):
                send_share(early)

        hidden = h[...]
        zbuf[...] = jnp.dot(
            hidden.astype(jnp.bfloat16), W[b, 9].reshape(D, D), preferred_element_type=jnp.float32
        )
        z1 = zbuf[...]
        kept = valid * z1
        sums_start(
            2 * b, jnp.sum(kept, 0, keepdims=True), jnp.sum(kept * z1, 0, keepdims=True)
        )
        share(b, 1, hidden)

        @pl.when(b < 2)
        def _():
            gather_first(b + 1)


        norms = aff[b]
        center, spread = moments(sums_finish(2 * b))
        gi[b, 0:1] = norms[0:1] * spread
        for i in range(0, R, 64):
            xhat = (zbuf[i : i + 64] - center) * spread
            value, slope = mish_terms(norms[0:1] * xhat + norms[1:2])
            sv[b, 0, i : i + 64] = xhat.astype(sv.dtype)
            sv[b, 1, i : i + 64] = slope.astype(sv.dtype)
            abuf[i : i + 64] = value.astype(jnp.bfloat16)
        mixed = abuf[...]
        for k in range(9):
            Hb[:, k * D : (k + 1) * D] = jnp.dot(
                Gm[c, pl.ds(k * R, R)], mixed, preferred_element_type=jnp.float32
            ).astype(jnp.bfloat16)
        zbuf[...] = jnp.dot(
            Hb[...], W[b, 0:9].reshape(9 * D, D), preferred_element_type=jnp.float32
        )
        z2 = zbuf[...]
        kept = valid * z2
        sums_start(
            2 * b + 1, jnp.sum(kept, 0, keepdims=True), jnp.sum(kept * z2, 0, keepdims=True)
        )
        share(b, 0, mixed.astype(jnp.float32))

        @pl.when(b == 0)
        def _():
            gather_z(2)

        @pl.when(b == 1)
        def _():
            own_ready(3, z)
            gather_z(3)

        @pl.when(b == 2)
        def _():
            gather_first(3)

        center, spread = moments(sums_finish(2 * b + 1))
        gi[b, 1:2] = norms[2:3] * spread
        for i in range(0, R, 64):
            xhat = (zbuf[i : i + 64] - center) * spread
            value, slope = mish_terms(norms[2:3] * xhat + norms[3:4])
            sv[b, 2, i : i + 64] = xhat.astype(sv.dtype)
            sv[b, 3, i : i + 64] = slope.astype(sv.dtype)
            h[i : i + 64] = h[i : i + 64] + valid[i : i + 64] * value

    gather_z(0)
    gather_first(0)
    gather_z(1)
    gather_second(0)

    @pl.loop(0, 4)
    def _(b):
        forward(b)

        @pl.when(b < 3)
        def _():
            gather_second(b + 1)

    out_grad_rows = pltpu.make_async_copy(out_grad.at[s], abuf, sL.at[11])
    out_features = pltpu.make_async_copy(h, features.at[0], sO_s.at[0])
    out_features.start()
    out_grad_rows.start()
    out_grad_rows.wait()
    g[...] = abuf[...].astype(jnp.float32)

    @jax.named_scope("close_gather")
    def close_gather():
        drain(aff.at[pl.ds(0, 3)], sF_s)
        drain(st_own.at[pl.ds(0, 11)], sC_s)
        drain(stage_a.at[pl.ds(0, 2)], sQ_s.at[3, 1])

        @pl.when(c == 0)
        def _():
            drain(wown.at[:, pl.ds(0, 3)], sS_s)

        @pl.when(c == 1)
        def _():
            drain(wown, sS_s)

        @pl.loop(0, 4)
        def _(b):
            drain(W.at[b, half, :, s], sA_s.at[b])
            for which in range(2):
                drain(W.at[b, half, :, s], sB_s.at[b, which])
            for which in range(3):
                drain(W.at[b, half, :, s], sD_s.at[b, which])

            @pl.when(c == 0)
            def _():
                drain(W.at[b, :, pl.ds(0, 6), s], sZ_s.at[b])
                drain(W.at[b, :, :, s], sH_s.at[b])

    @jax.named_scope("close_rest")
    def close_rest():
        @pl.loop(0, 4)
        def _(b):
            drain(stage.at[b, pl.ds(0, 3)], sQ_s.at[b, 0])
            drain(dzq.at[b, pl.ds(0, 3)], sX_s.at[b])
            dz_one_copy(b).wait_send()
            point_copy(b).wait_send()

            @pl.when(b != s)
            def _():
                drain(gsend.at[b], sO_s.at[4 + b])

            for i in range(len(CHUNKS)):
                y_copy(b, i).wait_send()

        @pl.when(c == 1)
        def _():
            for i, (at, size) in enumerate(CHUNKS):
                drain(zs1.at[pl.ds(at, size)], sK_s.at[3, i])

        def close_z(b, parts):
            for i in range(len(CHUNKS)):
                drain(near_like(b, i, parts), sN_s.at[b, i])
                drain(far_like(b, i, parts), sT_s.at[b, i])

        for b in range(4):
            carriers(b, functools.partial(close_z, b))

        @pl.loop(0, 16)
        def _(e):
            sums_close(e)

    CHUNKS = ((0, 3), (3, 3), (6, 3), (9, 1))
    LAST = len(CHUNKS) - 1

    def dz_copy(b, j):
        mine, _, near = pairing(b)
        v = 2 * mine + c
        v = v ^ 2 if j == 3 else v
        ref = dzq.at[b, v]
        return swap_copy(
            ref, ref, sX_s.at[b], sX_r.at[b, v], s ^ near if j == 2 else s, bat if j == 2 else bat ^ 1
        )

    def send_dz(b):
        dz_copy(b, 2).start()
        dz_copy(b, 1).start()

    @jax.named_scope("forward_dz")
    def forward_dz(b):
        v = (2 * pairing(b)[0] + c) ^ 2
        drain(dzq.at[b, v], sX_r.at[b, v])
        dz_copy(b, 3).start()

    @jax.named_scope("wait_dz")
    def wait_dz(b):
        u = 2 * pairing(b)[0] + c
        for v in (u ^ 1, u ^ 3):
            drain(dzq.at[b, v], sX_r.at[b, v])

    def dz_one_copy(b):
        ref = dz1q.at[b, c]
        return swap_copy(ref, ref, sM_s.at[b], sM_r.at[b], s, bat ^ 1)

    def point_copy(b):
        mine, _, near = pairing(b)
        return swap_copy(
            pgrad.at[b, 1 - mine], precv.at[b], sP_s.at[b], sP_r.at[b], s ^ near, bat
        )

    def y_copy(b, i):
        at, size = CHUNKS[i]
        return swap_copy(
            gout.at[b, 1 - pairing(b)[1], pl.ds(at, size)], yrecv.at[b, pl.ds(at, size)],
            sY_s.at[b, i], sY_r.at[b, i], s ^ 3 ^ pairing(b)[2], bat,
        )

    def grad_tap(b, k, left, right):
        part = jnp.dot(left, right, preferred_element_type=jnp.float32).astype(jnp.bfloat16)
        for yy in range(2):
            gout[b, yy, k] = part[64 * yy : 64 * yy + 64].reshape(4, 16, D)

    @jax.named_scope("grad_spatial")
    def grad_spatial(b):
        wait_share(b, 0)
        wait_dz(b)
        mine, _, near = pairing(b)
        tables = [jnp.where(mine == v // 2, 0, 2 * near) + v % 2 for v in range(4)]
        right = dzq[b].reshape(4 * R, D)
        for k in range(9):
            left = [
                lax.dot_general(
                    caq[b, 0, v].reshape(128, R), Gm[tables[v], pl.ds(k * R, R)], NT,
                    preferred_element_type=jnp.float32,
                ).astype(jnp.bfloat16)
                for v in range(4)
            ]
            grad_tap(b, k, jnp.concatenate(left, axis=1), right)
            if k % 3 == 2:
                y_copy(b, k // 3).start()

    @jax.named_scope("grad_point")
    def grad_point(b):
        wait_share(b, 1)
        drain(dz1q.at[b, 1 - c], sM_r.at[b])
        left = jnp.concatenate(
            [
                jnp.concatenate([caq[b, 1, 2 * v + k].reshape(128, R) for v in range(2)], axis=0)
                for k in range(2)
            ],
            axis=1,
        )
        part = jnp.dot(
            left, dz1q[b].reshape(2 * R, D), preferred_element_type=jnp.float32
        ).astype(jnp.bfloat16)
        pgrad[b] = part.reshape(2, 2, 4, 16, D)
        point_copy(b).start()

    @jax.named_scope("pair_point")
    def pair_point(b):
        point_copy(b).wait_recv()
        mine = pairing(b)[0]
        for yy in range(2):
            gout[b, yy, 9] = (
                pgrad[b, mine, yy].astype(jnp.float32) + precv[b, yy].astype(jnp.float32)
            ).astype(jnp.bfloat16)
        y_copy(b, LAST).start()

    def core_copy(b, i):
        at, size = CHUNKS[i]
        return swap_copy(
            yrecv.at[b, pl.ds(at, size)], zs1.at[pl.ds(at, size)],
            sK_s.at[b, i], sK_r.at[b, i], s, bat ^ 1,
        )

    @jax.named_scope("reduce_plane")
    def reduce_plane(b, i):
        at, size = CHUNKS[i]
        y_copy(b, i).wait_recv()
        rest = pairing(b)[1]
        for k in range(at, at + size):
            yrecv[b, k] = (
                yrecv[b, k].astype(jnp.float32) + gout[b, rest, k].astype(jnp.float32)
            ).astype(jnp.bfloat16)

        if b == 3:

            @pl.when(c == 1)
            def _():
                core_copy(b, i).start()

    def carriers(b, work):
        if b == 3:
            pl.when(c == 0)(functools.partial(work, (0, 1)))
        else:
            work((0,))

    def z_near(b, i, cc, slot):
        at, size = CHUNKS[i]
        return swap_copy(
            (yrecv.at[b], zs1)[cc].at[pl.ds(at, size), z ^ (3 if slot else 1)],
            zrecv.at[b + cc, slot, pl.ds(at, size)], sN_s.at[b, i], sN_r.at[b, i], s, bat ^ 2,
        )

    def z_far(b, i, cc):
        at, size = CHUNKS[i]
        return swap_copy(
            zrecv.at[b + cc, 1, pl.ds(at, size)], zrecv.at[b + cc, 2, pl.ds(at, size)],
            sT_s.at[b, i], sT_r.at[b, i], s, bat ^ 4,
        )

    def near_like(b, i, parts):
        at, size = CHUNKS[i]
        return zrecv.at[pl.ds(b, len(parts)), pl.ds(0, 2), pl.ds(at, size)]

    def far_like(b, i, parts):
        at, size = CHUNKS[i]
        return zrecv.at[pl.ds(b, len(parts)), 2, pl.ds(at, size)]

    @jax.named_scope("reduce_near")
    def reduce_near(b, i):
        def work(parts):
            if b == 3:
                core_copy(b, i).wait_recv()
            for slot in (1, 0):
                for cc in parts:
                    z_near(b, i, cc, slot).start()

        carriers(b, work)

    @jax.named_scope("reduce_far")
    def reduce_far(b, i):
        at, size = CHUNKS[i]

        def work(parts):
            drain(near_like(b, i, parts), sN_r.at[b, i])
            for cc in parts:
                mine = (yrecv.at[b], zs1)[cc]
                for k in range(at, at + size):
                    zrecv[b + cc, 1, k] = (
                        zrecv[b + cc, 1, k].astype(jnp.float32) + mine[k, z ^ 2].astype(jnp.float32)
                    ).astype(jnp.bfloat16)
                z_far(b, i, cc).start()

        carriers(b, work)

    def deliver(b, i, cc, section, core):
        at, size = CHUNKS[i]
        swap_copy(
            zrecv.at[b + cc, 0, pl.ds(at, size)], gfin.at[pl.ds(at, size), s],
            sG_s.at[b, cc], sG_r.at[s], section, 2 * z + core,
        ).start()

    @jax.named_scope("finish")
    def finish(b, i):
        at, size = CHUNKS[i]

        def work(parts):
            drain(far_like(b, i, parts), sT_r.at[b, i])
            for cc in parts:
                mine = (yrecv.at[b], zs1)[cc]
                for k in range(at, at + size):
                    zrecv[b + cc, 0, k] = (
                        zrecv[b + cc, 0, k].astype(jnp.float32)
                        + zrecv[b + cc, 2, k].astype(jnp.float32)
                        + mine[k, z].astype(jnp.float32)
                    ).astype(jnp.bfloat16)

                @pl.when(b != s)
                def _():
                    deliver(b, i, cc, b, cc if b == 3 else c)

                @pl.when(b == s)
                def _():
                    if cc == 0:
                        for k in range(at, at + size):
                            gfin[k, s] = zrecv[b, 0, k]
                    else:
                        deliver(b, i, 1, s, 1)

        carriers(b, work)

    @jax.named_scope("backward")
    def backward(bi):
        b = 3 - bi
        e = 8 + 2 * bi
        u = 2 * pairing(b)[0] + c
        first_sum = jnp.zeros((1, D), jnp.float32)
        second_sum = jnp.zeros((1, D), jnp.float32)
        for i in range(0, R, 64):
            du = valid[i : i + 64] * g[i : i + 64] * sv[b, 3, i : i + 64].astype(jnp.float32)
            zbuf[i : i + 64] = du
            first_sum += jnp.sum(du, 0, keepdims=True)
            second_sum += jnp.sum(du * sv[b, 2, i : i + 64].astype(jnp.float32), 0, keepdims=True)
        sums_start(e, first_sum, second_sum)

        @pl.when(bi == 0)
        def _():
            close_gather()

        @pl.when(bi == 3)
        def _():
            reduce_near(3, 1)

        @pl.when(bi > 0)
        def _():
            forward_dz(b + 1)
            grad_point(b + 1)

        @pl.when(bi == 2)
        def _():
            pair_point(3)
            reduce_plane(3, 0)

        @pl.when(bi == 3)
        def _():
            reduce_plane(3, 2)
            reduce_far(3, 0)

        total_first, total_second = sums_finish(e)
        for i in range(0, R, 64):
            xhat = sv[b, 2, i : i + 64].astype(jnp.float32)
            inner = zbuf[i : i + 64] - valid[i : i + 64] * (
                (total_first + xhat * total_second) / row_count
            )
            dzq[b, u, i : i + 64] = (gi[b, 1:2] * inner).astype(jnp.bfloat16)
        send_dz(b)
        gsend[b, 2:3] = total_second
        gsend[b, 3:4] = total_first
        d_two = dzq[b, u]
        for k in range(9):
            Hb[:, k * D : (k + 1) * D] = jnp.dot(
                Gm[c, pl.ds((8 - k) * R, R)], d_two, preferred_element_type=jnp.float32
            ).astype(jnp.bfloat16)
        mixed = None
        for k in range(9):
            part = lax.dot_general(
                Hb[:, k * D : (k + 1) * D], W[b, k].reshape(D, D), NT,
                preferred_element_type=jnp.float32,
            )
            mixed = part if mixed is None else mixed + part
        zbuf[...] = mixed
        first_sum = jnp.zeros((1, D), jnp.float32)
        second_sum = jnp.zeros((1, D), jnp.float32)
        for i in range(0, R, 64):
            du = zbuf[i : i + 64] * sv[b, 1, i : i + 64].astype(jnp.float32)
            zbuf[i : i + 64] = du
            first_sum += jnp.sum(du, 0, keepdims=True)
            second_sum += jnp.sum(du * sv[b, 0, i : i + 64].astype(jnp.float32), 0, keepdims=True)
        sums_start(e + 1, first_sum, second_sum)

        @pl.when(bi == 2)
        def _():
            reduce_near(3, 0)

        @pl.when(bi == 3)
        def _():
            reduce_near(3, 2)

        @pl.when(bi > 0)
        def _():
            grad_spatial(b + 1)

        @pl.when(bi == 2)
        def _():
            reduce_plane(3, 1)

        @pl.when(bi == 3)
        def _():
            reduce_plane(3, 3)
            reduce_plane(2, 0)
            reduce_far(3, 1)
            reduce_near(2, 0)

        total_first, total_second = sums_finish(e + 1)
        for i in range(0, R, 64):
            xhat = sv[b, 0, i : i + 64].astype(jnp.float32)
            inner = zbuf[i : i + 64] - valid[i : i + 64] * (
                (total_first + xhat * total_second) / row_count
            )
            dz1q[b, c, i : i + 64] = (gi[b, 0:1] * inner).astype(jnp.bfloat16)
        dz_one_copy(b).start()
        gsend[b, 0:1] = total_second
        gsend[b, 1:2] = total_first
        g[...] = g[...] + lax.dot_general(
            dz1q[b, c], W[b, 9].reshape(D, D), NT, preferred_element_type=jnp.float32
        )

        @pl.when(b == s)
        def _():
            gaff[s] = gsend[b]

        @pl.when(b != s)
        def _():
            swap_copy(gsend.at[b], gaff.at[s], sO_s.at[4 + b], sO_r, b, bat).start()

    @pl.loop(0, 4)
    def _(bi):
        backward(bi)

    out_grad_in = pltpu.make_async_copy(g, in_grad.at[0], sO_s.at[1])
    out_grad_in.start()

    reduce_near(3, 3)
    forward_dz(0)
    pair_point(2)
    reduce_plane(2, 1)
    reduce_near(2, 1)
    grad_spatial(0)
    grad_point(0)
    reduce_far(3, 2)
    reduce_far(2, 0)
    pair_point(1)
    reduce_plane(2, 2)
    reduce_near(2, 2)
    reduce_far(3, 3)
    finish(3, 0)
    reduce_plane(1, 0)
    reduce_near(1, 0)
    reduce_far(2, 1)
    reduce_plane(2, 3)
    reduce_near(2, 3)
    finish(3, 1)
    finish(2, 0)
    reduce_plane(1, 1)
    reduce_near(1, 1)
    reduce_far(2, 2)
    finish(3, 2)
    reduce_plane(1, 2)
    reduce_near(1, 2)
    reduce_far(1, 0)
    finish(3, 3)
    finish(2, 1)
    pair_point(0)
    reduce_plane(0, 0)
    reduce_near(0, 0)
    reduce_far(2, 3)
    reduce_far(1, 1)
    reduce_plane(1, 3)
    reduce_near(1, 3)
    finish(2, 2)
    finish(1, 0)
    reduce_plane(0, 1)
    reduce_near(0, 1)
    reduce_far(1, 2)
    reduce_plane(0, 2)
    reduce_near(0, 2)
    reduce_plane(0, 3)
    reduce_near(0, 3)
    reduce_far(0, 0)
    finish(2, 3)
    finish(1, 1)
    reduce_far(1, 3)
    reduce_far(0, 1)
    finish(1, 2)
    finish(1, 3)
    finish(0, 0)
    reduce_far(0, 2)
    reduce_far(0, 3)
    finish(0, 1)
    close_rest()
    finish(0, 2)
    finish(0, 3)
    for d in range(1, 4):
        drain(gfin.at[:, s ^ d], sG_r.at[s ^ d])

    @pl.when((c == 1) & (s == 3))
    def _():
        drain(gfin.at[:, s], sG_r.at[s])

    grads_out = pltpu.make_async_copy(gfin, grads, sO_s.at[2])
    grads_out.start()

    def lane_sum(v):
        return jnp.sum(v, axis=1, keepdims=True)

    gspatial_squares = jnp.zeros((1, D), jnp.float32)
    for k in range(9):
        gspatial_squares += square(gfin[k].astype(jnp.float32).reshape(64, D))
    gpoint_squares = square(gfin[9].astype(jnp.float32).reshape(64, D))
    lanes = lax.broadcasted_iota(jnp.int32, (1, D), 1)
    tile = jnp.zeros((1, D), jnp.float32)
    for i, part in enumerate((point_squares, spatial_squares, gpoint_squares, gspatial_squares)):
        tile = jnp.where(lanes == i, lane_sum(part), tile)
    sums_start(16, tile, tile)
    drain(gaff.at[pl.ds(0, 3)], sO_r)
    affine_out[...] = gaff[0] + gaff[1] + gaff[2] + gaff[3]
    totals, _ = sums_finish(16)
    totals_out[...] = jnp.concatenate([totals] * 8, axis=0)

    with jax.named_scope("close_last"):
        sums_close(16)

        @pl.when(c == 0)
        def _():
            drain(zrecv.at[4, 0], sG_s.at[3, 1])

        @pl.loop(0, 4)
        def _(b):
            @pl.when((b != s) & ((b < 3) | (c == 0)))
            def _():
                drain(zrecv.at[b, 0], sG_s.at[b, 0])

    with jax.named_scope("close_outputs"):
        grads_out.wait()
        out_features.wait()
        out_grad_in.wait()


def lars_kernel(
    feat, ing, grads_in, totals_in, affine_in, w_point, w_spatial, norm_in, mom_point, mom_spatial, mom_norm,
    features, in_grad, new_point, new_spatial, new_norm, new_mom_point, new_mom_spatial, new_mom_norm,
    P, M, G, feat_rows, grad_rows, totals, affine_grad, affine, affine_mom, sem, out_sem,
):
    loads = [
        (totals_in, totals), (affine_in, affine_grad), (norm_in.at[0], affine), (mom_norm.at[0], affine_mom),
        (grads_in, G), (w_spatial.at[0], P.at[pl.ds(0, 9)]), (mom_spatial.at[0], M.at[pl.ds(0, 9)]),
        (w_point.at[0], P.at[9]), (mom_point.at[0], M.at[9]),
    ]
    loads = [pltpu.make_async_copy(a, b, sem.at[i]) for i, (a, b) in enumerate(loads)]
    for load in loads:
        load.start()
    passed = [
        pltpu.make_async_copy(feat, feat_rows, sem.at[9]),
        pltpu.make_async_copy(ing, grad_rows, sem.at[10]),
    ]
    for copy in passed:
        copy.start()
    for load in loads:
        load.wait()
    D = affine.shape[1]
    rate = BASE_RATE * (STEP + 1) / WARMUP
    point_sq, spatial_sq, gpoint_sq, gspatial_sq = [totals[0:1, i : i + 1] for i in range(4)]
    step_point = rate * TRUST_COEF * jnp.sqrt(point_sq) / (jnp.sqrt(gpoint_sq) + EPS_NORM)
    step_spatial = rate * TRUST_COEF * jnp.sqrt(spatial_sq) / (jnp.sqrt(gspatial_sq) + EPS_NORM)
    outs = []

    def store(source, target):
        outs.append(pltpu.make_async_copy(source, target, out_sem.at[len(outs)]))
        outs[-1].start()

    for k in range(10):
        grad = G[k].astype(jnp.float32).reshape(64, D)
        moved = MOMENTUM * M[k] + (step_point if k == 9 else step_spatial) * grad
        M[k] = moved
        P[k] = P[k] - moved
        if k in (2, 5, 8):
            taps = pl.ds(k - 2, 3)
            store(M.at[taps], new_mom_spatial.at[0, taps])
            store(P.at[taps], new_spatial.at[0, taps])
    for copy, rows, target in zip(passed, (feat_rows, grad_rows), (features, in_grad)):
        copy.wait()
        store(rows, target)
    store(M.at[9], new_mom_point.at[0])
    store(P.at[9], new_point.at[0])
    grad = affine_grad[0:4]
    old = affine[...]
    affine_sq = jnp.sum(old * old, axis=1, keepdims=True)
    gaffine_sq = jnp.sum(grad * grad, axis=1, keepdims=True)
    trust = TRUST_COEF * jnp.sqrt(affine_sq) / (jnp.sqrt(gaffine_sq) + EPS_NORM)
    moved = MOMENTUM * affine_mom[...] + rate * trust * grad
    affine_mom[...] = moved
    affine[...] = old - moved
    store(affine_mom, new_mom_norm.at[0])
    store(affine, new_norm.at[0])
    for copy in outs:
        copy.wait()


def train_step(images, crop, w_point, w_spatial, norm_params, mom_point, mom_spatial, mom_norm, out_grad):
    R, D = images.shape[1:]
    f32, bf16 = jnp.float32, jnp.bfloat16
    dma = pltpu.SemaphoreType.DMA
    anywhere = pl.BlockSpec(memory_space=pl.ANY)
    vmem = pl.BlockSpec(memory_space=pltpu.VMEM)
    hbm = pl.BlockSpec(memory_space=pltpu.HBM)
    smem = pl.BlockSpec(memory_space=pltpu.SMEM)
    V = pltpu.VMEM
    scratch = dict(
        W=V((4, TAPS, 8, 4, 16, D), bf16), wown=V((TAPS, 4, 16, D), bf16),
        F=V((3 * R, D), f32),
        sv=V((4, 4, R, D), bf16), gi=V((4, 8, D), f32),
        abuf=V((R, D), bf16),
        Gm=V((6, 9 * R, R), bf16), caq=V((4, 2, 4, 8, 16, R), bf16),
        stage=V((4, 4, 8, 16, R), bf16), stage_a=V((4, 8, 16, R), bf16), Hb=V((R, 9 * D), bf16),
        dzq=V((4, 4, R, D), bf16), dz1q=V((4, 2, R, D), bf16),
        pgrad=V((4, 2, 2, 4, 16, D), bf16), precv=V((4, 2, 4, 16, D), bf16),
        gout=V((4, 2, TAPS, 4, 16, D), bf16), yrecv=V((4, TAPS, 4, 16, D), bf16),
        zs1=V((TAPS, 4, 16, D), bf16), zrecv=V((5, 3, TAPS, 16, D), bf16),
        gfin=V((TAPS, 4, 16, D), bf16),
        aff=V((4, 8, D), f32), gaff=V((4, 8, D), f32), gsend=V((4, 8, D), f32),
        st_in=V((17, 8, 128), f32), st_own=V((17, 8, 128), f32), st_all=V((17, 4, 8, 128), f32),
        cnt=V((8, 8, 128), f32), cntx=V((6, 8, 128), f32), cown=V((8, 128), f32),
        sL=dma((12,)), sS_s=dma, sS_r=dma((4, 2)), sZ_s=dma((4,)), sZ_r=dma((4, 4)),
        sH_s=dma((4,)), sH_r=dma((4, 4)), sA_s=dma((4,)), sA_r=dma((4, 4)),
        sB_s=dma((4, 2)), sB_r=dma((4, 2)), sD_s=dma((4, 3)), sD_r=dma((4, 3)),
        sE_in_s=dma((17,)), sE_in_r=dma((17,)), sE_s=dma((17,)), sE_r=dma((17,)),
        sC_s=dma, sC_r=dma((2,)), sF_s=dma, sF_r=dma,
        sQ_s=dma((4, 2)), sQ_r=dma((4, 2)), sX_s=dma((4,)), sX_r=dma((4, 4)), sM_s=dma((4,)), sM_r=dma((4,)), sP_s=dma((4,)), sP_r=dma((4,)),
        sY_s=dma((4, 4)), sY_r=dma((4, 4)), sK_s=dma((4, 4)), sK_r=dma((4, 4)),
        sN_s=dma((4, 4)), sN_r=dma((4, 4)), sT_s=dma((4, 4)), sT_r=dma((4, 4)), sG_s=dma((4, 2)), sG_r=dma((4,)),
        sO_s=dma((8,)), sO_r=dma,
    )
    shape = jax.ShapeDtypeStruct
    feat, ing, grads, totals, affine_grad = pl.pallas_call(
        train_kernel,
        out_shape=(
            shape((1, R, D), f32), shape((1, R, D), f32), shape((TAPS, 4, 16, D), bf16),
            shape((8, D), f32), shape((8, D), f32),
        ),
        in_specs=[anywhere, smem, anywhere, anywhere, vmem, anywhere],
        out_specs=(anywhere, anywhere, anywhere, vmem, vmem),
        scratch_shapes=list(scratch.values()),
        compiler_params=pltpu.CompilerParams(
            collective_id=0, has_side_effects=True, vmem_limit_bytes=64 * 1024 * 1024
        ),
    )(images, crop.T, w_point, w_spatial, norm_params, out_grad)
    return pl.pallas_call(
        lars_kernel,
        out_shape=(
            shape((1, R, D), f32), shape((1, R, D), f32),
            shape(w_point.shape, f32), shape(w_spatial.shape, f32), shape(norm_params.shape, f32),
            shape(w_point.shape, f32), shape(w_spatial.shape, f32), shape(norm_params.shape, f32),
        ),
        in_specs=[hbm] * 11,
        out_specs=(hbm,) * 8,
        scratch_shapes=[
            V((TAPS, 64, D), f32), V((TAPS, 64, D), f32), V((TAPS, 4, 16, D), bf16), V((1, R, D), f32),
            V((1, R, D), f32), V((8, D), f32), V((8, D), f32), V((4, D), f32), V((4, D), f32), dma((11,)), dma((12,)),
        ],
        compiler_params=pltpu.CompilerParams(vmem_limit_bytes=64 * 1024 * 1024),
    )(feat, ing, grads, totals, affine_grad, w_point, w_spatial, norm_params, mom_point, mom_spatial, mom_norm)


def solution(mesh):
    tuned = mesh.shape["section"] == 4 and mesh.shape["batch"] == 8
    return jax.shard_map(
        train_step if tuned else on_device,
        mesh=mesh,
        in_specs=(
            P(None, "batch", None),
            P(None, "batch"),
            P("section", "batch", None),
            P("section", None, "batch", None),
            P("section", None, None),
            P("section", "batch", None),
            P("section", None, "batch", None),
            P("section", None, None),
            P(None, "batch", None),
        ),
        out_specs=(
            P("section", "batch", None),
            P("section", "batch", None),
            P("section", "batch", None),
            P("section", None, "batch", None),
            P("section", None, None),
            P("section", "batch", None),
            P("section", None, "batch", None),
            P("section", None, None),
        ),
        check_vma=False,
    )
```

```python
import functools

import jax
import jax.numpy as jnp
from jax import lax
from jax.experimental import pallas as pl
from jax.experimental.pallas import tpu as pltpu
from jax.sharding import PartitionSpec as P

BIG_SIDE = 7
SMALL_SIDE = 3
WARMUP = 20
STEP = 9


EPS = 1e-05
EPS_NORM = 1e-06
BASE_RATE = 6.0
MOMENTUM = 0.9
TRUST_COEF = 0.1


def from_behind(block, axis, distance):
    devices = range(lax.axis_size(axis))
    route = [(i - distance, i) for i in devices if i - distance in devices]
    return lax.ppermute(block, axis, route)


def crop_table(big_count, total_rows):
    places = jnp.arange(total_rows, dtype=jnp.int32)
    big_area = BIG_SIDE * BIG_SIDE
    small_area = SMALL_SIDE * SMALL_SIDE
    big_rows = big_count * big_area
    small_rows = (total_rows - big_rows) // small_area * small_area
    in_big = places < big_rows
    offsets = places - big_rows
    sides = jnp.where(in_big, BIG_SIDE, SMALL_SIDE)
    within = jnp.where(in_big, places % big_area, offsets % small_area)
    starts = places - within
    valid_rows = places < big_rows + small_rows
    row_pos = within // sides
    col_pos = within % sides
    indices = []
    masks = []
    for row_step in (-1, 0, 1):
        for col_step in (-1, 0, 1):
            new_row = row_pos + row_step
            new_col = col_pos + col_step
            inside = (
                valid_rows & (new_row >= 0) & (new_row < sides) & (new_col >= 0) & (new_col < sides)
            )
            indices.append(jnp.where(inside, starts + new_row * sides + new_col, places))
            masks.append(inside)
    return (
        jnp.stack(indices, 1),
        jnp.stack(masks, 1).astype(jnp.float32),
        valid_rows.astype(jnp.float32),
    )


def mish(values):
    return values * jnp.tanh(jax.nn.softplus(values))


def mish_parts(values):
    tangent = jnp.tanh(jax.nn.softplus(values))
    slope = tangent + values * jax.nn.sigmoid(values) * (1.0 - tangent * tangent)
    return (values * tangent, slope)


def mish_slope(values):
    tangent = jnp.tanh(jax.nn.softplus(values))
    return tangent + values * jax.nn.sigmoid(values) * (1.0 - tangent * tangent)


def batch_moments(proj, valid_rows):
    weighted = valid_rows[:, None] * proj
    summed, squared, row_count = lax.psum(
        (jnp.sum(weighted, 0), jnp.sum(weighted * proj, 0), jnp.sum(valid_rows)), "batch"
    )
    center = summed / row_count
    inv_std = lax.rsqrt(squared / row_count - center * center + EPS)
    return (center, inv_std, row_count)


def spatial_apply(source, tap_index, tap_mask, weights):
    stacked = source[tap_index] * tap_mask[:, :, None].astype(source.dtype)
    result = lax.dot_general(
        stacked, weights, (((1, 2), (0, 1)), ((), ())), preferred_element_type=jnp.float32
    )
    return (result, stacked)


def forward_block(hidden, point_low, spatial_low, affine, tap_index, tap_mask, valid_rows):
    proj_one = jnp.dot(hidden.astype(jnp.bfloat16), point_low, preferred_element_type=jnp.float32)
    center_one, inv_one, row_count = batch_moments(proj_one, valid_rows)
    mixed_one = mish(affine[0] * ((proj_one - center_one) * inv_one) + affine[1])
    proj_two, stacked = spatial_apply(
        mixed_one.astype(jnp.bfloat16), tap_index, tap_mask, spatial_low
    )
    center_two, inv_two, count_two = batch_moments(proj_two, valid_rows)
    mixed_two = mish(affine[2] * ((proj_two - center_two) * inv_two) + affine[3])
    moments = jnp.stack([center_one, inv_one, center_two, inv_two])
    return (hidden + valid_rows[:, None] * mixed_two, moments, row_count)


def norm_back(d_value, normed, inv_std, gain, valid_rows, row_count):
    first_sum, second_sum = lax.psum((jnp.sum(d_value, 0), jnp.sum(d_value * normed, 0)), "batch")
    d_proj = (
        gain
        * inv_std
        * (d_value - valid_rows[:, None] * (first_sum + normed * second_sum) / row_count)
    )
    return (d_proj.astype(jnp.bfloat16), first_sum, second_sum)


def backward_block(
    hidden,
    upstream,
    point_low,
    spatial_low,
    affine,
    moments,
    row_count,
    tap_index,
    tap_mask,
    valid_rows,
):
    inputs = hidden.astype(jnp.bfloat16)
    proj_one = jnp.dot(inputs, point_low, preferred_element_type=jnp.float32)
    normed_one = (proj_one - moments[0]) * moments[1]
    mixed_one, slope_one = mish_parts(affine[0] * normed_one + affine[1])
    proj_two, stacked = spatial_apply(
        mixed_one.astype(jnp.bfloat16), tap_index, tap_mask, spatial_low
    )
    normed_two = (proj_two - moments[2]) * moments[3]
    slope_two = mish_slope(affine[2] * normed_two + affine[3])
    d_two, first_two, second_two = norm_back(
        valid_rows[:, None] * upstream * slope_two,
        normed_two,
        moments[3],
        affine[2],
        valid_rows,
        row_count,
    )
    grad_spatial = lax.dot_general(
        stacked, d_two, (((0,), (0,)), ((), ())), preferred_element_type=jnp.float32
    )
    flipped = d_two[tap_index[:, ::-1]] * tap_mask[:, ::-1, None].astype(jnp.bfloat16)
    d_mixed = lax.dot_general(
        flipped, spatial_low, (((1, 2), (0, 2)), ((), ())), preferred_element_type=jnp.float32
    )
    d_one, first_one, second_one = norm_back(
        d_mixed * slope_one, normed_one, moments[1], affine[0], valid_rows, row_count
    )
    grad_point = lax.dot_general(
        inputs, d_one, (((0,), (0,)), ((), ())), preferred_element_type=jnp.float32
    )
    d_hidden = upstream + lax.dot_general(
        d_one, point_low, (((1,), (1,)), ((), ())), preferred_element_type=jnp.float32
    )
    grad_affine = jnp.stack([second_one, first_one, second_two, first_two])
    return (d_hidden, grad_point, grad_spatial, grad_affine)


def store_slot(buffer, value, slot_index, active):
    previous = lax.dynamic_index_in_dim(buffer, slot_index, 0, keepdims=False)
    return lax.dynamic_update_index_in_dim(
        buffer, jnp.where(active, value, previous), slot_index, 0
    )


def lars_update(param, grad, momentum, param_sq, grad_sq, rate):
    trust = TRUST_COEF * jnp.sqrt(param_sq) / (jnp.sqrt(grad_sq) + EPS_NORM)
    new_mom = MOMENTUM * momentum + rate * trust * grad
    return (param - new_mom, new_mom)


def on_device(
    images, crop_big, w_point, w_spatial, norm_params, mom_point, mom_spatial, mom_norm, out_grad
):
    section_count = lax.axis_size("section")
    section_rank = lax.axis_index("section")
    micro_count = images.shape[0]
    total_rows = images.shape[1]
    width = images.shape[2]
    point = w_point[0]
    spatial = w_spatial[0]
    affine = norm_params[0]
    crop_counts = crop_big[:, 0]
    turns = micro_count + section_count - 1
    point_low, spatial_low = (
        lax.all_gather(point.astype(jnp.bfloat16), "batch", axis=0, tiled=True),
        lax.all_gather(spatial.astype(jnp.bfloat16), "batch", axis=1, tiled=True),
    )
    kept_inputs = jnp.zeros((micro_count, total_rows, width), jnp.float32)
    kept_moments = jnp.zeros((micro_count, 4, width), jnp.float32)
    kept_counts = jnp.zeros((micro_count,), jnp.float32)
    results = jnp.zeros((micro_count, total_rows, width), jnp.float32)
    incoming = jnp.zeros((total_rows, width), jnp.float32)
    for phase_turn in range(turns):
        slot_raw = phase_turn - section_rank
        active = (slot_raw >= 0) & (slot_raw < micro_count)
        slot_index = jnp.clip(slot_raw, 0, micro_count - 1)
        fresh_rows = lax.dynamic_index_in_dim(images, slot_index, 0, keepdims=False).astype(
            jnp.float32
        )
        hidden = jnp.where(section_rank == 0, fresh_rows, incoming)
        tap_index, tap_mask, valid_rows = crop_table(crop_counts[slot_index], total_rows)
        output, moments, row_count = forward_block(
            hidden, point_low, spatial_low, affine, tap_index, tap_mask, valid_rows
        )
        kept_inputs = store_slot(kept_inputs, hidden, slot_index, active)
        kept_moments = store_slot(kept_moments, moments, slot_index, active)
        kept_counts = store_slot(kept_counts, row_count, slot_index, active)
        results = store_slot(
            results, output, slot_index, active & (section_rank == section_count - 1)
        )
        if phase_turn + 1 < turns:
            incoming = from_behind(output.astype(jnp.bfloat16), "section", 1).astype(output.dtype)
    point_low, spatial_low = (
        lax.all_gather(point.astype(jnp.bfloat16), "batch", axis=0, tiled=True),
        lax.all_gather(spatial.astype(jnp.bfloat16), "batch", axis=1, tiled=True),
    )
    grad_point = jnp.zeros((width, width), jnp.float32)
    grad_spatial = jnp.zeros((9, width, width), jnp.float32)
    grad_affine = jnp.zeros((4, width), jnp.float32)
    collected = jnp.zeros((micro_count, total_rows, width), jnp.float32)
    returning = jnp.zeros((total_rows, width), jnp.float32)
    for phase_turn in range(turns):
        slot_raw = micro_count - 1 - phase_turn + (section_count - 1 - section_rank)
        active = (slot_raw >= 0) & (slot_raw < micro_count)
        slot_index = jnp.clip(slot_raw, 0, micro_count - 1)
        seeded = lax.dynamic_index_in_dim(out_grad, slot_index, 0, keepdims=False).astype(
            jnp.float32
        )
        upstream = jnp.where(section_rank == section_count - 1, seeded, returning)
        upstream = jnp.where(active, upstream, 0.0)
        tap_index, tap_mask, valid_rows = crop_table(crop_counts[slot_index], total_rows)
        hidden = lax.dynamic_index_in_dim(kept_inputs, slot_index, 0, keepdims=False)
        moments = lax.dynamic_index_in_dim(kept_moments, slot_index, 0, keepdims=False)
        row_count = lax.dynamic_index_in_dim(kept_counts, slot_index, 0, keepdims=False)
        d_hidden, part_point, part_spatial, part_affine = backward_block(
            hidden,
            upstream,
            point_low,
            spatial_low,
            affine,
            moments,
            row_count,
            tap_index,
            tap_mask,
            valid_rows,
        )
        grad_point = grad_point + part_point
        grad_spatial = grad_spatial + part_spatial
        grad_affine = grad_affine + part_affine
        collected = store_slot(collected, d_hidden, slot_index, active & (section_rank == 0))
        if phase_turn + 1 < turns:
            returning = from_behind(d_hidden.astype(jnp.bfloat16), "section", -1).astype(
                d_hidden.dtype
            )
    point_grad, spatial_grad = (
        lax.psum_scatter(grad_point, "batch", scatter_dimension=0, tiled=True),
        lax.psum_scatter(grad_spatial, "batch", scatter_dimension=1, tiled=True),
    )
    point_sq, spatial_sq, gpoint_sq, gspatial_sq = lax.psum(
        (
            jnp.sum(point * point),
            jnp.sum(spatial * spatial),
            jnp.sum(point_grad * point_grad),
            jnp.sum(spatial_grad * spatial_grad),
        ),
        "batch",
    )
    rate = BASE_RATE * (STEP + 1) / WARMUP
    new_point, new_mom_point = lars_update(
        point, point_grad, mom_point[0], point_sq, gpoint_sq, rate
    )
    new_spatial, new_mom_spatial = lars_update(
        spatial, spatial_grad, mom_spatial[0], spatial_sq, gspatial_sq, rate
    )
    affine_sq = jnp.sum(affine * affine, 1, keepdims=True)
    gaffine_sq = jnp.sum(grad_affine * grad_affine, 1, keepdims=True)
    new_affine, new_mom_affine = lars_update(
        affine, grad_affine, mom_norm[0], affine_sq, gaffine_sq, rate
    )
    sent_out = jnp.where(section_rank == section_count - 1, results, 0.0)
    sent_back = jnp.where(section_rank == 0, collected, 0.0)
    got_out, got_back = (
        lax.all_to_all(
            sent_out.astype(jnp.bfloat16), "section", split_axis=0, concat_axis=0, tiled=True
        ).astype(sent_out.dtype),
        lax.all_to_all(
            sent_back.astype(jnp.bfloat16), "section", split_axis=0, concat_axis=0, tiled=True
        ).astype(sent_back.dtype),
    )
    features = got_out[section_count - 1 : section_count]
    in_grad = got_back[0:1]
    return (
        features,
        in_grad,
        new_point[None],
        new_spatial[None],
        new_affine[None],
        new_mom_point[None],
        new_mom_spatial[None],
        new_mom_affine[None],
    )


def swap_copy(source, target, sent, landed, section, batch):
    return pltpu.make_async_remote_copy(
        src_ref=source,
        dst_ref=target,
        send_sem=sent,
        recv_sem=landed,
        device_id=(section, batch),
        device_id_type=pl.DeviceIdType.MESH,
    )


def drain(like, sem):
    pltpu.make_async_copy(like, like, sem).wait()


def mish_terms(v):
    e = jnp.exp(jnp.minimum(v, 20.0))
    w = e * (e + 2.0)
    r = 1.0 / (w + 2.0)
    t = w * r
    return v * t, t + v * (4.0 * e * (1.0 + e)) * (r * r)


def pack(first, second):
    parts = [v[:, i * 128 : (i + 1) * 128] for v in (first, second) for i in range(4)]
    return jnp.concatenate(parts, axis=0)


def unpack(tile):
    rows = [tile[i : i + 1] for i in range(8)]
    return jnp.concatenate(rows[:4], axis=1), jnp.concatenate(rows[4:], axis=1)


def crop_codes(places, big, total_rows):
    big_area = float(BIG_SIDE * BIG_SIDE)
    small_area = float(SMALL_SIDE * SMALL_SIDE)
    big_rows = big * big_area
    small_rows = jnp.floor((total_rows - big_rows + 0.5) / small_area) * small_area
    in_big = places < big_rows
    offset = jnp.where(in_big, places, places - big_rows)
    area = jnp.where(in_big, big_area, small_area)
    side = jnp.where(in_big, float(BIG_SIDE), float(SMALL_SIDE))
    crop = jnp.floor((offset + 0.5) / area)
    within = offset - crop * area
    row = jnp.floor((within + 0.5) / side)
    col = within - row * side
    crop = jnp.where(in_big, crop, crop + big)
    return crop * 1024.0 + (row + 1.0) * 32.0 + (col + 1.0), places < big_rows + small_rows


NT = (((1,), (1,)), ((), ()))
TAPS = 10
WHOLE = 2
HALF = (TAPS - WHOLE) // 2


def train_kernel(
    images, crop, w_point, w_spatial, norm_in, out_grad,
    features, in_grad, grads, totals_out, affine_out,
    W, wown, F, sv, gi, abuf, Gm, caq, stage, stage_a, Hb, dzq, dz1q, pgrad, precv, gout, yrecv,
    zs1, zrecv, gfin, aff, gaff, gsend, st_in, st_own, st_all, cnt, cntx, cown,
    sL, sS_s, sS_r, sU_s, sU_r, sV_s, sV_r, sJ_s, sJ_r, sZ_s, sZ_r, sH_s, sH_r, sA_s, sA_r, sB_r, sD_r,
    sE_in_s, sE_in_r, sE_s, sE_r, sC_s, sC_r, sF_s, sF_r, sQ_s, sQ_r, sX_s, sX_r, sM_s, sM_r, sP_s, sP_r,
    sY_s, sY_r, sK_s, sK_r, sN_s, sN_r, sT_s, sT_r, sG_s, sG_r, sO_s, sO_r,
):
    s = lax.axis_index("section")
    bat = lax.axis_index("batch")
    z = bat // 2
    c = lax.rem(bat, 2)
    x = lax.rem(s, 2)
    y = s // 2
    R, D = abuf.shape
    h = F.at[pl.ds(0, R)]
    g = F.at[pl.ds(R, R)]
    zbuf = F.at[pl.ds(2 * R, R)]

    loads = [
        pltpu.make_async_copy(w_point.at[0], F.at[pl.ds(9 * 64, 64)], sL.at[0]),
        *[
            pltpu.make_async_copy(w_spatial.at[0, k], F.at[pl.ds(k * 64, 64)], sL.at[0])
            for k in range(9)
        ],
        pltpu.make_async_copy(images.at[s], abuf, sL.at[1]),
    ]
    for load in loads:
        load.start()

    barrier = pltpu.get_barrier_semaphore()
    greet = [(s, bat ^ j) for j in range(1, 8)]
    greet += [(s ^ d, bat ^ j) for d in range(1, 4) for j in range(2)]
    for sec, other in greet:
        pl.semaphore_signal(
            barrier, inc=1, device_id=(sec, other), device_id_type=pl.DeviceIdType.MESH
        )

    def square(rows):
        return jnp.sum(rows * rows, 0, keepdims=True)

    spatial_squares = jnp.zeros((1, D), jnp.float32)
    drain(F.at[pl.ds(0, 64 * TAPS)], sL.at[0])
    for k in range(TAPS):
        rows = F[k * 64 : k * 64 + 64]
        wown[k] = rows.astype(jnp.bfloat16).reshape(4, 16, D)
        if k < 9:
            spatial_squares += square(rows)
        else:
            point_squares = square(rows)
    with jax.named_scope("greet"):
        pl.semaphore_wait(barrier, len(greet))

    cown[...] = jnp.full((8, 128), crop[0, s].astype(jnp.float32))
    aff[s] = jnp.concatenate([norm_in[0], jnp.zeros((4, D), jnp.float32)], axis=0)
    cnt[bat] = cown[...]
    cntx[c] = cown[...]
    for j in range(1, 8):
        swap_copy(cown, cnt.at[bat], sC_s, sC_r.at[0], s, bat ^ j).start()
    for j in range(2):
        for near in (1, 2):
            swap_copy(cown, cntx.at[2 * near + c], sC_s, sC_r.at[1], s ^ near, bat ^ j).start()
    for d in range(1, 4):
        swap_copy(aff.at[s], aff.at[s], sF_s, sF_r, s ^ d, bat).start()

    def scatter(d):
        q = s ^ d
        return swap_copy(
            wown.at[split, q], W.at[s, split, bat, q], sS_s, sS_r.at[s], q, 2 * z
        )

    def scatter_whole(d):
        return swap_copy(
            wown.at[whole], W.at[s, whole, bat], sU_s, sU_r.at[s], s ^ d, 2 * z
        )

    split, whole = pl.ds(0, 2 * HALF), pl.ds(2 * HALF, WHOLE)
    for send in (scatter, scatter_whole):
        for d in range(1, 4):
            send(d).start()

        @pl.when(c == 1)
        def _():
            send(0).start()

    @pl.when(c == 0)
    def _():
        pltpu.make_async_copy(wown.at[split, s], W.at[s, split, bat, s], sS_r.at[s]).start()
        pltpu.make_async_copy(wown.at[whole], W.at[s, whole, bat], sU_r.at[s]).start()

    half = pl.ds(HALF * c, HALF)
    first = jnp.where(c == 0, s ^ 1, s ^ 2)
    second = jnp.where(c == 0, s ^ 2, s ^ 1)
    both = s ^ 3

    def pair(b, taps, zz, q):
        return W.at[b, taps, pl.ds(2 * zz, 2), q]

    def to_sibling(b, zz):
        ref = pair(b, split, zz, s)
        return swap_copy(ref, ref, sH_s, sH_r.at[b, zz], s, bat ^ 1)

    def along_first(b, zz):
        ref = pair(b, half, zz, s)
        return swap_copy(ref, ref, sA_s, sA_r.at[b, zz], first, bat)

    def along_second(b, which, zz):
        ref = pair(b, half, zz, s if which == 0 else first)
        return swap_copy(ref, ref, sA_s, sB_r.at[b, which], second, bat)

    def quarter_to_sibling(b, which):
        ref = W.at[b, half, :, (first, second, both)[which]]
        return swap_copy(ref, ref, sA_s, sD_r.at[b], s, bat ^ 1)

    def own_ready(b, zz):
        @pl.when(c == 0)
        def _():
            to_sibling(b, zz).start()

        @pl.when(c == 1)
        def _():
            to_sibling(b, zz).wait_recv()

        along_first(b, zz).start()
        along_second(b, 0, zz).start()

    def along_z(b, zz, j):
        ref = pair(b, split, zz, s)
        return swap_copy(ref, ref, sZ_s, sZ_r.at[b, zz], s, bat ^ (2 * j))

    def whole_along_z(b, zz, j):
        ref = W.at[b, whole, pl.ds(2 * zz, 2)]
        return swap_copy(ref, ref, sV_s, sV_r.at[b, j - 1], s, bat ^ (2 * j))

    def whole_to_sibling(b, zz):
        ref = W.at[b, whole, pl.ds(2 * zz, 2)]
        return swap_copy(ref, ref, sJ_s, sJ_r.at[b], s, bat ^ 1)

    def on_first_core(work):
        pl.when(c == 0)(work)

    @jax.named_scope("own_quarter")
    def own_quarter(b):
        @on_first_core
        def _():
            drain(pair(b, split, z, s), sS_r.at[b])

        own_ready(b, z)

    @jax.named_scope("start_z")
    def start_z(b):
        @on_first_core
        def _():
            along_z(b, z, 2).start()
            along_z(b, z, 1).start()

    @jax.named_scope("start_whole")
    def start_whole(b):
        @on_first_core
        def _():
            drain(W.at[b, whole, pl.ds(2 * z, 2)], sU_r.at[b])
            whole_along_z(b, z, 2).start()
            whole_along_z(b, z, 1).start()
            whole_to_sibling(b, z).start()

    @jax.named_scope("relay_z")
    def relay_z(b):
        @on_first_core
        def _():
            drain(pair(b, split, z ^ 2, s), sZ_r.at[b, z ^ 2])
            along_z(b, z ^ 2, 1).start()

        own_ready(b, z ^ 2)

    @jax.named_scope("rest_z")
    def rest_z(b):
        for j in (1, 3):
            @on_first_core
            def _():
                drain(pair(b, split, z ^ j, s), sZ_r.at[b, z ^ j])

            own_ready(b, z ^ j)

    @jax.named_scope("relay_whole")
    def relay_whole(b):
        @on_first_core
        def _():
            drain(W.at[b, whole, pl.ds(2 * (z ^ 2), 2)], sV_r.at[b, 1])
            whole_along_z(b, z ^ 2, 1).start()
            whole_to_sibling(b, z ^ 2).start()

    @jax.named_scope("rest_whole")
    def rest_whole(b):
        @on_first_core
        def _():
            drain(W.at[b, whole, pl.ds(0, 4)], sV_r.at[b, 0])
            for j in (1, 3):
                whole_to_sibling(b, z ^ j).start()

    @jax.named_scope("gather_first")
    def gather_first(b):
        for j in range(4):
            zz = z ^ j
            ref = pair(b, half, zz, first)
            swap_copy(ref, ref, sA_s, sA_r.at[b, zz], first, bat).wait_recv()
            along_second(b, 1, zz).start()
        quarter_to_sibling(b, 0).start()

    @jax.named_scope("gather_second")
    def gather_second(b):
        for which in range(2):
            drain(W.at[b, half, :, (second, both)[which]], sB_r.at[b, which])
            quarter_to_sibling(b, 1 + which).start()

    @jax.named_scope("gather_last")
    def gather_last(b):
        other = pl.ds(HALF * (1 - c), HALF)
        drain(W.at[b, other, :, pl.ds(0, 3)], sD_r.at[b])

        @pl.when(c == 1)
        def _():
            drain(W.at[b, whole], sJ_r.at[b])

    for b in range(3):
        own_quarter(b)
        if b == 0:
            start_z(0)
    relay_z(0)
    start_whole(0)
    start_z(1)

    drain(cnt.at[pl.ds(0, 7)], sC_r.at[0])
    drain(cntx.at[pl.ds(2, 4)], sC_r.at[1])
    cntx[1 - c] = cnt[bat ^ 1]
    total = jnp.zeros((1, 1), jnp.float32)
    for j in range(8):
        big = cnt[j][0:1, 0:1]
        big_rows = big * float(BIG_SIDE * BIG_SIDE)
        area = float(SMALL_SIDE * SMALL_SIDE)
        total = total + big_rows + jnp.floor((R - big_rows + 0.5) / area) * area
    row_count = total
    down = lax.broadcasted_iota(jnp.int32, (R, 1), 0).astype(jnp.float32)
    across = lax.broadcasted_iota(jnp.int32, (1, R), 1).astype(jnp.float32)

    @pl.loop(0, 6)
    @jax.named_scope("tables")
    def _(v):
        big = cntx[v][0:1, 0:1]
        code_down, ok_down = crop_codes(down, big, R)
        code_across, ok_across = crop_codes(across, big, R)
        code_down = jnp.where(ok_down, code_down, -5000.0)
        code_across = jnp.where(ok_across, code_across, -1.0)
        for k in range(9):
            step = float(32 * (k // 3 - 1) + (k % 3 - 1))
            hit = (code_down + step) == code_across
            Gm[v, pl.ds(k * R, R)] = jnp.where(hit, 1.0, 0.0).astype(jnp.bfloat16)

    _, own_valid = crop_codes(down, cown[0:1, 0:1], R)
    valid = own_valid.astype(jnp.float32)
    drain(aff.at[pl.ds(0, 3)], sF_r)
    loads[10].wait()
    h[...] = abuf[...].astype(jnp.float32)

    @jax.named_scope("sums_start")
    def sums_start(e, first_sum, second_sum):
        slot = lax.rem(e, 2)
        st_own[e] = pack(first_sum, second_sum)
        to_core = swap_copy(st_own.at[e], st_in.at[e], sE_in_s.at[slot], sE_in_r.at[slot], s, bat ^ 1)

        @pl.when(e > 1)
        def _():
            sums_close(e)

        @pl.when(c == 0)
        def _():
            to_core.start()

        @pl.when(c == 1)
        def _():
            to_core.wait_recv()
            st_all[e, z] = st_own[e] + st_in[e]
            for j in (7, 6, 5, 4, 3, 2, 1):
                swap_copy(
                    st_all.at[e, z], st_all.at[e, z], sE_s.at[slot], sE_r.at[slot], s, bat ^ j
                ).start()

    @jax.named_scope("sums_finish")
    def sums_finish(e):
        slot = lax.rem(e, 2)

        @pl.when(c == 0)
        def _():
            drain(st_all.at[e], sE_r.at[slot])

        @pl.when(c == 1)
        def _():
            drain(st_all.at[e, pl.ds(0, 3)], sE_r.at[slot])

        return unpack(st_all[e, 0] + st_all[e, 1] + st_all[e, 2] + st_all[e, 3])

    def sums_close(e):
        slot = lax.rem(e, 2)

        @pl.when(c == 0)
        def _():
            drain(st_own.at[0], sE_in_s.at[slot])

        @pl.when(c == 1)
        def _():
            drain(cnt.at[pl.ds(0, 7)], sE_s.at[slot])

    def moments(sums):
        center = sums[0] / row_count
        spread = lax.rsqrt(sums[1] / row_count - center * center + EPS)
        return center, spread

    def pairing(b):
        odd = lax.rem(b, 2) == 1
        return jnp.where(odd, x, y), jnp.where(odd, y, x), jnp.where(odd, 1, 2)

    @jax.named_scope("share")
    def share(b, kind, rows):
        turned = rows.T
        rows_to = stage_a if kind == 1 else stage.at[b]
        if kind == 1:
            @pl.when(b > 0)
            def _():
                drain(stage_a.at[pl.ds(0, 2)], sQ_s.at[1])

        odd = lax.rem(b, 2) == 1
        for cc in range(2):
            for xx in range(2):
                for yy in range(2):
                    one, two = jnp.where(odd, xx, yy), jnp.where(odd, yy, xx)
                    for zz in range(4):
                        at = (2 * zz + cc) * 64 + (2 * yy + xx) * 16
                        rows_to[2 * one + cc, 4 * two + zz] = turned[at : at + 16].astype(
                            jnp.bfloat16
                        )
        if kind == 1:
            for half_of_pair in range(2):
                v = 2 * half_of_pair
                caq[b, 1, v + c] = stage_a[v + c]
                swap_copy(
                    stage_a.at[v + 1 - c], caq.at[b, 1, v + c], sQ_s.at[1], sQ_r.at[b, 1], s, bat ^ 1
                ).start()
        else:
            u = 2 * pairing(b)[0] + c
            caq[b, 0, u] = stage[b, u]

            @pl.when(b == 3)
            def _():
                send_share(b)

    def send_share(b):
        mine, _, near = pairing(b)
        u = 2 * mine + c
        for j in range(1, 4):
            swap_copy(
                stage.at[b, u ^ j], caq.at[b, 0, u], sQ_s.at[0], sQ_r.at[b, 0],
                s ^ near if j > 1 else s, bat ^ (j % 2),
            ).start()

    def wait_share(b, kind):
        drain(caq.at[b, kind, pl.ds(0, 2 if kind == 1 else 3)], sQ_r.at[b, kind])

    @jax.named_scope("forward")
    def forward(b):
        gather_last(b)

        @pl.when(b == 3)
        def _():
            for early in (2, 1, 0):
                send_share(early)

        hidden = h[...]
        zbuf[...] = jnp.dot(
            hidden.astype(jnp.bfloat16), W[b, 9].reshape(D, D), preferred_element_type=jnp.float32
        )
        z1 = zbuf[...]
        kept = valid * z1
        sums_start(
            2 * b, jnp.sum(kept, 0, keepdims=True), jnp.sum(kept * z1, 0, keepdims=True)
        )
        share(b, 1, hidden)

        @pl.when(b == 0)
        def _():
            gather_first(1)
            relay_whole(1)
            own_quarter(3)
            start_z(3)

        @pl.when(b == 1)
        def _():
            relay_z(3)
            gather_first(2)

        @pl.when(b == 2)
        def _():
            gather_first(3)
            relay_whole(3)

        norms = aff[b]
        center, spread = moments(sums_finish(2 * b))
        gi[b, 0:1] = norms[0:1] * spread
        for i in range(0, R, 64):
            xhat = (zbuf[i : i + 64] - center) * spread
            value, slope = mish_terms(norms[0:1] * xhat + norms[1:2])
            sv[b, 0, i : i + 64] = xhat.astype(sv.dtype)
            sv[b, 1, i : i + 64] = slope.astype(sv.dtype)
            abuf[i : i + 64] = value.astype(jnp.bfloat16)
        mixed = abuf[...]
        for k in range(9):
            Hb[:, k * D : (k + 1) * D] = jnp.dot(
                Gm[c, pl.ds(k * R, R)], mixed, preferred_element_type=jnp.float32
            ).astype(jnp.bfloat16)
        zbuf[...] = jnp.dot(
            Hb[...], W[b, 0:9].reshape(9 * D, D), preferred_element_type=jnp.float32
        )
        z2 = zbuf[...]
        kept = valid * z2
        sums_start(
            2 * b + 1, jnp.sum(kept, 0, keepdims=True), jnp.sum(kept * z2, 0, keepdims=True)
        )
        share(b, 0, mixed.astype(jnp.float32))

        @pl.when(b == 0)
        def _():
            rest_z(2)
            start_whole(2)

        @pl.when(b == 1)
        def _():
            relay_whole(2)
            rest_z(3)
            start_whole(3)

        @pl.when(b == 2)
        def _():
            rest_whole(3)

        center, spread = moments(sums_finish(2 * b + 1))
        gi[b, 1:2] = norms[2:3] * spread
        for i in range(0, R, 64):
            xhat = (zbuf[i : i + 64] - center) * spread
            value, slope = mish_terms(norms[2:3] * xhat + norms[3:4])
            sv[b, 2, i : i + 64] = xhat.astype(sv.dtype)
            sv[b, 3, i : i + 64] = slope.astype(sv.dtype)
            h[i : i + 64] = h[i : i + 64] + valid[i : i + 64] * value

    rest_z(0)
    relay_whole(0)
    start_z(2)
    gather_first(0)
    relay_z(1)
    start_whole(1)
    rest_whole(0)
    gather_second(0)
    relay_z(2)
    rest_z(1)

    @pl.loop(0, 4)
    def _(b):
        forward(b)

        @pl.when(b < 2)
        def _():
            rest_whole(b + 1)

        @pl.when(b < 3)
        def _():
            gather_second(b + 1)

    out_grad_rows = pltpu.make_async_copy(out_grad.at[s], abuf, sL.at[2])
    out_features = pltpu.make_async_copy(h, features.at[0], sO_s.at[0])
    out_features.start()
    out_grad_rows.start()
    out_grad_rows.wait()
    g[...] = abuf[...].astype(jnp.float32)

    @jax.named_scope("close_gather")
    def close_gather():
        drain(aff.at[pl.ds(0, 3)], sF_s)
        drain(st_own.at[pl.ds(0, 11)], sC_s)
        drain(stage_a.at[pl.ds(0, 2)], sQ_s.at[1])

        @pl.when(c == 0)
        def _():
            drain(wown.at[split, pl.ds(0, 3)], sS_s)
            drain(W.at[0, whole, pl.ds(0, 3)], sU_s)

        @pl.when(c == 1)
        def _():
            drain(wown.at[split], sS_s)
            drain(W.at[0, whole, pl.ds(0, 4)], sU_s)

        drain(W.at[:, split, :, pl.ds(0, 3)], sA_s)

        @on_first_core
        def _():
            drain(W.at[:, split, pl.ds(0, 6), s], sZ_s)
            drain(W.at[:, split, :, s], sH_s)
            drain(W.at[:, whole, pl.ds(0, 6)], sV_s)
            drain(W.at[:, whole], sJ_s)

    @jax.named_scope("close_rest")
    def close_rest():
        drain(stage.at[:, pl.ds(0, 3)], sQ_s.at[0])
        drain(dzq.at[:, pl.ds(0, 3)], sX_s)
        drain(dz1q.at[:, 0], sM_s)
        drain(precv, sP_s)
        drain(gsend.at[pl.ds(0, 3)], sO_s.at[3])
        drain(gout.at[:, 0], sY_s)

        @pl.when(c == 0)
        def _():
            drain(zrecv.at[:, pl.ds(0, 2)], sN_s)
            drain(zrecv.at[:, 2], sT_s)

        @pl.when(c == 1)
        def _():
            drain(zs1, sK_s)
            drain(zrecv.at[pl.ds(0, 3), pl.ds(0, 2)], sN_s)
            drain(zrecv.at[pl.ds(0, 3), 2], sT_s)

    CHUNKS = ((0, 3), (3, 3), (6, 3), (9, 1))
    LAST = len(CHUNKS) - 1

    def dz_copy(b, j):
        mine, _, near = pairing(b)
        v = 2 * mine + c
        v = v ^ 2 if j == 3 else v
        ref = dzq.at[b, v]
        return swap_copy(
            ref, ref, sX_s, sX_r.at[b, 0 if j == 2 else 1], s ^ near if j == 2 else s, bat if j == 2 else bat ^ 1
        )

    def send_dz(b):
        dz_copy(b, 2).start()
        dz_copy(b, 1).start()

    @jax.named_scope("forward_dz")
    def forward_dz(b):
        v = (2 * pairing(b)[0] + c) ^ 2
        drain(dzq.at[b, v], sX_r.at[b, 0])
        dz_copy(b, 3).start()

    @jax.named_scope("wait_dz")
    def wait_dz(b):
        drain(dzq.at[b, pl.ds(0, 2)], sX_r.at[b, 1])

    def dz_one_copy(b):
        ref = dz1q.at[b, c]
        return swap_copy(ref, ref, sM_s, sM_r.at[b], s, bat ^ 1)

    def point_copy(b):
        mine, _, near = pairing(b)
        return swap_copy(
            pgrad.at[b, 1 - mine], precv.at[b], sP_s, sP_r.at[b], s ^ near, bat
        )

    def y_copy(b, i):
        at, size = CHUNKS[i]
        return swap_copy(
            gout.at[b, 1 - pairing(b)[1], pl.ds(at, size)], yrecv.at[b, pl.ds(at, size)],
            sY_s, sY_r.at[b, i], s ^ 3 ^ pairing(b)[2], bat,
        )

    def grad_tap(b, k, left, right):
        part = jnp.dot(left, right, preferred_element_type=jnp.float32).astype(jnp.bfloat16)
        for yy in range(2):
            gout[b, yy, k] = part[64 * yy : 64 * yy + 64].reshape(4, 16, D)

    @jax.named_scope("grad_spatial")
    def grad_spatial(b):
        wait_share(b, 0)
        wait_dz(b)
        mine, _, near = pairing(b)
        tables = [jnp.where(mine == v // 2, 0, 2 * near) + v % 2 for v in range(4)]
        right = dzq[b].reshape(4 * R, D)
        for k in range(9):
            left = [
                lax.dot_general(
                    caq[b, 0, v].reshape(128, R), Gm[tables[v], pl.ds(k * R, R)], NT,
                    preferred_element_type=jnp.float32,
                ).astype(jnp.bfloat16)
                for v in range(4)
            ]
            grad_tap(b, k, jnp.concatenate(left, axis=1), right)
            if k % 3 == 2:
                y_copy(b, k // 3).start()

    @jax.named_scope("grad_point")
    def grad_point(b):
        wait_share(b, 1)
        drain(dz1q.at[b, 1 - c], sM_r.at[b])
        left = jnp.concatenate(
            [
                jnp.concatenate([caq[b, 1, 2 * v + k].reshape(128, R) for v in range(2)], axis=0)
                for k in range(2)
            ],
            axis=1,
        )
        part = jnp.dot(
            left, dz1q[b].reshape(2 * R, D), preferred_element_type=jnp.float32
        ).astype(jnp.bfloat16)
        pgrad[b] = part.reshape(2, 2, 4, 16, D)
        point_copy(b).start()

    @jax.named_scope("pair_point")
    def pair_point(b):
        point_copy(b).wait_recv()
        mine = pairing(b)[0]
        for yy in range(2):
            gout[b, yy, 9] = (
                pgrad[b, mine, yy].astype(jnp.float32) + precv[b, yy].astype(jnp.float32)
            ).astype(jnp.bfloat16)
        y_copy(b, LAST).start()

    def core_copy(b, i):
        at, size = CHUNKS[i]
        return swap_copy(
            yrecv.at[b, pl.ds(at, size)], zs1.at[pl.ds(at, size)],
            sK_s, sK_r.at[i], s, bat ^ 1,
        )

    @jax.named_scope("reduce_plane")
    def reduce_plane(b, i):
        at, size = CHUNKS[i]
        y_copy(b, i).wait_recv()
        rest = pairing(b)[1]
        for k in range(at, at + size):
            yrecv[b, k] = (
                yrecv[b, k].astype(jnp.float32) + gout[b, rest, k].astype(jnp.float32)
            ).astype(jnp.bfloat16)

        if b == 3:

            @pl.when(c == 1)
            def _():
                core_copy(b, i).start()

    def carriers(b, work):
        if b == 3:
            pl.when(c == 0)(functools.partial(work, (0, 1)))
        else:
            work((0,))

    def z_near(b, i, cc, slot):
        at, size = CHUNKS[i]
        return swap_copy(
            (yrecv.at[b], zs1)[cc].at[pl.ds(at, size), z ^ (3 if slot else 1)],
            zrecv.at[b + cc, slot, pl.ds(at, size)], sN_s, sN_r.at[b, i], s, bat ^ 2,
        )

    def z_far(b, i, cc):
        at, size = CHUNKS[i]
        return swap_copy(
            zrecv.at[b + cc, 1, pl.ds(at, size)], zrecv.at[b + cc, 2, pl.ds(at, size)],
            sT_s, sT_r.at[b, i], s, bat ^ 4,
        )

    def near_like(b, i, parts):
        at, size = CHUNKS[i]
        return zrecv.at[pl.ds(b, len(parts)), pl.ds(0, 2), pl.ds(at, size)]

    def far_like(b, i, parts):
        at, size = CHUNKS[i]
        return zrecv.at[pl.ds(b, len(parts)), 2, pl.ds(at, size)]

    @jax.named_scope("reduce_near")
    def reduce_near(b, i):
        def work(parts):
            if b == 3:
                core_copy(b, i).wait_recv()
            for slot in (1, 0):
                for cc in parts:
                    z_near(b, i, cc, slot).start()

        carriers(b, work)

    @jax.named_scope("reduce_far")
    def reduce_far(b, i):
        at, size = CHUNKS[i]

        def work(parts):
            drain(near_like(b, i, parts), sN_r.at[b, i])
            for cc in parts:
                mine = (yrecv.at[b], zs1)[cc]
                for k in range(at, at + size):
                    zrecv[b + cc, 1, k] = (
                        zrecv[b + cc, 1, k].astype(jnp.float32) + mine[k, z ^ 2].astype(jnp.float32)
                    ).astype(jnp.bfloat16)
                z_far(b, i, cc).start()

        carriers(b, work)

    def deliver(b, i, cc, section, core):
        at, size = CHUNKS[i]
        swap_copy(
            zrecv.at[b + cc, 0, pl.ds(at, size)], gfin.at[pl.ds(at, size), s],
            sG_s, sG_r.at[s], section, 2 * z + core,
        ).start()

    @jax.named_scope("finish")
    def finish(b, i):
        at, size = CHUNKS[i]

        def work(parts):
            drain(far_like(b, i, parts), sT_r.at[b, i])
            for cc in parts:
                mine = (yrecv.at[b], zs1)[cc]
                for k in range(at, at + size):
                    zrecv[b + cc, 0, k] = (
                        zrecv[b + cc, 0, k].astype(jnp.float32)
                        + zrecv[b + cc, 2, k].astype(jnp.float32)
                        + mine[k, z].astype(jnp.float32)
                    ).astype(jnp.bfloat16)

                @pl.when(b != s)
                def _():
                    deliver(b, i, cc, b, cc if b == 3 else c)

                @pl.when(b == s)
                def _():
                    if cc == 0:
                        for k in range(at, at + size):
                            gfin[k, s] = zrecv[b, 0, k]
                    else:
                        deliver(b, i, 1, s, 1)

        carriers(b, work)

    @jax.named_scope("backward")
    def backward(bi):
        b = 3 - bi
        e = 8 + 2 * bi
        u = 2 * pairing(b)[0] + c
        first_sum = jnp.zeros((1, D), jnp.float32)
        second_sum = jnp.zeros((1, D), jnp.float32)
        for i in range(0, R, 64):
            du = valid[i : i + 64] * g[i : i + 64] * sv[b, 3, i : i + 64].astype(jnp.float32)
            zbuf[i : i + 64] = du
            first_sum += jnp.sum(du, 0, keepdims=True)
            second_sum += jnp.sum(du * sv[b, 2, i : i + 64].astype(jnp.float32), 0, keepdims=True)
        sums_start(e, first_sum, second_sum)

        @pl.when(bi == 0)
        def _():
            close_gather()

        @pl.when(bi == 3)
        def _():
            reduce_near(3, 1)

        @pl.when(bi > 0)
        def _():
            forward_dz(b + 1)
            grad_point(b + 1)

        @pl.when(bi == 2)
        def _():
            pair_point(3)

        @pl.when(bi == 3)
        def _():
            reduce_plane(3, 2)
            reduce_far(3, 0)

        total_first, total_second = sums_finish(e)
        for i in range(0, R, 64):
            xhat = sv[b, 2, i : i + 64].astype(jnp.float32)
            inner = zbuf[i : i + 64] - valid[i : i + 64] * (
                (total_first + xhat * total_second) / row_count
            )
            dzq[b, u, i : i + 64] = (gi[b, 1:2] * inner).astype(jnp.bfloat16)
        send_dz(b)
        gsend[b, 2:3] = total_second
        gsend[b, 3:4] = total_first
        d_two = dzq[b, u]
        for k in range(9):
            Hb[:, k * D : (k + 1) * D] = jnp.dot(
                Gm[c, pl.ds((8 - k) * R, R)], d_two, preferred_element_type=jnp.float32
            ).astype(jnp.bfloat16)
        mixed = None
        for k in range(9):
            part = lax.dot_general(
                Hb[:, k * D : (k + 1) * D], W[b, k].reshape(D, D), NT,
                preferred_element_type=jnp.float32,
            )
            mixed = part if mixed is None else mixed + part
        zbuf[...] = mixed
        first_sum = jnp.zeros((1, D), jnp.float32)
        second_sum = jnp.zeros((1, D), jnp.float32)
        for i in range(0, R, 64):
            du = zbuf[i : i + 64] * sv[b, 1, i : i + 64].astype(jnp.float32)
            zbuf[i : i + 64] = du
            first_sum += jnp.sum(du, 0, keepdims=True)
            second_sum += jnp.sum(du * sv[b, 0, i : i + 64].astype(jnp.float32), 0, keepdims=True)
        sums_start(e + 1, first_sum, second_sum)

        @pl.when(bi == 2)
        def _():
            reduce_plane(3, 0)

        @pl.when(bi == 3)
        def _():
            reduce_near(3, 2)
            reduce_plane(2, 0)
            reduce_near(2, 0)

        @pl.when(bi > 0)
        def _():
            grad_spatial(b + 1)

        @pl.when(bi == 2)
        def _():
            reduce_near(3, 0)
            reduce_plane(3, 1)

        @pl.when(bi == 3)
        def _():
            reduce_plane(3, 3)
            reduce_far(3, 1)
            reduce_plane(2, 1)
            reduce_near(2, 1)

        total_first, total_second = sums_finish(e + 1)
        for i in range(0, R, 64):
            xhat = sv[b, 0, i : i + 64].astype(jnp.float32)
            inner = zbuf[i : i + 64] - valid[i : i + 64] * (
                (total_first + xhat * total_second) / row_count
            )
            dz1q[b, c, i : i + 64] = (gi[b, 0:1] * inner).astype(jnp.bfloat16)
        dz_one_copy(b).start()
        gsend[b, 0:1] = total_second
        gsend[b, 1:2] = total_first
        g[...] = g[...] + lax.dot_general(
            dz1q[b, c], W[b, 9].reshape(D, D), NT, preferred_element_type=jnp.float32
        )

        @pl.when(b == s)
        def _():
            gaff[s] = gsend[b]

        @pl.when(b != s)
        def _():
            swap_copy(gsend.at[b], gaff.at[s], sO_s.at[3], sO_r, b, bat).start()

    @pl.loop(0, 4)
    def _(bi):
        backward(bi)

    out_grad_in = pltpu.make_async_copy(g, in_grad.at[0], sO_s.at[1])
    out_grad_in.start()

    reduce_near(3, 3)
    forward_dz(0)
    pair_point(2)
    reduce_far(2, 0)
    reduce_far(3, 2)
    reduce_plane(2, 2)
    reduce_near(2, 2)
    grad_spatial(0)
    grad_point(0)
    pair_point(1)
    reduce_far(2, 1)
    finish(3, 0)
    reduce_plane(2, 3)
    reduce_near(2, 3)
    reduce_plane(1, 0)
    reduce_near(1, 0)
    reduce_far(3, 3)
    finish(3, 1)
    reduce_far(2, 2)
    finish(2, 0)
    reduce_plane(1, 1)
    reduce_near(1, 1)
    finish(3, 2)
    reduce_far(1, 0)
    reduce_plane(1, 2)
    reduce_near(1, 2)
    finish(3, 3)
    finish(2, 1)
    pair_point(0)
    reduce_far(2, 3)
    reduce_plane(0, 0)
    reduce_near(0, 0)
    reduce_far(1, 1)
    reduce_plane(1, 3)
    reduce_near(1, 3)
    finish(2, 2)
    finish(1, 0)
    reduce_far(1, 2)
    reduce_plane(0, 1)
    reduce_near(0, 1)
    reduce_plane(0, 2)
    reduce_near(0, 2)
    reduce_plane(0, 3)
    reduce_near(0, 3)
    reduce_far(0, 0)
    finish(2, 3)
    finish(1, 1)
    reduce_far(1, 3)
    reduce_far(0, 1)
    finish(1, 2)
    finish(1, 3)
    finish(0, 0)
    reduce_far(0, 2)
    reduce_far(0, 3)
    finish(0, 1)
    close_rest()
    finish(0, 2)
    finish(0, 3)
    for d in range(1, 4):
        drain(gfin.at[:, s ^ d], sG_r.at[s ^ d])

    @pl.when((c == 1) & (s == 3))
    def _():
        drain(gfin.at[:, s], sG_r.at[s])

    grads_out = pltpu.make_async_copy(gfin, grads, sO_s.at[2])
    grads_out.start()

    def lane_sum(v):
        return jnp.sum(v, axis=1, keepdims=True)

    gspatial_squares = jnp.zeros((1, D), jnp.float32)
    for k in range(9):
        gspatial_squares += square(gfin[k].astype(jnp.float32).reshape(64, D))
    gpoint_squares = square(gfin[9].astype(jnp.float32).reshape(64, D))
    lanes = lax.broadcasted_iota(jnp.int32, (1, D), 1)
    tile = jnp.zeros((1, D), jnp.float32)
    for i, part in enumerate((point_squares, spatial_squares, gpoint_squares, gspatial_squares)):
        tile = jnp.where(lanes == i, lane_sum(part), tile)
    sums_start(jnp.int32(16), tile, tile)
    drain(gaff.at[pl.ds(0, 3)], sO_r)
    affine_out[...] = gaff[0] + gaff[1] + gaff[2] + gaff[3]
    totals, _ = sums_finish(16)
    totals_out[...] = jnp.concatenate([totals] * 8, axis=0)

    with jax.named_scope("close_last"):
        sums_close(0)
        sums_close(1)

        @pl.when(c == 0)
        def _():
            drain(zrecv.at[pl.ds(0, 4), 0], sG_s)

        @pl.when((c == 1) & (s == 3))
        def _():
            drain(zrecv.at[pl.ds(0, 3), 0], sG_s)

        @pl.when((c == 1) & (s != 3))
        def _():
            drain(zrecv.at[pl.ds(0, 2), 0], sG_s)

    with jax.named_scope("close_outputs"):
        grads_out.wait()
        out_features.wait()
        out_grad_in.wait()


def lars_kernel(
    feat, ing, grads_in, totals_in, affine_in, w_point, w_spatial, norm_in, mom_point, mom_spatial, mom_norm,
    features, in_grad, new_point, new_spatial, new_norm, new_mom_point, new_mom_spatial, new_mom_norm,
    P, M, G, feat_rows, grad_rows, totals, affine_grad, affine, affine_mom, sem, out_sem,
):
    loads = [
        (totals_in, totals), (affine_in, affine_grad), (norm_in.at[0], affine), (mom_norm.at[0], affine_mom),
        (grads_in, G), (w_spatial.at[0], P.at[pl.ds(0, 9)]), (mom_spatial.at[0], M.at[pl.ds(0, 9)]),
        (w_point.at[0], P.at[9]), (mom_point.at[0], M.at[9]),
    ]
    loads = [pltpu.make_async_copy(a, b, sem.at[i]) for i, (a, b) in enumerate(loads)]
    for load in loads:
        load.start()
    passed = [
        pltpu.make_async_copy(feat, feat_rows, sem.at[9]),
        pltpu.make_async_copy(ing, grad_rows, sem.at[10]),
    ]
    for copy in passed:
        copy.start()
    for load in loads:
        load.wait()
    D = affine.shape[1]
    rate = BASE_RATE * (STEP + 1) / WARMUP
    point_sq, spatial_sq, gpoint_sq, gspatial_sq = [totals[0:1, i : i + 1] for i in range(4)]
    step_point = rate * TRUST_COEF * jnp.sqrt(point_sq) / (jnp.sqrt(gpoint_sq) + EPS_NORM)
    step_spatial = rate * TRUST_COEF * jnp.sqrt(spatial_sq) / (jnp.sqrt(gspatial_sq) + EPS_NORM)
    outs = []

    def store(source, target):
        outs.append(pltpu.make_async_copy(source, target, out_sem.at[len(outs)]))
        outs[-1].start()

    for k in range(10):
        grad = G[k].astype(jnp.float32).reshape(64, D)
        moved = MOMENTUM * M[k] + (step_point if k == 9 else step_spatial) * grad
        M[k] = moved
        P[k] = P[k] - moved
        if k in (2, 5, 8):
            taps = pl.ds(k - 2, 3)
            store(M.at[taps], new_mom_spatial.at[0, taps])
            store(P.at[taps], new_spatial.at[0, taps])
    for copy, rows, target in zip(passed, (feat_rows, grad_rows), (features, in_grad)):
        copy.wait()
        store(rows, target)
    store(M.at[9], new_mom_point.at[0])
    store(P.at[9], new_point.at[0])
    grad = affine_grad[0:4]
    old = affine[...]
    affine_sq = jnp.sum(old * old, axis=1, keepdims=True)
    gaffine_sq = jnp.sum(grad * grad, axis=1, keepdims=True)
    trust = TRUST_COEF * jnp.sqrt(affine_sq) / (jnp.sqrt(gaffine_sq) + EPS_NORM)
    moved = MOMENTUM * affine_mom[...] + rate * trust * grad
    affine_mom[...] = moved
    affine[...] = old - moved
    store(affine_mom, new_mom_norm.at[0])
    store(affine, new_norm.at[0])
    for copy in outs:
        copy.wait()


def train_step(images, crop, w_point, w_spatial, norm_params, mom_point, mom_spatial, mom_norm, out_grad):
    R, D = images.shape[1:]
    f32, bf16 = jnp.float32, jnp.bfloat16
    dma = pltpu.SemaphoreType.DMA
    anywhere = pl.BlockSpec(memory_space=pl.ANY)
    vmem = pl.BlockSpec(memory_space=pltpu.VMEM)
    hbm = pl.BlockSpec(memory_space=pltpu.HBM)
    smem = pl.BlockSpec(memory_space=pltpu.SMEM)
    V = pltpu.VMEM
    scratch = dict(
        W=V((4, TAPS, 8, 4, 16, D), bf16), wown=V((TAPS, 4, 16, D), bf16),
        F=V((3 * R, D), f32),
        sv=V((4, 4, R, D), bf16), gi=V((4, 8, D), f32),
        abuf=V((R, D), bf16),
        Gm=V((6, 9 * R, R), bf16), caq=V((4, 2, 4, 8, 16, R), bf16),
        stage=V((4, 4, 8, 16, R), bf16), stage_a=V((4, 8, 16, R), bf16), Hb=V((R, 9 * D), bf16),
        dzq=V((4, 4, R, D), bf16), dz1q=V((4, 2, R, D), bf16),
        pgrad=V((4, 2, 2, 4, 16, D), bf16), precv=V((4, 2, 4, 16, D), bf16),
        gout=V((4, 2, TAPS, 4, 16, D), bf16), yrecv=V((4, TAPS, 4, 16, D), bf16),
        zs1=V((TAPS, 4, 16, D), bf16), zrecv=V((5, 3, TAPS, 16, D), bf16),
        gfin=V((TAPS, 4, 16, D), bf16),
        aff=V((4, 8, D), f32), gaff=V((4, 8, D), f32), gsend=V((4, 8, D), f32),
        st_in=V((17, 8, 128), f32), st_own=V((17, 8, 128), f32), st_all=V((17, 4, 8, 128), f32),
        cnt=V((8, 8, 128), f32), cntx=V((6, 8, 128), f32), cown=V((8, 128), f32),
        sL=dma((3,)), sS_s=dma, sS_r=dma((4,)), sU_s=dma, sU_r=dma((4,)), sV_s=dma, sV_r=dma((4, 2)),
        sJ_s=dma, sJ_r=dma((4,)), sZ_s=dma, sZ_r=dma((4, 4)),
        sH_s=dma, sH_r=dma((4, 4)), sA_s=dma, sA_r=dma((4, 4)),
        sB_r=dma((4, 2)), sD_r=dma((4,)),
        sE_in_s=dma((2,)), sE_in_r=dma((2,)), sE_s=dma((2,)), sE_r=dma((2,)),
        sC_s=dma, sC_r=dma((2,)), sF_s=dma, sF_r=dma,
        sQ_s=dma((2,)), sQ_r=dma((4, 2)), sX_s=dma, sX_r=dma((4, 2)), sM_s=dma, sM_r=dma((4,)), sP_s=dma, sP_r=dma((4,)),
        sY_s=dma, sY_r=dma((4, 4)), sK_s=dma, sK_r=dma((4,)),
        sN_s=dma, sN_r=dma((4, 4)), sT_s=dma, sT_r=dma((4, 4)), sG_s=dma, sG_r=dma((4,)),
        sO_s=dma((4,)), sO_r=dma,
    )
    shape = jax.ShapeDtypeStruct
    feat, ing, grads, totals, affine_grad = pl.pallas_call(
        train_kernel,
        out_shape=(
            shape((1, R, D), f32), shape((1, R, D), f32), shape((TAPS, 4, 16, D), bf16),
            shape((8, D), f32), shape((8, D), f32),
        ),
        in_specs=[anywhere, smem, anywhere, anywhere, vmem, anywhere],
        out_specs=(anywhere, anywhere, anywhere, vmem, vmem),
        scratch_shapes=list(scratch.values()),
        compiler_params=pltpu.CompilerParams(
            collective_id=0, has_side_effects=True, vmem_limit_bytes=64 * 1024 * 1024
        ),
    )(images, crop.T, w_point, w_spatial, norm_params, out_grad)
    return pl.pallas_call(
        lars_kernel,
        out_shape=(
            shape((1, R, D), f32), shape((1, R, D), f32),
            shape(w_point.shape, f32), shape(w_spatial.shape, f32), shape(norm_params.shape, f32),
            shape(w_point.shape, f32), shape(w_spatial.shape, f32), shape(norm_params.shape, f32),
        ),
        in_specs=[hbm] * 11,
        out_specs=(hbm,) * 8,
        scratch_shapes=[
            V((TAPS, 64, D), f32), V((TAPS, 64, D), f32), V((TAPS, 4, 16, D), bf16), V((1, R, D), f32),
            V((1, R, D), f32), V((8, D), f32), V((8, D), f32), V((4, D), f32), V((4, D), f32), dma((11,)), dma((12,)),
        ],
        compiler_params=pltpu.CompilerParams(vmem_limit_bytes=64 * 1024 * 1024),
    )(feat, ing, grads, totals, affine_grad, w_point, w_spatial, norm_params, mom_point, mom_spatial, mom_norm)


def solution(mesh):
    tuned = mesh.shape["section"] == 4 and mesh.shape["batch"] == 8
    return jax.shard_map(
        train_step if tuned else on_device,
        mesh=mesh,
        in_specs=(
            P(None, "batch", None),
            P(None, "batch"),
            P("section", "batch", None),
            P("section", None, "batch", None),
            P("section", None, None),
            P("section", "batch", None),
            P("section", None, "batch", None),
            P("section", None, None),
            P(None, "batch", None),
        ),
        out_specs=(
            P("section", "batch", None),
            P("section", "batch", None),
            P("section", "batch", None),
            P("section", None, "batch", None),
            P("section", None, None),
            P("section", "batch", None),
            P("section", None, "batch", None),
            P("section", None, None),
        ),
        check_vma=False,
    )
```

```python
import functools

import jax
import jax.numpy as jnp
from jax import lax
from jax.experimental import pallas as pl
from jax.experimental.pallas import tpu as pltpu
from jax.sharding import PartitionSpec as P

BIG_SIDE = 7
SMALL_SIDE = 3
WARMUP = 20
STEP = 9


EPS = 1e-05
EPS_NORM = 1e-06
BASE_RATE = 6.0
MOMENTUM = 0.9
TRUST_COEF = 0.1


def from_behind(block, axis, distance):
    devices = range(lax.axis_size(axis))
    route = [(i - distance, i) for i in devices if i - distance in devices]
    return lax.ppermute(block, axis, route)


def crop_table(big_count, total_rows):
    places = jnp.arange(total_rows, dtype=jnp.int32)
    big_area = BIG_SIDE * BIG_SIDE
    small_area = SMALL_SIDE * SMALL_SIDE
    big_rows = big_count * big_area
    small_rows = (total_rows - big_rows) // small_area * small_area
    in_big = places < big_rows
    offsets = places - big_rows
    sides = jnp.where(in_big, BIG_SIDE, SMALL_SIDE)
    within = jnp.where(in_big, places % big_area, offsets % small_area)
    starts = places - within
    valid_rows = places < big_rows + small_rows
    row_pos = within // sides
    col_pos = within % sides
    indices = []
    masks = []
    for row_step in (-1, 0, 1):
        for col_step in (-1, 0, 1):
            new_row = row_pos + row_step
            new_col = col_pos + col_step
            inside = (
                valid_rows & (new_row >= 0) & (new_row < sides) & (new_col >= 0) & (new_col < sides)
            )
            indices.append(jnp.where(inside, starts + new_row * sides + new_col, places))
            masks.append(inside)
    return (
        jnp.stack(indices, 1),
        jnp.stack(masks, 1).astype(jnp.float32),
        valid_rows.astype(jnp.float32),
    )


def mish(values):
    return values * jnp.tanh(jax.nn.softplus(values))


def mish_parts(values):
    tangent = jnp.tanh(jax.nn.softplus(values))
    slope = tangent + values * jax.nn.sigmoid(values) * (1.0 - tangent * tangent)
    return (values * tangent, slope)


def mish_slope(values):
    tangent = jnp.tanh(jax.nn.softplus(values))
    return tangent + values * jax.nn.sigmoid(values) * (1.0 - tangent * tangent)


def batch_moments(proj, valid_rows):
    weighted = valid_rows[:, None] * proj
    summed, squared, row_count = lax.psum(
        (jnp.sum(weighted, 0), jnp.sum(weighted * proj, 0), jnp.sum(valid_rows)), "batch"
    )
    center = summed / row_count
    inv_std = lax.rsqrt(squared / row_count - center * center + EPS)
    return (center, inv_std, row_count)


def spatial_apply(source, tap_index, tap_mask, weights):
    stacked = source[tap_index] * tap_mask[:, :, None].astype(source.dtype)
    result = lax.dot_general(
        stacked, weights, (((1, 2), (0, 1)), ((), ())), preferred_element_type=jnp.float32
    )
    return (result, stacked)


def forward_block(hidden, point_low, spatial_low, affine, tap_index, tap_mask, valid_rows):
    proj_one = jnp.dot(hidden.astype(jnp.bfloat16), point_low, preferred_element_type=jnp.float32)
    center_one, inv_one, row_count = batch_moments(proj_one, valid_rows)
    mixed_one = mish(affine[0] * ((proj_one - center_one) * inv_one) + affine[1])
    proj_two, stacked = spatial_apply(
        mixed_one.astype(jnp.bfloat16), tap_index, tap_mask, spatial_low
    )
    center_two, inv_two, count_two = batch_moments(proj_two, valid_rows)
    mixed_two = mish(affine[2] * ((proj_two - center_two) * inv_two) + affine[3])
    moments = jnp.stack([center_one, inv_one, center_two, inv_two])
    return (hidden + valid_rows[:, None] * mixed_two, moments, row_count)


def norm_back(d_value, normed, inv_std, gain, valid_rows, row_count):
    first_sum, second_sum = lax.psum((jnp.sum(d_value, 0), jnp.sum(d_value * normed, 0)), "batch")
    d_proj = (
        gain
        * inv_std
        * (d_value - valid_rows[:, None] * (first_sum + normed * second_sum) / row_count)
    )
    return (d_proj.astype(jnp.bfloat16), first_sum, second_sum)


def backward_block(
    hidden,
    upstream,
    point_low,
    spatial_low,
    affine,
    moments,
    row_count,
    tap_index,
    tap_mask,
    valid_rows,
):
    inputs = hidden.astype(jnp.bfloat16)
    proj_one = jnp.dot(inputs, point_low, preferred_element_type=jnp.float32)
    normed_one = (proj_one - moments[0]) * moments[1]
    mixed_one, slope_one = mish_parts(affine[0] * normed_one + affine[1])
    proj_two, stacked = spatial_apply(
        mixed_one.astype(jnp.bfloat16), tap_index, tap_mask, spatial_low
    )
    normed_two = (proj_two - moments[2]) * moments[3]
    slope_two = mish_slope(affine[2] * normed_two + affine[3])
    d_two, first_two, second_two = norm_back(
        valid_rows[:, None] * upstream * slope_two,
        normed_two,
        moments[3],
        affine[2],
        valid_rows,
        row_count,
    )
    grad_spatial = lax.dot_general(
        stacked, d_two, (((0,), (0,)), ((), ())), preferred_element_type=jnp.float32
    )
    flipped = d_two[tap_index[:, ::-1]] * tap_mask[:, ::-1, None].astype(jnp.bfloat16)
    d_mixed = lax.dot_general(
        flipped, spatial_low, (((1, 2), (0, 2)), ((), ())), preferred_element_type=jnp.float32
    )
    d_one, first_one, second_one = norm_back(
        d_mixed * slope_one, normed_one, moments[1], affine[0], valid_rows, row_count
    )
    grad_point = lax.dot_general(
        inputs, d_one, (((0,), (0,)), ((), ())), preferred_element_type=jnp.float32
    )
    d_hidden = upstream + lax.dot_general(
        d_one, point_low, (((1,), (1,)), ((), ())), preferred_element_type=jnp.float32
    )
    grad_affine = jnp.stack([second_one, first_one, second_two, first_two])
    return (d_hidden, grad_point, grad_spatial, grad_affine)


def store_slot(buffer, value, slot_index, active):
    previous = lax.dynamic_index_in_dim(buffer, slot_index, 0, keepdims=False)
    return lax.dynamic_update_index_in_dim(
        buffer, jnp.where(active, value, previous), slot_index, 0
    )


def lars_update(param, grad, momentum, param_sq, grad_sq, rate):
    trust = TRUST_COEF * jnp.sqrt(param_sq) / (jnp.sqrt(grad_sq) + EPS_NORM)
    new_mom = MOMENTUM * momentum + rate * trust * grad
    return (param - new_mom, new_mom)


def on_device(
    images, crop_big, w_point, w_spatial, norm_params, mom_point, mom_spatial, mom_norm, out_grad
):
    section_count = lax.axis_size("section")
    section_rank = lax.axis_index("section")
    micro_count = images.shape[0]
    total_rows = images.shape[1]
    width = images.shape[2]
    point = w_point[0]
    spatial = w_spatial[0]
    affine = norm_params[0]
    crop_counts = crop_big[:, 0]
    turns = micro_count + section_count - 1
    point_low, spatial_low = (
        lax.all_gather(point.astype(jnp.bfloat16), "batch", axis=0, tiled=True),
        lax.all_gather(spatial.astype(jnp.bfloat16), "batch", axis=1, tiled=True),
    )
    kept_inputs = jnp.zeros((micro_count, total_rows, width), jnp.float32)
    kept_moments = jnp.zeros((micro_count, 4, width), jnp.float32)
    kept_counts = jnp.zeros((micro_count,), jnp.float32)
    results = jnp.zeros((micro_count, total_rows, width), jnp.float32)
    incoming = jnp.zeros((total_rows, width), jnp.float32)
    for phase_turn in range(turns):
        slot_raw = phase_turn - section_rank
        active = (slot_raw >= 0) & (slot_raw < micro_count)
        slot_index = jnp.clip(slot_raw, 0, micro_count - 1)
        fresh_rows = lax.dynamic_index_in_dim(images, slot_index, 0, keepdims=False).astype(
            jnp.float32
        )
        hidden = jnp.where(section_rank == 0, fresh_rows, incoming)
        tap_index, tap_mask, valid_rows = crop_table(crop_counts[slot_index], total_rows)
        output, moments, row_count = forward_block(
            hidden, point_low, spatial_low, affine, tap_index, tap_mask, valid_rows
        )
        kept_inputs = store_slot(kept_inputs, hidden, slot_index, active)
        kept_moments = store_slot(kept_moments, moments, slot_index, active)
        kept_counts = store_slot(kept_counts, row_count, slot_index, active)
        results = store_slot(
            results, output, slot_index, active & (section_rank == section_count - 1)
        )
        if phase_turn + 1 < turns:
            incoming = from_behind(output.astype(jnp.bfloat16), "section", 1).astype(output.dtype)
    point_low, spatial_low = (
        lax.all_gather(point.astype(jnp.bfloat16), "batch", axis=0, tiled=True),
        lax.all_gather(spatial.astype(jnp.bfloat16), "batch", axis=1, tiled=True),
    )
    grad_point = jnp.zeros((width, width), jnp.float32)
    grad_spatial = jnp.zeros((9, width, width), jnp.float32)
    grad_affine = jnp.zeros((4, width), jnp.float32)
    collected = jnp.zeros((micro_count, total_rows, width), jnp.float32)
    returning = jnp.zeros((total_rows, width), jnp.float32)
    for phase_turn in range(turns):
        slot_raw = micro_count - 1 - phase_turn + (section_count - 1 - section_rank)
        active = (slot_raw >= 0) & (slot_raw < micro_count)
        slot_index = jnp.clip(slot_raw, 0, micro_count - 1)
        seeded = lax.dynamic_index_in_dim(out_grad, slot_index, 0, keepdims=False).astype(
            jnp.float32
        )
        upstream = jnp.where(section_rank == section_count - 1, seeded, returning)
        upstream = jnp.where(active, upstream, 0.0)
        tap_index, tap_mask, valid_rows = crop_table(crop_counts[slot_index], total_rows)
        hidden = lax.dynamic_index_in_dim(kept_inputs, slot_index, 0, keepdims=False)
        moments = lax.dynamic_index_in_dim(kept_moments, slot_index, 0, keepdims=False)
        row_count = lax.dynamic_index_in_dim(kept_counts, slot_index, 0, keepdims=False)
        d_hidden, part_point, part_spatial, part_affine = backward_block(
            hidden,
            upstream,
            point_low,
            spatial_low,
            affine,
            moments,
            row_count,
            tap_index,
            tap_mask,
            valid_rows,
        )
        grad_point = grad_point + part_point
        grad_spatial = grad_spatial + part_spatial
        grad_affine = grad_affine + part_affine
        collected = store_slot(collected, d_hidden, slot_index, active & (section_rank == 0))
        if phase_turn + 1 < turns:
            returning = from_behind(d_hidden.astype(jnp.bfloat16), "section", -1).astype(
                d_hidden.dtype
            )
    point_grad, spatial_grad = (
        lax.psum_scatter(grad_point, "batch", scatter_dimension=0, tiled=True),
        lax.psum_scatter(grad_spatial, "batch", scatter_dimension=1, tiled=True),
    )
    point_sq, spatial_sq, gpoint_sq, gspatial_sq = lax.psum(
        (
            jnp.sum(point * point),
            jnp.sum(spatial * spatial),
            jnp.sum(point_grad * point_grad),
            jnp.sum(spatial_grad * spatial_grad),
        ),
        "batch",
    )
    rate = BASE_RATE * (STEP + 1) / WARMUP
    new_point, new_mom_point = lars_update(
        point, point_grad, mom_point[0], point_sq, gpoint_sq, rate
    )
    new_spatial, new_mom_spatial = lars_update(
        spatial, spatial_grad, mom_spatial[0], spatial_sq, gspatial_sq, rate
    )
    affine_sq = jnp.sum(affine * affine, 1, keepdims=True)
    gaffine_sq = jnp.sum(grad_affine * grad_affine, 1, keepdims=True)
    new_affine, new_mom_affine = lars_update(
        affine, grad_affine, mom_norm[0], affine_sq, gaffine_sq, rate
    )
    sent_out = jnp.where(section_rank == section_count - 1, results, 0.0)
    sent_back = jnp.where(section_rank == 0, collected, 0.0)
    got_out, got_back = (
        lax.all_to_all(
            sent_out.astype(jnp.bfloat16), "section", split_axis=0, concat_axis=0, tiled=True
        ).astype(sent_out.dtype),
        lax.all_to_all(
            sent_back.astype(jnp.bfloat16), "section", split_axis=0, concat_axis=0, tiled=True
        ).astype(sent_back.dtype),
    )
    features = got_out[section_count - 1 : section_count]
    in_grad = got_back[0:1]
    return (
        features,
        in_grad,
        new_point[None],
        new_spatial[None],
        new_affine[None],
        new_mom_point[None],
        new_mom_spatial[None],
        new_mom_affine[None],
    )


def swap_copy(source, target, sent, landed, section, batch):
    return pltpu.make_async_remote_copy(
        src_ref=source,
        dst_ref=target,
        send_sem=sent,
        recv_sem=landed,
        device_id=(section, batch),
        device_id_type=pl.DeviceIdType.MESH,
    )


def drain(like, sem):
    pltpu.make_async_copy(like, like, sem).wait()


def mish_terms(v):
    e = jnp.exp(jnp.minimum(v, 20.0))
    w = e * (e + 2.0)
    r = 1.0 / (w + 2.0)
    t = w * r
    return v * t, t + v * (4.0 * e * (1.0 + e)) * (r * r)


def pack(first, second):
    parts = [v[:, i * 128 : (i + 1) * 128] for v in (first, second) for i in range(4)]
    return jnp.concatenate(parts, axis=0)


def unpack(tile):
    rows = [tile[i : i + 1] for i in range(8)]
    return jnp.concatenate(rows[:4], axis=1), jnp.concatenate(rows[4:], axis=1)


def crop_codes(places, big, total_rows):
    big_area = float(BIG_SIDE * BIG_SIDE)
    small_area = float(SMALL_SIDE * SMALL_SIDE)
    big_rows = big * big_area
    small_rows = jnp.floor((total_rows - big_rows + 0.5) / small_area) * small_area
    in_big = places < big_rows
    offset = jnp.where(in_big, places, places - big_rows)
    area = jnp.where(in_big, big_area, small_area)
    side = jnp.where(in_big, float(BIG_SIDE), float(SMALL_SIDE))
    crop = jnp.floor((offset + 0.5) / area)
    within = offset - crop * area
    row = jnp.floor((within + 0.5) / side)
    col = within - row * side
    crop = jnp.where(in_big, crop, crop + big)
    return crop * 1024.0 + (row + 1.0) * 32.0 + (col + 1.0), places < big_rows + small_rows


NT = (((1,), (1,)), ((), ()))
TAPS = 10
WHOLE = 2
HALF = (TAPS - WHOLE) // 2


def train_kernel(
    images, crop, w_point, w_spatial, norm_in, out_grad,
    features, in_grad, grads, totals_out, affine_out,
    W, wown, F, sv, gi, abuf, Gm, caq, stage, stage_a, Hb, dzq, dz1q, pgrad, precv, gout, yrecv,
    zs1, zrecv, gfin, sq_in, sq_own, sq_acc, psq, aff, gaff, gsend, st_in, st_own, st_all, cnt, cntx, cown,
    sL, sS_s, sS_r, sU_s, sU_r, sV_s, sV_r, sJ_s, sJ_r, sZ_s, sZ_r, sH_s, sH_r, sA_s, sA_r, sB_r, sD_r,
    sE_in_s, sE_in_r, sE_s, sE_r, sC_s, sC_r, sF_s, sF_r, sQ_s, sQ_r, sX_s, sX_r, sM_s, sM_r, sP_s, sP_r,
    sW_s, sW_r, sY_s, sY_r, sK_s, sK_r, sN_s, sN_r, sT_s, sT_r, sG_s, sG_r, sO_s, sO_r,
):
    s = lax.axis_index("section")
    bat = lax.axis_index("batch")
    z = bat // 2
    c = lax.rem(bat, 2)
    x = lax.rem(s, 2)
    y = s // 2
    R, D = abuf.shape
    h = F.at[pl.ds(0, R)]
    g = F.at[pl.ds(R, R)]
    zbuf = F.at[pl.ds(2 * R, R)]

    loads = [
        pltpu.make_async_copy(w_point.at[0], F.at[pl.ds(9 * 64, 64)], sL.at[0]),
        *[
            pltpu.make_async_copy(w_spatial.at[0, k], F.at[pl.ds(k * 64, 64)], sL.at[0])
            for k in range(9)
        ],
        pltpu.make_async_copy(images.at[s], abuf, sL.at[1]),
    ]
    for load in loads:
        load.start()

    barrier = pltpu.get_barrier_semaphore()
    greet = [(s, bat ^ j) for j in range(1, 8)]
    greet += [(s ^ d, bat ^ j) for d in range(1, 4) for j in range(2)]
    for sec, other in greet:
        pl.semaphore_signal(
            barrier, inc=1, device_id=(sec, other), device_id_type=pl.DeviceIdType.MESH
        )

    def square(rows):
        return jnp.sum(rows * rows, 0, keepdims=True)

    spatial_squares = jnp.zeros((1, D), jnp.float32)
    drain(F.at[pl.ds(0, 64 * TAPS)], sL.at[0])
    for k in range(TAPS):
        rows = F[k * 64 : k * 64 + 64]
        wown[k] = rows.astype(jnp.bfloat16).reshape(4, 16, D)
        if k < 9:
            spatial_squares += square(rows)
        else:
            point_squares = square(rows)
    sq_in[...] = jnp.zeros_like(sq_in)
    with jax.named_scope("greet"):
        pl.semaphore_wait(barrier, len(greet))

    cown[...] = jnp.full((8, 128), crop[0, s].astype(jnp.float32))
    aff[s] = jnp.concatenate([norm_in[0], jnp.zeros((4, D), jnp.float32)], axis=0)
    cnt[bat] = cown[...]
    cntx[c] = cown[...]
    for j in range(1, 8):
        swap_copy(cown, cnt.at[bat], sC_s, sC_r.at[0], s, bat ^ j).start()
    for j in range(2):
        for near in (1, 2):
            swap_copy(cown, cntx.at[2 * near + c], sC_s, sC_r.at[1], s ^ near, bat ^ j).start()
    for d in range(1, 4):
        swap_copy(aff.at[s], aff.at[s], sF_s, sF_r, s ^ d, bat).start()

    def scatter(d):
        q = s ^ d
        return swap_copy(
            wown.at[split, q], W.at[s, split, bat, q], sS_s, sS_r.at[s], q, 2 * z
        )

    def scatter_whole(d):
        return swap_copy(
            wown.at[whole], W.at[s, whole, bat], sU_s, sU_r.at[s], s ^ d, 2 * z
        )

    split, whole = pl.ds(0, 2 * HALF), pl.ds(2 * HALF, WHOLE)
    for send in (scatter, scatter_whole):
        for d in range(1, 4):
            send(d).start()

        @pl.when(c == 1)
        def _():
            send(0).start()

    @pl.when(c == 0)
    def _():
        pltpu.make_async_copy(wown.at[split, s], W.at[s, split, bat, s], sS_r.at[s]).start()
        pltpu.make_async_copy(wown.at[whole], W.at[s, whole, bat], sU_r.at[s]).start()

    @jax.named_scope("sums_start")
    def sums_start(e, first_sum, second_sum):
        slot = lax.rem(e, 2)
        st_own[e] = pack(first_sum, second_sum)
        to_core = swap_copy(st_own.at[e], st_in.at[e], sE_in_s.at[slot], sE_in_r.at[slot], s, bat ^ 1)

        if not isinstance(e, int):

            @pl.when(e > 1)
            def _():
                sums_close(e)

        @pl.when(c == 0)
        def _():
            to_core.start()

        @pl.when(c == 1)
        def _():
            to_core.wait_recv()
            st_all[e, z] = st_own[e] + st_in[e]
            for j in (7, 6, 5, 4, 3, 2, 1):
                swap_copy(
                    st_all.at[e, z], st_all.at[e, z], sE_s.at[slot], sE_r.at[slot], s, bat ^ j
                ).start()

    @jax.named_scope("sums_finish")
    def sums_finish(e):
        slot = lax.rem(e, 2)

        @pl.when(c == 0)
        def _():
            drain(st_all.at[e], sE_r.at[slot])

        @pl.when(c == 1)
        def _():
            drain(st_all.at[e, pl.ds(0, 3)], sE_r.at[slot])

        return unpack(st_all[e, 0] + st_all[e, 1] + st_all[e, 2] + st_all[e, 3])

    def sums_close(e):
        slot = lax.rem(e, 2)

        @pl.when(c == 0)
        def _():
            drain(st_own.at[0], sE_in_s.at[slot])

        @pl.when(c == 1)
        def _():
            drain(cnt.at[pl.ds(0, 7)], sE_s.at[slot])

    sums_start(0, point_squares, spatial_squares)

    half = pl.ds(HALF * c, HALF)
    first = jnp.where(c == 0, s ^ 1, s ^ 2)
    second = jnp.where(c == 0, s ^ 2, s ^ 1)
    both = s ^ 3

    def pair(b, taps, zz, q):
        return W.at[b, taps, pl.ds(2 * zz, 2), q]

    def to_sibling(b, zz):
        ref = pair(b, split, zz, s)
        return swap_copy(ref, ref, sH_s, sH_r.at[b, zz], s, bat ^ 1)

    def along_first(b, zz):
        ref = pair(b, half, zz, s)
        return swap_copy(ref, ref, sA_s, sA_r.at[b, zz], first, bat)

    def along_second(b, which, zz):
        ref = pair(b, half, zz, s if which == 0 else first)
        return swap_copy(ref, ref, sA_s, sB_r.at[b, which], second, bat)

    def quarter_to_sibling(b, which):
        ref = W.at[b, half, :, (first, second, both)[which]]
        return swap_copy(ref, ref, sA_s, sD_r.at[b], s, bat ^ 1)

    def own_ready(b, zz):
        @pl.when(c == 0)
        def _():
            to_sibling(b, zz).start()

        @pl.when(c == 1)
        def _():
            to_sibling(b, zz).wait_recv()

        along_first(b, zz).start()
        along_second(b, 0, zz).start()

    def along_z(b, zz, j):
        ref = pair(b, split, zz, s)
        return swap_copy(ref, ref, sZ_s, sZ_r.at[b, zz], s, bat ^ (2 * j))

    def whole_along_z(b, zz, j):
        ref = W.at[b, whole, pl.ds(2 * zz, 2)]
        return swap_copy(ref, ref, sV_s, sV_r.at[b, j - 1], s, bat ^ (2 * j))

    def whole_to_sibling(b, zz):
        ref = W.at[b, whole, pl.ds(2 * zz, 2)]
        return swap_copy(ref, ref, sJ_s, sJ_r.at[b], s, bat ^ 1)

    def on_first_core(work):
        pl.when(c == 0)(work)

    @jax.named_scope("own_quarter")
    def own_quarter(b):
        @on_first_core
        def _():
            drain(pair(b, split, z, s), sS_r.at[b])

        own_ready(b, z)

    @jax.named_scope("start_z")
    def start_z(b):
        @on_first_core
        def _():
            along_z(b, z, 2).start()
            along_z(b, z, 1).start()

    @jax.named_scope("start_whole")
    def start_whole(b):
        @on_first_core
        def _():
            drain(W.at[b, whole, pl.ds(2 * z, 2)], sU_r.at[b])
            whole_along_z(b, z, 2).start()
            whole_along_z(b, z, 1).start()
            whole_to_sibling(b, z).start()

    @jax.named_scope("relay_z")
    def relay_z(b):
        @on_first_core
        def _():
            drain(pair(b, split, z ^ 2, s), sZ_r.at[b, z ^ 2])
            along_z(b, z ^ 2, 1).start()

        own_ready(b, z ^ 2)

    @jax.named_scope("rest_z")
    def rest_z(b):
        for j in (1, 3):
            @on_first_core
            def _():
                drain(pair(b, split, z ^ j, s), sZ_r.at[b, z ^ j])

            own_ready(b, z ^ j)

    @jax.named_scope("relay_whole")
    def relay_whole(b):
        @on_first_core
        def _():
            drain(W.at[b, whole, pl.ds(2 * (z ^ 2), 2)], sV_r.at[b, 1])
            whole_along_z(b, z ^ 2, 1).start()
            whole_to_sibling(b, z ^ 2).start()

    @jax.named_scope("rest_whole")
    def rest_whole(b):
        @on_first_core
        def _():
            drain(W.at[b, whole, pl.ds(0, 4)], sV_r.at[b, 0])
            for j in (1, 3):
                whole_to_sibling(b, z ^ j).start()

    @jax.named_scope("gather_first")
    def gather_first(b):
        for j in range(4):
            zz = z ^ j
            ref = pair(b, half, zz, first)
            swap_copy(ref, ref, sA_s, sA_r.at[b, zz], first, bat).wait_recv()
            along_second(b, 1, zz).start()
        quarter_to_sibling(b, 0).start()

    @jax.named_scope("gather_second")
    def gather_second(b):
        for which in range(2):
            drain(W.at[b, half, :, (second, both)[which]], sB_r.at[b, which])
            quarter_to_sibling(b, 1 + which).start()

    @jax.named_scope("gather_last")
    def gather_last(b):
        other = pl.ds(HALF * (1 - c), HALF)
        drain(W.at[b, other, :, pl.ds(0, 3)], sD_r.at[b])

    for b in range(3):
        own_quarter(b)
        if b == 0:
            start_z(0)
    relay_z(0)
    start_whole(0)
    start_z(1)

    drain(cnt.at[pl.ds(0, 7)], sC_r.at[0])
    drain(cntx.at[pl.ds(2, 4)], sC_r.at[1])
    cntx[1 - c] = cnt[bat ^ 1]
    total = jnp.zeros((1, 1), jnp.float32)
    for j in range(8):
        big = cnt[j][0:1, 0:1]
        big_rows = big * float(BIG_SIDE * BIG_SIDE)
        area = float(SMALL_SIDE * SMALL_SIDE)
        total = total + big_rows + jnp.floor((R - big_rows + 0.5) / area) * area
    row_count = total
    down = lax.broadcasted_iota(jnp.int32, (R, 1), 0).astype(jnp.float32)
    across = lax.broadcasted_iota(jnp.int32, (1, R), 1).astype(jnp.float32)

    @pl.loop(0, 6)
    @jax.named_scope("tables")
    def _(v):
        big = cntx[v][0:1, 0:1]
        code_down, ok_down = crop_codes(down, big, R)
        code_across, ok_across = crop_codes(across, big, R)
        code_down = jnp.where(ok_down, code_down, -5000.0)
        code_across = jnp.where(ok_across, code_across, -1.0)
        for k in range(9):
            step = float(32 * (k // 3 - 1) + (k % 3 - 1))
            hit = (code_down + step) == code_across
            Gm[v, pl.ds(k * R, R)] = jnp.where(hit, 1.0, 0.0).astype(jnp.bfloat16)

    _, own_valid = crop_codes(down, cown[0:1, 0:1], R)
    valid = own_valid.astype(jnp.float32)
    drain(aff.at[pl.ds(0, 3)], sF_r)
    loads[10].wait()
    h[...] = abuf[...].astype(jnp.float32)

    def moments(sums):
        center = sums[0] / row_count
        spread = lax.rsqrt(sums[1] / row_count - center * center + EPS)
        return center, spread

    def pairing(b):
        odd = lax.rem(b, 2) == 1
        return jnp.where(odd, x, y), jnp.where(odd, y, x), jnp.where(odd, 1, 2)

    @jax.named_scope("share")
    def share(b, kind, rows):
        turned = rows.T
        rows_to = stage_a if kind == 1 else stage.at[b]
        if kind == 1:
            @pl.when(b > 0)
            def _():
                drain(stage_a.at[pl.ds(0, 2)], sQ_s.at[1])

        odd = lax.rem(b, 2) == 1
        for cc in range(2):
            for xx in range(2):
                for yy in range(2):
                    one, two = jnp.where(odd, xx, yy), jnp.where(odd, yy, xx)
                    for zz in range(4):
                        at = (2 * zz + cc) * 64 + (2 * yy + xx) * 16
                        rows_to[2 * one + cc, 4 * two + zz] = turned[at : at + 16].astype(
                            jnp.bfloat16
                        )
        if kind == 1:
            for half_of_pair in range(2):
                v = 2 * half_of_pair
                caq[b, 1, v + c] = stage_a[v + c]
                swap_copy(
                    stage_a.at[v + 1 - c], caq.at[b, 1, v + c], sQ_s.at[1], sQ_r.at[b, 1], s, bat ^ 1
                ).start()
        else:
            u = 2 * pairing(b)[0] + c
            caq[b, 0, u] = stage[b, u]

            @pl.when(b == 3)
            def _():
                send_share(b)

    def send_share(b):
        mine, _, near = pairing(b)
        u = 2 * mine + c
        for j in range(1, 4):
            swap_copy(
                stage.at[b, u ^ j], caq.at[b, 0, u], sQ_s.at[0], sQ_r.at[b, 0],
                s ^ near if j > 1 else s, bat ^ (j % 2),
            ).start()

    def wait_share(b, kind):
        drain(caq.at[b, kind, pl.ds(0, 2 if kind == 1 else 3)], sQ_r.at[b, kind])

    @jax.named_scope("forward")
    def forward(b):
        @pl.when(c == 1)
        def _():
            drain(W.at[b, whole], sJ_r.at[b])

        @pl.when(b == 3)
        def _():
            for early in (2, 1, 0):
                send_share(early)

        hidden = h[...]
        zbuf[...] = jnp.dot(
            hidden.astype(jnp.bfloat16), W[b, 9].reshape(D, D), preferred_element_type=jnp.float32
        )
        z1 = zbuf[...]
        kept = valid * z1
        sums_start(
            2 * b + 1, jnp.sum(kept, 0, keepdims=True), jnp.sum(kept * z1, 0, keepdims=True)
        )
        share(b, 1, hidden)

        @pl.when(b == 0)
        def _():
            relay_z(2)
            rest_z(1)

        @pl.when(b == 1)
        def _():
            relay_z(3)
            gather_first(2)
            relay_whole(2)
            start_whole(3)

        @pl.when(b == 2)
        def _():
            gather_first(3)
            relay_whole(3)

        gather_second(b)
        norms = aff[b]
        center, spread = moments(sums_finish(2 * b + 1))
        gi[b, 0:1] = norms[0:1] * spread
        for i in range(0, R, 64):
            xhat = (zbuf[i : i + 64] - center) * spread
            value, slope = mish_terms(norms[0:1] * xhat + norms[1:2])
            sv[b, 0, i : i + 64] = xhat.astype(sv.dtype)
            sv[b, 1, i : i + 64] = slope.astype(sv.dtype)
            abuf[i : i + 64] = value.astype(jnp.bfloat16)
        mixed = abuf[...]
        gather_last(b)
        for k in range(9):
            Hb[:, k * D : (k + 1) * D] = jnp.dot(
                Gm[c, pl.ds(k * R, R)], mixed, preferred_element_type=jnp.float32
            ).astype(jnp.bfloat16)
        zbuf[...] = jnp.dot(
            Hb[...], W[b, 0:9].reshape(9 * D, D), preferred_element_type=jnp.float32
        )
        z2 = zbuf[...]
        kept = valid * z2
        sums_start(
            2 * b + 2, jnp.sum(kept, 0, keepdims=True), jnp.sum(kept * z2, 0, keepdims=True)
        )
        share(b, 0, mixed.astype(jnp.float32))

        @pl.when(b == 0)
        def _():
            relay_whole(1)
            gather_first(1)
            own_quarter(3)
            start_z(3)

        @pl.when(b == 1)
        def _():
            rest_z(3)

        center, spread = moments(sums_finish(2 * b + 2))
        gi[b, 1:2] = norms[2:3] * spread
        for i in range(0, R, 64):
            xhat = (zbuf[i : i + 64] - center) * spread
            value, slope = mish_terms(norms[2:3] * xhat + norms[3:4])
            sv[b, 2, i : i + 64] = xhat.astype(sv.dtype)
            sv[b, 3, i : i + 64] = slope.astype(sv.dtype)
            h[i : i + 64] = h[i : i + 64] + valid[i : i + 64] * value

    rest_z(0)
    relay_whole(0)
    start_z(2)
    gather_first(0)
    relay_z(1)
    start_whole(1)
    rest_whole(0)
    psq[...] = jnp.concatenate(sums_finish(0), axis=0)

    @pl.loop(0, 4)
    def _(b):
        forward(b)

        @pl.when(b == 0)
        def _():
            rest_z(2)
            start_whole(2)

        @pl.when(b < 3)
        def _():
            rest_whole(b + 1)

    out_grad_rows = pltpu.make_async_copy(out_grad.at[s], abuf, sL.at[2])
    out_features = pltpu.make_async_copy(h, features.at[0], sO_s.at[0])
    out_features.start()
    out_grad_rows.start()
    out_grad_rows.wait()
    g[...] = abuf[...].astype(jnp.float32)

    @jax.named_scope("close_gather")
    def close_gather():
        drain(aff.at[pl.ds(0, 3)], sF_s)
        drain(st_own.at[pl.ds(0, 11)], sC_s)
        drain(stage_a.at[pl.ds(0, 2)], sQ_s.at[1])

        @pl.when(c == 0)
        def _():
            drain(wown.at[split, pl.ds(0, 3)], sS_s)
            drain(W.at[0, whole, pl.ds(0, 3)], sU_s)

        @pl.when(c == 1)
        def _():
            drain(wown.at[split], sS_s)
            drain(W.at[0, whole, pl.ds(0, 4)], sU_s)

        drain(W.at[:, split, :, pl.ds(0, 3)], sA_s)

        @on_first_core
        def _():
            drain(W.at[:, split, pl.ds(0, 6), s], sZ_s)
            drain(W.at[:, split, :, s], sH_s)
            drain(W.at[:, whole, pl.ds(0, 6)], sV_s)
            drain(W.at[:, whole], sJ_s)

    @jax.named_scope("close_rest")
    def close_rest():
        drain(stage.at[:, pl.ds(0, 3)], sQ_s.at[0])
        drain(dzq.at[:, pl.ds(0, 3)], sX_s)
        drain(dz1q.at[:, 0], sM_s)
        drain(precv, sP_s)
        drain(gsend.at[pl.ds(0, 3)], sO_s.at[3])
        drain(gout.at[:, 0], sY_s)

        @pl.when(c == 0)
        def _():
            drain(zrecv.at[:, pl.ds(0, 2)], sN_s)
            drain(zrecv.at[:, 2], sT_s)

        @pl.when(c == 1)
        def _():
            drain(zs1, sK_s)
            drain(zrecv.at[pl.ds(0, 3), pl.ds(0, 2)], sN_s)
            drain(zrecv.at[pl.ds(0, 3), 2], sT_s)

    CHUNKS = ((0, 3), (3, 3), (6, 3), (9, 1))
    LAST = len(CHUNKS) - 1

    def dz_copy(b, j):
        mine, _, near = pairing(b)
        v = 2 * mine + c
        v = v ^ 2 if j == 3 else v
        ref = dzq.at[b, v]
        return swap_copy(
            ref, ref, sX_s, sX_r.at[b, 0 if j == 2 else 1], s ^ near if j == 2 else s, bat if j == 2 else bat ^ 1
        )

    def send_dz(b):
        dz_copy(b, 2).start()
        dz_copy(b, 1).start()

    @jax.named_scope("forward_dz")
    def forward_dz(b):
        v = (2 * pairing(b)[0] + c) ^ 2
        drain(dzq.at[b, v], sX_r.at[b, 0])
        dz_copy(b, 3).start()

    @jax.named_scope("wait_dz")
    def wait_dz(b):
        drain(dzq.at[b, pl.ds(0, 2)], sX_r.at[b, 1])

    def dz_one_copy(b):
        ref = dz1q.at[b, c]
        return swap_copy(ref, ref, sM_s, sM_r.at[b], s, bat ^ 1)

    def point_copy(b):
        mine, _, near = pairing(b)
        return swap_copy(
            pgrad.at[b, 1 - mine], precv.at[b], sP_s, sP_r.at[b], s ^ near, bat
        )

    def y_copy(b, i):
        at, size = CHUNKS[i]
        return swap_copy(
            gout.at[b, 1 - pairing(b)[1], pl.ds(at, size)], yrecv.at[b, pl.ds(at, size)],
            sY_s, sY_r.at[b, i], s ^ 3 ^ pairing(b)[2], bat,
        )

    def grad_tap(b, k, left, right):
        part = jnp.dot(left, right, preferred_element_type=jnp.float32).astype(jnp.bfloat16)
        for yy in range(2):
            gout[b, yy, k] = part[64 * yy : 64 * yy + 64].reshape(4, 16, D)

    @jax.named_scope("grad_spatial")
    def grad_spatial(b):
        wait_share(b, 0)
        wait_dz(b)
        mine, _, near = pairing(b)
        tables = [jnp.where(mine == v // 2, 0, 2 * near) + v % 2 for v in range(4)]
        right = dzq[b].reshape(4 * R, D)
        for k in range(9):
            left = [
                lax.dot_general(
                    caq[b, 0, v].reshape(128, R), Gm[tables[v], pl.ds(k * R, R)], NT,
                    preferred_element_type=jnp.float32,
                ).astype(jnp.bfloat16)
                for v in range(4)
            ]
            grad_tap(b, k, jnp.concatenate(left, axis=1), right)
            if k % 3 == 2:
                y_copy(b, k // 3).start()

    @jax.named_scope("grad_point")
    def grad_point(b):
        wait_share(b, 1)
        drain(dz1q.at[b, 1 - c], sM_r.at[b])
        left = jnp.concatenate(
            [
                jnp.concatenate([caq[b, 1, 2 * v + k].reshape(128, R) for v in range(2)], axis=0)
                for k in range(2)
            ],
            axis=1,
        )
        part = jnp.dot(
            left, dz1q[b].reshape(2 * R, D), preferred_element_type=jnp.float32
        ).astype(jnp.bfloat16)
        pgrad[b] = part.reshape(2, 2, 4, 16, D)
        point_copy(b).start()

    @jax.named_scope("pair_point")
    def pair_point(b):
        point_copy(b).wait_recv()
        mine = pairing(b)[0]
        for yy in range(2):
            gout[b, yy, 9] = (
                pgrad[b, mine, yy].astype(jnp.float32) + precv[b, yy].astype(jnp.float32)
            ).astype(jnp.bfloat16)
        y_copy(b, LAST).start()

    def core_copy(b, i):
        at, size = CHUNKS[i]
        return swap_copy(
            yrecv.at[b, pl.ds(at, size)], zs1.at[pl.ds(at, size)],
            sK_s, sK_r.at[i], s, bat ^ 1,
        )

    @jax.named_scope("reduce_plane")
    def reduce_plane(b, i):
        at, size = CHUNKS[i]
        y_copy(b, i).wait_recv()
        rest = pairing(b)[1]
        for k in range(at, at + size):
            yrecv[b, k] = (
                yrecv[b, k].astype(jnp.float32) + gout[b, rest, k].astype(jnp.float32)
            ).astype(jnp.bfloat16)

        if b == 3:

            @pl.when(c == 1)
            def _():
                core_copy(b, i).start()

    def carriers(b, work):
        if b == 3:
            pl.when(c == 0)(functools.partial(work, (0, 1)))
        else:
            work((0,))

    def z_near(b, i, cc, slot):
        at, size = CHUNKS[i]
        return swap_copy(
            (yrecv.at[b], zs1)[cc].at[pl.ds(at, size), z ^ (3 if slot else 1)],
            zrecv.at[b + cc, slot, pl.ds(at, size)], sN_s, sN_r.at[b, i], s, bat ^ 2,
        )

    def z_far(b, i, cc):
        at, size = CHUNKS[i]
        return swap_copy(
            zrecv.at[b + cc, 1, pl.ds(at, size)], zrecv.at[b + cc, 2, pl.ds(at, size)],
            sT_s, sT_r.at[b, i], s, bat ^ 4,
        )

    def near_like(b, i, parts):
        at, size = CHUNKS[i]
        return zrecv.at[pl.ds(b, len(parts)), pl.ds(0, 2), pl.ds(at, size)]

    def far_like(b, i, parts):
        at, size = CHUNKS[i]
        return zrecv.at[pl.ds(b, len(parts)), 2, pl.ds(at, size)]

    @jax.named_scope("reduce_near")
    def reduce_near(b, i):
        def work(parts):
            if b == 3:
                core_copy(b, i).wait_recv()
            for slot in (1, 0):
                for cc in parts:
                    z_near(b, i, cc, slot).start()

        carriers(b, work)

    @jax.named_scope("reduce_far")
    def reduce_far(b, i):
        at, size = CHUNKS[i]

        def work(parts):
            drain(near_like(b, i, parts), sN_r.at[b, i])
            for cc in parts:
                mine = (yrecv.at[b], zs1)[cc]
                for k in range(at, at + size):
                    zrecv[b + cc, 1, k] = (
                        zrecv[b + cc, 1, k].astype(jnp.float32) + mine[k, z ^ 2].astype(jnp.float32)
                    ).astype(jnp.bfloat16)
                z_far(b, i, cc).start()

        carriers(b, work)

    def deliver(b, i, cc, section, core):
        at, size = CHUNKS[i]
        swap_copy(
            zrecv.at[b + cc, 0, pl.ds(at, size)], gfin.at[pl.ds(at, size), s],
            sG_s, sG_r.at[s], section, 2 * z + core,
        ).start()

    def send_squares(b):
        def to(j):
            return swap_copy(
                sq_own.at[b], sq_in.at[s, bat], sW_s, sW_r, b, bat ^ j
            )

        sq_own[b] = pack(sq_acc[b, 1:2], sq_acc[b, 0:1])

        @pl.when(b != s)
        def _():
            to(0).start()

        @pl.when(b == s)
        def _():
            sq_in[s, bat] = sq_own[b]

        for j in range(1, 8):
            to(j).start()

    @jax.named_scope("finish")
    def finish(b, i):
        at, size = CHUNKS[i]

        def work(parts):
            drain(far_like(b, i, parts), sT_r.at[b, i])
            squares = jnp.zeros((1, D), jnp.float32)
            for cc in parts:
                mine = (yrecv.at[b], zs1)[cc]
                for k in range(at, at + size):
                    done = (
                        zrecv[b + cc, 0, k].astype(jnp.float32)
                        + zrecv[b + cc, 2, k].astype(jnp.float32)
                        + mine[k, z].astype(jnp.float32)
                    ).astype(jnp.bfloat16)
                    zrecv[b + cc, 0, k] = done
                    squares += square(done.astype(jnp.float32))

                @pl.when(b != s)
                def _():
                    deliver(b, i, cc, b, cc if b == 3 else c)

                @pl.when(b == s)
                def _():
                    if cc == 0:
                        for k in range(at, at + size):
                            gfin[k, s] = zrecv[b, 0, k]
                    else:
                        deliver(b, i, 1, s, 1)

            row = 1 if i == LAST else 0
            sq_acc[b, row : row + 1] = squares + (0.0 if i in (0, LAST) else sq_acc[b, row : row + 1])
            if i == LAST:
                send_squares(b)

        carriers(b, work)

    @jax.named_scope("backward")
    def backward(bi):
        b = 3 - bi
        e = 9 + 2 * bi
        u = 2 * pairing(b)[0] + c
        first_sum = jnp.zeros((1, D), jnp.float32)
        second_sum = jnp.zeros((1, D), jnp.float32)
        for i in range(0, R, 64):
            du = valid[i : i + 64] * g[i : i + 64] * sv[b, 3, i : i + 64].astype(jnp.float32)
            zbuf[i : i + 64] = du
            first_sum += jnp.sum(du, 0, keepdims=True)
            second_sum += jnp.sum(du * sv[b, 2, i : i + 64].astype(jnp.float32), 0, keepdims=True)
        sums_start(e, first_sum, second_sum)

        @pl.when(bi == 0)
        def _():
            close_gather()

        @pl.when(bi == 3)
        def _():
            reduce_near(3, 1)

        @pl.when(bi > 0)
        def _():
            forward_dz(b + 1)
            grad_point(b + 1)

        @pl.when(bi == 2)
        def _():
            pair_point(3)

        @pl.when(bi == 3)
        def _():
            reduce_plane(3, 2)
            reduce_far(3, 0)

        total_first, total_second = sums_finish(e)
        for i in range(0, R, 64):
            xhat = sv[b, 2, i : i + 64].astype(jnp.float32)
            inner = zbuf[i : i + 64] - valid[i : i + 64] * (
                (total_first + xhat * total_second) / row_count
            )
            dzq[b, u, i : i + 64] = (gi[b, 1:2] * inner).astype(jnp.bfloat16)
        send_dz(b)
        gsend[b, 2:3] = total_second
        gsend[b, 3:4] = total_first
        d_two = dzq[b, u]
        for k in range(9):
            Hb[:, k * D : (k + 1) * D] = jnp.dot(
                Gm[c, pl.ds((8 - k) * R, R)], d_two, preferred_element_type=jnp.float32
            ).astype(jnp.bfloat16)
        mixed = None
        for k in range(9):
            part = lax.dot_general(
                Hb[:, k * D : (k + 1) * D], W[b, k].reshape(D, D), NT,
                preferred_element_type=jnp.float32,
            )
            mixed = part if mixed is None else mixed + part
        zbuf[...] = mixed
        first_sum = jnp.zeros((1, D), jnp.float32)
        second_sum = jnp.zeros((1, D), jnp.float32)
        for i in range(0, R, 64):
            du = zbuf[i : i + 64] * sv[b, 1, i : i + 64].astype(jnp.float32)
            zbuf[i : i + 64] = du
            first_sum += jnp.sum(du, 0, keepdims=True)
            second_sum += jnp.sum(du * sv[b, 0, i : i + 64].astype(jnp.float32), 0, keepdims=True)
        sums_start(e + 1, first_sum, second_sum)

        @pl.when(bi == 2)
        def _():
            reduce_plane(3, 0)
            reduce_near(3, 0)

        @pl.when(bi == 3)
        def _():
            reduce_near(3, 2)
            reduce_far(3, 1)
            reduce_plane(2, 0)
            reduce_near(2, 0)

        @pl.when(bi > 0)
        def _():
            grad_spatial(b + 1)

        @pl.when(bi == 2)
        def _():
            reduce_plane(3, 1)

        @pl.when(bi == 3)
        def _():
            reduce_plane(3, 3)
            reduce_plane(2, 1)
            reduce_near(2, 1)

        total_first, total_second = sums_finish(e + 1)
        for i in range(0, R, 64):
            xhat = sv[b, 0, i : i + 64].astype(jnp.float32)
            inner = zbuf[i : i + 64] - valid[i : i + 64] * (
                (total_first + xhat * total_second) / row_count
            )
            dz1q[b, c, i : i + 64] = (gi[b, 0:1] * inner).astype(jnp.bfloat16)
        dz_one_copy(b).start()
        gsend[b, 0:1] = total_second
        gsend[b, 1:2] = total_first
        g[...] = g[...] + lax.dot_general(
            dz1q[b, c], W[b, 9].reshape(D, D), NT, preferred_element_type=jnp.float32
        )

        @pl.when(b == s)
        def _():
            gaff[s] = gsend[b]

        @pl.when(b != s)
        def _():
            swap_copy(gsend.at[b], gaff.at[s], sO_s.at[3], sO_r, b, bat).start()

    @pl.loop(0, 4)
    def _(bi):
        backward(bi)

    out_grad_in = pltpu.make_async_copy(g, in_grad.at[0], sO_s.at[1])
    out_grad_in.start()

    reduce_near(3, 3)
    forward_dz(0)
    pair_point(2)
    reduce_far(2, 0)
    reduce_far(3, 2)
    reduce_plane(2, 2)
    reduce_near(2, 2)
    grad_spatial(0)
    reduce_far(2, 1)
    grad_point(0)
    reduce_far(3, 3)
    pair_point(1)
    finish(3, 0)
    reduce_plane(2, 3)
    reduce_near(2, 3)
    reduce_plane(1, 0)
    reduce_near(1, 0)
    finish(3, 1)
    reduce_far(2, 2)
    finish(2, 0)
    reduce_plane(1, 1)
    reduce_near(1, 1)
    finish(3, 2)
    reduce_far(1, 0)
    reduce_plane(1, 2)
    reduce_near(1, 2)
    finish(3, 3)
    finish(2, 1)
    pair_point(0)
    reduce_far(2, 3)
    reduce_plane(0, 0)
    reduce_near(0, 0)
    reduce_far(1, 1)
    reduce_plane(1, 3)
    reduce_near(1, 3)
    finish(2, 2)
    finish(1, 0)
    reduce_far(1, 2)
    reduce_plane(0, 1)
    reduce_near(0, 1)
    reduce_plane(0, 2)
    reduce_near(0, 2)
    reduce_plane(0, 3)
    reduce_near(0, 3)
    reduce_far(0, 0)
    finish(2, 3)
    finish(1, 1)
    reduce_far(1, 3)
    reduce_far(0, 1)
    finish(1, 2)
    finish(1, 3)
    finish(0, 0)
    reduce_far(0, 2)
    reduce_far(0, 3)
    finish(0, 1)
    close_rest()
    finish(0, 2)
    finish(0, 3)
    for d in range(1, 4):
        drain(gfin.at[:, s ^ d], sG_r.at[s ^ d])

    @pl.when((c == 1) & (s == 3))
    def _():
        drain(gfin.at[:, s], sG_r.at[s])

    grads_out = pltpu.make_async_copy(gfin, grads, sO_s.at[2])
    grads_out.start()

    drain(gaff.at[pl.ds(0, 3)], sO_r)
    affine_out[...] = gaff[0] + gaff[1] + gaff[2] + gaff[3]
    squares_in = sq_in.reshape(32, 8, 128)

    @pl.when(s != 3)
    def _():
        drain(squares_in.at[pl.ds(0, 31)], sW_r)

    @pl.when((s == 3) & (c == 0))
    def _():
        drain(squares_in.at[pl.ds(0, 15)], sW_r)

    @pl.when((s == 3) & (c == 1))
    def _():
        drain(squares_in.at[pl.ds(0, 16)], sW_r)

    gpoint_squares, gspatial_squares = unpack(jnp.sum(squares_in[...], axis=0))
    totals_out[...] = jnp.concatenate(
        [psq[...], gpoint_squares, gspatial_squares, jnp.zeros((4, D), jnp.float32)], axis=0
    )

    with jax.named_scope("close_last"):
        sums_close(0)
        sums_close(1)

        @pl.when(c == 0)
        def _():
            drain(zrecv.at[pl.ds(0, 4), 0], sG_s)

        @pl.when(c == 0)
        def _():
            drain(squares_in.at[pl.ds(0, 31)], sW_s)

        @pl.when((c == 1) & (s == 3))
        def _():
            drain(zrecv.at[pl.ds(0, 3), 0], sG_s)
            drain(squares_in.at[pl.ds(0, 24)], sW_s)

        @pl.when((c == 1) & (s != 3))
        def _():
            drain(zrecv.at[pl.ds(0, 2), 0], sG_s)
            drain(squares_in.at[pl.ds(0, 23)], sW_s)

    with jax.named_scope("close_outputs"):
        grads_out.wait()
        out_features.wait()
        out_grad_in.wait()


def lars_kernel(
    feat, ing, grads_in, totals_in, affine_in, w_point, w_spatial, norm_in, mom_point, mom_spatial, mom_norm,
    features, in_grad, new_point, new_spatial, new_norm, new_mom_point, new_mom_spatial, new_mom_norm,
    P, M, G, feat_rows, grad_rows, totals, affine_grad, affine, affine_mom, sem, out_sem,
):
    THIRDS = 3
    small = [
        (totals_in, totals), (affine_in, affine_grad), (norm_in.at[0], affine), (mom_norm.at[0], affine_mom),
        (w_point.at[0], P.at[9]), (mom_point.at[0], M.at[9]), (grads_in.at[9], G.at[9]),
    ]
    large = []
    for i in range(THIRDS):
        taps = pl.ds(3 * i, 3)
        large += [
            (grads_in.at[taps], G.at[taps]), (w_spatial.at[0, taps], P.at[taps]),
            (mom_spatial.at[0, taps], M.at[taps]),
        ]
    rows = [(feat, feat_rows), (ing, grad_rows)]
    loads = [
        pltpu.make_async_copy(a, b, sem.at[i]) for i, (a, b) in enumerate(small + large + rows)
    ]
    for load in loads:
        load.start()
    for load in loads[: len(small)]:
        load.wait()
    D = affine.shape[1]
    rate = BASE_RATE * (STEP + 1) / WARMUP
    point_sq, spatial_sq, gpoint_sq, gspatial_sq = [
        jnp.sum(totals[i : i + 1], axis=1, keepdims=True) for i in range(4)
    ]
    step_point = rate * TRUST_COEF * jnp.sqrt(point_sq) / (jnp.sqrt(gpoint_sq) + EPS_NORM)
    step_spatial = rate * TRUST_COEF * jnp.sqrt(spatial_sq) / (jnp.sqrt(gspatial_sq) + EPS_NORM)
    outs = []

    def store(source, target):
        outs.append(pltpu.make_async_copy(source, target, out_sem.at[len(outs)]))
        outs[-1].start()

    def move(k, step):
        moved = MOMENTUM * M[k] + step * G[k].astype(jnp.float32).reshape(64, D)
        M[k] = moved
        P[k] = P[k] - moved

    for i in range(THIRDS):
        for load in loads[len(small) + 3 * i :][:3]:
            load.wait()
        for k in range(3 * i, 3 * i + 3):
            move(k, step_spatial)
        taps = pl.ds(3 * i, 3)
        store(M.at[taps], new_mom_spatial.at[0, taps])
        store(P.at[taps], new_spatial.at[0, taps])
    move(9, step_point)
    store(M.at[9], new_mom_point.at[0])
    store(P.at[9], new_point.at[0])
    for load, source, target in zip(loads[-2:], (feat_rows, grad_rows), (features, in_grad)):
        load.wait()
        store(source, target)
    grad = affine_grad[0:4]
    old = affine[...]
    affine_sq = jnp.sum(old * old, axis=1, keepdims=True)
    gaffine_sq = jnp.sum(grad * grad, axis=1, keepdims=True)
    trust = TRUST_COEF * jnp.sqrt(affine_sq) / (jnp.sqrt(gaffine_sq) + EPS_NORM)
    moved = MOMENTUM * affine_mom[...] + rate * trust * grad
    affine_mom[...] = moved
    affine[...] = old - moved
    store(affine_mom, new_mom_norm.at[0])
    store(affine, new_norm.at[0])
    for copy in outs:
        copy.wait()


def train_step(images, crop, w_point, w_spatial, norm_params, mom_point, mom_spatial, mom_norm, out_grad):
    R, D = images.shape[1:]
    f32, bf16 = jnp.float32, jnp.bfloat16
    dma = pltpu.SemaphoreType.DMA
    anywhere = pl.BlockSpec(memory_space=pl.ANY)
    vmem = pl.BlockSpec(memory_space=pltpu.VMEM)
    hbm = pl.BlockSpec(memory_space=pltpu.HBM)
    smem = pl.BlockSpec(memory_space=pltpu.SMEM)
    V = pltpu.VMEM
    scratch = dict(
        W=V((4, TAPS, 8, 4, 16, D), bf16), wown=V((TAPS, 4, 16, D), bf16),
        F=V((3 * R, D), f32),
        sv=V((4, 4, R, D), bf16), gi=V((4, 8, D), f32),
        abuf=V((R, D), bf16),
        Gm=V((6, 9 * R, R), bf16), caq=V((4, 2, 4, 8, 16, R), bf16),
        stage=V((4, 4, 8, 16, R), bf16), stage_a=V((4, 8, 16, R), bf16), Hb=V((R, 9 * D), bf16),
        dzq=V((4, 4, R, D), bf16), dz1q=V((4, 2, R, D), bf16),
        pgrad=V((4, 2, 2, 4, 16, D), bf16), precv=V((4, 2, 4, 16, D), bf16),
        gout=V((4, 2, TAPS, 4, 16, D), bf16), yrecv=V((4, TAPS, 4, 16, D), bf16),
        zs1=V((TAPS, 4, 16, D), bf16), zrecv=V((5, 3, TAPS, 16, D), bf16),
        gfin=V((TAPS, 4, 16, D), bf16),
        sq_in=V((4, 8, 8, 128), f32), sq_own=V((4, 8, 128), f32), sq_acc=V((4, 8, D), f32), psq=V((2, D), f32),
        aff=V((4, 8, D), f32), gaff=V((4, 8, D), f32), gsend=V((4, 8, D), f32),
        st_in=V((17, 8, 128), f32), st_own=V((17, 8, 128), f32), st_all=V((17, 4, 8, 128), f32),
        cnt=V((8, 8, 128), f32), cntx=V((6, 8, 128), f32), cown=V((8, 128), f32),
        sL=dma((3,)), sS_s=dma, sS_r=dma((4,)), sU_s=dma, sU_r=dma((4,)), sV_s=dma, sV_r=dma((4, 2)),
        sJ_s=dma, sJ_r=dma((4,)), sZ_s=dma, sZ_r=dma((4, 4)),
        sH_s=dma, sH_r=dma((4, 4)), sA_s=dma, sA_r=dma((4, 4)),
        sB_r=dma((4, 2)), sD_r=dma((4,)),
        sE_in_s=dma((2,)), sE_in_r=dma((2,)), sE_s=dma((2,)), sE_r=dma((2,)),
        sC_s=dma, sC_r=dma((2,)), sF_s=dma, sF_r=dma,
        sQ_s=dma((2,)), sQ_r=dma((4, 2)), sX_s=dma, sX_r=dma((4, 2)), sM_s=dma, sM_r=dma((4,)), sP_s=dma, sP_r=dma((4,)),
        sW_s=dma, sW_r=dma,
        sY_s=dma, sY_r=dma((4, 4)), sK_s=dma, sK_r=dma((4,)),
        sN_s=dma, sN_r=dma((4, 4)), sT_s=dma, sT_r=dma((4, 4)), sG_s=dma, sG_r=dma((4,)),
        sO_s=dma((4,)), sO_r=dma,
    )
    shape = jax.ShapeDtypeStruct
    feat, ing, grads, totals, affine_grad = pl.pallas_call(
        train_kernel,
        out_shape=(
            shape((1, R, D), f32), shape((1, R, D), f32), shape((TAPS, 4, 16, D), bf16),
            shape((8, D), f32), shape((8, D), f32),
        ),
        in_specs=[anywhere, smem, anywhere, anywhere, vmem, anywhere],
        out_specs=(anywhere, anywhere, anywhere, vmem, vmem),
        scratch_shapes=list(scratch.values()),
        compiler_params=pltpu.CompilerParams(
            collective_id=0, has_side_effects=True, vmem_limit_bytes=64 * 1024 * 1024
        ),
    )(images, crop.T, w_point, w_spatial, norm_params, out_grad)
    return pl.pallas_call(
        lars_kernel,
        out_shape=(
            shape((1, R, D), f32), shape((1, R, D), f32),
            shape(w_point.shape, f32), shape(w_spatial.shape, f32), shape(norm_params.shape, f32),
            shape(w_point.shape, f32), shape(w_spatial.shape, f32), shape(norm_params.shape, f32),
        ),
        in_specs=[hbm] * 11,
        out_specs=(hbm,) * 8,
        scratch_shapes=[
            V((TAPS, 64, D), f32), V((TAPS, 64, D), f32), V((TAPS, 4, 16, D), bf16), V((1, R, D), f32),
            V((1, R, D), f32), V((8, D), f32), V((8, D), f32), V((4, D), f32), V((4, D), f32), dma((18,)), dma((12,)),
        ],
        compiler_params=pltpu.CompilerParams(vmem_limit_bytes=64 * 1024 * 1024),
    )(feat, ing, grads, totals, affine_grad, w_point, w_spatial, norm_params, mom_point, mom_spatial, mom_norm)


def solution(mesh):
    tuned = mesh.shape["section"] == 4 and mesh.shape["batch"] == 8
    return jax.shard_map(
        train_step if tuned else on_device,
        mesh=mesh,
        in_specs=(
            P(None, "batch", None),
            P(None, "batch"),
            P("section", "batch", None),
            P("section", None, "batch", None),
            P("section", None, None),
            P("section", "batch", None),
            P("section", None, "batch", None),
            P("section", None, None),
            P(None, "batch", None),
        ),
        out_specs=(
            P("section", "batch", None),
            P("section", "batch", None),
            P("section", "batch", None),
            P("section", None, "batch", None),
            P("section", None, None),
            P("section", "batch", None),
            P("section", None, "batch", None),
            P("section", None, None),
        ),
        check_vma=False,
    )
```

```python
import functools

import jax
import jax.numpy as jnp
from jax import lax
from jax.experimental import pallas as pl
from jax.experimental.pallas import tpu as pltpu
from jax.sharding import PartitionSpec as P

BIG_SIDE = 7
SMALL_SIDE = 3
WARMUP = 20
STEP = 9


EPS = 1e-05
EPS_NORM = 1e-06
BASE_RATE = 6.0
MOMENTUM = 0.9
TRUST_COEF = 0.1


def from_behind(block, axis, distance):
    devices = range(lax.axis_size(axis))
    route = [(i - distance, i) for i in devices if i - distance in devices]
    return lax.ppermute(block, axis, route)


def crop_table(big_count, total_rows):
    places = jnp.arange(total_rows, dtype=jnp.int32)
    big_area = BIG_SIDE * BIG_SIDE
    small_area = SMALL_SIDE * SMALL_SIDE
    big_rows = big_count * big_area
    small_rows = (total_rows - big_rows) // small_area * small_area
    in_big = places < big_rows
    offsets = places - big_rows
    sides = jnp.where(in_big, BIG_SIDE, SMALL_SIDE)
    within = jnp.where(in_big, places % big_area, offsets % small_area)
    starts = places - within
    valid_rows = places < big_rows + small_rows
    row_pos = within // sides
    col_pos = within % sides
    indices = []
    masks = []
    for row_step in (-1, 0, 1):
        for col_step in (-1, 0, 1):
            new_row = row_pos + row_step
            new_col = col_pos + col_step
            inside = (
                valid_rows & (new_row >= 0) & (new_row < sides) & (new_col >= 0) & (new_col < sides)
            )
            indices.append(jnp.where(inside, starts + new_row * sides + new_col, places))
            masks.append(inside)
    return (
        jnp.stack(indices, 1),
        jnp.stack(masks, 1).astype(jnp.float32),
        valid_rows.astype(jnp.float32),
    )


def mish(values):
    return values * jnp.tanh(jax.nn.softplus(values))


def mish_parts(values):
    tangent = jnp.tanh(jax.nn.softplus(values))
    slope = tangent + values * jax.nn.sigmoid(values) * (1.0 - tangent * tangent)
    return (values * tangent, slope)


def mish_slope(values):
    tangent = jnp.tanh(jax.nn.softplus(values))
    return tangent + values * jax.nn.sigmoid(values) * (1.0 - tangent * tangent)


def batch_moments(proj, valid_rows):
    weighted = valid_rows[:, None] * proj
    summed, squared, row_count = lax.psum(
        (jnp.sum(weighted, 0), jnp.sum(weighted * proj, 0), jnp.sum(valid_rows)), "batch"
    )
    center = summed / row_count
    inv_std = lax.rsqrt(squared / row_count - center * center + EPS)
    return (center, inv_std, row_count)


def spatial_apply(source, tap_index, tap_mask, weights):
    stacked = source[tap_index] * tap_mask[:, :, None].astype(source.dtype)
    result = lax.dot_general(
        stacked, weights, (((1, 2), (0, 1)), ((), ())), preferred_element_type=jnp.float32
    )
    return (result, stacked)


def forward_block(hidden, point_low, spatial_low, affine, tap_index, tap_mask, valid_rows):
    proj_one = jnp.dot(hidden.astype(jnp.bfloat16), point_low, preferred_element_type=jnp.float32)
    center_one, inv_one, row_count = batch_moments(proj_one, valid_rows)
    mixed_one = mish(affine[0] * ((proj_one - center_one) * inv_one) + affine[1])
    proj_two, stacked = spatial_apply(
        mixed_one.astype(jnp.bfloat16), tap_index, tap_mask, spatial_low
    )
    center_two, inv_two, count_two = batch_moments(proj_two, valid_rows)
    mixed_two = mish(affine[2] * ((proj_two - center_two) * inv_two) + affine[3])
    moments = jnp.stack([center_one, inv_one, center_two, inv_two])
    return (hidden + valid_rows[:, None] * mixed_two, moments, row_count)


def norm_back(d_value, normed, inv_std, gain, valid_rows, row_count):
    first_sum, second_sum = lax.psum((jnp.sum(d_value, 0), jnp.sum(d_value * normed, 0)), "batch")
    d_proj = (
        gain
        * inv_std
        * (d_value - valid_rows[:, None] * (first_sum + normed * second_sum) / row_count)
    )
    return (d_proj.astype(jnp.bfloat16), first_sum, second_sum)


def backward_block(
    hidden,
    upstream,
    point_low,
    spatial_low,
    affine,
    moments,
    row_count,
    tap_index,
    tap_mask,
    valid_rows,
):
    inputs = hidden.astype(jnp.bfloat16)
    proj_one = jnp.dot(inputs, point_low, preferred_element_type=jnp.float32)
    normed_one = (proj_one - moments[0]) * moments[1]
    mixed_one, slope_one = mish_parts(affine[0] * normed_one + affine[1])
    proj_two, stacked = spatial_apply(
        mixed_one.astype(jnp.bfloat16), tap_index, tap_mask, spatial_low
    )
    normed_two = (proj_two - moments[2]) * moments[3]
    slope_two = mish_slope(affine[2] * normed_two + affine[3])
    d_two, first_two, second_two = norm_back(
        valid_rows[:, None] * upstream * slope_two,
        normed_two,
        moments[3],
        affine[2],
        valid_rows,
        row_count,
    )
    grad_spatial = lax.dot_general(
        stacked, d_two, (((0,), (0,)), ((), ())), preferred_element_type=jnp.float32
    )
    flipped = d_two[tap_index[:, ::-1]] * tap_mask[:, ::-1, None].astype(jnp.bfloat16)
    d_mixed = lax.dot_general(
        flipped, spatial_low, (((1, 2), (0, 2)), ((), ())), preferred_element_type=jnp.float32
    )
    d_one, first_one, second_one = norm_back(
        d_mixed * slope_one, normed_one, moments[1], affine[0], valid_rows, row_count
    )
    grad_point = lax.dot_general(
        inputs, d_one, (((0,), (0,)), ((), ())), preferred_element_type=jnp.float32
    )
    d_hidden = upstream + lax.dot_general(
        d_one, point_low, (((1,), (1,)), ((), ())), preferred_element_type=jnp.float32
    )
    grad_affine = jnp.stack([second_one, first_one, second_two, first_two])
    return (d_hidden, grad_point, grad_spatial, grad_affine)


def store_slot(buffer, value, slot_index, active):
    previous = lax.dynamic_index_in_dim(buffer, slot_index, 0, keepdims=False)
    return lax.dynamic_update_index_in_dim(
        buffer, jnp.where(active, value, previous), slot_index, 0
    )


def lars_update(param, grad, momentum, param_sq, grad_sq, rate):
    trust = TRUST_COEF * jnp.sqrt(param_sq) / (jnp.sqrt(grad_sq) + EPS_NORM)
    new_mom = MOMENTUM * momentum + rate * trust * grad
    return (param - new_mom, new_mom)


def on_device(
    images, crop_big, w_point, w_spatial, norm_params, mom_point, mom_spatial, mom_norm, out_grad
):
    section_count = lax.axis_size("section")
    section_rank = lax.axis_index("section")
    micro_count = images.shape[0]
    total_rows = images.shape[1]
    width = images.shape[2]
    point = w_point[0]
    spatial = w_spatial[0]
    affine = norm_params[0]
    crop_counts = crop_big[:, 0]
    turns = micro_count + section_count - 1
    point_low, spatial_low = (
        lax.all_gather(point.astype(jnp.bfloat16), "batch", axis=0, tiled=True),
        lax.all_gather(spatial.astype(jnp.bfloat16), "batch", axis=1, tiled=True),
    )
    kept_inputs = jnp.zeros((micro_count, total_rows, width), jnp.float32)
    kept_moments = jnp.zeros((micro_count, 4, width), jnp.float32)
    kept_counts = jnp.zeros((micro_count,), jnp.float32)
    results = jnp.zeros((micro_count, total_rows, width), jnp.float32)
    incoming = jnp.zeros((total_rows, width), jnp.float32)
    for phase_turn in range(turns):
        slot_raw = phase_turn - section_rank
        active = (slot_raw >= 0) & (slot_raw < micro_count)
        slot_index = jnp.clip(slot_raw, 0, micro_count - 1)
        fresh_rows = lax.dynamic_index_in_dim(images, slot_index, 0, keepdims=False).astype(
            jnp.float32
        )
        hidden = jnp.where(section_rank == 0, fresh_rows, incoming)
        tap_index, tap_mask, valid_rows = crop_table(crop_counts[slot_index], total_rows)
        output, moments, row_count = forward_block(
            hidden, point_low, spatial_low, affine, tap_index, tap_mask, valid_rows
        )
        kept_inputs = store_slot(kept_inputs, hidden, slot_index, active)
        kept_moments = store_slot(kept_moments, moments, slot_index, active)
        kept_counts = store_slot(kept_counts, row_count, slot_index, active)
        results = store_slot(
            results, output, slot_index, active & (section_rank == section_count - 1)
        )
        if phase_turn + 1 < turns:
            incoming = from_behind(output.astype(jnp.bfloat16), "section", 1).astype(output.dtype)
    point_low, spatial_low = (
        lax.all_gather(point.astype(jnp.bfloat16), "batch", axis=0, tiled=True),
        lax.all_gather(spatial.astype(jnp.bfloat16), "batch", axis=1, tiled=True),
    )
    grad_point = jnp.zeros((width, width), jnp.float32)
    grad_spatial = jnp.zeros((9, width, width), jnp.float32)
    grad_affine = jnp.zeros((4, width), jnp.float32)
    collected = jnp.zeros((micro_count, total_rows, width), jnp.float32)
    returning = jnp.zeros((total_rows, width), jnp.float32)
    for phase_turn in range(turns):
        slot_raw = micro_count - 1 - phase_turn + (section_count - 1 - section_rank)
        active = (slot_raw >= 0) & (slot_raw < micro_count)
        slot_index = jnp.clip(slot_raw, 0, micro_count - 1)
        seeded = lax.dynamic_index_in_dim(out_grad, slot_index, 0, keepdims=False).astype(
            jnp.float32
        )
        upstream = jnp.where(section_rank == section_count - 1, seeded, returning)
        upstream = jnp.where(active, upstream, 0.0)
        tap_index, tap_mask, valid_rows = crop_table(crop_counts[slot_index], total_rows)
        hidden = lax.dynamic_index_in_dim(kept_inputs, slot_index, 0, keepdims=False)
        moments = lax.dynamic_index_in_dim(kept_moments, slot_index, 0, keepdims=False)
        row_count = lax.dynamic_index_in_dim(kept_counts, slot_index, 0, keepdims=False)
        d_hidden, part_point, part_spatial, part_affine = backward_block(
            hidden,
            upstream,
            point_low,
            spatial_low,
            affine,
            moments,
            row_count,
            tap_index,
            tap_mask,
            valid_rows,
        )
        grad_point = grad_point + part_point
        grad_spatial = grad_spatial + part_spatial
        grad_affine = grad_affine + part_affine
        collected = store_slot(collected, d_hidden, slot_index, active & (section_rank == 0))
        if phase_turn + 1 < turns:
            returning = from_behind(d_hidden.astype(jnp.bfloat16), "section", -1).astype(
                d_hidden.dtype
            )
    point_grad, spatial_grad = (
        lax.psum_scatter(grad_point, "batch", scatter_dimension=0, tiled=True),
        lax.psum_scatter(grad_spatial, "batch", scatter_dimension=1, tiled=True),
    )
    point_sq, spatial_sq, gpoint_sq, gspatial_sq = lax.psum(
        (
            jnp.sum(point * point),
            jnp.sum(spatial * spatial),
            jnp.sum(point_grad * point_grad),
            jnp.sum(spatial_grad * spatial_grad),
        ),
        "batch",
    )
    rate = BASE_RATE * (STEP + 1) / WARMUP
    new_point, new_mom_point = lars_update(
        point, point_grad, mom_point[0], point_sq, gpoint_sq, rate
    )
    new_spatial, new_mom_spatial = lars_update(
        spatial, spatial_grad, mom_spatial[0], spatial_sq, gspatial_sq, rate
    )
    affine_sq = jnp.sum(affine * affine, 1, keepdims=True)
    gaffine_sq = jnp.sum(grad_affine * grad_affine, 1, keepdims=True)
    new_affine, new_mom_affine = lars_update(
        affine, grad_affine, mom_norm[0], affine_sq, gaffine_sq, rate
    )
    sent_out = jnp.where(section_rank == section_count - 1, results, 0.0)
    sent_back = jnp.where(section_rank == 0, collected, 0.0)
    got_out, got_back = (
        lax.all_to_all(
            sent_out.astype(jnp.bfloat16), "section", split_axis=0, concat_axis=0, tiled=True
        ).astype(sent_out.dtype),
        lax.all_to_all(
            sent_back.astype(jnp.bfloat16), "section", split_axis=0, concat_axis=0, tiled=True
        ).astype(sent_back.dtype),
    )
    features = got_out[section_count - 1 : section_count]
    in_grad = got_back[0:1]
    return (
        features,
        in_grad,
        new_point[None],
        new_spatial[None],
        new_affine[None],
        new_mom_point[None],
        new_mom_spatial[None],
        new_mom_affine[None],
    )


def swap_copy(source, target, sent, landed, section, batch):
    return pltpu.make_async_remote_copy(
        src_ref=source,
        dst_ref=target,
        send_sem=sent,
        recv_sem=landed,
        device_id=(section, batch),
        device_id_type=pl.DeviceIdType.MESH,
    )


def drain(like, sem):
    pltpu.make_async_copy(like, like, sem).wait()


def mish_terms(v):
    e = jnp.exp(jnp.minimum(v, 20.0))
    w = e * (e + 2.0)
    r = 1.0 / (w + 2.0)
    t = w * r
    return v * t, t + v * (4.0 * e * (1.0 + e)) * (r * r)


def pack(first, second):
    parts = [v[:, i * 128 : (i + 1) * 128] for v in (first, second) for i in range(4)]
    return jnp.concatenate(parts, axis=0)


def unpack(tile):
    rows = [tile[i : i + 1] for i in range(8)]
    return jnp.concatenate(rows[:4], axis=1), jnp.concatenate(rows[4:], axis=1)


def crop_codes(places, big, total_rows):
    big_area = float(BIG_SIDE * BIG_SIDE)
    small_area = float(SMALL_SIDE * SMALL_SIDE)
    big_rows = big * big_area
    small_rows = jnp.floor((total_rows - big_rows + 0.5) / small_area) * small_area
    in_big = places < big_rows
    offset = jnp.where(in_big, places, places - big_rows)
    area = jnp.where(in_big, big_area, small_area)
    side = jnp.where(in_big, float(BIG_SIDE), float(SMALL_SIDE))
    crop = jnp.floor((offset + 0.5) / area)
    within = offset - crop * area
    row = jnp.floor((within + 0.5) / side)
    col = within - row * side
    crop = jnp.where(in_big, crop, crop + big)
    return crop * 1024.0 + (row + 1.0) * 32.0 + (col + 1.0), places < big_rows + small_rows


NT = (((1,), (1,)), ((), ()))
TAPS = 10
WHOLE = 2
HALF = (TAPS - WHOLE) // 2


def train_kernel(
    images, crop, w_point, w_spatial, norm_in, out_grad,
    features, in_grad, grads, totals_out, affine_out,
    W, wown, F, sv, gi, abuf, Gm, caq, stage, stage_a, Hb, dzq, dz1q, pgrad, precv, gout, yrecv,
    zs1, zrecv, gfin, sq_in, sq_own, sq_acc, psq, aff, gaff, gsend, st_in, st_own, st_all, cnt, cntx, cown,
    sL, sS_s, sS_r, sU_s, sU_r, sV_s, sV_r, sJ_s, sJ_r, sZ_s, sZ_r, sH_s, sH_r, sA_s, sA_r, sB_r, sD_r,
    sE_in_s, sE_in_r, sE_s, sE_r, sC_s, sC_r, sF_s, sF_r, sQ_s, sQ_r, sX_s, sX_r, sM_s, sM_r, sP_s, sP_r,
    sW_s, sW_r, sY_s, sY_r, sK_s, sK_r, sN_s, sN_r, sT_s, sT_r, sG_s, sG_r, sO_s, sO_r,
):
    s = lax.axis_index("section")
    bat = lax.axis_index("batch")
    z = bat // 2
    c = lax.rem(bat, 2)
    x = lax.rem(s, 2)
    y = s // 2
    R, D = abuf.shape
    h = F.at[pl.ds(0, R)]
    g = F.at[pl.ds(R, R)]
    zbuf = F.at[pl.ds(2 * R, R)]

    loads = [
        pltpu.make_async_copy(w_point.at[0], F.at[pl.ds(9 * 64, 64)], sL.at[0]),
        *[
            pltpu.make_async_copy(w_spatial.at[0, k], F.at[pl.ds(k * 64, 64)], sL.at[0])
            for k in range(9)
        ],
        pltpu.make_async_copy(images.at[s], abuf, sL.at[1]),
    ]
    for load in loads:
        load.start()

    barrier = pltpu.get_barrier_semaphore()
    greet = [(s, bat ^ j) for j in range(1, 8)]
    greet += [(s ^ d, bat ^ j) for d in range(1, 4) for j in range(2)]
    for sec, other in greet:
        pl.semaphore_signal(
            barrier, inc=1, device_id=(sec, other), device_id_type=pl.DeviceIdType.MESH
        )

    def square(rows):
        return jnp.sum(rows * rows, 0, keepdims=True)

    spatial_squares = jnp.zeros((1, D), jnp.float32)
    drain(F.at[pl.ds(0, 64 * TAPS)], sL.at[0])
    for k in range(TAPS):
        rows = F[k * 64 : k * 64 + 64]
        wown[k] = rows.astype(jnp.bfloat16).reshape(4, 16, D)
        if k < 9:
            spatial_squares += square(rows)
        else:
            point_squares = square(rows)
    sq_in[...] = jnp.zeros_like(sq_in)
    with jax.named_scope("greet"):
        pl.semaphore_wait(barrier, len(greet))

    cown[...] = jnp.full((8, 128), crop[0, s].astype(jnp.float32))
    aff[s] = jnp.concatenate([norm_in[0], jnp.zeros((4, D), jnp.float32)], axis=0)
    cnt[bat] = cown[...]
    cntx[c] = cown[...]
    for j in range(1, 8):
        swap_copy(cown, cnt.at[bat], sC_s, sC_r.at[0], s, bat ^ j).start()
    for j in range(2):
        for near in (1, 2):
            swap_copy(cown, cntx.at[2 * near + c], sC_s, sC_r.at[1], s ^ near, bat ^ j).start()
    for d in range(1, 4):
        swap_copy(aff.at[s], aff.at[s], sF_s, sF_r, s ^ d, bat).start()

    def scatter(d):
        q = s ^ d
        return swap_copy(
            wown.at[split, q], W.at[s, split, bat, q], sS_s, sS_r.at[s], q, 2 * z
        )

    def scatter_whole(d):
        return swap_copy(
            wown.at[whole], W.at[s, whole, bat], sU_s, sU_r.at[s], s ^ d, 2 * z
        )

    split, whole = pl.ds(0, 2 * HALF), pl.ds(2 * HALF, WHOLE)
    for send in (scatter, scatter_whole):
        for d in range(1, 4):
            send(d).start()

        @pl.when(c == 1)
        def _():
            send(0).start()

    @pl.when(c == 0)
    def _():
        pltpu.make_async_copy(wown.at[split, s], W.at[s, split, bat, s], sS_r.at[s]).start()
        pltpu.make_async_copy(wown.at[whole], W.at[s, whole, bat], sU_r.at[s]).start()

    @jax.named_scope("sums_start")
    def sums_start(e, first_sum, second_sum):
        slot = lax.rem(e, 2)
        st_own[e] = pack(first_sum, second_sum)
        to_core = swap_copy(st_own.at[e], st_in.at[e], sE_in_s.at[slot], sE_in_r.at[slot], s, bat ^ 1)

        if not isinstance(e, int):

            @pl.when(e > 1)
            def _():
                sums_close(e)

        @pl.when(c == 0)
        def _():
            to_core.start()

        @pl.when(c == 1)
        def _():
            to_core.wait_recv()
            st_all[e, z] = st_own[e] + st_in[e]
            for j in (7, 6, 5, 4, 3, 2, 1):
                swap_copy(
                    st_all.at[e, z], st_all.at[e, z], sE_s.at[slot], sE_r.at[slot], s, bat ^ j
                ).start()

    @jax.named_scope("sums_finish")
    def sums_finish(e):
        slot = lax.rem(e, 2)

        @pl.when(c == 0)
        def _():
            drain(st_all.at[e], sE_r.at[slot])

        @pl.when(c == 1)
        def _():
            drain(st_all.at[e, pl.ds(0, 3)], sE_r.at[slot])

        return unpack(st_all[e, 0] + st_all[e, 1] + st_all[e, 2] + st_all[e, 3])

    def sums_close(e):
        slot = lax.rem(e, 2)

        @pl.when(c == 0)
        def _():
            drain(st_own.at[0], sE_in_s.at[slot])

        @pl.when(c == 1)
        def _():
            drain(cnt.at[pl.ds(0, 7)], sE_s.at[slot])

    sums_start(0, point_squares, spatial_squares)

    half = pl.ds(HALF * c, HALF)
    first = jnp.where(c == 0, s ^ 1, s ^ 2)
    second = jnp.where(c == 0, s ^ 2, s ^ 1)
    both = s ^ 3

    def pair(b, taps, zz, q):
        return W.at[b, taps, pl.ds(2 * zz, 2), q]

    def to_sibling(b, zz):
        ref = pair(b, split, zz, s)
        return swap_copy(ref, ref, sH_s, sH_r.at[b, zz], s, bat ^ 1)

    def along_first(b, zz):
        ref = pair(b, half, zz, s)
        return swap_copy(ref, ref, sA_s, sA_r.at[b, zz], first, bat)

    def along_second(b, which, zz):
        ref = pair(b, half, zz, s if which == 0 else first)
        return swap_copy(ref, ref, sA_s, sB_r.at[b, which], second, bat)

    def quarter_to_sibling(b, which):
        ref = W.at[b, half, :, (first, second, both)[which]]
        return swap_copy(ref, ref, sA_s, sD_r.at[b], s, bat ^ 1)

    def own_ready(b, zz):
        @pl.when(c == 0)
        def _():
            to_sibling(b, zz).start()

        @pl.when(c == 1)
        def _():
            to_sibling(b, zz).wait_recv()

        along_first(b, zz).start()
        along_second(b, 0, zz).start()

    def along_z(b, zz, j):
        ref = pair(b, split, zz, s)
        return swap_copy(ref, ref, sZ_s, sZ_r.at[b, zz], s, bat ^ (2 * j))

    def whole_along_z(b, zz, j):
        ref = W.at[b, whole, pl.ds(2 * zz, 2)]
        return swap_copy(ref, ref, sV_s, sV_r.at[b, j - 1], s, bat ^ (2 * j))

    def whole_to_sibling(b, zz):
        ref = W.at[b, whole, pl.ds(2 * zz, 2)]
        return swap_copy(ref, ref, sJ_s, sJ_r.at[b], s, bat ^ 1)

    def on_first_core(work):
        pl.when(c == 0)(work)

    @jax.named_scope("own_quarter")
    def own_quarter(b):
        @on_first_core
        def _():
            drain(pair(b, split, z, s), sS_r.at[b])

        own_ready(b, z)

    @jax.named_scope("start_z")
    def start_z(b):
        @on_first_core
        def _():
            along_z(b, z, 2).start()
            along_z(b, z, 1).start()

    @jax.named_scope("start_whole")
    def start_whole(b):
        @on_first_core
        def _():
            drain(W.at[b, whole, pl.ds(2 * z, 2)], sU_r.at[b])
            whole_along_z(b, z, 2).start()
            whole_along_z(b, z, 1).start()
            whole_to_sibling(b, z).start()

    @jax.named_scope("relay_z")
    def relay_z(b):
        @on_first_core
        def _():
            drain(pair(b, split, z ^ 2, s), sZ_r.at[b, z ^ 2])
            along_z(b, z ^ 2, 1).start()

        own_ready(b, z ^ 2)

    @jax.named_scope("rest_z")
    def rest_z(b):
        for j in (1, 3):
            @on_first_core
            def _():
                drain(pair(b, split, z ^ j, s), sZ_r.at[b, z ^ j])

            own_ready(b, z ^ j)

    @jax.named_scope("relay_whole")
    def relay_whole(b):
        @on_first_core
        def _():
            drain(W.at[b, whole, pl.ds(2 * (z ^ 2), 2)], sV_r.at[b, 1])
            whole_along_z(b, z ^ 2, 1).start()
            whole_to_sibling(b, z ^ 2).start()

    @jax.named_scope("rest_whole")
    def rest_whole(b):
        @on_first_core
        def _():
            drain(W.at[b, whole, pl.ds(0, 4)], sV_r.at[b, 0])
            for j in (1, 3):
                whole_to_sibling(b, z ^ j).start()

    @jax.named_scope("gather_first")
    def gather_first(b, pieces=(0, 2, 1, 3)):
        for j in pieces:
            zz = z ^ j
            ref = pair(b, half, zz, first)
            swap_copy(ref, ref, sA_s, sA_r.at[b, zz], first, bat).wait_recv()
            along_second(b, 1, zz).start()
        if 3 in pieces:
            quarter_to_sibling(b, 0).start()

    @jax.named_scope("gather_second")
    def gather_second(b):
        for which in range(2):
            drain(W.at[b, half, :, (second, both)[which]], sB_r.at[b, which])
            quarter_to_sibling(b, 1 + which).start()

    @jax.named_scope("gather_last")
    def gather_last(b):
        other = pl.ds(HALF * (1 - c), HALF)
        drain(W.at[b, other, :, pl.ds(0, 3)], sD_r.at[b])

    for b in range(2):
        own_quarter(b)
        if b == 0:
            start_z(0)
    relay_z(0)
    start_whole(0)
    start_z(1)

    drain(cnt.at[pl.ds(0, 7)], sC_r.at[0])
    drain(cntx.at[pl.ds(2, 4)], sC_r.at[1])
    cntx[1 - c] = cnt[bat ^ 1]
    total = jnp.zeros((1, 1), jnp.float32)
    for j in range(8):
        big = cnt[j][0:1, 0:1]
        big_rows = big * float(BIG_SIDE * BIG_SIDE)
        area = float(SMALL_SIDE * SMALL_SIDE)
        total = total + big_rows + jnp.floor((R - big_rows + 0.5) / area) * area
    row_count = total
    down = lax.broadcasted_iota(jnp.int32, (R, 1), 0).astype(jnp.float32)
    across = lax.broadcasted_iota(jnp.int32, (1, R), 1).astype(jnp.float32)

    @pl.loop(0, 6)
    @jax.named_scope("tables")
    def _(v):
        big = cntx[v][0:1, 0:1]
        code_down, ok_down = crop_codes(down, big, R)
        code_across, ok_across = crop_codes(across, big, R)
        code_down = jnp.where(ok_down, code_down, -5000.0)
        code_across = jnp.where(ok_across, code_across, -1.0)
        for k in range(9):
            step = float(32 * (k // 3 - 1) + (k % 3 - 1))
            hit = (code_down + step) == code_across
            Gm[v, pl.ds(k * R, R)] = jnp.where(hit, 1.0, 0.0).astype(jnp.bfloat16)

    _, own_valid = crop_codes(down, cown[0:1, 0:1], R)
    valid = own_valid.astype(jnp.float32)
    drain(aff.at[pl.ds(0, 3)], sF_r)
    loads[10].wait()
    h[...] = abuf[...].astype(jnp.float32)

    def moments(sums):
        center = sums[0] / row_count
        spread = lax.rsqrt(sums[1] / row_count - center * center + EPS)
        return center, spread

    def pairing(b):
        odd = lax.rem(b, 2) == 1
        return jnp.where(odd, x, y), jnp.where(odd, y, x), jnp.where(odd, 1, 2)

    @jax.named_scope("share")
    def share(b, kind, rows):
        turned = rows.T
        rows_to = stage_a if kind == 1 else stage.at[b]
        if kind == 1:
            @pl.when(b > 0)
            def _():
                drain(stage_a.at[pl.ds(0, 2)], sQ_s.at[1])

        odd = lax.rem(b, 2) == 1
        for cc in range(2):
            for xx in range(2):
                for yy in range(2):
                    one, two = jnp.where(odd, xx, yy), jnp.where(odd, yy, xx)
                    for zz in range(4):
                        at = (2 * zz + cc) * 64 + (2 * yy + xx) * 16
                        rows_to[2 * one + cc, 4 * two + zz] = turned[at : at + 16].astype(
                            jnp.bfloat16
                        )
        if kind == 1:
            for half_of_pair in range(2):
                v = 2 * half_of_pair
                caq[b, 1, v + c] = stage_a[v + c]
                swap_copy(
                    stage_a.at[v + 1 - c], caq.at[b, 1, v + c], sQ_s.at[1], sQ_r.at[b, 1], s, bat ^ 1
                ).start()
        else:
            u = 2 * pairing(b)[0] + c
            caq[b, 0, u] = stage[b, u]

            @pl.when(b == 3)
            def _():
                send_share(b)

    def send_share(b):
        mine, _, near = pairing(b)
        u = 2 * mine + c
        for j in range(1, 4):
            swap_copy(
                stage.at[b, u ^ j], caq.at[b, 0, u], sQ_s.at[0], sQ_r.at[b, 0],
                s ^ near if j > 1 else s, bat ^ (j % 2),
            ).start()

    def wait_share(b, kind):
        drain(caq.at[b, kind, pl.ds(0, 2 if kind == 1 else 3)], sQ_r.at[b, kind])

    @jax.named_scope("forward")
    def forward(b):
        with jax.named_scope("whole_here"):

            @pl.when(c == 1)
            def _():
                drain(W.at[b, whole], sJ_r.at[b])

        @pl.when(b == 3)
        def _():
            for early in (2, 1, 0):
                send_share(early)

        hidden = h[...]
        zbuf[...] = jnp.dot(
            hidden.astype(jnp.bfloat16), W[b, 9].reshape(D, D), preferred_element_type=jnp.float32
        )
        z1 = zbuf[...]
        kept = valid * z1
        sums_start(
            2 * b + 1, jnp.sum(kept, 0, keepdims=True), jnp.sum(kept * z1, 0, keepdims=True)
        )
        share(b, 1, hidden)

        @pl.when(b == 2)
        def _():
            rest_z(3)
            gather_first(3, (0, 2))

        gather_second(b)

        @pl.when(b == 0)
        def _():
            gather_first(1, (1, 3))
            relay_z(2)

        @pl.when(b == 1)
        def _():
            gather_first(2)
            relay_whole(2)

        @pl.when(b == 2)
        def _():
            relay_whole(3)

        norms = aff[b]
        center, spread = moments(sums_finish(2 * b + 1))
        gi[b, 0:1] = norms[0:1] * spread
        for i in range(0, R, 64):
            xhat = (zbuf[i : i + 64] - center) * spread
            value, slope = mish_terms(norms[0:1] * xhat + norms[1:2])
            sv[b, 0, i : i + 64] = xhat.astype(sv.dtype)
            sv[b, 1, i : i + 64] = slope.astype(sv.dtype)
            abuf[i : i + 64] = value.astype(jnp.bfloat16)
        mixed = abuf[...]
        gather_last(b)
        for k in range(9):
            Hb[:, k * D : (k + 1) * D] = jnp.dot(
                Gm[c, pl.ds(k * R, R)], mixed, preferred_element_type=jnp.float32
            ).astype(jnp.bfloat16)
        zbuf[...] = jnp.dot(
            Hb[...], W[b, 0:9].reshape(9 * D, D), preferred_element_type=jnp.float32
        )
        z2 = zbuf[...]
        kept = valid * z2
        sums_start(
            2 * b + 2, jnp.sum(kept, 0, keepdims=True), jnp.sum(kept * z2, 0, keepdims=True)
        )
        share(b, 0, mixed.astype(jnp.float32))

        @pl.when(b == 0)
        def _():
            relay_whole(1)
            own_quarter(3)
            start_whole(2)
            start_z(3)

        @pl.when(b == 1)
        def _():
            relay_z(3)
            start_whole(3)

        @pl.when(b == 2)
        def _():
            gather_first(3, (1, 3))

        center, spread = moments(sums_finish(2 * b + 2))
        gi[b, 1:2] = norms[2:3] * spread
        for i in range(0, R, 64):
            xhat = (zbuf[i : i + 64] - center) * spread
            value, slope = mish_terms(norms[2:3] * xhat + norms[3:4])
            sv[b, 2, i : i + 64] = xhat.astype(sv.dtype)
            sv[b, 3, i : i + 64] = slope.astype(sv.dtype)
            h[i : i + 64] = h[i : i + 64] + valid[i : i + 64] * value

    rest_z(0)
    relay_whole(0)
    own_quarter(2)
    gather_first(0, (0, 2))
    relay_z(1)
    start_z(2)
    start_whole(1)
    gather_first(0, (1, 3))
    gather_first(1, (0, 2))
    rest_z(1)
    rest_whole(0)
    psq[...] = jnp.concatenate(sums_finish(0), axis=0)

    @pl.loop(0, 4)
    def _(b):
        forward(b)

        @pl.when(b == 0)
        def _():
            rest_z(2)

        @pl.when(b < 3)
        def _():
            rest_whole(b + 1)

    out_grad_rows = pltpu.make_async_copy(out_grad.at[s], abuf, sL.at[2])
    out_features = pltpu.make_async_copy(h, features.at[0], sO_s.at[0])
    out_features.start()
    out_grad_rows.start()
    out_grad_rows.wait()
    g[...] = abuf[...].astype(jnp.float32)

    @jax.named_scope("close_gather")
    def close_gather():
        drain(aff.at[pl.ds(0, 3)], sF_s)
        drain(st_own.at[pl.ds(0, 11)], sC_s)
        drain(stage_a.at[pl.ds(0, 2)], sQ_s.at[1])

        @pl.when(c == 0)
        def _():
            drain(wown.at[split, pl.ds(0, 3)], sS_s)
            drain(W.at[0, whole, pl.ds(0, 3)], sU_s)

        @pl.when(c == 1)
        def _():
            drain(wown.at[split], sS_s)
            drain(W.at[0, whole, pl.ds(0, 4)], sU_s)

        drain(W.at[:, split, :, pl.ds(0, 3)], sA_s)

        @on_first_core
        def _():
            drain(W.at[:, split, pl.ds(0, 6), s], sZ_s)
            drain(W.at[:, split, :, s], sH_s)
            drain(W.at[:, whole, pl.ds(0, 6)], sV_s)
            drain(W.at[:, whole], sJ_s)

    @jax.named_scope("close_rest")
    def close_rest():
        drain(stage.at[:, pl.ds(0, 3)], sQ_s.at[0])
        drain(dzq.at[:, pl.ds(0, 3)], sX_s)
        drain(dz1q.at[:, 0], sM_s)
        drain(precv, sP_s)
        drain(gsend.at[pl.ds(0, 3)], sO_s.at[3])
        drain(gout.at[:, 0], sY_s)

        @pl.when(c == 0)
        def _():
            drain(zrecv.at[:, pl.ds(0, 2)], sN_s)
            drain(zrecv.at[:, 2], sT_s)

        @pl.when(c == 1)
        def _():
            drain(zs1, sK_s)
            drain(zrecv.at[pl.ds(0, 3), pl.ds(0, 2)], sN_s)
            drain(zrecv.at[pl.ds(0, 3), 2], sT_s)

    CHUNKS = ((0, 3), (3, 3), (6, 3), (9, 1))
    LAST = len(CHUNKS) - 1

    def dz_copy(b, j):
        mine, _, near = pairing(b)
        v = 2 * mine + c
        v = v ^ 2 if j == 3 else v
        ref = dzq.at[b, v]
        return swap_copy(
            ref, ref, sX_s, sX_r.at[b, 0 if j == 2 else 1], s ^ near if j == 2 else s, bat if j == 2 else bat ^ 1
        )

    def send_dz(b):
        dz_copy(b, 2).start()
        dz_copy(b, 1).start()

    @jax.named_scope("forward_dz")
    def forward_dz(b):
        v = (2 * pairing(b)[0] + c) ^ 2
        drain(dzq.at[b, v], sX_r.at[b, 0])
        dz_copy(b, 3).start()

    @jax.named_scope("wait_dz")
    def wait_dz(b):
        drain(dzq.at[b, pl.ds(0, 2)], sX_r.at[b, 1])

    def dz_one_copy(b):
        ref = dz1q.at[b, c]
        return swap_copy(ref, ref, sM_s, sM_r.at[b], s, bat ^ 1)

    def point_copy(b):
        mine, _, near = pairing(b)
        return swap_copy(
            pgrad.at[b, 1 - mine], precv.at[b], sP_s, sP_r.at[b], s ^ near, bat
        )

    def y_copy(b, i):
        at, size = CHUNKS[i]
        return swap_copy(
            gout.at[b, 1 - pairing(b)[1], pl.ds(at, size)], yrecv.at[b, pl.ds(at, size)],
            sY_s, sY_r.at[b, i], s ^ 3 ^ pairing(b)[2], bat,
        )

    def grad_tap(b, k, left, right):
        part = jnp.dot(left, right, preferred_element_type=jnp.float32).astype(jnp.bfloat16)
        for yy in range(2):
            gout[b, yy, k] = part[64 * yy : 64 * yy + 64].reshape(4, 16, D)

    @jax.named_scope("grad_spatial")
    def grad_spatial(b):
        wait_share(b, 0)
        wait_dz(b)
        mine, _, near = pairing(b)
        tables = [jnp.where(mine == v // 2, 0, 2 * near) + v % 2 for v in range(4)]
        right = dzq[b].reshape(4 * R, D)
        for k in range(9):
            left = [
                lax.dot_general(
                    caq[b, 0, v].reshape(128, R), Gm[tables[v], pl.ds(k * R, R)], NT,
                    preferred_element_type=jnp.float32,
                ).astype(jnp.bfloat16)
                for v in range(4)
            ]
            grad_tap(b, k, jnp.concatenate(left, axis=1), right)
            if k % 3 == 2:
                y_copy(b, k // 3).start()

    @jax.named_scope("grad_point")
    def grad_point(b):
        wait_share(b, 1)
        drain(dz1q.at[b, 1 - c], sM_r.at[b])
        left = jnp.concatenate(
            [
                jnp.concatenate([caq[b, 1, 2 * v + k].reshape(128, R) for v in range(2)], axis=0)
                for k in range(2)
            ],
            axis=1,
        )
        part = jnp.dot(
            left, dz1q[b].reshape(2 * R, D), preferred_element_type=jnp.float32
        ).astype(jnp.bfloat16)
        pgrad[b] = part.reshape(2, 2, 4, 16, D)
        point_copy(b).start()

    @jax.named_scope("pair_point")
    def pair_point(b):
        point_copy(b).wait_recv()
        mine = pairing(b)[0]
        for yy in range(2):
            gout[b, yy, 9] = (
                pgrad[b, mine, yy].astype(jnp.float32) + precv[b, yy].astype(jnp.float32)
            ).astype(jnp.bfloat16)
        y_copy(b, LAST).start()

    def core_copy(b, i):
        at, size = CHUNKS[i]
        return swap_copy(
            yrecv.at[b, pl.ds(at, size)], zs1.at[pl.ds(at, size)],
            sK_s, sK_r.at[i], s, bat ^ 1,
        )

    @jax.named_scope("reduce_plane")
    def reduce_plane(b, i):
        at, size = CHUNKS[i]
        y_copy(b, i).wait_recv()
        rest = pairing(b)[1]
        for k in range(at, at + size):
            yrecv[b, k] = (
                yrecv[b, k].astype(jnp.float32) + gout[b, rest, k].astype(jnp.float32)
            ).astype(jnp.bfloat16)

        if b == 3:

            @pl.when(c == 1)
            def _():
                core_copy(b, i).start()

    def carriers(b, work):
        if b == 3:
            pl.when(c == 0)(functools.partial(work, (0, 1)))
        else:
            work((0,))

    def z_near(b, i, cc, slot):
        at, size = CHUNKS[i]
        return swap_copy(
            (yrecv.at[b], zs1)[cc].at[pl.ds(at, size), z ^ (3 if slot else 1)],
            zrecv.at[b + cc, slot, pl.ds(at, size)], sN_s, sN_r.at[b, i], s, bat ^ 2,
        )

    def z_far(b, i, cc):
        at, size = CHUNKS[i]
        return swap_copy(
            zrecv.at[b + cc, 1, pl.ds(at, size)], zrecv.at[b + cc, 2, pl.ds(at, size)],
            sT_s, sT_r.at[b, i], s, bat ^ 4,
        )

    def near_like(b, i, parts):
        at, size = CHUNKS[i]
        return zrecv.at[pl.ds(b, len(parts)), pl.ds(0, 2), pl.ds(at, size)]

    def far_like(b, i, parts):
        at, size = CHUNKS[i]
        return zrecv.at[pl.ds(b, len(parts)), 2, pl.ds(at, size)]

    @jax.named_scope("reduce_near")
    def reduce_near(b, i):
        def work(parts):
            if b == 3:
                core_copy(b, i).wait_recv()
            for slot in (1, 0):
                for cc in parts:
                    z_near(b, i, cc, slot).start()

        carriers(b, work)

    @jax.named_scope("reduce_far")
    def reduce_far(b, i):
        at, size = CHUNKS[i]

        def work(parts):
            drain(near_like(b, i, parts), sN_r.at[b, i])
            for cc in parts:
                mine = (yrecv.at[b], zs1)[cc]
                for k in range(at, at + size):
                    zrecv[b + cc, 1, k] = (
                        zrecv[b + cc, 1, k].astype(jnp.float32) + mine[k, z ^ 2].astype(jnp.float32)
                    ).astype(jnp.bfloat16)
                z_far(b, i, cc).start()

        carriers(b, work)

    def deliver(b, i, cc, section, core):
        at, size = CHUNKS[i]
        swap_copy(
            zrecv.at[b + cc, 0, pl.ds(at, size)], gfin.at[pl.ds(at, size), s],
            sG_s, sG_r.at[s], section, 2 * z + core,
        ).start()

    def send_squares(b):
        def to(j):
            return swap_copy(
                sq_own.at[b], sq_in.at[s, bat], sW_s, sW_r, b, bat ^ j
            )

        sq_own[b] = pack(sq_acc[b, 1:2], sq_acc[b, 0:1])

        @pl.when(b != s)
        def _():
            to(0).start()

        @pl.when(b == s)
        def _():
            sq_in[s, bat] = sq_own[b]

        for j in range(1, 8):
            to(j).start()

    @jax.named_scope("finish")
    def finish(b, i):
        at, size = CHUNKS[i]

        def work(parts):
            drain(far_like(b, i, parts), sT_r.at[b, i])
            squares = jnp.zeros((1, D), jnp.float32)
            for cc in parts:
                mine = (yrecv.at[b], zs1)[cc]
                for k in range(at, at + size):
                    done = (
                        zrecv[b + cc, 0, k].astype(jnp.float32)
                        + zrecv[b + cc, 2, k].astype(jnp.float32)
                        + mine[k, z].astype(jnp.float32)
                    ).astype(jnp.bfloat16)
                    zrecv[b + cc, 0, k] = done
                    squares += square(done.astype(jnp.float32))

                @pl.when(b != s)
                def _():
                    deliver(b, i, cc, b, cc if b == 3 else c)

                @pl.when(b == s)
                def _():
                    if cc == 0:
                        for k in range(at, at + size):
                            gfin[k, s] = zrecv[b, 0, k]
                    else:
                        deliver(b, i, 1, s, 1)

            row = 1 if i == LAST else 0
            sq_acc[b, row : row + 1] = squares + (0.0 if i in (0, LAST) else sq_acc[b, row : row + 1])
            if i == LAST:
                send_squares(b)

        carriers(b, work)

    @jax.named_scope("backward")
    def backward(bi):
        b = 3 - bi
        e = 9 + 2 * bi
        u = 2 * pairing(b)[0] + c
        first_sum = jnp.zeros((1, D), jnp.float32)
        second_sum = jnp.zeros((1, D), jnp.float32)
        for i in range(0, R, 64):
            du = valid[i : i + 64] * g[i : i + 64] * sv[b, 3, i : i + 64].astype(jnp.float32)
            zbuf[i : i + 64] = du
            first_sum += jnp.sum(du, 0, keepdims=True)
            second_sum += jnp.sum(du * sv[b, 2, i : i + 64].astype(jnp.float32), 0, keepdims=True)
        sums_start(e, first_sum, second_sum)

        @pl.when(bi == 0)
        def _():
            close_gather()

        @pl.when(bi == 3)
        def _():
            reduce_near(3, 1)

        @pl.when(bi > 0)
        def _():
            forward_dz(b + 1)
            grad_point(b + 1)

        @pl.when(bi == 2)
        def _():
            pair_point(3)

        @pl.when(bi == 3)
        def _():
            reduce_plane(3, 2)
            reduce_far(3, 0)

        total_first, total_second = sums_finish(e)
        for i in range(0, R, 64):
            xhat = sv[b, 2, i : i + 64].astype(jnp.float32)
            inner = zbuf[i : i + 64] - valid[i : i + 64] * (
                (total_first + xhat * total_second) / row_count
            )
            dzq[b, u, i : i + 64] = (gi[b, 1:2] * inner).astype(jnp.bfloat16)
        send_dz(b)
        gsend[b, 2:3] = total_second
        gsend[b, 3:4] = total_first
        d_two = dzq[b, u]
        for k in range(9):
            Hb[:, k * D : (k + 1) * D] = jnp.dot(
                Gm[c, pl.ds((8 - k) * R, R)], d_two, preferred_element_type=jnp.float32
            ).astype(jnp.bfloat16)
        mixed = None
        for k in range(9):
            part = lax.dot_general(
                Hb[:, k * D : (k + 1) * D], W[b, k].reshape(D, D), NT,
                preferred_element_type=jnp.float32,
            )
            mixed = part if mixed is None else mixed + part
        zbuf[...] = mixed
        first_sum = jnp.zeros((1, D), jnp.float32)
        second_sum = jnp.zeros((1, D), jnp.float32)
        for i in range(0, R, 64):
            du = zbuf[i : i + 64] * sv[b, 1, i : i + 64].astype(jnp.float32)
            zbuf[i : i + 64] = du
            first_sum += jnp.sum(du, 0, keepdims=True)
            second_sum += jnp.sum(du * sv[b, 0, i : i + 64].astype(jnp.float32), 0, keepdims=True)
        sums_start(e + 1, first_sum, second_sum)

        @pl.when(bi == 2)
        def _():
            reduce_plane(3, 0)
            reduce_near(3, 0)

        @pl.when(bi == 3)
        def _():
            reduce_near(3, 2)
            reduce_far(3, 1)
            reduce_plane(2, 0)
            reduce_near(2, 0)

        @pl.when(bi > 0)
        def _():
            grad_spatial(b + 1)

        @pl.when(bi == 2)
        def _():
            reduce_plane(3, 1)

        @pl.when(bi == 3)
        def _():
            reduce_plane(3, 3)
            reduce_plane(2, 1)
            reduce_near(2, 1)

        total_first, total_second = sums_finish(e + 1)
        for i in range(0, R, 64):
            xhat = sv[b, 0, i : i + 64].astype(jnp.float32)
            inner = zbuf[i : i + 64] - valid[i : i + 64] * (
                (total_first + xhat * total_second) / row_count
            )
            dz1q[b, c, i : i + 64] = (gi[b, 0:1] * inner).astype(jnp.bfloat16)
        dz_one_copy(b).start()
        gsend[b, 0:1] = total_second
        gsend[b, 1:2] = total_first
        g[...] = g[...] + lax.dot_general(
            dz1q[b, c], W[b, 9].reshape(D, D), NT, preferred_element_type=jnp.float32
        )

        @pl.when(b == s)
        def _():
            gaff[s] = gsend[b]

        @pl.when(b != s)
        def _():
            swap_copy(gsend.at[b], gaff.at[s], sO_s.at[3], sO_r, b, bat).start()

    @pl.loop(0, 4)
    def _(bi):
        backward(bi)

    out_grad_in = pltpu.make_async_copy(g, in_grad.at[0], sO_s.at[1])
    out_grad_in.start()

    reduce_near(3, 3)
    forward_dz(0)
    pair_point(2)
    reduce_far(2, 0)
    reduce_far(3, 2)
    reduce_plane(2, 2)
    reduce_near(2, 2)
    grad_spatial(0)
    reduce_far(2, 1)
    grad_point(0)
    reduce_far(3, 3)
    pair_point(1)
    finish(3, 0)
    reduce_plane(2, 3)
    reduce_near(2, 3)
    reduce_plane(1, 0)
    reduce_near(1, 0)
    finish(3, 1)
    reduce_far(2, 2)
    finish(2, 0)
    reduce_plane(1, 1)
    reduce_near(1, 1)
    finish(3, 2)
    reduce_far(1, 0)
    reduce_plane(1, 2)
    reduce_near(1, 2)
    finish(3, 3)
    finish(2, 1)
    pair_point(0)
    reduce_far(2, 3)
    reduce_plane(0, 0)
    reduce_near(0, 0)
    reduce_far(1, 1)
    reduce_plane(1, 3)
    reduce_near(1, 3)
    finish(2, 2)
    finish(1, 0)
    reduce_far(1, 2)
    reduce_plane(0, 1)
    reduce_near(0, 1)
    reduce_plane(0, 2)
    reduce_near(0, 2)
    reduce_plane(0, 3)
    reduce_near(0, 3)
    reduce_far(0, 0)
    finish(2, 3)
    finish(1, 1)
    reduce_far(1, 3)
    reduce_far(0, 1)
    finish(1, 2)
    finish(1, 3)
    finish(0, 0)
    reduce_far(0, 2)
    reduce_far(0, 3)
    finish(0, 1)
    close_rest()
    finish(0, 2)
    finish(0, 3)
    for d in range(1, 4):
        drain(gfin.at[:, s ^ d], sG_r.at[s ^ d])

    @pl.when((c == 1) & (s == 3))
    def _():
        drain(gfin.at[:, s], sG_r.at[s])

    grads_out = pltpu.make_async_copy(gfin, grads, sO_s.at[2])
    grads_out.start()

    drain(gaff.at[pl.ds(0, 3)], sO_r)
    affine_out[...] = gaff[0] + gaff[1] + gaff[2] + gaff[3]
    squares_in = sq_in.reshape(32, 8, 128)

    @pl.when(s != 3)
    def _():
        drain(squares_in.at[pl.ds(0, 31)], sW_r)

    @pl.when((s == 3) & (c == 0))
    def _():
        drain(squares_in.at[pl.ds(0, 15)], sW_r)

    @pl.when((s == 3) & (c == 1))
    def _():
        drain(squares_in.at[pl.ds(0, 16)], sW_r)

    gpoint_squares, gspatial_squares = unpack(jnp.sum(squares_in[...], axis=0))
    totals_out[...] = jnp.concatenate(
        [psq[...], gpoint_squares, gspatial_squares, jnp.zeros((4, D), jnp.float32)], axis=0
    )

    with jax.named_scope("close_last"):
        sums_close(0)
        sums_close(1)

        @pl.when(c == 0)
        def _():
            drain(zrecv.at[pl.ds(0, 4), 0], sG_s)

        @pl.when(c == 0)
        def _():
            drain(squares_in.at[pl.ds(0, 31)], sW_s)

        @pl.when((c == 1) & (s == 3))
        def _():
            drain(zrecv.at[pl.ds(0, 3), 0], sG_s)
            drain(squares_in.at[pl.ds(0, 24)], sW_s)

        @pl.when((c == 1) & (s != 3))
        def _():
            drain(zrecv.at[pl.ds(0, 2), 0], sG_s)
            drain(squares_in.at[pl.ds(0, 23)], sW_s)

    with jax.named_scope("close_outputs"):
        grads_out.wait()
        out_features.wait()
        out_grad_in.wait()


def lars_kernel(
    feat, ing, grads_in, totals_in, affine_in, w_point, w_spatial, norm_in, mom_point, mom_spatial, mom_norm,
    features, in_grad, new_point, new_spatial, new_norm, new_mom_point, new_mom_spatial, new_mom_norm,
    P, M, G, feat_rows, grad_rows, totals, affine_grad, affine, affine_mom, sem, out_sem,
):
    THIRDS = 3
    small = [
        (totals_in, totals), (affine_in, affine_grad), (norm_in.at[0], affine), (mom_norm.at[0], affine_mom),
        (w_point.at[0], P.at[9]), (mom_point.at[0], M.at[9]), (grads_in.at[9], G.at[9]),
    ]
    large = []
    for i in range(THIRDS):
        taps = pl.ds(3 * i, 3)
        large += [
            (grads_in.at[taps], G.at[taps]), (w_spatial.at[0, taps], P.at[taps]),
            (mom_spatial.at[0, taps], M.at[taps]),
        ]
    rows = [(feat, feat_rows), (ing, grad_rows)]
    loads = [
        pltpu.make_async_copy(a, b, sem.at[i]) for i, (a, b) in enumerate(small + large + rows)
    ]
    for load in loads:
        load.start()
    for load in loads[: len(small)]:
        load.wait()
    D = affine.shape[1]
    rate = BASE_RATE * (STEP + 1) / WARMUP
    point_sq, spatial_sq, gpoint_sq, gspatial_sq = [
        jnp.sum(totals[i : i + 1], axis=1, keepdims=True) for i in range(4)
    ]
    step_point = rate * TRUST_COEF * jnp.sqrt(point_sq) / (jnp.sqrt(gpoint_sq) + EPS_NORM)
    step_spatial = rate * TRUST_COEF * jnp.sqrt(spatial_sq) / (jnp.sqrt(gspatial_sq) + EPS_NORM)
    outs = []

    def store(source, target):
        outs.append(pltpu.make_async_copy(source, target, out_sem.at[len(outs)]))
        outs[-1].start()

    def move(k, step):
        moved = MOMENTUM * M[k] + step * G[k].astype(jnp.float32).reshape(64, D)
        M[k] = moved
        P[k] = P[k] - moved

    for i in range(THIRDS):
        for load in loads[len(small) + 3 * i :][:3]:
            load.wait()
        for k in range(3 * i, 3 * i + 3):
            move(k, step_spatial)
        taps = pl.ds(3 * i, 3)
        store(M.at[taps], new_mom_spatial.at[0, taps])
        store(P.at[taps], new_spatial.at[0, taps])
    move(9, step_point)
    store(M.at[9], new_mom_point.at[0])
    store(P.at[9], new_point.at[0])
    for load, source, target in zip(loads[-2:], (feat_rows, grad_rows), (features, in_grad)):
        load.wait()
        store(source, target)
    grad = affine_grad[0:4]
    old = affine[...]
    affine_sq = jnp.sum(old * old, axis=1, keepdims=True)
    gaffine_sq = jnp.sum(grad * grad, axis=1, keepdims=True)
    trust = TRUST_COEF * jnp.sqrt(affine_sq) / (jnp.sqrt(gaffine_sq) + EPS_NORM)
    moved = MOMENTUM * affine_mom[...] + rate * trust * grad
    affine_mom[...] = moved
    affine[...] = old - moved
    store(affine_mom, new_mom_norm.at[0])
    store(affine, new_norm.at[0])
    for copy in outs:
        copy.wait()


def train_step(images, crop, w_point, w_spatial, norm_params, mom_point, mom_spatial, mom_norm, out_grad):
    R, D = images.shape[1:]
    f32, bf16 = jnp.float32, jnp.bfloat16
    dma = pltpu.SemaphoreType.DMA
    anywhere = pl.BlockSpec(memory_space=pl.ANY)
    vmem = pl.BlockSpec(memory_space=pltpu.VMEM)
    hbm = pl.BlockSpec(memory_space=pltpu.HBM)
    smem = pl.BlockSpec(memory_space=pltpu.SMEM)
    V = pltpu.VMEM
    scratch = dict(
        W=V((4, TAPS, 8, 4, 16, D), bf16), wown=V((TAPS, 4, 16, D), bf16),
        F=V((3 * R, D), f32),
        sv=V((4, 4, R, D), bf16), gi=V((4, 8, D), f32),
        abuf=V((R, D), bf16),
        Gm=V((6, 9 * R, R), bf16), caq=V((4, 2, 4, 8, 16, R), bf16),
        stage=V((4, 4, 8, 16, R), bf16), stage_a=V((4, 8, 16, R), bf16), Hb=V((R, 9 * D), bf16),
        dzq=V((4, 4, R, D), bf16), dz1q=V((4, 2, R, D), bf16),
        pgrad=V((4, 2, 2, 4, 16, D), bf16), precv=V((4, 2, 4, 16, D), bf16),
        gout=V((4, 2, TAPS, 4, 16, D), bf16), yrecv=V((4, TAPS, 4, 16, D), bf16),
        zs1=V((TAPS, 4, 16, D), bf16), zrecv=V((5, 3, TAPS, 16, D), bf16),
        gfin=V((TAPS, 4, 16, D), bf16),
        sq_in=V((4, 8, 8, 128), f32), sq_own=V((4, 8, 128), f32), sq_acc=V((4, 8, D), f32), psq=V((2, D), f32),
        aff=V((4, 8, D), f32), gaff=V((4, 8, D), f32), gsend=V((4, 8, D), f32),
        st_in=V((17, 8, 128), f32), st_own=V((17, 8, 128), f32), st_all=V((17, 4, 8, 128), f32),
        cnt=V((8, 8, 128), f32), cntx=V((6, 8, 128), f32), cown=V((8, 128), f32),
        sL=dma((3,)), sS_s=dma, sS_r=dma((4,)), sU_s=dma, sU_r=dma((4,)), sV_s=dma, sV_r=dma((4, 2)),
        sJ_s=dma, sJ_r=dma((4,)), sZ_s=dma, sZ_r=dma((4, 4)),
        sH_s=dma, sH_r=dma((4, 4)), sA_s=dma, sA_r=dma((4, 4)),
        sB_r=dma((4, 2)), sD_r=dma((4,)),
        sE_in_s=dma((2,)), sE_in_r=dma((2,)), sE_s=dma((2,)), sE_r=dma((2,)),
        sC_s=dma, sC_r=dma((2,)), sF_s=dma, sF_r=dma,
        sQ_s=dma((2,)), sQ_r=dma((4, 2)), sX_s=dma, sX_r=dma((4, 2)), sM_s=dma, sM_r=dma((4,)), sP_s=dma, sP_r=dma((4,)),
        sW_s=dma, sW_r=dma,
        sY_s=dma, sY_r=dma((4, 4)), sK_s=dma, sK_r=dma((4,)),
        sN_s=dma, sN_r=dma((4, 4)), sT_s=dma, sT_r=dma((4, 4)), sG_s=dma, sG_r=dma((4,)),
        sO_s=dma((4,)), sO_r=dma,
    )
    shape = jax.ShapeDtypeStruct
    feat, ing, grads, totals, affine_grad = pl.pallas_call(
        train_kernel,
        out_shape=(
            shape((1, R, D), f32), shape((1, R, D), f32), shape((TAPS, 4, 16, D), bf16),
            shape((8, D), f32), shape((8, D), f32),
        ),
        in_specs=[anywhere, smem, anywhere, anywhere, vmem, anywhere],
        out_specs=(anywhere, anywhere, anywhere, vmem, vmem),
        scratch_shapes=list(scratch.values()),
        compiler_params=pltpu.CompilerParams(
            collective_id=0, has_side_effects=True, vmem_limit_bytes=64 * 1024 * 1024
        ),
    )(images, crop.T, w_point, w_spatial, norm_params, out_grad)
    return pl.pallas_call(
        lars_kernel,
        out_shape=(
            shape((1, R, D), f32), shape((1, R, D), f32),
            shape(w_point.shape, f32), shape(w_spatial.shape, f32), shape(norm_params.shape, f32),
            shape(w_point.shape, f32), shape(w_spatial.shape, f32), shape(norm_params.shape, f32),
        ),
        in_specs=[hbm] * 11,
        out_specs=(hbm,) * 8,
        scratch_shapes=[
            V((TAPS, 64, D), f32), V((TAPS, 64, D), f32), V((TAPS, 4, 16, D), bf16), V((1, R, D), f32),
            V((1, R, D), f32), V((8, D), f32), V((8, D), f32), V((4, D), f32), V((4, D), f32), dma((18,)), dma((12,)),
        ],
        compiler_params=pltpu.CompilerParams(vmem_limit_bytes=64 * 1024 * 1024),
    )(feat, ing, grads, totals, affine_grad, w_point, w_spatial, norm_params, mom_point, mom_spatial, mom_norm)


def solution(mesh):
    tuned = mesh.shape["section"] == 4 and mesh.shape["batch"] == 8
    return jax.shard_map(
        train_step if tuned else on_device,
        mesh=mesh,
        in_specs=(
            P(None, "batch", None),
            P(None, "batch"),
            P("section", "batch", None),
            P("section", None, "batch", None),
            P("section", None, None),
            P("section", "batch", None),
            P("section", None, "batch", None),
            P("section", None, None),
            P(None, "batch", None),
        ),
        out_specs=(
            P("section", "batch", None),
            P("section", "batch", None),
            P("section", "batch", None),
            P("section", None, "batch", None),
            P("section", None, None),
            P("section", "batch", None),
            P("section", None, "batch", None),
            P("section", None, None),
        ),
        check_vma=False,
    )
```

```python
import functools

import jax
import jax.numpy as jnp
from jax import lax
from jax.experimental import pallas as pl
from jax.experimental.pallas import tpu as pltpu
from jax.sharding import PartitionSpec as P

BIG_SIDE = 7
SMALL_SIDE = 3
WARMUP = 20
STEP = 9


EPS = 1e-05
EPS_NORM = 1e-06
BASE_RATE = 6.0
MOMENTUM = 0.9
TRUST_COEF = 0.1


def from_behind(block, axis, distance):
    devices = range(lax.axis_size(axis))
    route = [(i - distance, i) for i in devices if i - distance in devices]
    return lax.ppermute(block, axis, route)


def crop_table(big_count, total_rows):
    places = jnp.arange(total_rows, dtype=jnp.int32)
    big_area = BIG_SIDE * BIG_SIDE
    small_area = SMALL_SIDE * SMALL_SIDE
    big_rows = big_count * big_area
    small_rows = (total_rows - big_rows) // small_area * small_area
    in_big = places < big_rows
    offsets = places - big_rows
    sides = jnp.where(in_big, BIG_SIDE, SMALL_SIDE)
    within = jnp.where(in_big, places % big_area, offsets % small_area)
    starts = places - within
    valid_rows = places < big_rows + small_rows
    row_pos = within // sides
    col_pos = within % sides
    indices = []
    masks = []
    for row_step in (-1, 0, 1):
        for col_step in (-1, 0, 1):
            new_row = row_pos + row_step
            new_col = col_pos + col_step
            inside = (
                valid_rows & (new_row >= 0) & (new_row < sides) & (new_col >= 0) & (new_col < sides)
            )
            indices.append(jnp.where(inside, starts + new_row * sides + new_col, places))
            masks.append(inside)
    return (
        jnp.stack(indices, 1),
        jnp.stack(masks, 1).astype(jnp.float32),
        valid_rows.astype(jnp.float32),
    )


def mish(values):
    return values * jnp.tanh(jax.nn.softplus(values))


def mish_parts(values):
    tangent = jnp.tanh(jax.nn.softplus(values))
    slope = tangent + values * jax.nn.sigmoid(values) * (1.0 - tangent * tangent)
    return (values * tangent, slope)


def mish_slope(values):
    tangent = jnp.tanh(jax.nn.softplus(values))
    return tangent + values * jax.nn.sigmoid(values) * (1.0 - tangent * tangent)


def batch_moments(proj, valid_rows):
    weighted = valid_rows[:, None] * proj
    summed, squared, row_count = lax.psum(
        (jnp.sum(weighted, 0), jnp.sum(weighted * proj, 0), jnp.sum(valid_rows)), "batch"
    )
    center = summed / row_count
    inv_std = lax.rsqrt(squared / row_count - center * center + EPS)
    return (center, inv_std, row_count)


def spatial_apply(source, tap_index, tap_mask, weights):
    stacked = source[tap_index] * tap_mask[:, :, None].astype(source.dtype)
    result = lax.dot_general(
        stacked, weights, (((1, 2), (0, 1)), ((), ())), preferred_element_type=jnp.float32
    )
    return (result, stacked)


def forward_block(hidden, point_low, spatial_low, affine, tap_index, tap_mask, valid_rows):
    proj_one = jnp.dot(hidden.astype(jnp.bfloat16), point_low, preferred_element_type=jnp.float32)
    center_one, inv_one, row_count = batch_moments(proj_one, valid_rows)
    mixed_one = mish(affine[0] * ((proj_one - center_one) * inv_one) + affine[1])
    proj_two, stacked = spatial_apply(
        mixed_one.astype(jnp.bfloat16), tap_index, tap_mask, spatial_low
    )
    center_two, inv_two, count_two = batch_moments(proj_two, valid_rows)
    mixed_two = mish(affine[2] * ((proj_two - center_two) * inv_two) + affine[3])
    moments = jnp.stack([center_one, inv_one, center_two, inv_two])
    return (hidden + valid_rows[:, None] * mixed_two, moments, row_count)


def norm_back(d_value, normed, inv_std, gain, valid_rows, row_count):
    first_sum, second_sum = lax.psum((jnp.sum(d_value, 0), jnp.sum(d_value * normed, 0)), "batch")
    d_proj = (
        gain
        * inv_std
        * (d_value - valid_rows[:, None] * (first_sum + normed * second_sum) / row_count)
    )
    return (d_proj.astype(jnp.bfloat16), first_sum, second_sum)


def backward_block(
    hidden,
    upstream,
    point_low,
    spatial_low,
    affine,
    moments,
    row_count,
    tap_index,
    tap_mask,
    valid_rows,
):
    inputs = hidden.astype(jnp.bfloat16)
    proj_one = jnp.dot(inputs, point_low, preferred_element_type=jnp.float32)
    normed_one = (proj_one - moments[0]) * moments[1]
    mixed_one, slope_one = mish_parts(affine[0] * normed_one + affine[1])
    proj_two, stacked = spatial_apply(
        mixed_one.astype(jnp.bfloat16), tap_index, tap_mask, spatial_low
    )
    normed_two = (proj_two - moments[2]) * moments[3]
    slope_two = mish_slope(affine[2] * normed_two + affine[3])
    d_two, first_two, second_two = norm_back(
        valid_rows[:, None] * upstream * slope_two,
        normed_two,
        moments[3],
        affine[2],
        valid_rows,
        row_count,
    )
    grad_spatial = lax.dot_general(
        stacked, d_two, (((0,), (0,)), ((), ())), preferred_element_type=jnp.float32
    )
    flipped = d_two[tap_index[:, ::-1]] * tap_mask[:, ::-1, None].astype(jnp.bfloat16)
    d_mixed = lax.dot_general(
        flipped, spatial_low, (((1, 2), (0, 2)), ((), ())), preferred_element_type=jnp.float32
    )
    d_one, first_one, second_one = norm_back(
        d_mixed * slope_one, normed_one, moments[1], affine[0], valid_rows, row_count
    )
    grad_point = lax.dot_general(
        inputs, d_one, (((0,), (0,)), ((), ())), preferred_element_type=jnp.float32
    )
    d_hidden = upstream + lax.dot_general(
        d_one, point_low, (((1,), (1,)), ((), ())), preferred_element_type=jnp.float32
    )
    grad_affine = jnp.stack([second_one, first_one, second_two, first_two])
    return (d_hidden, grad_point, grad_spatial, grad_affine)


def store_slot(buffer, value, slot_index, active):
    previous = lax.dynamic_index_in_dim(buffer, slot_index, 0, keepdims=False)
    return lax.dynamic_update_index_in_dim(
        buffer, jnp.where(active, value, previous), slot_index, 0
    )


def lars_update(param, grad, momentum, param_sq, grad_sq, rate):
    trust = TRUST_COEF * jnp.sqrt(param_sq) / (jnp.sqrt(grad_sq) + EPS_NORM)
    new_mom = MOMENTUM * momentum + rate * trust * grad
    return (param - new_mom, new_mom)


def on_device(
    images, crop_big, w_point, w_spatial, norm_params, mom_point, mom_spatial, mom_norm, out_grad
):
    section_count = lax.axis_size("section")
    section_rank = lax.axis_index("section")
    micro_count = images.shape[0]
    total_rows = images.shape[1]
    width = images.shape[2]
    point = w_point[0]
    spatial = w_spatial[0]
    affine = norm_params[0]
    crop_counts = crop_big[:, 0]
    turns = micro_count + section_count - 1
    point_low, spatial_low = (
        lax.all_gather(point.astype(jnp.bfloat16), "batch", axis=0, tiled=True),
        lax.all_gather(spatial.astype(jnp.bfloat16), "batch", axis=1, tiled=True),
    )
    kept_inputs = jnp.zeros((micro_count, total_rows, width), jnp.float32)
    kept_moments = jnp.zeros((micro_count, 4, width), jnp.float32)
    kept_counts = jnp.zeros((micro_count,), jnp.float32)
    results = jnp.zeros((micro_count, total_rows, width), jnp.float32)
    incoming = jnp.zeros((total_rows, width), jnp.float32)
    for phase_turn in range(turns):
        slot_raw = phase_turn - section_rank
        active = (slot_raw >= 0) & (slot_raw < micro_count)
        slot_index = jnp.clip(slot_raw, 0, micro_count - 1)
        fresh_rows = lax.dynamic_index_in_dim(images, slot_index, 0, keepdims=False).astype(
            jnp.float32
        )
        hidden = jnp.where(section_rank == 0, fresh_rows, incoming)
        tap_index, tap_mask, valid_rows = crop_table(crop_counts[slot_index], total_rows)
        output, moments, row_count = forward_block(
            hidden, point_low, spatial_low, affine, tap_index, tap_mask, valid_rows
        )
        kept_inputs = store_slot(kept_inputs, hidden, slot_index, active)
        kept_moments = store_slot(kept_moments, moments, slot_index, active)
        kept_counts = store_slot(kept_counts, row_count, slot_index, active)
        results = store_slot(
            results, output, slot_index, active & (section_rank == section_count - 1)
        )
        if phase_turn + 1 < turns:
            incoming = from_behind(output.astype(jnp.bfloat16), "section", 1).astype(output.dtype)
    point_low, spatial_low = (
        lax.all_gather(point.astype(jnp.bfloat16), "batch", axis=0, tiled=True),
        lax.all_gather(spatial.astype(jnp.bfloat16), "batch", axis=1, tiled=True),
    )
    grad_point = jnp.zeros((width, width), jnp.float32)
    grad_spatial = jnp.zeros((9, width, width), jnp.float32)
    grad_affine = jnp.zeros((4, width), jnp.float32)
    collected = jnp.zeros((micro_count, total_rows, width), jnp.float32)
    returning = jnp.zeros((total_rows, width), jnp.float32)
    for phase_turn in range(turns):
        slot_raw = micro_count - 1 - phase_turn + (section_count - 1 - section_rank)
        active = (slot_raw >= 0) & (slot_raw < micro_count)
        slot_index = jnp.clip(slot_raw, 0, micro_count - 1)
        seeded = lax.dynamic_index_in_dim(out_grad, slot_index, 0, keepdims=False).astype(
            jnp.float32
        )
        upstream = jnp.where(section_rank == section_count - 1, seeded, returning)
        upstream = jnp.where(active, upstream, 0.0)
        tap_index, tap_mask, valid_rows = crop_table(crop_counts[slot_index], total_rows)
        hidden = lax.dynamic_index_in_dim(kept_inputs, slot_index, 0, keepdims=False)
        moments = lax.dynamic_index_in_dim(kept_moments, slot_index, 0, keepdims=False)
        row_count = lax.dynamic_index_in_dim(kept_counts, slot_index, 0, keepdims=False)
        d_hidden, part_point, part_spatial, part_affine = backward_block(
            hidden,
            upstream,
            point_low,
            spatial_low,
            affine,
            moments,
            row_count,
            tap_index,
            tap_mask,
            valid_rows,
        )
        grad_point = grad_point + part_point
        grad_spatial = grad_spatial + part_spatial
        grad_affine = grad_affine + part_affine
        collected = store_slot(collected, d_hidden, slot_index, active & (section_rank == 0))
        if phase_turn + 1 < turns:
            returning = from_behind(d_hidden.astype(jnp.bfloat16), "section", -1).astype(
                d_hidden.dtype
            )
    point_grad, spatial_grad = (
        lax.psum_scatter(grad_point, "batch", scatter_dimension=0, tiled=True),
        lax.psum_scatter(grad_spatial, "batch", scatter_dimension=1, tiled=True),
    )
    point_sq, spatial_sq, gpoint_sq, gspatial_sq = lax.psum(
        (
            jnp.sum(point * point),
            jnp.sum(spatial * spatial),
            jnp.sum(point_grad * point_grad),
            jnp.sum(spatial_grad * spatial_grad),
        ),
        "batch",
    )
    rate = BASE_RATE * (STEP + 1) / WARMUP
    new_point, new_mom_point = lars_update(
        point, point_grad, mom_point[0], point_sq, gpoint_sq, rate
    )
    new_spatial, new_mom_spatial = lars_update(
        spatial, spatial_grad, mom_spatial[0], spatial_sq, gspatial_sq, rate
    )
    affine_sq = jnp.sum(affine * affine, 1, keepdims=True)
    gaffine_sq = jnp.sum(grad_affine * grad_affine, 1, keepdims=True)
    new_affine, new_mom_affine = lars_update(
        affine, grad_affine, mom_norm[0], affine_sq, gaffine_sq, rate
    )
    sent_out = jnp.where(section_rank == section_count - 1, results, 0.0)
    sent_back = jnp.where(section_rank == 0, collected, 0.0)
    got_out, got_back = (
        lax.all_to_all(
            sent_out.astype(jnp.bfloat16), "section", split_axis=0, concat_axis=0, tiled=True
        ).astype(sent_out.dtype),
        lax.all_to_all(
            sent_back.astype(jnp.bfloat16), "section", split_axis=0, concat_axis=0, tiled=True
        ).astype(sent_back.dtype),
    )
    features = got_out[section_count - 1 : section_count]
    in_grad = got_back[0:1]
    return (
        features,
        in_grad,
        new_point[None],
        new_spatial[None],
        new_affine[None],
        new_mom_point[None],
        new_mom_spatial[None],
        new_mom_affine[None],
    )


def swap_copy(source, target, sent, landed, section, batch):
    return pltpu.make_async_remote_copy(
        src_ref=source,
        dst_ref=target,
        send_sem=sent,
        recv_sem=landed,
        device_id=(section, batch),
        device_id_type=pl.DeviceIdType.MESH,
    )


def drain(like, sem):
    pltpu.make_async_copy(like, like, sem).wait()


def mish_terms(v):
    e = jnp.exp(jnp.minimum(v, 20.0))
    w = e * (e + 2.0)
    r = 1.0 / (w + 2.0)
    t = w * r
    return v * t, t + v * (4.0 * e * (1.0 + e)) * (r * r)


def pack(first, second):
    parts = [v[:, i * 128 : (i + 1) * 128] for v in (first, second) for i in range(4)]
    return jnp.concatenate(parts, axis=0)


def unpack(tile):
    rows = [tile[i : i + 1] for i in range(8)]
    return jnp.concatenate(rows[:4], axis=1), jnp.concatenate(rows[4:], axis=1)


def fold(row):
    return sum(row[:, i * 128 : (i + 1) * 128] for i in range(4))


def crop_codes(places, big, total_rows):
    big_area = float(BIG_SIDE * BIG_SIDE)
    small_area = float(SMALL_SIDE * SMALL_SIDE)
    big_rows = big * big_area
    small_rows = jnp.floor((total_rows - big_rows + 0.5) / small_area) * small_area
    in_big = places < big_rows
    offset = jnp.where(in_big, places, places - big_rows)
    area = jnp.where(in_big, big_area, small_area)
    side = jnp.where(in_big, float(BIG_SIDE), float(SMALL_SIDE))
    crop = jnp.floor((offset + 0.5) / area)
    within = offset - crop * area
    row = jnp.floor((within + 0.5) / side)
    col = within - row * side
    crop = jnp.where(in_big, crop, crop + big)
    return crop * 1024.0 + (row + 1.0) * 32.0 + (col + 1.0), places < big_rows + small_rows


NT = (((1,), (1,)), ((), ()))
TAPS = 10
WHOLE = 2
HALF = (TAPS - WHOLE) // 2


def train_kernel(
    images, crop, w_point, w_spatial, norm_in, out_grad,
    features, in_grad, grads, totals_out, affine_out,
    W, wown, F, sv, gi, abuf, Gm, caq, stage, stage_a, Hb, dzq, dz1q, pgrad, precv, gout, yrecv,
    zs1, zrecv, gfin, sq_in, sq_own, sq_acc, psq, aff, gaff, gsend, st_in, st_own, st_all, cnt, cntx, cown,
    sL, sS_s, sS_r, sU_s, sU_r, sV_s, sV_r, sJ_s, sJ_r, sZ_s, sZ_r, sH_s, sH_r, sA_s, sA_r, sB_r, sD_r,
    sE_in_s, sE_in_r, sE_s, sE_r, sC_s, sC_r, sF_s, sF_r, sQ_s, sQ_r, sX_s, sX_r, sM_s, sM_r, sP_s, sP_r,
    sW_s, sW_r, sY_s, sY_r, sK_s, sK_r, sN_s, sN_r, sT_s, sT_r, sG_s, sG_r, sO_s, sO_r,
):
    s = lax.axis_index("section")
    bat = lax.axis_index("batch")
    z = bat // 2
    c = lax.rem(bat, 2)
    x = lax.rem(s, 2)
    y = s // 2
    R, D = abuf.shape
    h = F.at[pl.ds(0, R)]
    g = F.at[pl.ds(R, R)]
    zbuf = F.at[pl.ds(2 * R, R)]

    loads = [
        pltpu.make_async_copy(w_point.at[0], F.at[pl.ds(9 * 64, 64)], sL.at[0]),
        *[
            pltpu.make_async_copy(w_spatial.at[0, k], F.at[pl.ds(k * 64, 64)], sL.at[0])
            for k in range(9)
        ],
        pltpu.make_async_copy(images.at[s], abuf, sL.at[1]),
    ]
    for load in loads:
        load.start()

    barrier = pltpu.get_barrier_semaphore()
    greet = [(s, bat ^ j) for j in range(1, 8)]
    greet += [(s ^ d, bat ^ j) for d in range(1, 4) for j in range(2)]
    for sec, other in greet:
        pl.semaphore_signal(
            barrier, inc=1, device_id=(sec, other), device_id_type=pl.DeviceIdType.MESH
        )

    def square(rows):
        return jnp.sum(rows * rows, 0, keepdims=True)

    spatial_squares = jnp.zeros((1, D), jnp.float32)
    drain(F.at[pl.ds(0, 64 * TAPS)], sL.at[0])
    for k in range(TAPS):
        rows = F[k * 64 : k * 64 + 64]
        wown[k] = rows.astype(jnp.bfloat16).reshape(4, 16, D)
        if k < 9:
            spatial_squares += square(rows)
        else:
            point_squares = square(rows)
    sq_in[...] = jnp.zeros_like(sq_in)
    with jax.named_scope("greet"):
        pl.semaphore_wait(barrier, len(greet))

    cown[...] = jnp.full((8, 128), crop[0, s].astype(jnp.float32))
    aff[s] = jnp.concatenate([norm_in[0], jnp.zeros((4, D), jnp.float32)], axis=0)
    cnt[bat] = cown[...]
    cntx[c] = cown[...]
    for j in range(1, 8):
        swap_copy(cown, cnt.at[bat], sC_s, sC_r.at[0], s, bat ^ j).start()
    for j in range(2):
        for near in (1, 2):
            swap_copy(cown, cntx.at[2 * near + c], sC_s, sC_r.at[1], s ^ near, bat ^ j).start()
    for d in range(1, 4):
        swap_copy(aff.at[s], aff.at[s], sF_s, sF_r, s ^ d, bat).start()

    def scatter(d):
        q = s ^ d
        return swap_copy(
            wown.at[split, q], W.at[s, split, bat, q], sS_s, sS_r.at[s], q, 2 * z
        )

    def scatter_whole(d):
        return swap_copy(
            wown.at[whole], W.at[s, whole, bat], sU_s, sU_r.at[s], s ^ d, 2 * z
        )

    split, whole = pl.ds(0, 2 * HALF), pl.ds(2 * HALF, WHOLE)
    for send in (scatter, scatter_whole):
        for d in range(1, 4):
            send(d).start()

        @pl.when(c == 1)
        def _():
            send(0).start()

    @pl.when(c == 0)
    def _():
        pltpu.make_async_copy(wown.at[split, s], W.at[s, split, bat, s], sS_r.at[s]).start()
        pltpu.make_async_copy(wown.at[whole], W.at[s, whole, bat], sU_r.at[s]).start()

    @jax.named_scope("sums_start")
    def sums_start(e, first_sum, second_sum):
        slot = lax.rem(e, 2)
        st_own[e] = pack(first_sum, second_sum)
        to_core = swap_copy(st_own.at[e], st_in.at[e], sE_in_s.at[slot], sE_in_r.at[slot], s, bat ^ 1)

        if not isinstance(e, int):

            @pl.when(e > 1)
            def _():
                sums_close(e)

        @pl.when(c == 0)
        def _():
            to_core.start()

        @pl.when(c == 1)
        def _():
            to_core.wait_recv()
            st_all[e, z] = st_own[e] + st_in[e]
            for j in (7, 6, 5, 4, 3, 2, 1):
                swap_copy(
                    st_all.at[e, z], st_all.at[e, z], sE_s.at[slot], sE_r.at[slot], s, bat ^ j
                ).start()

    @jax.named_scope("sums_finish")
    def sums_finish(e):
        slot = lax.rem(e, 2)

        @pl.when(c == 0)
        def _():
            drain(st_all.at[e], sE_r.at[slot])

        @pl.when(c == 1)
        def _():
            drain(st_all.at[e, pl.ds(0, 3)], sE_r.at[slot])

        return unpack(st_all[e, 0] + st_all[e, 1] + st_all[e, 2] + st_all[e, 3])

    def sums_close(e):
        slot = lax.rem(e, 2)

        @pl.when(c == 0)
        def _():
            drain(st_own.at[0], sE_in_s.at[slot])

        @pl.when(c == 1)
        def _():
            drain(cnt.at[pl.ds(0, 7)], sE_s.at[slot])

    sums_start(0, point_squares, spatial_squares)

    half = pl.ds(HALF * c, HALF)
    first = jnp.where(c == 0, s ^ 1, s ^ 2)
    second = jnp.where(c == 0, s ^ 2, s ^ 1)
    both = s ^ 3

    def pair(b, taps, zz, q):
        return W.at[b, taps, pl.ds(2 * zz, 2), q]

    def to_sibling(b, zz):
        ref = pair(b, split, zz, s)
        return swap_copy(ref, ref, sH_s, sH_r.at[b, zz], s, bat ^ 1)

    def along_first(b, zz):
        ref = pair(b, half, zz, s)
        return swap_copy(ref, ref, sA_s, sA_r.at[b, zz], first, bat)

    def along_second(b, which, zz):
        ref = pair(b, half, zz, s if which == 0 else first)
        return swap_copy(ref, ref, sA_s, sB_r.at[b, which], second, bat)

    def quarter_to_sibling(b, which):
        ref = W.at[b, half, :, (first, second, both)[which]]
        return swap_copy(ref, ref, sA_s, sD_r.at[b], s, bat ^ 1)

    def own_ready(b, zz):
        @pl.when(c == 0)
        def _():
            to_sibling(b, zz).start()

        @pl.when(c == 1)
        def _():
            to_sibling(b, zz).wait_recv()

        along_first(b, zz).start()
        along_second(b, 0, zz).start()

    def along_z(b, zz, j):
        ref = pair(b, split, zz, s)
        return swap_copy(ref, ref, sZ_s, sZ_r.at[b, zz], s, bat ^ (2 * j))

    def whole_along_z(b, zz, j):
        ref = W.at[b, whole, pl.ds(2 * zz, 2)]
        return swap_copy(ref, ref, sV_s, sV_r.at[b, j - 1], s, bat ^ (2 * j))

    def whole_to_sibling(b, zz):
        ref = W.at[b, whole, pl.ds(2 * zz, 2)]
        return swap_copy(ref, ref, sJ_s, sJ_r.at[b], s, bat ^ 1)

    def on_first_core(work):
        pl.when(c == 0)(work)

    @jax.named_scope("own_quarter")
    def own_quarter(b):
        @on_first_core
        def _():
            drain(pair(b, split, z, s), sS_r.at[b])

        own_ready(b, z)

    @jax.named_scope("start_z")
    def start_z(b):
        @on_first_core
        def _():
            along_z(b, z, 2).start()
            along_z(b, z, 1).start()

    @jax.named_scope("start_whole")
    def start_whole(b):
        @on_first_core
        def _():
            drain(W.at[b, whole, pl.ds(2 * z, 2)], sU_r.at[b])
            whole_along_z(b, z, 2).start()
            whole_along_z(b, z, 1).start()
            whole_to_sibling(b, z).start()

    @jax.named_scope("relay_z")
    def relay_z(b):
        @on_first_core
        def _():
            drain(pair(b, split, z ^ 2, s), sZ_r.at[b, z ^ 2])
            along_z(b, z ^ 2, 1).start()

        own_ready(b, z ^ 2)

    @jax.named_scope("rest_z")
    def rest_z(b):
        for j in (1, 3):
            @on_first_core
            def _():
                drain(pair(b, split, z ^ j, s), sZ_r.at[b, z ^ j])

            own_ready(b, z ^ j)

    @jax.named_scope("relay_whole")
    def relay_whole(b):
        @on_first_core
        def _():
            drain(W.at[b, whole, pl.ds(2 * (z ^ 2), 2)], sV_r.at[b, 1])
            whole_along_z(b, z ^ 2, 1).start()
            whole_to_sibling(b, z ^ 2).start()

    @jax.named_scope("rest_whole")
    def rest_whole(b):
        @on_first_core
        def _():
            drain(W.at[b, whole, pl.ds(0, 4)], sV_r.at[b, 0])
            for j in (1, 3):
                whole_to_sibling(b, z ^ j).start()

    @jax.named_scope("gather_first")
    def gather_first(b, pieces=(0, 2, 1, 3)):
        for j in pieces:
            zz = z ^ j
            ref = pair(b, half, zz, first)
            swap_copy(ref, ref, sA_s, sA_r.at[b, zz], first, bat).wait_recv()
            along_second(b, 1, zz).start()
        if 3 in pieces:
            quarter_to_sibling(b, 0).start()

    @jax.named_scope("gather_second")
    def gather_second(b):
        for which in range(2):
            drain(W.at[b, half, :, (second, both)[which]], sB_r.at[b, which])
            quarter_to_sibling(b, 1 + which).start()

    @jax.named_scope("gather_last")
    def gather_last(b):
        other = pl.ds(HALF * (1 - c), HALF)
        drain(W.at[b, other, :, pl.ds(0, 3)], sD_r.at[b])

    for b in range(2):
        own_quarter(b)
        if b == 0:
            start_z(0)
    relay_z(0)
    start_whole(0)
    start_z(1)

    drain(cnt.at[pl.ds(0, 7)], sC_r.at[0])
    drain(cntx.at[pl.ds(2, 4)], sC_r.at[1])
    cntx[1 - c] = cnt[bat ^ 1]
    total = jnp.zeros((1, 1), jnp.float32)
    for j in range(8):
        big = cnt[j][0:1, 0:1]
        big_rows = big * float(BIG_SIDE * BIG_SIDE)
        area = float(SMALL_SIDE * SMALL_SIDE)
        total = total + big_rows + jnp.floor((R - big_rows + 0.5) / area) * area
    row_count = total
    down = lax.broadcasted_iota(jnp.int32, (R, 1), 0).astype(jnp.float32)
    across = lax.broadcasted_iota(jnp.int32, (1, R), 1).astype(jnp.float32)

    @pl.loop(0, 6)
    @jax.named_scope("tables")
    def _(v):
        big = cntx[v][0:1, 0:1]
        code_down, ok_down = crop_codes(down, big, R)
        code_across, ok_across = crop_codes(across, big, R)
        code_down = jnp.where(ok_down, code_down, -5000.0)
        code_across = jnp.where(ok_across, code_across, -1.0)
        for k in range(9):
            step = float(32 * (k // 3 - 1) + (k % 3 - 1))
            hit = (code_down + step) == code_across
            Gm[v, pl.ds(k * R, R)] = jnp.where(hit, 1.0, 0.0).astype(jnp.bfloat16)

    _, own_valid = crop_codes(down, cown[0:1, 0:1], R)
    valid = own_valid.astype(jnp.float32)
    drain(aff.at[pl.ds(0, 3)], sF_r)
    loads[10].wait()
    h[...] = abuf[...].astype(jnp.float32)

    def moments(sums):
        center = sums[0] / row_count
        spread = lax.rsqrt(sums[1] / row_count - center * center + EPS)
        return center, spread

    def pairing(b):
        odd = lax.rem(b, 2) == 1
        return jnp.where(odd, x, y), jnp.where(odd, y, x), jnp.where(odd, 1, 2)

    @jax.named_scope("share")
    def share(b, kind, rows):
        turned = rows.T
        rows_to = stage_a if kind == 1 else stage.at[b]
        if kind == 1:
            @pl.when(b > 0)
            def _():
                drain(stage_a.at[pl.ds(0, 2)], sQ_s.at[1])

        odd = lax.rem(b, 2) == 1
        for cc in range(2):
            for xx in range(2):
                for yy in range(2):
                    one, two = jnp.where(odd, xx, yy), jnp.where(odd, yy, xx)
                    for zz in range(4):
                        at = (2 * zz + cc) * 64 + (2 * yy + xx) * 16
                        rows_to[2 * one + cc, 4 * two + zz] = turned[at : at + 16].astype(
                            jnp.bfloat16
                        )
        if kind == 1:
            for half_of_pair in range(2):
                v = 2 * half_of_pair
                caq[b, 1, v + c] = stage_a[v + c]
                swap_copy(
                    stage_a.at[v + 1 - c], caq.at[b, 1, v + c], sQ_s.at[1], sQ_r.at[b, 1], s, bat ^ 1
                ).start()
        else:
            u = 2 * pairing(b)[0] + c
            caq[b, 0, u] = stage[b, u]

            @pl.when(b == 3)
            def _():
                send_share(b)

    def send_share(b):
        mine, _, near = pairing(b)
        u = 2 * mine + c
        for j in range(1, 4):
            swap_copy(
                stage.at[b, u ^ j], caq.at[b, 0, u], sQ_s.at[0], sQ_r.at[b, 0],
                s ^ near if j > 1 else s, bat ^ (j % 2),
            ).start()

    def wait_share(b, kind):
        drain(caq.at[b, kind, pl.ds(0, 2 if kind == 1 else 3)], sQ_r.at[b, kind])

    @jax.named_scope("forward")
    def forward(b):
        with jax.named_scope("whole_here"):

            @pl.when(c == 1)
            def _():
                drain(W.at[b, whole], sJ_r.at[b])

        @pl.when(b == 3)
        def _():
            for early in (2, 1, 0):
                send_share(early)

        hidden = h[...]
        zbuf[...] = jnp.dot(
            hidden.astype(jnp.bfloat16), W[b, 9].reshape(D, D), preferred_element_type=jnp.float32
        )
        z1 = zbuf[...]
        kept = valid * z1
        sums_start(
            2 * b + 1, jnp.sum(kept, 0, keepdims=True), jnp.sum(kept * z1, 0, keepdims=True)
        )
        share(b, 1, hidden)

        @pl.when(b == 2)
        def _():
            rest_z(3)
            gather_first(3, (0, 2))

        gather_second(b)

        @pl.when(b == 0)
        def _():
            gather_first(1, (1, 3))
            relay_z(2)

        @pl.when(b == 1)
        def _():
            gather_first(2)
            relay_whole(2)

        @pl.when(b == 2)
        def _():
            relay_whole(3)

        norms = aff[b]
        center, spread = moments(sums_finish(2 * b + 1))
        gi[b, 0:1] = norms[0:1] * spread
        for i in range(0, R, 64):
            xhat = (zbuf[i : i + 64] - center) * spread
            value, slope = mish_terms(norms[0:1] * xhat + norms[1:2])
            sv[b, 0, i : i + 64] = xhat.astype(sv.dtype)
            sv[b, 1, i : i + 64] = slope.astype(sv.dtype)
            abuf[i : i + 64] = value.astype(jnp.bfloat16)
        mixed = abuf[...]
        gather_last(b)
        for k in range(9):
            Hb[:, k * D : (k + 1) * D] = jnp.dot(
                Gm[c, pl.ds(k * R, R)], mixed, preferred_element_type=jnp.float32
            ).astype(jnp.bfloat16)
        zbuf[...] = jnp.dot(
            Hb[...], W[b, 0:9].reshape(9 * D, D), preferred_element_type=jnp.float32
        )
        z2 = zbuf[...]
        kept = valid * z2
        sums_start(
            2 * b + 2, jnp.sum(kept, 0, keepdims=True), jnp.sum(kept * z2, 0, keepdims=True)
        )
        share(b, 0, mixed.astype(jnp.float32))

        @pl.when(b == 0)
        def _():
            relay_whole(1)
            own_quarter(3)
            start_whole(2)
            start_z(3)

        @pl.when(b == 1)
        def _():
            relay_z(3)
            start_whole(3)

        @pl.when(b == 2)
        def _():
            gather_first(3, (1, 3))

        center, spread = moments(sums_finish(2 * b + 2))
        gi[b, 1:2] = norms[2:3] * spread
        for i in range(0, R, 64):
            xhat = (zbuf[i : i + 64] - center) * spread
            value, slope = mish_terms(norms[2:3] * xhat + norms[3:4])
            sv[b, 2, i : i + 64] = xhat.astype(sv.dtype)
            sv[b, 3, i : i + 64] = slope.astype(sv.dtype)
            h[i : i + 64] = h[i : i + 64] + valid[i : i + 64] * value

    rest_z(0)
    relay_whole(0)
    own_quarter(2)
    gather_first(0, (0, 2))
    relay_z(1)
    start_z(2)
    start_whole(1)
    gather_first(0, (1, 3))
    gather_first(1, (0, 2))
    rest_z(1)
    rest_whole(0)
    psq[...] = jnp.concatenate(sums_finish(0), axis=0)

    @pl.loop(0, 4)
    def _(b):
        forward(b)

        @pl.when(b == 0)
        def _():
            rest_z(2)

        @pl.when(b < 3)
        def _():
            rest_whole(b + 1)

    out_grad_rows = pltpu.make_async_copy(out_grad.at[s], abuf, sL.at[2])
    out_features = pltpu.make_async_copy(h, features.at[0], sO_s.at[0])
    out_features.start()
    out_grad_rows.start()
    out_grad_rows.wait()
    g[...] = abuf[...].astype(jnp.float32)

    @jax.named_scope("close_gather")
    def close_gather():
        drain(aff.at[pl.ds(0, 3)], sF_s)
        drain(st_own.at[pl.ds(0, 11)], sC_s)
        drain(stage_a.at[pl.ds(0, 2)], sQ_s.at[1])

        @pl.when(c == 0)
        def _():
            drain(wown.at[split, pl.ds(0, 3)], sS_s)
            drain(W.at[0, whole, pl.ds(0, 3)], sU_s)

        @pl.when(c == 1)
        def _():
            drain(wown.at[split], sS_s)
            drain(W.at[0, whole, pl.ds(0, 4)], sU_s)

        drain(W.at[:, split, :, pl.ds(0, 3)], sA_s)

        @on_first_core
        def _():
            drain(W.at[:, split, pl.ds(0, 6), s], sZ_s)
            drain(W.at[:, split, :, s], sH_s)
            drain(W.at[:, whole, pl.ds(0, 6)], sV_s)
            drain(W.at[:, whole], sJ_s)

    @jax.named_scope("close_rest")
    def close_rest():
        drain(stage.at[:, pl.ds(0, 3)], sQ_s.at[0])
        drain(dzq.at[:, pl.ds(0, 3)], sX_s)
        drain(dz1q.at[:, 0], sM_s)
        drain(precv, sP_s)
        drain(gsend.at[pl.ds(0, 3)], sO_s.at[3])
        drain(gout.at[:, 0], sY_s)

        @pl.when(c == 0)
        def _():
            drain(zrecv.at[:, pl.ds(0, 2)], sN_s)
            drain(zrecv.at[:, 2], sT_s)

        @pl.when(c == 1)
        def _():
            drain(zs1, sK_s)
            drain(zrecv.at[pl.ds(0, 3), pl.ds(0, 2)], sN_s)
            drain(zrecv.at[pl.ds(0, 3), 2], sT_s)

    CHUNKS = ((0, 3), (3, 3), (6, 3), (9, 1))
    LAST = len(CHUNKS) - 1

    def dz_copy(b, j):
        mine, _, near = pairing(b)
        v = 2 * mine + c
        v = v ^ 2 if j == 3 else v
        ref = dzq.at[b, v]
        return swap_copy(
            ref, ref, sX_s, sX_r.at[b, 0 if j == 2 else 1], s ^ near if j == 2 else s, bat if j == 2 else bat ^ 1
        )

    def send_dz(b):
        dz_copy(b, 2).start()
        dz_copy(b, 1).start()

    @jax.named_scope("forward_dz")
    def forward_dz(b):
        v = (2 * pairing(b)[0] + c) ^ 2
        drain(dzq.at[b, v], sX_r.at[b, 0])
        dz_copy(b, 3).start()

    @jax.named_scope("wait_dz")
    def wait_dz(b):
        drain(dzq.at[b, pl.ds(0, 2)], sX_r.at[b, 1])

    def dz_one_copy(b):
        ref = dz1q.at[b, c]
        return swap_copy(ref, ref, sM_s, sM_r.at[b], s, bat ^ 1)

    def point_copy(b):
        mine, _, near = pairing(b)
        return swap_copy(
            pgrad.at[b, 1 - mine], precv.at[b], sP_s, sP_r.at[b], s ^ near, bat
        )

    def y_copy(b, i):
        at, size = CHUNKS[i]
        return swap_copy(
            gout.at[b, 1 - pairing(b)[1], pl.ds(at, size)], yrecv.at[b, pl.ds(at, size)],
            sY_s, sY_r.at[b, i], s ^ 3 ^ pairing(b)[2], bat,
        )

    def grad_tap(b, k, left, right):
        part = jnp.dot(left, right, preferred_element_type=jnp.float32).astype(jnp.bfloat16)
        for yy in range(2):
            gout[b, yy, k] = part[64 * yy : 64 * yy + 64].reshape(4, 16, D)

    @jax.named_scope("grad_spatial")
    def grad_spatial(b):
        wait_share(b, 0)
        wait_dz(b)
        mine, _, near = pairing(b)
        tables = [jnp.where(mine == v // 2, 0, 2 * near) + v % 2 for v in range(4)]
        right = dzq[b].reshape(4 * R, D)
        for k in range(9):
            left = [
                lax.dot_general(
                    caq[b, 0, v].reshape(128, R), Gm[tables[v], pl.ds(k * R, R)], NT,
                    preferred_element_type=jnp.float32,
                ).astype(jnp.bfloat16)
                for v in range(4)
            ]
            grad_tap(b, k, jnp.concatenate(left, axis=1), right)
            if k % 3 == 2:
                y_copy(b, k // 3).start()

    @jax.named_scope("grad_point")
    def grad_point(b):
        wait_share(b, 1)
        drain(dz1q.at[b, 1 - c], sM_r.at[b])
        left = jnp.concatenate(
            [
                jnp.concatenate([caq[b, 1, 2 * v + k].reshape(128, R) for v in range(2)], axis=0)
                for k in range(2)
            ],
            axis=1,
        )
        part = jnp.dot(
            left, dz1q[b].reshape(2 * R, D), preferred_element_type=jnp.float32
        ).astype(jnp.bfloat16)
        pgrad[b] = part.reshape(2, 2, 4, 16, D)
        point_copy(b).start()

    @jax.named_scope("pair_point")
    def pair_point(b):
        point_copy(b).wait_recv()
        mine = pairing(b)[0]
        for yy in range(2):
            gout[b, yy, 9] = (
                pgrad[b, mine, yy].astype(jnp.float32) + precv[b, yy].astype(jnp.float32)
            ).astype(jnp.bfloat16)
        y_copy(b, LAST).start()

    def core_copy(b, i):
        at, size = CHUNKS[i]
        return swap_copy(
            yrecv.at[b, pl.ds(at, size)], zs1.at[pl.ds(at, size)],
            sK_s, sK_r.at[i], s, bat ^ 1,
        )

    @jax.named_scope("reduce_plane")
    def reduce_plane(b, i):
        at, size = CHUNKS[i]
        y_copy(b, i).wait_recv()
        rest = pairing(b)[1]
        for k in range(at, at + size):
            yrecv[b, k] = (
                yrecv[b, k].astype(jnp.float32) + gout[b, rest, k].astype(jnp.float32)
            ).astype(jnp.bfloat16)

        if b == 3:

            @pl.when(c == 1)
            def _():
                core_copy(b, i).start()

    def carriers(b, work):
        if b == 3:
            pl.when(c == 0)(functools.partial(work, (0, 1)))
        else:
            work((0,))

    def z_near(b, i, cc, slot):
        at, size = CHUNKS[i]
        return swap_copy(
            (yrecv.at[b], zs1)[cc].at[pl.ds(at, size), z ^ (3 if slot else 1)],
            zrecv.at[b + cc, slot, pl.ds(at, size)], sN_s, sN_r.at[b, i], s, bat ^ 2,
        )

    def z_far(b, i, cc):
        at, size = CHUNKS[i]
        return swap_copy(
            zrecv.at[b + cc, 1, pl.ds(at, size)], zrecv.at[b + cc, 2, pl.ds(at, size)],
            sT_s, sT_r.at[b, i], s, bat ^ 4,
        )

    def near_like(b, i, parts):
        at, size = CHUNKS[i]
        return zrecv.at[pl.ds(b, len(parts)), pl.ds(0, 2), pl.ds(at, size)]

    def far_like(b, i, parts):
        at, size = CHUNKS[i]
        return zrecv.at[pl.ds(b, len(parts)), 2, pl.ds(at, size)]

    @jax.named_scope("reduce_near")
    def reduce_near(b, i):
        def work(parts):
            if b == 3:
                core_copy(b, i).wait_recv()
            for slot in (1, 0):
                for cc in parts:
                    z_near(b, i, cc, slot).start()

        carriers(b, work)

    @jax.named_scope("reduce_far")
    def reduce_far(b, i):
        at, size = CHUNKS[i]

        def work(parts):
            drain(near_like(b, i, parts), sN_r.at[b, i])
            for cc in parts:
                mine = (yrecv.at[b], zs1)[cc]
                for k in range(at, at + size):
                    zrecv[b + cc, 1, k] = (
                        zrecv[b + cc, 1, k].astype(jnp.float32) + mine[k, z ^ 2].astype(jnp.float32)
                    ).astype(jnp.bfloat16)
                z_far(b, i, cc).start()

        carriers(b, work)

    def deliver(b, i, cc, section, core):
        at, size = CHUNKS[i]
        swap_copy(
            zrecv.at[b + cc, 0, pl.ds(at, size)], gfin.at[pl.ds(at, size), s],
            sG_s, sG_r.at[s], section, 2 * z + core,
        ).start()

    def send_squares(b):
        def to(j):
            return swap_copy(
                sq_own.at[b], sq_in.at[s, bat], sW_s, sW_r, b, bat ^ j
            )

        sq_own[b] = jnp.concatenate([fold(sq_acc[b, 1:2]), fold(sq_acc[b, 0:1])], axis=0)

        @pl.when(b != s)
        def _():
            to(0).start()

        @pl.when(b == s)
        def _():
            sq_in[s, bat] = sq_own[b]

        for j in range(1, 8):
            to(j).start()

    @jax.named_scope("finish")
    def finish(b, i):
        at, size = CHUNKS[i]

        def work(parts):
            drain(far_like(b, i, parts), sT_r.at[b, i])
            squares = jnp.zeros((1, D), jnp.float32)
            for cc in parts:
                mine = (yrecv.at[b], zs1)[cc]
                for k in range(at, at + size):
                    done = (
                        zrecv[b + cc, 0, k].astype(jnp.float32)
                        + zrecv[b + cc, 2, k].astype(jnp.float32)
                        + mine[k, z].astype(jnp.float32)
                    ).astype(jnp.bfloat16)
                    zrecv[b + cc, 0, k] = done
                    squares += square(done.astype(jnp.float32))

                @pl.when(b != s)
                def _():
                    deliver(b, i, cc, b, cc if b == 3 else c)

                @pl.when(b == s)
                def _():
                    if cc == 0:
                        for k in range(at, at + size):
                            gfin[k, s] = zrecv[b, 0, k]
                    else:
                        deliver(b, i, 1, s, 1)

            row = 1 if i == LAST else 0
            sq_acc[b, row : row + 1] = squares + (0.0 if i in (0, LAST) else sq_acc[b, row : row + 1])
            if i == LAST:
                send_squares(b)

        carriers(b, work)

    @jax.named_scope("backward")
    def backward(bi):
        b = 3 - bi
        e = 9 + 2 * bi
        u = 2 * pairing(b)[0] + c
        first_sum = jnp.zeros((1, D), jnp.float32)
        second_sum = jnp.zeros((1, D), jnp.float32)
        for i in range(0, R, 64):
            du = valid[i : i + 64] * g[i : i + 64] * sv[b, 3, i : i + 64].astype(jnp.float32)
            zbuf[i : i + 64] = du
            first_sum += jnp.sum(du, 0, keepdims=True)
            second_sum += jnp.sum(du * sv[b, 2, i : i + 64].astype(jnp.float32), 0, keepdims=True)
        sums_start(e, first_sum, second_sum)

        @pl.when(bi == 0)
        def _():
            close_gather()

        @pl.when(bi == 3)
        def _():
            reduce_near(3, 1)

        @pl.when(bi > 0)
        def _():
            forward_dz(b + 1)
            grad_point(b + 1)

        @pl.when(bi == 2)
        def _():
            pair_point(3)

        @pl.when(bi == 3)
        def _():
            reduce_plane(3, 2)
            reduce_far(3, 0)

        total_first, total_second = sums_finish(e)
        for i in range(0, R, 64):
            xhat = sv[b, 2, i : i + 64].astype(jnp.float32)
            inner = zbuf[i : i + 64] - valid[i : i + 64] * (
                (total_first + xhat * total_second) / row_count
            )
            dzq[b, u, i : i + 64] = (gi[b, 1:2] * inner).astype(jnp.bfloat16)
        send_dz(b)
        gsend[b, 2:3] = total_second
        gsend[b, 3:4] = total_first
        d_two = dzq[b, u]
        for k in range(9):
            Hb[:, k * D : (k + 1) * D] = jnp.dot(
                Gm[c, pl.ds((8 - k) * R, R)], d_two, preferred_element_type=jnp.float32
            ).astype(jnp.bfloat16)
        mixed = None
        for k in range(9):
            part = lax.dot_general(
                Hb[:, k * D : (k + 1) * D], W[b, k].reshape(D, D), NT,
                preferred_element_type=jnp.float32,
            )
            mixed = part if mixed is None else mixed + part
        zbuf[...] = mixed
        first_sum = jnp.zeros((1, D), jnp.float32)
        second_sum = jnp.zeros((1, D), jnp.float32)
        for i in range(0, R, 64):
            du = zbuf[i : i + 64] * sv[b, 1, i : i + 64].astype(jnp.float32)
            zbuf[i : i + 64] = du
            first_sum += jnp.sum(du, 0, keepdims=True)
            second_sum += jnp.sum(du * sv[b, 0, i : i + 64].astype(jnp.float32), 0, keepdims=True)
        sums_start(e + 1, first_sum, second_sum)

        @pl.when(bi == 2)
        def _():
            reduce_plane(3, 0)
            reduce_near(3, 0)

        @pl.when(bi == 3)
        def _():
            reduce_near(3, 2)
            reduce_far(3, 1)
            reduce_plane(2, 0)
            reduce_near(2, 0)

        @pl.when(bi > 0)
        def _():
            grad_spatial(b + 1)

        @pl.when(bi == 2)
        def _():
            reduce_plane(3, 1)

        @pl.when(bi == 3)
        def _():
            reduce_plane(3, 3)
            reduce_plane(2, 1)
            reduce_near(2, 1)

        total_first, total_second = sums_finish(e + 1)
        for i in range(0, R, 64):
            xhat = sv[b, 0, i : i + 64].astype(jnp.float32)
            inner = zbuf[i : i + 64] - valid[i : i + 64] * (
                (total_first + xhat * total_second) / row_count
            )
            dz1q[b, c, i : i + 64] = (gi[b, 0:1] * inner).astype(jnp.bfloat16)
        dz_one_copy(b).start()
        gsend[b, 0:1] = total_second
        gsend[b, 1:2] = total_first
        g[...] = g[...] + lax.dot_general(
            dz1q[b, c], W[b, 9].reshape(D, D), NT, preferred_element_type=jnp.float32
        )

        @pl.when(b == s)
        def _():
            gaff[s] = gsend[b]

        @pl.when(b != s)
        def _():
            swap_copy(gsend.at[b], gaff.at[s], sO_s.at[3], sO_r, b, bat).start()

    @pl.loop(0, 4)
    def _(bi):
        backward(bi)

    out_grad_in = pltpu.make_async_copy(g, in_grad.at[0], sO_s.at[1])
    out_grad_in.start()

    reduce_near(3, 3)
    forward_dz(0)
    pair_point(2)
    reduce_far(2, 0)
    reduce_far(3, 2)
    reduce_plane(2, 2)
    reduce_near(2, 2)
    grad_spatial(0)
    reduce_far(2, 1)
    grad_point(0)
    reduce_far(3, 3)
    pair_point(1)
    finish(3, 0)
    reduce_plane(2, 3)
    reduce_near(2, 3)
    reduce_plane(1, 0)
    reduce_near(1, 0)
    finish(3, 1)
    reduce_far(2, 2)
    finish(2, 0)
    reduce_plane(1, 1)
    reduce_near(1, 1)
    finish(3, 2)
    reduce_far(1, 0)
    reduce_plane(1, 2)
    reduce_near(1, 2)
    finish(3, 3)
    finish(2, 1)
    pair_point(0)
    reduce_far(2, 3)
    reduce_plane(0, 0)
    reduce_near(0, 0)
    reduce_far(1, 1)
    reduce_plane(1, 3)
    reduce_near(1, 3)
    finish(2, 2)
    finish(1, 0)
    reduce_far(1, 2)
    reduce_plane(0, 1)
    reduce_near(0, 1)
    reduce_plane(0, 2)
    reduce_near(0, 2)
    reduce_far(0, 0)
    reduce_plane(0, 3)
    reduce_near(0, 3)
    finish(2, 3)
    finish(1, 1)
    reduce_far(1, 3)
    reduce_far(0, 1)
    finish(0, 0)
    finish(1, 2)
    reduce_far(0, 2)
    reduce_far(0, 3)
    finish(1, 3)
    finish(0, 1)
    close_rest()
    finish(0, 2)
    finish(0, 3)
    for d in range(1, 4):
        drain(gfin.at[:, s ^ d], sG_r.at[s ^ d])

    @pl.when((c == 1) & (s == 3))
    def _():
        drain(gfin.at[:, s], sG_r.at[s])

    grads_out = pltpu.make_async_copy(gfin, grads, sO_s.at[2])
    grads_out.start()

    drain(gaff.at[pl.ds(0, 3)], sO_r)
    affine_out[...] = gaff[0] + gaff[1] + gaff[2] + gaff[3]
    squares_in = sq_in.reshape(32, 2, 128)

    @pl.when(s != 3)
    def _():
        drain(squares_in.at[pl.ds(0, 31)], sW_r)

    @pl.when((s == 3) & (c == 0))
    def _():
        drain(squares_in.at[pl.ds(0, 15)], sW_r)

    @pl.when((s == 3) & (c == 1))
    def _():
        drain(squares_in.at[pl.ds(0, 16)], sW_r)

    totals_out[...] = jnp.concatenate(
        [fold(psq[...]), jnp.sum(squares_in[...], axis=0), jnp.zeros((4, 128), jnp.float32)], axis=0
    )

    with jax.named_scope("close_last"):
        sums_close(0)
        sums_close(1)

        @pl.when(c == 0)
        def _():
            drain(zrecv.at[pl.ds(0, 4), 0], sG_s)

        @pl.when(c == 0)
        def _():
            drain(squares_in.at[pl.ds(0, 31)], sW_s)

        @pl.when((c == 1) & (s == 3))
        def _():
            drain(zrecv.at[pl.ds(0, 3), 0], sG_s)
            drain(squares_in.at[pl.ds(0, 24)], sW_s)

        @pl.when((c == 1) & (s != 3))
        def _():
            drain(zrecv.at[pl.ds(0, 2), 0], sG_s)
            drain(squares_in.at[pl.ds(0, 23)], sW_s)

    with jax.named_scope("close_outputs"):
        grads_out.wait()
        out_features.wait()
        out_grad_in.wait()


def lars_kernel(
    feat, ing, grads_in, totals_in, affine_in, w_point, w_spatial, norm_in, mom_point, mom_spatial, mom_norm,
    features, in_grad, new_point, new_spatial, new_norm, new_mom_point, new_mom_spatial, new_mom_norm,
    P, M, G, feat_rows, grad_rows, totals, affine_grad, affine, affine_mom, sem, out_sem,
):
    THIRDS = 3
    small = [
        (totals_in, totals), (affine_in, affine_grad), (norm_in.at[0], affine), (mom_norm.at[0], affine_mom),
        (w_point.at[0], P.at[9]), (mom_point.at[0], M.at[9]), (grads_in.at[9], G.at[9]),
    ]
    large = []
    for i in range(THIRDS):
        taps = pl.ds(3 * i, 3)
        large += [
            (grads_in.at[taps], G.at[taps]), (w_spatial.at[0, taps], P.at[taps]),
            (mom_spatial.at[0, taps], M.at[taps]),
        ]
    rows = [(feat, feat_rows), (ing, grad_rows)]
    loads = [
        pltpu.make_async_copy(a, b, sem.at[i]) for i, (a, b) in enumerate(small + large + rows)
    ]
    for load in loads:
        load.start()
    for load in loads[: len(small)]:
        load.wait()
    D = affine.shape[1]
    rate = BASE_RATE * (STEP + 1) / WARMUP
    point_sq, spatial_sq, gpoint_sq, gspatial_sq = [
        jnp.sum(totals[i : i + 1], axis=1, keepdims=True) for i in range(4)
    ]
    step_point = rate * TRUST_COEF * jnp.sqrt(point_sq) / (jnp.sqrt(gpoint_sq) + EPS_NORM)
    step_spatial = rate * TRUST_COEF * jnp.sqrt(spatial_sq) / (jnp.sqrt(gspatial_sq) + EPS_NORM)
    outs = []

    def store(source, target):
        outs.append(pltpu.make_async_copy(source, target, out_sem.at[len(outs)]))
        outs[-1].start()

    def move(k, step):
        moved = MOMENTUM * M[k] + step * G[k].astype(jnp.float32).reshape(64, D)
        M[k] = moved
        P[k] = P[k] - moved

    for i in range(THIRDS):
        for load in loads[len(small) + 3 * i :][:3]:
            load.wait()
        for k in range(3 * i, 3 * i + 3):
            move(k, step_spatial)
        taps = pl.ds(3 * i, 3)
        store(M.at[taps], new_mom_spatial.at[0, taps])
        store(P.at[taps], new_spatial.at[0, taps])
    move(9, step_point)
    store(M.at[9], new_mom_point.at[0])
    store(P.at[9], new_point.at[0])
    for load, source, target in zip(loads[-2:], (feat_rows, grad_rows), (features, in_grad)):
        load.wait()
        store(source, target)
    grad = affine_grad[0:4]
    old = affine[...]
    affine_sq = jnp.sum(old * old, axis=1, keepdims=True)
    gaffine_sq = jnp.sum(grad * grad, axis=1, keepdims=True)
    trust = TRUST_COEF * jnp.sqrt(affine_sq) / (jnp.sqrt(gaffine_sq) + EPS_NORM)
    moved = MOMENTUM * affine_mom[...] + rate * trust * grad
    affine_mom[...] = moved
    affine[...] = old - moved
    store(affine_mom, new_mom_norm.at[0])
    store(affine, new_norm.at[0])
    for copy in outs:
        copy.wait()


def train_step(images, crop, w_point, w_spatial, norm_params, mom_point, mom_spatial, mom_norm, out_grad):
    R, D = images.shape[1:]
    f32, bf16 = jnp.float32, jnp.bfloat16
    dma = pltpu.SemaphoreType.DMA
    anywhere = pl.BlockSpec(memory_space=pl.ANY)
    vmem = pl.BlockSpec(memory_space=pltpu.VMEM)
    hbm = pl.BlockSpec(memory_space=pltpu.HBM)
    smem = pl.BlockSpec(memory_space=pltpu.SMEM)
    V = pltpu.VMEM
    scratch = dict(
        W=V((4, TAPS, 8, 4, 16, D), bf16), wown=V((TAPS, 4, 16, D), bf16),
        F=V((3 * R, D), f32),
        sv=V((4, 4, R, D), bf16), gi=V((4, 8, D), f32),
        abuf=V((R, D), bf16),
        Gm=V((6, 9 * R, R), bf16), caq=V((4, 2, 4, 8, 16, R), bf16),
        stage=V((4, 4, 8, 16, R), bf16), stage_a=V((4, 8, 16, R), bf16), Hb=V((R, 9 * D), bf16),
        dzq=V((4, 4, R, D), bf16), dz1q=V((4, 2, R, D), bf16),
        pgrad=V((4, 2, 2, 4, 16, D), bf16), precv=V((4, 2, 4, 16, D), bf16),
        gout=V((4, 2, TAPS, 4, 16, D), bf16), yrecv=V((4, TAPS, 4, 16, D), bf16),
        zs1=V((TAPS, 4, 16, D), bf16), zrecv=V((5, 3, TAPS, 16, D), bf16),
        gfin=V((TAPS, 4, 16, D), bf16),
        sq_in=V((4, 8, 2, 128), f32), sq_own=V((4, 2, 128), f32), sq_acc=V((4, 8, D), f32), psq=V((2, D), f32),
        aff=V((4, 8, D), f32), gaff=V((4, 8, D), f32), gsend=V((4, 8, D), f32),
        st_in=V((17, 8, 128), f32), st_own=V((17, 8, 128), f32), st_all=V((17, 4, 8, 128), f32),
        cnt=V((8, 8, 128), f32), cntx=V((6, 8, 128), f32), cown=V((8, 128), f32),
        sL=dma((3,)), sS_s=dma, sS_r=dma((4,)), sU_s=dma, sU_r=dma((4,)), sV_s=dma, sV_r=dma((4, 2)),
        sJ_s=dma, sJ_r=dma((4,)), sZ_s=dma, sZ_r=dma((4, 4)),
        sH_s=dma, sH_r=dma((4, 4)), sA_s=dma, sA_r=dma((4, 4)),
        sB_r=dma((4, 2)), sD_r=dma((4,)),
        sE_in_s=dma((2,)), sE_in_r=dma((2,)), sE_s=dma((2,)), sE_r=dma((2,)),
        sC_s=dma, sC_r=dma((2,)), sF_s=dma, sF_r=dma,
        sQ_s=dma((2,)), sQ_r=dma((4, 2)), sX_s=dma, sX_r=dma((4, 2)), sM_s=dma, sM_r=dma((4,)), sP_s=dma, sP_r=dma((4,)),
        sW_s=dma, sW_r=dma,
        sY_s=dma, sY_r=dma((4, 4)), sK_s=dma, sK_r=dma((4,)),
        sN_s=dma, sN_r=dma((4, 4)), sT_s=dma, sT_r=dma((4, 4)), sG_s=dma, sG_r=dma((4,)),
        sO_s=dma((4,)), sO_r=dma,
    )
    shape = jax.ShapeDtypeStruct
    feat, ing, grads, totals, affine_grad = pl.pallas_call(
        train_kernel,
        out_shape=(
            shape((1, R, D), f32), shape((1, R, D), f32), shape((TAPS, 4, 16, D), bf16),
            shape((8, 128), f32), shape((8, D), f32),
        ),
        in_specs=[anywhere, smem, anywhere, anywhere, vmem, anywhere],
        out_specs=(anywhere, anywhere, anywhere, vmem, vmem),
        scratch_shapes=list(scratch.values()),
        compiler_params=pltpu.CompilerParams(
            collective_id=0, has_side_effects=True, vmem_limit_bytes=64 * 1024 * 1024
        ),
    )(images, crop.T, w_point, w_spatial, norm_params, out_grad)
    return pl.pallas_call(
        lars_kernel,
        out_shape=(
            shape((1, R, D), f32), shape((1, R, D), f32),
            shape(w_point.shape, f32), shape(w_spatial.shape, f32), shape(norm_params.shape, f32),
            shape(w_point.shape, f32), shape(w_spatial.shape, f32), shape(norm_params.shape, f32),
        ),
        in_specs=[hbm] * 11,
        out_specs=(hbm,) * 8,
        scratch_shapes=[
            V((TAPS, 64, D), f32), V((TAPS, 64, D), f32), V((TAPS, 4, 16, D), bf16), V((1, R, D), f32),
            V((1, R, D), f32), V((8, 128), f32), V((8, D), f32), V((4, D), f32), V((4, D), f32), dma((18,)), dma((12,)),
        ],
        compiler_params=pltpu.CompilerParams(vmem_limit_bytes=64 * 1024 * 1024),
    )(feat, ing, grads, totals, affine_grad, w_point, w_spatial, norm_params, mom_point, mom_spatial, mom_norm)


def solution(mesh):
    tuned = mesh.shape["section"] == 4 and mesh.shape["batch"] == 8
    return jax.shard_map(
        train_step if tuned else on_device,
        mesh=mesh,
        in_specs=(
            P(None, "batch", None),
            P(None, "batch"),
            P("section", "batch", None),
            P("section", None, "batch", None),
            P("section", None, None),
            P("section", "batch", None),
            P("section", None, "batch", None),
            P("section", None, None),
            P(None, "batch", None),
        ),
        out_specs=(
            P("section", "batch", None),
            P("section", "batch", None),
            P("section", "batch", None),
            P("section", None, "batch", None),
            P("section", None, None),
            P("section", "batch", None),
            P("section", None, "batch", None),
            P("section", None, None),
        ),
        check_vma=False,
    )
```

```python
import functools

import jax
import jax.numpy as jnp
from jax import lax
from jax.experimental import pallas as pl
from jax.experimental.pallas import tpu as pltpu
from jax.sharding import PartitionSpec as P

BIG_SIDE = 7
SMALL_SIDE = 3
WARMUP = 20
STEP = 9


EPS = 1e-05
EPS_NORM = 1e-06
BASE_RATE = 6.0
MOMENTUM = 0.9
TRUST_COEF = 0.1


def from_behind(block, axis, distance):
    devices = range(lax.axis_size(axis))
    route = [(i - distance, i) for i in devices if i - distance in devices]
    return lax.ppermute(block, axis, route)


def crop_table(big_count, total_rows):
    places = jnp.arange(total_rows, dtype=jnp.int32)
    big_area = BIG_SIDE * BIG_SIDE
    small_area = SMALL_SIDE * SMALL_SIDE
    big_rows = big_count * big_area
    small_rows = (total_rows - big_rows) // small_area * small_area
    in_big = places < big_rows
    offsets = places - big_rows
    sides = jnp.where(in_big, BIG_SIDE, SMALL_SIDE)
    within = jnp.where(in_big, places % big_area, offsets % small_area)
    starts = places - within
    valid_rows = places < big_rows + small_rows
    row_pos = within // sides
    col_pos = within % sides
    indices = []
    masks = []
    for row_step in (-1, 0, 1):
        for col_step in (-1, 0, 1):
            new_row = row_pos + row_step
            new_col = col_pos + col_step
            inside = (
                valid_rows & (new_row >= 0) & (new_row < sides) & (new_col >= 0) & (new_col < sides)
            )
            indices.append(jnp.where(inside, starts + new_row * sides + new_col, places))
            masks.append(inside)
    return (
        jnp.stack(indices, 1),
        jnp.stack(masks, 1).astype(jnp.float32),
        valid_rows.astype(jnp.float32),
    )


def mish(values):
    return values * jnp.tanh(jax.nn.softplus(values))


def mish_parts(values):
    tangent = jnp.tanh(jax.nn.softplus(values))
    slope = tangent + values * jax.nn.sigmoid(values) * (1.0 - tangent * tangent)
    return (values * tangent, slope)


def mish_slope(values):
    tangent = jnp.tanh(jax.nn.softplus(values))
    return tangent + values * jax.nn.sigmoid(values) * (1.0 - tangent * tangent)


def batch_moments(proj, valid_rows):
    weighted = valid_rows[:, None] * proj
    summed, squared, row_count = lax.psum(
        (jnp.sum(weighted, 0), jnp.sum(weighted * proj, 0), jnp.sum(valid_rows)), "batch"
    )
    center = summed / row_count
    inv_std = lax.rsqrt(squared / row_count - center * center + EPS)
    return (center, inv_std, row_count)


def spatial_apply(source, tap_index, tap_mask, weights):
    stacked = source[tap_index] * tap_mask[:, :, None].astype(source.dtype)
    result = lax.dot_general(
        stacked, weights, (((1, 2), (0, 1)), ((), ())), preferred_element_type=jnp.float32
    )
    return (result, stacked)


def forward_block(hidden, point_low, spatial_low, affine, tap_index, tap_mask, valid_rows):
    proj_one = jnp.dot(hidden.astype(jnp.bfloat16), point_low, preferred_element_type=jnp.float32)
    center_one, inv_one, row_count = batch_moments(proj_one, valid_rows)
    mixed_one = mish(affine[0] * ((proj_one - center_one) * inv_one) + affine[1])
    proj_two, stacked = spatial_apply(
        mixed_one.astype(jnp.bfloat16), tap_index, tap_mask, spatial_low
    )
    center_two, inv_two, count_two = batch_moments(proj_two, valid_rows)
    mixed_two = mish(affine[2] * ((proj_two - center_two) * inv_two) + affine[3])
    moments = jnp.stack([center_one, inv_one, center_two, inv_two])
    return (hidden + valid_rows[:, None] * mixed_two, moments, row_count)


def norm_back(d_value, normed, inv_std, gain, valid_rows, row_count):
    first_sum, second_sum = lax.psum((jnp.sum(d_value, 0), jnp.sum(d_value * normed, 0)), "batch")
    d_proj = (
        gain
        * inv_std
        * (d_value - valid_rows[:, None] * (first_sum + normed * second_sum) / row_count)
    )
    return (d_proj.astype(jnp.bfloat16), first_sum, second_sum)


def backward_block(
    hidden,
    upstream,
    point_low,
    spatial_low,
    affine,
    moments,
    row_count,
    tap_index,
    tap_mask,
    valid_rows,
):
    inputs = hidden.astype(jnp.bfloat16)
    proj_one = jnp.dot(inputs, point_low, preferred_element_type=jnp.float32)
    normed_one = (proj_one - moments[0]) * moments[1]
    mixed_one, slope_one = mish_parts(affine[0] * normed_one + affine[1])
    proj_two, stacked = spatial_apply(
        mixed_one.astype(jnp.bfloat16), tap_index, tap_mask, spatial_low
    )
    normed_two = (proj_two - moments[2]) * moments[3]
    slope_two = mish_slope(affine[2] * normed_two + affine[3])
    d_two, first_two, second_two = norm_back(
        valid_rows[:, None] * upstream * slope_two,
        normed_two,
        moments[3],
        affine[2],
        valid_rows,
        row_count,
    )
    grad_spatial = lax.dot_general(
        stacked, d_two, (((0,), (0,)), ((), ())), preferred_element_type=jnp.float32
    )
    flipped = d_two[tap_index[:, ::-1]] * tap_mask[:, ::-1, None].astype(jnp.bfloat16)
    d_mixed = lax.dot_general(
        flipped, spatial_low, (((1, 2), (0, 2)), ((), ())), preferred_element_type=jnp.float32
    )
    d_one, first_one, second_one = norm_back(
        d_mixed * slope_one, normed_one, moments[1], affine[0], valid_rows, row_count
    )
    grad_point = lax.dot_general(
        inputs, d_one, (((0,), (0,)), ((), ())), preferred_element_type=jnp.float32
    )
    d_hidden = upstream + lax.dot_general(
        d_one, point_low, (((1,), (1,)), ((), ())), preferred_element_type=jnp.float32
    )
    grad_affine = jnp.stack([second_one, first_one, second_two, first_two])
    return (d_hidden, grad_point, grad_spatial, grad_affine)


def store_slot(buffer, value, slot_index, active):
    previous = lax.dynamic_index_in_dim(buffer, slot_index, 0, keepdims=False)
    return lax.dynamic_update_index_in_dim(
        buffer, jnp.where(active, value, previous), slot_index, 0
    )


def lars_update(param, grad, momentum, param_sq, grad_sq, rate):
    trust = TRUST_COEF * jnp.sqrt(param_sq) / (jnp.sqrt(grad_sq) + EPS_NORM)
    new_mom = MOMENTUM * momentum + rate * trust * grad
    return (param - new_mom, new_mom)


def on_device(
    images, crop_big, w_point, w_spatial, norm_params, mom_point, mom_spatial, mom_norm, out_grad
):
    section_count = lax.axis_size("section")
    section_rank = lax.axis_index("section")
    micro_count = images.shape[0]
    total_rows = images.shape[1]
    width = images.shape[2]
    point = w_point[0]
    spatial = w_spatial[0]
    affine = norm_params[0]
    crop_counts = crop_big[:, 0]
    turns = micro_count + section_count - 1
    point_low, spatial_low = (
        lax.all_gather(point.astype(jnp.bfloat16), "batch", axis=0, tiled=True),
        lax.all_gather(spatial.astype(jnp.bfloat16), "batch", axis=1, tiled=True),
    )
    kept_inputs = jnp.zeros((micro_count, total_rows, width), jnp.float32)
    kept_moments = jnp.zeros((micro_count, 4, width), jnp.float32)
    kept_counts = jnp.zeros((micro_count,), jnp.float32)
    results = jnp.zeros((micro_count, total_rows, width), jnp.float32)
    incoming = jnp.zeros((total_rows, width), jnp.float32)
    for phase_turn in range(turns):
        slot_raw = phase_turn - section_rank
        active = (slot_raw >= 0) & (slot_raw < micro_count)
        slot_index = jnp.clip(slot_raw, 0, micro_count - 1)
        fresh_rows = lax.dynamic_index_in_dim(images, slot_index, 0, keepdims=False).astype(
            jnp.float32
        )
        hidden = jnp.where(section_rank == 0, fresh_rows, incoming)
        tap_index, tap_mask, valid_rows = crop_table(crop_counts[slot_index], total_rows)
        output, moments, row_count = forward_block(
            hidden, point_low, spatial_low, affine, tap_index, tap_mask, valid_rows
        )
        kept_inputs = store_slot(kept_inputs, hidden, slot_index, active)
        kept_moments = store_slot(kept_moments, moments, slot_index, active)
        kept_counts = store_slot(kept_counts, row_count, slot_index, active)
        results = store_slot(
            results, output, slot_index, active & (section_rank == section_count - 1)
        )
        if phase_turn + 1 < turns:
            incoming = from_behind(output.astype(jnp.bfloat16), "section", 1).astype(output.dtype)
    point_low, spatial_low = (
        lax.all_gather(point.astype(jnp.bfloat16), "batch", axis=0, tiled=True),
        lax.all_gather(spatial.astype(jnp.bfloat16), "batch", axis=1, tiled=True),
    )
    grad_point = jnp.zeros((width, width), jnp.float32)
    grad_spatial = jnp.zeros((9, width, width), jnp.float32)
    grad_affine = jnp.zeros((4, width), jnp.float32)
    collected = jnp.zeros((micro_count, total_rows, width), jnp.float32)
    returning = jnp.zeros((total_rows, width), jnp.float32)
    for phase_turn in range(turns):
        slot_raw = micro_count - 1 - phase_turn + (section_count - 1 - section_rank)
        active = (slot_raw >= 0) & (slot_raw < micro_count)
        slot_index = jnp.clip(slot_raw, 0, micro_count - 1)
        seeded = lax.dynamic_index_in_dim(out_grad, slot_index, 0, keepdims=False).astype(
            jnp.float32
        )
        upstream = jnp.where(section_rank == section_count - 1, seeded, returning)
        upstream = jnp.where(active, upstream, 0.0)
        tap_index, tap_mask, valid_rows = crop_table(crop_counts[slot_index], total_rows)
        hidden = lax.dynamic_index_in_dim(kept_inputs, slot_index, 0, keepdims=False)
        moments = lax.dynamic_index_in_dim(kept_moments, slot_index, 0, keepdims=False)
        row_count = lax.dynamic_index_in_dim(kept_counts, slot_index, 0, keepdims=False)
        d_hidden, part_point, part_spatial, part_affine = backward_block(
            hidden,
            upstream,
            point_low,
            spatial_low,
            affine,
            moments,
            row_count,
            tap_index,
            tap_mask,
            valid_rows,
        )
        grad_point = grad_point + part_point
        grad_spatial = grad_spatial + part_spatial
        grad_affine = grad_affine + part_affine
        collected = store_slot(collected, d_hidden, slot_index, active & (section_rank == 0))
        if phase_turn + 1 < turns:
            returning = from_behind(d_hidden.astype(jnp.bfloat16), "section", -1).astype(
                d_hidden.dtype
            )
    point_grad, spatial_grad = (
        lax.psum_scatter(grad_point, "batch", scatter_dimension=0, tiled=True),
        lax.psum_scatter(grad_spatial, "batch", scatter_dimension=1, tiled=True),
    )
    point_sq, spatial_sq, gpoint_sq, gspatial_sq = lax.psum(
        (
            jnp.sum(point * point),
            jnp.sum(spatial * spatial),
            jnp.sum(point_grad * point_grad),
            jnp.sum(spatial_grad * spatial_grad),
        ),
        "batch",
    )
    rate = BASE_RATE * (STEP + 1) / WARMUP
    new_point, new_mom_point = lars_update(
        point, point_grad, mom_point[0], point_sq, gpoint_sq, rate
    )
    new_spatial, new_mom_spatial = lars_update(
        spatial, spatial_grad, mom_spatial[0], spatial_sq, gspatial_sq, rate
    )
    affine_sq = jnp.sum(affine * affine, 1, keepdims=True)
    gaffine_sq = jnp.sum(grad_affine * grad_affine, 1, keepdims=True)
    new_affine, new_mom_affine = lars_update(
        affine, grad_affine, mom_norm[0], affine_sq, gaffine_sq, rate
    )
    sent_out = jnp.where(section_rank == section_count - 1, results, 0.0)
    sent_back = jnp.where(section_rank == 0, collected, 0.0)
    got_out, got_back = (
        lax.all_to_all(
            sent_out.astype(jnp.bfloat16), "section", split_axis=0, concat_axis=0, tiled=True
        ).astype(sent_out.dtype),
        lax.all_to_all(
            sent_back.astype(jnp.bfloat16), "section", split_axis=0, concat_axis=0, tiled=True
        ).astype(sent_back.dtype),
    )
    features = got_out[section_count - 1 : section_count]
    in_grad = got_back[0:1]
    return (
        features,
        in_grad,
        new_point[None],
        new_spatial[None],
        new_affine[None],
        new_mom_point[None],
        new_mom_spatial[None],
        new_mom_affine[None],
    )


def swap_copy(source, target, sent, landed, section, batch):
    return pltpu.make_async_remote_copy(
        src_ref=source,
        dst_ref=target,
        send_sem=sent,
        recv_sem=landed,
        device_id=(section, batch),
        device_id_type=pl.DeviceIdType.MESH,
    )


def drain(like, sem):
    pltpu.make_async_copy(like, like, sem).wait()


def mish_terms(v):
    e = jnp.exp(jnp.minimum(v, 20.0))
    w = e * (e + 2.0)
    r = 1.0 / (w + 2.0)
    t = w * r
    return v * t, t + v * (4.0 * e * (1.0 + e)) * (r * r)


def pack(first, second):
    parts = [v[:, i * 128 : (i + 1) * 128] for v in (first, second) for i in range(4)]
    return jnp.concatenate(parts, axis=0)


def unpack(tile):
    rows = [tile[i : i + 1] for i in range(8)]
    return jnp.concatenate(rows[:4], axis=1), jnp.concatenate(rows[4:], axis=1)


def fold(row):
    return sum(row[:, i * 128 : (i + 1) * 128] for i in range(4))


def crop_codes(places, big, total_rows):
    big_area = float(BIG_SIDE * BIG_SIDE)
    small_area = float(SMALL_SIDE * SMALL_SIDE)
    big_rows = big * big_area
    small_rows = jnp.floor((total_rows - big_rows + 0.5) / small_area) * small_area
    in_big = places < big_rows
    offset = jnp.where(in_big, places, places - big_rows)
    area = jnp.where(in_big, big_area, small_area)
    side = jnp.where(in_big, float(BIG_SIDE), float(SMALL_SIDE))
    crop = jnp.floor((offset + 0.5) / area)
    within = offset - crop * area
    row = jnp.floor((within + 0.5) / side)
    col = within - row * side
    crop = jnp.where(in_big, crop, crop + big)
    return crop * 1024.0 + (row + 1.0) * 32.0 + (col + 1.0), places < big_rows + small_rows


NT = (((1,), (1,)), ((), ()))
TAPS = 10
WHOLE = 2
HALF = (TAPS - WHOLE) // 2


def train_kernel(
    images, crop, w_point, w_spatial, norm_in, out_grad,
    features, in_grad, grads, totals_out, affine_out,
    W, wown, F, sv, gi, abuf, Gm, caq, stage, stage_a, Hb, dzq, dz1q, pgrad, precv, gout, yrecv,
    zs1, zrecv, gfin, sq_in, sq_own, sq_acc, psq, aff, gaff, gsend, st_in, st_own, st_all, cnt, cntx, cown,
    sL, sS_s, sS_r, sU_s, sU_r, sV_s, sV_r, sJ_s, sJ_r, sZ_s, sZ_r, sH_s, sH_r, sA_s, sA_r, sB_r, sD_r,
    sE_in_s, sE_in_r, sE_s, sE_r, sC_s, sC_r, sF_s, sF_r, sQ_s, sQ_r, sX_s, sX_r, sM_s, sM_r, sP_s, sP_r,
    sW_s, sW_r, sY_s, sY_r, sK_s, sK_r, sN_s, sN_r, sT_s, sT_r, sG_s, sG_r, sO_s, sO_r,
):
    s = lax.axis_index("section")
    bat = lax.axis_index("batch")
    z = bat // 2
    c = lax.rem(bat, 2)
    x = lax.rem(s, 2)
    y = s // 2
    R, D = abuf.shape
    h = F.at[pl.ds(0, R)]
    g = F.at[pl.ds(R, R)]
    zbuf = F.at[pl.ds(2 * R, R)]

    loads = [
        pltpu.make_async_copy(w_point.at[0], F.at[pl.ds(9 * 64, 64)], sL.at[0]),
        *[
            pltpu.make_async_copy(w_spatial.at[0, k], F.at[pl.ds(k * 64, 64)], sL.at[0])
            for k in range(9)
        ],
        pltpu.make_async_copy(images.at[s], abuf, sL.at[1]),
    ]
    for load in loads:
        load.start()

    barrier = pltpu.get_barrier_semaphore()
    greet = [(s, bat ^ j) for j in range(1, 8)]
    greet += [(s ^ d, bat ^ j) for d in range(1, 4) for j in range(2)]
    for sec, other in greet:
        pl.semaphore_signal(
            barrier, inc=1, device_id=(sec, other), device_id_type=pl.DeviceIdType.MESH
        )

    def square(rows):
        return jnp.sum(rows * rows, 0, keepdims=True)

    spatial_squares = jnp.zeros((1, D), jnp.float32)
    drain(F.at[pl.ds(0, 64 * TAPS)], sL.at[0])
    for k in range(TAPS):
        rows = F[k * 64 : k * 64 + 64]
        wown[k] = rows.astype(jnp.bfloat16).reshape(4, 16, D)
        if k < 9:
            spatial_squares += square(rows)
        else:
            point_squares = square(rows)
    sq_in[...] = jnp.zeros_like(sq_in)
    with jax.named_scope("greet"):
        pl.semaphore_wait(barrier, len(greet))

    cown[...] = jnp.full((8, 128), crop[0, s].astype(jnp.float32))
    aff[s] = jnp.concatenate([norm_in[0], jnp.zeros((4, D), jnp.float32)], axis=0)
    cnt[bat] = cown[...]
    cntx[c] = cown[...]
    for j in range(1, 8):
        swap_copy(cown, cnt.at[bat], sC_s, sC_r.at[0], s, bat ^ j).start()
    for j in range(2):
        for near in (1, 2):
            swap_copy(cown, cntx.at[2 * near + c], sC_s, sC_r.at[1], s ^ near, bat ^ j).start()
    for d in range(1, 4):
        swap_copy(aff.at[s], aff.at[s], sF_s, sF_r, s ^ d, bat).start()

    def scatter(d):
        q = s ^ d
        return swap_copy(
            wown.at[split, q], W.at[s, split, bat, q], sS_s, sS_r.at[s], q, 2 * z
        )

    def scatter_whole(d):
        return swap_copy(
            wown.at[whole], W.at[s, whole, bat], sU_s, sU_r.at[s], s ^ d, 2 * z
        )

    split, whole = pl.ds(0, 2 * HALF), pl.ds(2 * HALF, WHOLE)
    for send in (scatter, scatter_whole):
        for d in range(1, 4):
            send(d).start()

        @pl.when(c == 1)
        def _():
            send(0).start()

    @pl.when(c == 0)
    def _():
        pltpu.make_async_copy(wown.at[split, s], W.at[s, split, bat, s], sS_r.at[s]).start()
        pltpu.make_async_copy(wown.at[whole], W.at[s, whole, bat], sU_r.at[s]).start()

    @jax.named_scope("sums_start")
    def sums_start(e, first_sum, second_sum):
        slot = lax.rem(e, 2)
        st_own[e] = pack(first_sum, second_sum)
        to_core = swap_copy(st_own.at[e], st_in.at[e], sE_in_s.at[slot], sE_in_r.at[slot], s, bat ^ 1)

        if not isinstance(e, int):

            @pl.when(e > 1)
            def _():
                sums_close(e)

        @pl.when(c == 0)
        def _():
            to_core.start()

        @pl.when(c == 1)
        def _():
            to_core.wait_recv()
            st_all[e, z] = st_own[e] + st_in[e]
            for j in (7, 6, 5, 4, 3, 2, 1):
                swap_copy(
                    st_all.at[e, z], st_all.at[e, z], sE_s.at[slot], sE_r.at[slot], s, bat ^ j
                ).start()

    @jax.named_scope("sums_finish")
    def sums_finish(e):
        slot = lax.rem(e, 2)

        @pl.when(c == 0)
        def _():
            drain(st_all.at[e], sE_r.at[slot])

        @pl.when(c == 1)
        def _():
            drain(st_all.at[e, pl.ds(0, 3)], sE_r.at[slot])

        return unpack(st_all[e, 0] + st_all[e, 1] + st_all[e, 2] + st_all[e, 3])

    def sums_close(e):
        slot = lax.rem(e, 2)

        @pl.when(c == 0)
        def _():
            drain(st_own.at[0], sE_in_s.at[slot])

        @pl.when(c == 1)
        def _():
            drain(cnt.at[pl.ds(0, 7)], sE_s.at[slot])

    sums_start(0, point_squares, spatial_squares)

    half = pl.ds(HALF * c, HALF)
    first = jnp.where(c == 0, s ^ 1, s ^ 2)
    second = jnp.where(c == 0, s ^ 2, s ^ 1)
    both = s ^ 3

    def pair(b, taps, zz, q):
        return W.at[b, taps, pl.ds(2 * zz, 2), q]

    def to_sibling(b, zz):
        ref = pair(b, split, zz, s)
        return swap_copy(ref, ref, sH_s, sH_r.at[b, zz], s, bat ^ 1)

    def along_first(b, zz):
        ref = pair(b, half, zz, s)
        return swap_copy(ref, ref, sA_s, sA_r.at[b, zz], first, bat)

    def along_second(b, which, zz):
        ref = pair(b, half, zz, s if which == 0 else first)
        return swap_copy(ref, ref, sA_s, sB_r.at[b, which], second, bat)

    def quarter_to_sibling(b, which):
        ref = W.at[b, half, :, (first, second, both)[which]]
        return swap_copy(ref, ref, sA_s, sD_r.at[b], s, bat ^ 1)

    def own_ready(b, zz):
        @pl.when(c == 0)
        def _():
            to_sibling(b, zz).start()

        @pl.when(c == 1)
        def _():
            to_sibling(b, zz).wait_recv()

        along_first(b, zz).start()
        along_second(b, 0, zz).start()

    def along_z(b, zz, j):
        ref = pair(b, split, zz, s)
        return swap_copy(ref, ref, sZ_s, sZ_r.at[b, zz], s, bat ^ (2 * j))

    def whole_along_z(b, zz, j):
        ref = W.at[b, whole, pl.ds(2 * zz, 2)]
        return swap_copy(ref, ref, sV_s, sV_r.at[b, j - 1], s, bat ^ (2 * j))

    def whole_to_sibling(b, zz):
        ref = W.at[b, whole, pl.ds(2 * zz, 2)]
        return swap_copy(ref, ref, sJ_s, sJ_r.at[b], s, bat ^ 1)

    def on_first_core(work):
        pl.when(c == 0)(work)

    @jax.named_scope("own_quarter")
    def own_quarter(b):
        @on_first_core
        def _():
            drain(pair(b, split, z, s), sS_r.at[b])

        own_ready(b, z)

    @jax.named_scope("start_z")
    def start_z(b):
        @on_first_core
        def _():
            along_z(b, z, 2).start()
            along_z(b, z, 1).start()

    @jax.named_scope("start_whole")
    def start_whole(b):
        @on_first_core
        def _():
            drain(W.at[b, whole, pl.ds(2 * z, 2)], sU_r.at[b])
            whole_along_z(b, z, 2).start()
            whole_along_z(b, z, 1).start()
            whole_to_sibling(b, z).start()

    @jax.named_scope("relay_z")
    def relay_z(b):
        @on_first_core
        def _():
            drain(pair(b, split, z ^ 2, s), sZ_r.at[b, z ^ 2])
            along_z(b, z ^ 2, 1).start()

        own_ready(b, z ^ 2)

    @jax.named_scope("rest_z")
    def rest_z(b):
        for j in (1, 3):
            @on_first_core
            def _():
                drain(pair(b, split, z ^ j, s), sZ_r.at[b, z ^ j])

            own_ready(b, z ^ j)

    @jax.named_scope("relay_whole")
    def relay_whole(b):
        @on_first_core
        def _():
            drain(W.at[b, whole, pl.ds(2 * (z ^ 2), 2)], sV_r.at[b, 1])
            whole_along_z(b, z ^ 2, 1).start()
            whole_to_sibling(b, z ^ 2).start()

    @jax.named_scope("rest_whole")
    def rest_whole(b):
        @on_first_core
        def _():
            drain(W.at[b, whole, pl.ds(0, 4)], sV_r.at[b, 0])
            for j in (1, 3):
                whole_to_sibling(b, z ^ j).start()

    @jax.named_scope("gather_first")
    def gather_first(b, pieces=(0, 2, 1, 3)):
        for j in pieces:
            zz = z ^ j
            ref = pair(b, half, zz, first)
            swap_copy(ref, ref, sA_s, sA_r.at[b, zz], first, bat).wait_recv()
            along_second(b, 1, zz).start()
        if 3 in pieces:
            quarter_to_sibling(b, 0).start()

    @jax.named_scope("gather_second")
    def gather_second(b):
        for which in range(2):
            drain(W.at[b, half, :, (second, both)[which]], sB_r.at[b, which])
            quarter_to_sibling(b, 1 + which).start()

    @jax.named_scope("gather_last")
    def gather_last(b):
        other = pl.ds(HALF * (1 - c), HALF)
        drain(W.at[b, other, :, pl.ds(0, 3)], sD_r.at[b])

    for b in range(2):
        own_quarter(b)
        if b == 0:
            start_z(0)
    relay_z(0)
    start_whole(0)
    start_z(1)

    drain(cnt.at[pl.ds(0, 7)], sC_r.at[0])
    drain(cntx.at[pl.ds(2, 4)], sC_r.at[1])
    cntx[1 - c] = cnt[bat ^ 1]
    total = jnp.zeros((1, 1), jnp.float32)
    for j in range(8):
        big = cnt[j][0:1, 0:1]
        big_rows = big * float(BIG_SIDE * BIG_SIDE)
        area = float(SMALL_SIDE * SMALL_SIDE)
        total = total + big_rows + jnp.floor((R - big_rows + 0.5) / area) * area
    row_count = total
    down = lax.broadcasted_iota(jnp.int32, (R, 1), 0).astype(jnp.float32)
    across = lax.broadcasted_iota(jnp.int32, (1, R), 1).astype(jnp.float32)

    @pl.loop(0, 6)
    @jax.named_scope("tables")
    def _(v):
        big = cntx[v][0:1, 0:1]
        code_down, ok_down = crop_codes(down, big, R)
        code_across, ok_across = crop_codes(across, big, R)
        code_down = jnp.where(ok_down, code_down, -5000.0)
        code_across = jnp.where(ok_across, code_across, -1.0)
        for k in range(9):
            step = float(32 * (k // 3 - 1) + (k % 3 - 1))
            hit = (code_down + step) == code_across
            Gm[v, pl.ds(k * R, R)] = jnp.where(hit, 1.0, 0.0).astype(jnp.bfloat16)

    _, own_valid = crop_codes(down, cown[0:1, 0:1], R)
    valid = own_valid.astype(jnp.float32)
    drain(aff.at[pl.ds(0, 3)], sF_r)
    loads[10].wait()
    h[...] = abuf[...].astype(jnp.float32)

    def moments(sums):
        center = sums[0] / row_count
        spread = lax.rsqrt(sums[1] / row_count - center * center + EPS)
        return center, spread

    def pairing(b):
        odd = lax.rem(b, 2) == 1
        return jnp.where(odd, x, y), jnp.where(odd, y, x), jnp.where(odd, 1, 2)

    @jax.named_scope("share")
    def share(b, kind, rows):
        turned = rows.T
        rows_to = stage_a if kind == 1 else stage.at[b]
        if kind == 1:
            @pl.when(b > 0)
            def _():
                drain(stage_a.at[pl.ds(0, 2)], sQ_s.at[1])

        odd = lax.rem(b, 2) == 1
        for cc in range(2):
            for xx in range(2):
                for yy in range(2):
                    one, two = jnp.where(odd, xx, yy), jnp.where(odd, yy, xx)
                    for zz in range(4):
                        at = (2 * zz + cc) * 64 + (2 * yy + xx) * 16
                        rows_to[2 * one + cc, 4 * two + zz] = turned[at : at + 16].astype(
                            jnp.bfloat16
                        )
        if kind == 1:
            for half_of_pair in range(2):
                v = 2 * half_of_pair
                caq[b, 1, v + c] = stage_a[v + c]
                swap_copy(
                    stage_a.at[v + 1 - c], caq.at[b, 1, v + c], sQ_s.at[1], sQ_r.at[b, 1], s, bat ^ 1
                ).start()
        else:
            u = 2 * pairing(b)[0] + c
            caq[b, 0, u] = stage[b, u]

            @pl.when(b == 3)
            def _():
                send_share(b)

    def send_share(b):
        mine, _, near = pairing(b)
        u = 2 * mine + c
        for j in range(1, 4):
            swap_copy(
                stage.at[b, u ^ j], caq.at[b, 0, u], sQ_s.at[0], sQ_r.at[b, 0],
                s ^ near if j > 1 else s, bat ^ (j % 2),
            ).start()

    def wait_share(b, kind):
        drain(caq.at[b, kind, pl.ds(0, 2 if kind == 1 else 3)], sQ_r.at[b, kind])

    @jax.named_scope("forward")
    def forward(b):
        with jax.named_scope("whole_here"):

            @pl.when(c == 1)
            def _():
                drain(W.at[b, whole], sJ_r.at[b])

        @pl.when(b == 3)
        def _():
            for early in (2, 1, 0):
                send_share(early)

        hidden = h[...]
        zbuf[...] = jnp.dot(
            hidden.astype(jnp.bfloat16), W[b, 9].reshape(D, D), preferred_element_type=jnp.float32
        )
        z1 = zbuf[...]
        kept = valid * z1
        sums_start(
            2 * b + 1, jnp.sum(kept, 0, keepdims=True), jnp.sum(kept * z1, 0, keepdims=True)
        )
        share(b, 1, hidden)

        @pl.when(b == 2)
        def _():
            rest_z(3)
            gather_first(3, (0, 2))

        gather_second(b)

        @pl.when(b == 0)
        def _():
            gather_first(1, (1, 3))
            relay_z(2)

        @pl.when(b == 1)
        def _():
            gather_first(2)
            relay_whole(2)

        @pl.when(b == 2)
        def _():
            relay_whole(3)

        norms = aff[b]
        center, spread = moments(sums_finish(2 * b + 1))
        gi[b, 0:1] = norms[0:1] * spread
        for i in range(0, R, 64):
            xhat = (zbuf[i : i + 64] - center) * spread
            value, slope = mish_terms(norms[0:1] * xhat + norms[1:2])
            sv[b, 0, i : i + 64] = xhat.astype(sv.dtype)
            sv[b, 1, i : i + 64] = slope.astype(sv.dtype)
            abuf[i : i + 64] = value.astype(jnp.bfloat16)
        mixed = abuf[...]
        gather_last(b)
        for k in range(9):
            Hb[:, k * D : (k + 1) * D] = jnp.dot(
                Gm[c, pl.ds(k * R, R)], mixed, preferred_element_type=jnp.float32
            ).astype(jnp.bfloat16)
        zbuf[...] = jnp.dot(
            Hb[...], W[b, 0:9].reshape(9 * D, D), preferred_element_type=jnp.float32
        )
        z2 = zbuf[...]
        kept = valid * z2
        sums_start(
            2 * b + 2, jnp.sum(kept, 0, keepdims=True), jnp.sum(kept * z2, 0, keepdims=True)
        )
        share(b, 0, mixed.astype(jnp.float32))

        @pl.when(b == 0)
        def _():
            relay_whole(1)
            own_quarter(3)
            start_whole(2)
            start_z(3)

        @pl.when(b == 1)
        def _():
            relay_z(3)
            start_whole(3)

        @pl.when(b == 2)
        def _():
            gather_first(3, (1, 3))

        center, spread = moments(sums_finish(2 * b + 2))
        gi[b, 1:2] = norms[2:3] * spread
        for i in range(0, R, 64):
            xhat = (zbuf[i : i + 64] - center) * spread
            value, slope = mish_terms(norms[2:3] * xhat + norms[3:4])
            sv[b, 2, i : i + 64] = xhat.astype(sv.dtype)
            sv[b, 3, i : i + 64] = slope.astype(sv.dtype)
            h[i : i + 64] = h[i : i + 64] + valid[i : i + 64] * value

    rest_z(0)
    relay_whole(0)
    own_quarter(2)
    gather_first(0, (0, 2))
    relay_z(1)
    start_z(2)
    start_whole(1)
    gather_first(0, (1, 3))
    gather_first(1, (0, 2))
    rest_z(1)
    rest_whole(0)
    psq[...] = jnp.concatenate(sums_finish(0), axis=0)

    @pl.loop(0, 4)
    def _(b):
        forward(b)

        @pl.when(b == 0)
        def _():
            rest_z(2)

        @pl.when(b < 3)
        def _():
            rest_whole(b + 1)

    out_grad_rows = pltpu.make_async_copy(out_grad.at[s], abuf, sL.at[2])
    out_features = pltpu.make_async_copy(h, features.at[0], sO_s.at[0])
    out_features.start()
    out_grad_rows.start()
    out_grad_rows.wait()
    g[...] = abuf[...].astype(jnp.float32)

    @jax.named_scope("close_gather")
    def close_gather():
        drain(aff.at[pl.ds(0, 3)], sF_s)
        drain(st_own.at[pl.ds(0, 11)], sC_s)
        drain(stage_a.at[pl.ds(0, 2)], sQ_s.at[1])

        @pl.when(c == 0)
        def _():
            drain(wown.at[split, pl.ds(0, 3)], sS_s)
            drain(W.at[0, whole, pl.ds(0, 3)], sU_s)

        @pl.when(c == 1)
        def _():
            drain(wown.at[split], sS_s)
            drain(W.at[0, whole, pl.ds(0, 4)], sU_s)

        drain(W.at[:, split, :, pl.ds(0, 3)], sA_s)

        @on_first_core
        def _():
            drain(W.at[:, split, pl.ds(0, 6), s], sZ_s)
            drain(W.at[:, split, :, s], sH_s)
            drain(W.at[:, whole, pl.ds(0, 6)], sV_s)
            drain(W.at[:, whole], sJ_s)

    @jax.named_scope("close_rest")
    def close_rest():
        drain(stage.at[:, pl.ds(0, 3)], sQ_s.at[0])
        drain(dzq.at[:, pl.ds(0, 3)], sX_s)
        drain(dz1q.at[:, 0], sM_s)
        drain(precv, sP_s)
        drain(gsend.at[pl.ds(0, 3)], sO_s.at[3])
        drain(gout.at[:, 0], sY_s)

        @pl.when(c == 0)
        def _():
            drain(zrecv.at[:, pl.ds(0, 2)], sN_s)
            drain(zrecv.at[:, 2], sT_s)

        @pl.when(c == 1)
        def _():
            drain(zs1, sK_s)
            drain(zrecv.at[pl.ds(0, 3), pl.ds(0, 2)], sN_s)
            drain(zrecv.at[pl.ds(0, 3), 2], sT_s)

    CHUNKS = ((0, 3), (3, 4), (7, 2), (9, 1))
    LAST = len(CHUNKS) - 1

    def dz_copy(b, j):
        mine, _, near = pairing(b)
        v = 2 * mine + c
        v = v ^ 2 if j == 3 else v
        ref = dzq.at[b, v]
        return swap_copy(
            ref, ref, sX_s, sX_r.at[b, 0 if j == 2 else 1], s ^ near if j == 2 else s, bat if j == 2 else bat ^ 1
        )

    def send_dz(b):
        dz_copy(b, 2).start()
        dz_copy(b, 1).start()

    @jax.named_scope("forward_dz")
    def forward_dz(b):
        v = (2 * pairing(b)[0] + c) ^ 2
        drain(dzq.at[b, v], sX_r.at[b, 0])
        dz_copy(b, 3).start()

    @jax.named_scope("wait_dz")
    def wait_dz(b):
        drain(dzq.at[b, pl.ds(0, 2)], sX_r.at[b, 1])

    def dz_one_copy(b):
        ref = dz1q.at[b, c]
        return swap_copy(ref, ref, sM_s, sM_r.at[b], s, bat ^ 1)

    def point_copy(b):
        mine, _, near = pairing(b)
        return swap_copy(
            pgrad.at[b, 1 - mine], precv.at[b], sP_s, sP_r.at[b], s ^ near, bat
        )

    def y_copy(b, i):
        at, size = CHUNKS[i]
        return swap_copy(
            gout.at[b, 1 - pairing(b)[1], pl.ds(at, size)], yrecv.at[b, pl.ds(at, size)],
            sY_s, sY_r.at[b, i], s ^ 3 ^ pairing(b)[2], bat,
        )

    def grad_tap(b, k, left, right):
        part = jnp.dot(left, right, preferred_element_type=jnp.float32).astype(jnp.bfloat16)
        for yy in range(2):
            gout[b, yy, k] = part[64 * yy : 64 * yy + 64].reshape(4, 16, D)

    @jax.named_scope("grad_spatial")
    def grad_spatial(b):
        wait_share(b, 0)
        wait_dz(b)
        mine, _, near = pairing(b)
        tables = [jnp.where(mine == v // 2, 0, 2 * near) + v % 2 for v in range(4)]
        right = dzq[b].reshape(4 * R, D)
        for k in range(9):
            left = [
                lax.dot_general(
                    caq[b, 0, v].reshape(128, R), Gm[tables[v], pl.ds(k * R, R)], NT,
                    preferred_element_type=jnp.float32,
                ).astype(jnp.bfloat16)
                for v in range(4)
            ]
            grad_tap(b, k, jnp.concatenate(left, axis=1), right)
            for i in range(LAST):
                if k + 1 == sum(CHUNKS[i]):
                    y_copy(b, i).start()

    @jax.named_scope("grad_point")
    def grad_point(b):
        wait_share(b, 1)
        drain(dz1q.at[b, 1 - c], sM_r.at[b])
        left = jnp.concatenate(
            [
                jnp.concatenate([caq[b, 1, 2 * v + k].reshape(128, R) for v in range(2)], axis=0)
                for k in range(2)
            ],
            axis=1,
        )
        part = jnp.dot(
            left, dz1q[b].reshape(2 * R, D), preferred_element_type=jnp.float32
        ).astype(jnp.bfloat16)
        pgrad[b] = part.reshape(2, 2, 4, 16, D)
        point_copy(b).start()

    @jax.named_scope("pair_point")
    def pair_point(b):
        point_copy(b).wait_recv()
        mine = pairing(b)[0]
        for yy in range(2):
            gout[b, yy, 9] = (
                pgrad[b, mine, yy].astype(jnp.float32) + precv[b, yy].astype(jnp.float32)
            ).astype(jnp.bfloat16)
        y_copy(b, LAST).start()

    def core_copy(b, i):
        at, size = CHUNKS[i]
        return swap_copy(
            yrecv.at[b, pl.ds(at, size)], zs1.at[pl.ds(at, size)],
            sK_s, sK_r.at[i], s, bat ^ 1,
        )

    @jax.named_scope("reduce_plane")
    def reduce_plane(b, i):
        at, size = CHUNKS[i]
        y_copy(b, i).wait_recv()
        rest = pairing(b)[1]
        for k in range(at, at + size):
            yrecv[b, k] = (
                yrecv[b, k].astype(jnp.float32) + gout[b, rest, k].astype(jnp.float32)
            ).astype(jnp.bfloat16)

        if b == 3:

            @pl.when(c == 1)
            def _():
                core_copy(b, i).start()

    def carriers(b, work):
        if b == 3:
            pl.when(c == 0)(functools.partial(work, (0, 1)))
        else:
            work((0,))

    def z_near(b, i, cc, slot):
        at, size = CHUNKS[i]
        return swap_copy(
            (yrecv.at[b], zs1)[cc].at[pl.ds(at, size), z ^ (3 if slot else 1)],
            zrecv.at[b + cc, slot, pl.ds(at, size)], sN_s, sN_r.at[b, i], s, bat ^ 2,
        )

    def z_far(b, i, cc):
        at, size = CHUNKS[i]
        return swap_copy(
            zrecv.at[b + cc, 1, pl.ds(at, size)], zrecv.at[b + cc, 2, pl.ds(at, size)],
            sT_s, sT_r.at[b, i], s, bat ^ 4,
        )

    def near_like(b, i, parts):
        at, size = CHUNKS[i]
        return zrecv.at[pl.ds(b, len(parts)), pl.ds(0, 2), pl.ds(at, size)]

    def far_like(b, i, parts):
        at, size = CHUNKS[i]
        return zrecv.at[pl.ds(b, len(parts)), 2, pl.ds(at, size)]

    @jax.named_scope("reduce_near")
    def reduce_near(b, i):
        def work(parts):
            if b == 3:
                core_copy(b, i).wait_recv()
            for slot in (1, 0):
                for cc in parts:
                    z_near(b, i, cc, slot).start()

        carriers(b, work)

    @jax.named_scope("reduce_far")
    def reduce_far(b, i):
        at, size = CHUNKS[i]

        def work(parts):
            drain(near_like(b, i, parts), sN_r.at[b, i])
            for cc in parts:
                mine = (yrecv.at[b], zs1)[cc]
                for k in range(at, at + size):
                    zrecv[b + cc, 1, k] = (
                        zrecv[b + cc, 1, k].astype(jnp.float32) + mine[k, z ^ 2].astype(jnp.float32)
                    ).astype(jnp.bfloat16)
                z_far(b, i, cc).start()

        carriers(b, work)

    def deliver(b, i, cc, section, core):
        at, size = CHUNKS[i]
        swap_copy(
            zrecv.at[b + cc, 0, pl.ds(at, size)], gfin.at[pl.ds(at, size), s],
            sG_s, sG_r.at[s], section, 2 * z + core,
        ).start()

    def send_squares(b):
        def to(j):
            return swap_copy(
                sq_own.at[b], sq_in.at[s, bat], sW_s, sW_r, b, bat ^ j
            )

        sq_own[b] = jnp.concatenate([fold(sq_acc[b, 1:2]), fold(sq_acc[b, 0:1])], axis=0)

        @pl.when(b != s)
        def _():
            to(0).start()

        @pl.when(b == s)
        def _():
            sq_in[s, bat] = sq_own[b]

        for j in range(1, 8):
            to(j).start()

    @jax.named_scope("finish")
    def finish(b, i):
        at, size = CHUNKS[i]

        def work(parts):
            drain(far_like(b, i, parts), sT_r.at[b, i])
            squares = jnp.zeros((1, D), jnp.float32)
            for cc in parts:
                mine = (yrecv.at[b], zs1)[cc]
                for k in range(at, at + size):
                    done = (
                        zrecv[b + cc, 0, k].astype(jnp.float32)
                        + zrecv[b + cc, 2, k].astype(jnp.float32)
                        + mine[k, z].astype(jnp.float32)
                    ).astype(jnp.bfloat16)
                    zrecv[b + cc, 0, k] = done
                    squares += square(done.astype(jnp.float32))

                @pl.when(b != s)
                def _():
                    deliver(b, i, cc, b, cc if b == 3 else c)

                @pl.when(b == s)
                def _():
                    if cc == 0:
                        for k in range(at, at + size):
                            gfin[k, s] = zrecv[b, 0, k]
                    else:
                        deliver(b, i, 1, s, 1)

            row = 1 if i == LAST else 0
            sq_acc[b, row : row + 1] = squares + (0.0 if i in (0, LAST) else sq_acc[b, row : row + 1])
            if i == LAST:
                send_squares(b)

        carriers(b, work)

    @jax.named_scope("backward")
    def backward(bi):
        b = 3 - bi
        e = 9 + 2 * bi
        u = 2 * pairing(b)[0] + c
        first_sum = jnp.zeros((1, D), jnp.float32)
        second_sum = jnp.zeros((1, D), jnp.float32)
        for i in range(0, R, 64):
            du = valid[i : i + 64] * g[i : i + 64] * sv[b, 3, i : i + 64].astype(jnp.float32)
            zbuf[i : i + 64] = du
            first_sum += jnp.sum(du, 0, keepdims=True)
            second_sum += jnp.sum(du * sv[b, 2, i : i + 64].astype(jnp.float32), 0, keepdims=True)
        sums_start(e, first_sum, second_sum)

        @pl.when(bi == 0)
        def _():
            close_gather()

        @pl.when(bi == 3)
        def _():
            reduce_near(3, 1)

        @pl.when(bi > 0)
        def _():
            forward_dz(b + 1)
            grad_point(b + 1)

        @pl.when(bi == 2)
        def _():
            pair_point(3)

        @pl.when(bi == 3)
        def _():
            reduce_plane(3, 2)
            reduce_far(3, 0)

        total_first, total_second = sums_finish(e)
        for i in range(0, R, 64):
            xhat = sv[b, 2, i : i + 64].astype(jnp.float32)
            inner = zbuf[i : i + 64] - valid[i : i + 64] * (
                (total_first + xhat * total_second) / row_count
            )
            dzq[b, u, i : i + 64] = (gi[b, 1:2] * inner).astype(jnp.bfloat16)
        send_dz(b)
        gsend[b, 2:3] = total_second
        gsend[b, 3:4] = total_first
        d_two = dzq[b, u]
        for k in range(9):
            Hb[:, k * D : (k + 1) * D] = jnp.dot(
                Gm[c, pl.ds((8 - k) * R, R)], d_two, preferred_element_type=jnp.float32
            ).astype(jnp.bfloat16)
        mixed = None
        for k in range(9):
            part = lax.dot_general(
                Hb[:, k * D : (k + 1) * D], W[b, k].reshape(D, D), NT,
                preferred_element_type=jnp.float32,
            )
            mixed = part if mixed is None else mixed + part
        zbuf[...] = mixed
        first_sum = jnp.zeros((1, D), jnp.float32)
        second_sum = jnp.zeros((1, D), jnp.float32)
        for i in range(0, R, 64):
            du = zbuf[i : i + 64] * sv[b, 1, i : i + 64].astype(jnp.float32)
            zbuf[i : i + 64] = du
            first_sum += jnp.sum(du, 0, keepdims=True)
            second_sum += jnp.sum(du * sv[b, 0, i : i + 64].astype(jnp.float32), 0, keepdims=True)
        sums_start(e + 1, first_sum, second_sum)

        @pl.when(bi == 2)
        def _():
            reduce_plane(3, 0)
            reduce_near(3, 0)

        @pl.when(bi == 3)
        def _():
            reduce_near(3, 2)
            reduce_far(3, 1)
            reduce_plane(2, 0)
            reduce_near(2, 0)

        @pl.when(bi > 0)
        def _():
            grad_spatial(b + 1)

        @pl.when(bi == 2)
        def _():
            reduce_plane(3, 1)

        @pl.when(bi == 3)
        def _():
            reduce_plane(3, 3)
            reduce_plane(2, 1)
            reduce_near(2, 1)

        total_first, total_second = sums_finish(e + 1)
        for i in range(0, R, 64):
            xhat = sv[b, 0, i : i + 64].astype(jnp.float32)
            inner = zbuf[i : i + 64] - valid[i : i + 64] * (
                (total_first + xhat * total_second) / row_count
            )
            dz1q[b, c, i : i + 64] = (gi[b, 0:1] * inner).astype(jnp.bfloat16)
        dz_one_copy(b).start()
        gsend[b, 0:1] = total_second
        gsend[b, 1:2] = total_first
        g[...] = g[...] + lax.dot_general(
            dz1q[b, c], W[b, 9].reshape(D, D), NT, preferred_element_type=jnp.float32
        )

        @pl.when(b == s)
        def _():
            gaff[s] = gsend[b]

        @pl.when(b != s)
        def _():
            swap_copy(gsend.at[b], gaff.at[s], sO_s.at[3], sO_r, b, bat).start()

    @pl.loop(0, 4)
    def _(bi):
        backward(bi)

    out_grad_in = pltpu.make_async_copy(g, in_grad.at[0], sO_s.at[1])
    out_grad_in.start()

    reduce_near(3, 3)
    forward_dz(0)
    pair_point(2)
    reduce_far(2, 0)
    reduce_far(3, 2)
    reduce_plane(2, 2)
    reduce_near(2, 2)
    grad_spatial(0)
    reduce_far(2, 1)
    grad_point(0)
    reduce_far(3, 3)
    pair_point(1)
    finish(3, 0)
    reduce_plane(2, 3)
    reduce_near(2, 3)
    reduce_plane(1, 0)
    reduce_near(1, 0)
    finish(3, 1)
    reduce_far(2, 2)
    finish(2, 0)
    reduce_plane(1, 1)
    reduce_near(1, 1)
    finish(3, 2)
    reduce_far(1, 0)
    reduce_plane(1, 2)
    reduce_near(1, 2)
    finish(3, 3)
    finish(2, 1)
    pair_point(0)
    reduce_far(2, 3)
    reduce_plane(0, 0)
    reduce_near(0, 0)
    reduce_far(1, 1)
    reduce_plane(1, 3)
    reduce_near(1, 3)
    finish(2, 2)
    finish(1, 0)
    reduce_far(1, 2)
    reduce_plane(0, 1)
    reduce_near(0, 1)
    reduce_plane(0, 2)
    reduce_near(0, 2)
    reduce_far(0, 0)
    reduce_plane(0, 3)
    reduce_near(0, 3)
    finish(2, 3)
    finish(1, 1)
    reduce_far(1, 3)
    reduce_far(0, 1)
    finish(0, 0)
    finish(1, 2)
    reduce_far(0, 2)
    reduce_far(0, 3)
    finish(1, 3)
    finish(0, 1)
    close_rest()
    finish(0, 2)
    finish(0, 3)
    for d in range(1, 4):
        drain(gfin.at[:, s ^ d], sG_r.at[s ^ d])

    @pl.when((c == 1) & (s == 3))
    def _():
        drain(gfin.at[:, s], sG_r.at[s])

    grads_out = pltpu.make_async_copy(gfin, grads, sO_s.at[2])
    grads_out.start()

    drain(gaff.at[pl.ds(0, 3)], sO_r)
    affine_out[...] = gaff[0] + gaff[1] + gaff[2] + gaff[3]
    squares_in = sq_in.reshape(32, 2, 128)

    @pl.when(s != 3)
    def _():
        drain(squares_in.at[pl.ds(0, 31)], sW_r)

    @pl.when((s == 3) & (c == 0))
    def _():
        drain(squares_in.at[pl.ds(0, 15)], sW_r)

    @pl.when((s == 3) & (c == 1))
    def _():
        drain(squares_in.at[pl.ds(0, 16)], sW_r)

    totals_out[...] = jnp.concatenate(
        [fold(psq[...]), jnp.sum(squares_in[...], axis=0), jnp.zeros((4, 128), jnp.float32)], axis=0
    )

    with jax.named_scope("close_last"):
        sums_close(0)
        sums_close(1)

        @pl.when(c == 0)
        def _():
            drain(zrecv.at[pl.ds(0, 4), 0], sG_s)

        @pl.when(c == 0)
        def _():
            drain(squares_in.at[pl.ds(0, 31)], sW_s)

        @pl.when((c == 1) & (s == 3))
        def _():
            drain(zrecv.at[pl.ds(0, 3), 0], sG_s)
            drain(squares_in.at[pl.ds(0, 24)], sW_s)

        @pl.when((c == 1) & (s != 3))
        def _():
            drain(zrecv.at[pl.ds(0, 2), 0], sG_s)
            drain(squares_in.at[pl.ds(0, 23)], sW_s)

    with jax.named_scope("close_outputs"):
        grads_out.wait()
        out_features.wait()
        out_grad_in.wait()


def lars_kernel(
    feat, ing, grads_in, totals_in, affine_in, w_point, w_spatial, norm_in, mom_point, mom_spatial, mom_norm,
    features, in_grad, new_point, new_spatial, new_norm, new_mom_point, new_mom_spatial, new_mom_norm,
    P, M, G, feat_rows, grad_rows, totals, affine_grad, affine, affine_mom, sem, out_sem,
):
    THIRDS = 3
    small = [
        (totals_in, totals), (affine_in, affine_grad), (norm_in.at[0], affine), (mom_norm.at[0], affine_mom),
        (w_point.at[0], P.at[9]), (mom_point.at[0], M.at[9]), (grads_in.at[9], G.at[9]),
    ]
    large = []
    for i in range(THIRDS):
        taps = pl.ds(3 * i, 3)
        large += [
            (grads_in.at[taps], G.at[taps]), (w_spatial.at[0, taps], P.at[taps]),
            (mom_spatial.at[0, taps], M.at[taps]),
        ]
    rows = [(feat, feat_rows), (ing, grad_rows)]
    loads = [
        pltpu.make_async_copy(a, b, sem.at[i]) for i, (a, b) in enumerate(small + large + rows)
    ]
    for load in loads:
        load.start()
    for load in loads[: len(small)]:
        load.wait()
    D = affine.shape[1]
    rate = BASE_RATE * (STEP + 1) / WARMUP
    point_sq, spatial_sq, gpoint_sq, gspatial_sq = [
        jnp.sum(totals[i : i + 1], axis=1, keepdims=True) for i in range(4)
    ]
    step_point = rate * TRUST_COEF * jnp.sqrt(point_sq) / (jnp.sqrt(gpoint_sq) + EPS_NORM)
    step_spatial = rate * TRUST_COEF * jnp.sqrt(spatial_sq) / (jnp.sqrt(gspatial_sq) + EPS_NORM)
    outs = []

    def store(source, target):
        outs.append(pltpu.make_async_copy(source, target, out_sem.at[len(outs)]))
        outs[-1].start()

    def move(k, step):
        moved = MOMENTUM * M[k] + step * G[k].astype(jnp.float32).reshape(64, D)
        M[k] = moved
        P[k] = P[k] - moved

    for i in range(THIRDS):
        for load in loads[len(small) + 3 * i :][:3]:
            load.wait()
        for k in range(3 * i, 3 * i + 3):
            move(k, step_spatial)
        taps = pl.ds(3 * i, 3)
        store(M.at[taps], new_mom_spatial.at[0, taps])
        store(P.at[taps], new_spatial.at[0, taps])
    move(9, step_point)
    store(M.at[9], new_mom_point.at[0])
    store(P.at[9], new_point.at[0])
    for load, source, target in zip(loads[-2:], (feat_rows, grad_rows), (features, in_grad)):
        load.wait()
        store(source, target)
    grad = affine_grad[0:4]
    old = affine[...]
    affine_sq = jnp.sum(old * old, axis=1, keepdims=True)
    gaffine_sq = jnp.sum(grad * grad, axis=1, keepdims=True)
    trust = TRUST_COEF * jnp.sqrt(affine_sq) / (jnp.sqrt(gaffine_sq) + EPS_NORM)
    moved = MOMENTUM * affine_mom[...] + rate * trust * grad
    affine_mom[...] = moved
    affine[...] = old - moved
    store(affine_mom, new_mom_norm.at[0])
    store(affine, new_norm.at[0])
    for copy in outs:
        copy.wait()


def train_step(images, crop, w_point, w_spatial, norm_params, mom_point, mom_spatial, mom_norm, out_grad):
    R, D = images.shape[1:]
    f32, bf16 = jnp.float32, jnp.bfloat16
    dma = pltpu.SemaphoreType.DMA
    anywhere = pl.BlockSpec(memory_space=pl.ANY)
    vmem = pl.BlockSpec(memory_space=pltpu.VMEM)
    hbm = pl.BlockSpec(memory_space=pltpu.HBM)
    smem = pl.BlockSpec(memory_space=pltpu.SMEM)
    V = pltpu.VMEM
    scratch = dict(
        W=V((4, TAPS, 8, 4, 16, D), bf16), wown=V((TAPS, 4, 16, D), bf16),
        F=V((3 * R, D), f32),
        sv=V((4, 4, R, D), bf16), gi=V((4, 8, D), f32),
        abuf=V((R, D), bf16),
        Gm=V((6, 9 * R, R), bf16), caq=V((4, 2, 4, 8, 16, R), bf16),
        stage=V((4, 4, 8, 16, R), bf16), stage_a=V((4, 8, 16, R), bf16), Hb=V((R, 9 * D), bf16),
        dzq=V((4, 4, R, D), bf16), dz1q=V((4, 2, R, D), bf16),
        pgrad=V((4, 2, 2, 4, 16, D), bf16), precv=V((4, 2, 4, 16, D), bf16),
        gout=V((4, 2, TAPS, 4, 16, D), bf16), yrecv=V((4, TAPS, 4, 16, D), bf16),
        zs1=V((TAPS, 4, 16, D), bf16), zrecv=V((5, 3, TAPS, 16, D), bf16),
        gfin=V((TAPS, 4, 16, D), bf16),
        sq_in=V((4, 8, 2, 128), f32), sq_own=V((4, 2, 128), f32), sq_acc=V((4, 8, D), f32), psq=V((2, D), f32),
        aff=V((4, 8, D), f32), gaff=V((4, 8, D), f32), gsend=V((4, 8, D), f32),
        st_in=V((17, 8, 128), f32), st_own=V((17, 8, 128), f32), st_all=V((17, 4, 8, 128), f32),
        cnt=V((8, 8, 128), f32), cntx=V((6, 8, 128), f32), cown=V((8, 128), f32),
        sL=dma((3,)), sS_s=dma, sS_r=dma((4,)), sU_s=dma, sU_r=dma((4,)), sV_s=dma, sV_r=dma((4, 2)),
        sJ_s=dma, sJ_r=dma((4,)), sZ_s=dma, sZ_r=dma((4, 4)),
        sH_s=dma, sH_r=dma((4, 4)), sA_s=dma, sA_r=dma((4, 4)),
        sB_r=dma((4, 2)), sD_r=dma((4,)),
        sE_in_s=dma((2,)), sE_in_r=dma((2,)), sE_s=dma((2,)), sE_r=dma((2,)),
        sC_s=dma, sC_r=dma((2,)), sF_s=dma, sF_r=dma,
        sQ_s=dma((2,)), sQ_r=dma((4, 2)), sX_s=dma, sX_r=dma((4, 2)), sM_s=dma, sM_r=dma((4,)), sP_s=dma, sP_r=dma((4,)),
        sW_s=dma, sW_r=dma,
        sY_s=dma, sY_r=dma((4, 4)), sK_s=dma, sK_r=dma((4,)),
        sN_s=dma, sN_r=dma((4, 4)), sT_s=dma, sT_r=dma((4, 4)), sG_s=dma, sG_r=dma((4,)),
        sO_s=dma((4,)), sO_r=dma,
    )
    shape = jax.ShapeDtypeStruct
    feat, ing, grads, totals, affine_grad = pl.pallas_call(
        train_kernel,
        out_shape=(
            shape((1, R, D), f32), shape((1, R, D), f32), shape((TAPS, 4, 16, D), bf16),
            shape((8, 128), f32), shape((8, D), f32),
        ),
        in_specs=[anywhere, smem, anywhere, anywhere, vmem, anywhere],
        out_specs=(anywhere, anywhere, anywhere, vmem, vmem),
        scratch_shapes=list(scratch.values()),
        compiler_params=pltpu.CompilerParams(
            collective_id=0, has_side_effects=True, vmem_limit_bytes=64 * 1024 * 1024
        ),
    )(images, crop.T, w_point, w_spatial, norm_params, out_grad)
    return pl.pallas_call(
        lars_kernel,
        out_shape=(
            shape((1, R, D), f32), shape((1, R, D), f32),
            shape(w_point.shape, f32), shape(w_spatial.shape, f32), shape(norm_params.shape, f32),
            shape(w_point.shape, f32), shape(w_spatial.shape, f32), shape(norm_params.shape, f32),
        ),
        in_specs=[hbm] * 11,
        out_specs=(hbm,) * 8,
        scratch_shapes=[
            V((TAPS, 64, D), f32), V((TAPS, 64, D), f32), V((TAPS, 4, 16, D), bf16), V((1, R, D), f32),
            V((1, R, D), f32), V((8, 128), f32), V((8, D), f32), V((4, D), f32), V((4, D), f32), dma((18,)), dma((12,)),
        ],
        compiler_params=pltpu.CompilerParams(vmem_limit_bytes=64 * 1024 * 1024),
    )(feat, ing, grads, totals, affine_grad, w_point, w_spatial, norm_params, mom_point, mom_spatial, mom_norm)


def solution(mesh):
    tuned = mesh.shape["section"] == 4 and mesh.shape["batch"] == 8
    return jax.shard_map(
        train_step if tuned else on_device,
        mesh=mesh,
        in_specs=(
            P(None, "batch", None),
            P(None, "batch"),
            P("section", "batch", None),
            P("section", None, "batch", None),
            P("section", None, None),
            P("section", "batch", None),
            P("section", None, "batch", None),
            P("section", None, None),
            P(None, "batch", None),
        ),
        out_specs=(
            P("section", "batch", None),
            P("section", "batch", None),
            P("section", "batch", None),
            P("section", None, "batch", None),
            P("section", None, None),
            P("section", "batch", None),
            P("section", None, "batch", None),
            P("section", None, None),
        ),
        check_vma=False,
    )
```
